32 devices in a mesh: ctx: 8 (over z, y), fsdp: 4 (over x, core).
Axes of the slice: x: 2, y: 2, z: 4, core: 2. Of those that a mesh axis runs over, the one named last changes fastest.
Arguments:
- tokens: bfloat16 [4, 1024, 2560], P('fsdp', 'ctx'), may hold values from -6 to 6
- doc_bounds: int32 [4, 2], P('fsdp'), may hold values from 1 to 1023, as said below
- cotangent: bfloat16 [4, 1024, 2560], P('fsdp', 'ctx'), may hold values from -6 to 6
- norm_one: float32 [2560], replicated, may hold values from 0.25 to 1.75
- query_weight: bfloat16 [2560, 2560], P('fsdp'), may hold values from -0.125 to 0.125
- keyval_weight: bfloat16 [2560, 512], P('fsdp'), may hold values from -0.125 to 0.125
- out_weight: bfloat16 [2560, 2560], P('fsdp'), may hold values from -1 to 1
- norm_two: float32 [2560], replicated, may hold values from 0.25 to 1.75
- gate_up_weight: bfloat16 [2560, 15360], P('fsdp'), may hold values from -0.125 to 0.125
- down_weight: bfloat16 [7680, 2560], P('fsdp'), may hold values from -0.125 to 0.125
Outputs:
- result: bfloat16 [4, 1024, 2560], P('fsdp', 'ctx')
- input_grad: bfloat16 [4, 1024, 2560], P('fsdp', 'ctx')
- norm_one_grad: float32 [2560], P(('ctx', 'fsdp'))
- query_grad: float32 [2560, 2560], P('ctx', 'fsdp')
- keyval_grad: float32 [2560, 512], P('ctx', 'fsdp')
- out_grad: float32 [2560, 2560], P('ctx', 'fsdp')
- norm_two_grad: float32 [2560], P(('ctx', 'fsdp'))
- gate_up_grad: float32 [2560, 15360], P('ctx', 'fsdp')
- down_grad: float32 [7680, 2560], P('ctx', 'fsdp')
The draws below stay inside these ranges and needn't reach their ends.
Inputs may be any that keep to these rules, and one draw needn't show every extreme that they name: `doc_bounds`: row s holds a and b: its documents are tokens [0, a), [a, b) and [b, 1024), with 1 <= a < 128 and 896 < b < 1024.
All inputs are finite; a program needn't handle non-finite values.
Results may differ from the reference program's by a relative error of at most 0.022.
Values may be sent and summed in bfloat16 or wider, within the bound.
A program may use at most 576 MiB of HBM per device.

```python
import jax
import jax.numpy as jnp
from jax import lax

D = 2560
H = 10
HD = 256
FF = 7680
WINDOW = 2048
TOK_DEV = 128
SEQS = 4
LENGTH = 1024


def draw_doc_bounds(key, part):
    key = jax.random.fold_in(key, 11)
    early_key, late_key = jax.random.split(key)
    opening = jax.random.randint(early_key, (SEQS, 1), 1, TOK_DEV)
    closing = jax.random.randint(late_key, (SEQS, 1), LENGTH - TOK_DEV + 1, LENGTH)
    return jnp.concatenate([opening, closing], axis=1).astype(jnp.int32)


def levels(rng, shape, cuts, least, top_value):
    level, own = 1.0, jax.random.fold_in(rng, 6)
    for axis_at, parts in cuts:
        draws = jnp.exp(jax.random.uniform(jax.random.fold_in(own, axis_at), (parts,), jnp.float32, least / len(cuts), top_value / len(cuts)))
        level = level * jnp.repeat(draws, shape[axis_at] // parts).reshape([-1 if axis == axis_at else 1 for axis in range(len(shape))])
    return level


def normal_values(stream_key, shape, scale, reach, shards=(), kind=jnp.bfloat16):
    level = levels(stream_key, shape, shards, -0.22, 0.18) if shards else 1.0
    entries = jax.random.normal(stream_key, shape, jnp.float32) * scale * level
    return jnp.minimum(jnp.maximum(entries, -reach), reach).astype(kind)


def setup_inputs(seed: int = 0) -> dict:
    key_list = jax.random.split(jax.random.key(seed), 11)
    return {
        "tokens": normal_values(key_list[0], (SEQS, LENGTH, D), 1.0, 6.0, ((0, 4), (1, 8))),
        "doc_bounds": draw_doc_bounds(jax.random.fold_in(key_list[10], 71), 0),
        "cotangent": normal_values(key_list[2], (SEQS, LENGTH, D), 1.0, 6.0, ((0, 4), (1, 8))),
        "norm_one": jnp.clip(1.0 + 0.15 * jax.random.normal(key_list[3], (D,), jnp.float32), 0.25, 1.75),
        "query_weight": normal_values(key_list[4], (D, H * HD), D ** -0.5, 0.125, ((0, 4),)),
        "keyval_weight": normal_values(key_list[5], (D, 2 * HD), D ** -0.5, 0.125, ((0, 4),)),
        "out_weight": normal_values(key_list[6], (H * HD, D), (H * HD // 64) ** -0.5, 1.0, ((0, 4),)),
        "norm_two": jnp.clip(1.0 + 0.15 * jax.random.normal(key_list[7], (D,), jnp.float32), 0.25, 1.75),
        "gate_up_weight": normal_values(key_list[8], (D, 2 * FF), D ** -0.5, 0.125, ((0, 4),)),
        "down_weight": normal_values(key_list[9], (FF, D), (FF // 4) ** -0.5, 0.125, ((0, 4),)),
    }


@jax.custom_vjp
def low(v):
    return lax.optimization_barrier(v.astype(jnp.bfloat16)).astype(jnp.float32)

@jax.custom_vjp
def low_back(v):
    return v

def low_keep(v):
    return (low(v), None)

def low_pass(kept, grad):
    return (grad,)

def back_keep(v):
    return (v, None)

def back_low(kept, grad):
    return (low(grad),)
low.defvjp(low_keep, low_pass)
low_back.defvjp(back_keep, back_low)
epsilon = 1e-06
precise = lax.Precision.HIGHEST

def rms_norm(values, gain):
    return values * lax.rsqrt(lax.optimization_barrier(jnp.mean(values * values, axis=-1, keepdims=True)) + epsilon) * gain

def frequencies(quarter):
    return 10000.0 ** (-jnp.arange(quarter, dtype=jnp.float32) / quarter)

def rotate(values, angles):
    quarter = angles.shape[-1]
    cosine = jnp.cos(angles)[:, None, :]
    sine = jnp.sin(angles)[:, None, :]
    former = values[..., :quarter]
    latter = values[..., quarter:2 * quarter]
    return jnp.concatenate([former * cosine - latter * sine, latter * cosine + former * sine, values[..., 2 * quarter:]], axis=-1)

def documents(index, bounds):
    return (index >= bounds[0]).astype(jnp.int32) + (index >= bounds[1]).astype(jnp.int32)

def rotary_angles(index, bounds):
    member = documents(index, bounds)
    opening = jnp.where(member == 0, 0, jnp.where(member == 1, bounds[0], bounds[1])).astype(jnp.int32)
    return (index - opening).astype(jnp.float32)[:, None] * frequencies(HD // 4)[None, :]

def visible(query_index, key_index, bounds):
    apart = query_index[:, None] - key_index[None, :]
    same_doc = documents(query_index, bounds)[:, None] == documents(key_index, bounds)[None, :]
    return (apart >= 0) & (apart < WINDOW) & (key_index[None, :] >= 0) & same_doc

def attend(queries, keyval, bounds):
    length = queries.shape[0]
    block_rows = 512 if length % 512 == 0 else length
    padded = jnp.concatenate([jnp.zeros((WINDOW, keyval.shape[1]), jnp.float32), keyval], axis=0)

    def one_block(offset):
        query_rows = lax.dynamic_slice_in_dim(queries, offset, block_rows, 0)
        window = lax.dynamic_slice_in_dim(padded, offset, WINDOW + block_rows, 0)
        query_index = offset + jnp.arange(block_rows, dtype=jnp.int32)
        key_index = offset - WINDOW + jnp.arange(WINDOW + block_rows, dtype=jnp.int32)
        allowed = visible(query_index, key_index, bounds)
        scores = low_back(jnp.einsum('qhd,kd->hqk', query_rows, window[:, :HD], precision=precise))
        scores = jnp.where(allowed[None], scores, -1e+30)
        peak_score = lax.optimization_barrier(jnp.max(scores, axis=-1, keepdims=True))
        weights = jnp.exp(scores - peak_score)
        weights = weights / lax.optimization_barrier(jnp.sum(weights, axis=-1, keepdims=True))
        return jnp.einsum('hqk,kd->qhd', low(weights), window[:, HD:], precision=precise)
    offsets = jnp.arange(length // block_rows, dtype=jnp.int32) * block_rows
    mixed = lax.map(jax.checkpoint(one_block), offsets)
    return mixed.reshape(length, queries.shape[1] * HD)

def layer(source, bounds, norm_one, query_weight, keyval_weight, out_weight, norm_two, gate_up_weight, down_weight):
    length = source.shape[0]
    index = jnp.arange(length, dtype=jnp.int32)
    angles = rotary_angles(index, bounds)
    normed = low(rms_norm(source, norm_one))
    query_linear = low_back(jnp.dot(normed, query_weight, precision=precise))
    keyval_linear = low_back(jnp.dot(normed, keyval_weight, precision=precise))
    queries = low(rotate(query_linear.reshape(length, H, HD), angles) * HD ** (-0.5))
    key_rot = rotate(keyval_linear[:, None, :HD], angles)[:, 0]
    keyval = low(jnp.concatenate([key_rot, keyval_linear[:, HD:]], axis=1))
    mixed = low(low_back(attend(queries, keyval, bounds)))
    middle = source + low_back(jnp.dot(mixed, out_weight, precision=precise))
    normed_two = low(rms_norm(middle, norm_two))
    projected = low_back(jnp.dot(normed_two, gate_up_weight, precision=precise))
    hidden = low(jax.nn.gelu(projected[:, :FF], approximate=True) * projected[:, FF:])
    return middle + low_back(jnp.dot(hidden, down_weight, precision=precise))

def reference(tokens, doc_bounds, cotangent, norm_one, query_weight, keyval_weight, out_weight, norm_two, gate_up_weight, down_weight):
    params = tuple((weight.astype(jnp.float32) for weight in (norm_one, query_weight, keyval_weight, out_weight, norm_two, gate_up_weight, down_weight)))

    def one_sequence(running, item):
        seq_tokens, seq_bounds, seq_cotangent = item

        def forward(source, *weights):
            return layer(source, seq_bounds, *weights)
        outputs, pullback = jax.vjp(forward, seq_tokens.astype(jnp.float32), *params)
        gradients = pullback(seq_cotangent.astype(jnp.float32))
        running = tuple((old + new for old, new in zip(running, gradients[1:])))
        return (running, (outputs.astype(jnp.bfloat16), gradients[0].astype(jnp.bfloat16)))
    zeros = tuple((jnp.zeros(weight.shape, jnp.float32) for weight in params))
    running, (result, input_grad) = lax.scan(one_sequence, zeros, (tokens, doc_bounds, cotangent))
    return (result, input_grad, running[0], running[1], running[2], running[3], running[4], running[5], running[6])
```

```python
import jax
import jax.numpy as jnp
from jax import lax
from jax.sharding import PartitionSpec as P

HD = 256
WINDOW = 2048


epsilon = 1e-06


def rms_norm(values, gain):
    return values * lax.rsqrt(jnp.mean(values * values, axis=-1, keepdims=True) + epsilon) * gain


def frequencies(quarter):
    return 10000.0 ** (-jnp.arange(quarter, dtype=jnp.float32) / quarter)


def rotate(values, angles):
    quarter = angles.shape[-1]
    cosine = jnp.cos(angles)[:, None, :]
    sine = jnp.sin(angles)[:, None, :]
    former = values[..., :quarter]
    latter = values[..., quarter : 2 * quarter]
    return jnp.concatenate(
        [
            former * cosine - latter * sine,
            latter * cosine + former * sine,
            values[..., 2 * quarter :],
        ],
        axis=-1,
    )


def documents(index, bounds):
    return (index >= bounds[0]).astype(jnp.int32) + (index >= bounds[1]).astype(jnp.int32)


def rotary_angles(index, bounds):
    member = documents(index, bounds)
    opening = jnp.where(member == 0, 0, jnp.where(member == 1, bounds[0], bounds[1]))
    return (index - opening).astype(jnp.float32)[:, None] * frequencies(HD // 4)[None, :]


def visible(query_index, key_index, bounds):
    apart = query_index[:, None] - key_index[None, :]
    same_doc = documents(query_index, bounds)[:, None] == documents(key_index, bounds)[None, :]
    return (apart >= 0) & (apart < WINDOW) & (key_index[None, :] >= 0) & same_doc


def contract_rows(left, right):
    return lax.dot_general(
        left, right, (((1,), (1,)), ((), ())), preferred_element_type=jnp.float32
    )


def contract_tokens(left, right):
    return lax.dot_general(
        left, right, (((0,), (0,)), ((), ())), preferred_element_type=jnp.float32
    )


def gelu_product(gate_part, up_part):
    return jax.nn.gelu(gate_part, approximate=True) * up_part


def owner_block(weight, ctx_size, fsdp_size):
    block = weight.shape[0] * fsdp_size // ctx_size
    per_owner = ctx_size // fsdp_size
    ctx_place = lax.axis_index("ctx")
    fsdp_place = lax.axis_index("fsdp")
    part = lax.dynamic_slice_in_dim(weight, (ctx_place % per_owner) * block, block, 0)
    owner = ctx_place // per_owner
    half = fsdp_size // 2
    over = [
        (c * fsdp_size + c // per_owner, c * fsdp_size + (c // per_owner + half) % fsdp_size)
        for c in range(ctx_size)
    ]
    moved = lax.ppermute(part, ("ctx", "fsdp"), over)
    part = jnp.where(fsdp_place == owner, part, moved)
    twin = [
        (c * fsdp_size + g, c * fsdp_size + (g ^ 1))
        for c in range(ctx_size)
        for g in (c // per_owner, (c // per_owner + half) % fsdp_size)
    ]
    moved = lax.ppermute(part, ("ctx", "fsdp"), twin)
    return jnp.where(fsdp_place % half == owner % half, part, moved)


def per_device(
    tokens,
    doc_bounds,
    cotangent,
    norm_one,
    query_weight,
    keyval_weight,
    out_weight,
    norm_two,
    gate_up_weight,
    down_weight,
):
    ctx_size = lax.axis_size("ctx")
    fsdp_size = lax.axis_size("fsdp")
    rows = tokens.shape[1]
    width = tokens.shape[2]
    length = rows * ctx_size
    inner_width = query_weight.shape[1]
    head_count = inner_width // HD
    hidden_width = gate_up_weight.shape[1] // 2
    part_width = hidden_width // ctx_size
    ctx_place = lax.axis_index("ctx")
    source = tokens[0].astype(jnp.float32)
    bounds = doc_bounds[0]
    query_index = ctx_place * rows + jnp.arange(rows, dtype=jnp.int32)
    key_index = jnp.arange(length, dtype=jnp.int32)
    allowed = visible(query_index, key_index, bounds)
    angles = rotary_angles(query_index, bounds)

    gate_cols = lax.dynamic_slice_in_dim(gate_up_weight, ctx_place * part_width, part_width, 1)
    up_cols = lax.dynamic_slice_in_dim(
        gate_up_weight, hidden_width + ctx_place * part_width, part_width, 1
    )
    cot_rows = cotangent[0]
    cot_all = lax.all_gather(cot_rows, "ctx", axis=0, tiled=True)
    w_gate_up = lax.all_gather(
        jnp.concatenate([gate_cols, up_cols], axis=1), "fsdp", axis=0, tiled=True
    )
    w_down = owner_block(down_weight, ctx_size, fsdp_size)
    w_qkv = jnp.concatenate([query_weight, keyval_weight], axis=1)

    def spread(value):
        return lax.all_to_all(value, "fsdp", split_axis=1, concat_axis=0, tiled=True)

    def collect(value):
        return lax.all_to_all(value, "fsdp", split_axis=0, concat_axis=1, tiled=True)

    normed_full, norm_back_one = jax.vjp(rms_norm, source, norm_one)
    normed = spread(normed_full.astype(jnp.bfloat16))
    linear = lax.psum_scatter(
        jnp.dot(normed, w_qkv, preferred_element_type=jnp.float32).astype(jnp.bfloat16),
        "fsdp",
        scatter_dimension=0,
        tiled=True,
    ).astype(jnp.float32)

    def shape_heads(part):
        query_part, keyval_part = part[:, :inner_width], part[:, inner_width:]
        query_rot = rotate(query_part.reshape(rows, head_count, HD), angles) * HD ** (-0.5)
        key_rot = rotate(keyval_part[:, None, :HD], angles)[:, 0]
        return (query_rot, jnp.concatenate([key_rot, keyval_part[:, HD:]], axis=1))

    (queries_full, keyval_full), shape_back = jax.vjp(shape_heads, linear)
    queries = queries_full.astype(jnp.bfloat16)
    window = lax.all_gather(keyval_full.astype(jnp.bfloat16), "ctx", axis=0, tiled=True)
    key_rows = window[:, :HD]
    value_rows = window[:, HD:]
    scores = jnp.einsum("thd,kd->htk", queries, key_rows, preferred_element_type=jnp.float32)
    scores = jnp.where(allowed[None], scores, -1e30)
    peak_score = jnp.max(scores, axis=-1, keepdims=True)
    weights = jnp.exp(scores - peak_score)
    denominator = jnp.sum(weights, axis=-1, keepdims=True)
    weights = weights / denominator
    log_total = peak_score + jnp.log(denominator)
    mixed = jnp.einsum(
        "htk,kd->thd", weights.astype(jnp.bfloat16), value_rows, preferred_element_type=jnp.float32
    )
    mixed = spread(mixed.reshape(rows, inner_width).astype(jnp.bfloat16))
    middle = source + lax.psum_scatter(
        jnp.dot(mixed, out_weight, preferred_element_type=jnp.float32).astype(jnp.bfloat16),
        "fsdp",
        scatter_dimension=0,
        tiled=True,
    ).astype(jnp.float32)
    normed_two_full, norm_back_two = jax.vjp(rms_norm, middle, norm_two)
    normed_two = lax.all_gather(
        normed_two_full.astype(jnp.bfloat16), "ctx", axis=0, tiled=True
    )
    projected = jnp.dot(normed_two, w_gate_up, preferred_element_type=jnp.float32)
    hidden_full, gelu_back = jax.vjp(
        gelu_product, projected[:, :part_width], projected[:, part_width:]
    )
    hidden = hidden_full.astype(jnp.bfloat16)
    grad_hidden = contract_rows(cot_all, w_down)
    grad_gate, grad_up = gelu_back(grad_hidden)
    grad_gate_up = jnp.concatenate([grad_gate, grad_up], axis=1).astype(jnp.bfloat16)
    grad_normed_two = lax.psum_scatter(
        contract_rows(grad_gate_up, w_gate_up).astype(jnp.bfloat16),
        "ctx",
        scatter_dimension=0,
        tiled=True,
    ).astype(jnp.float32)
    branch_two = lax.psum_scatter(
        jnp.dot(hidden, w_down, preferred_element_type=jnp.float32).astype(jnp.bfloat16),
        "ctx",
        scatter_dimension=0,
        tiled=True,
    ).astype(jnp.float32)
    result = (middle + branch_two).astype(jnp.bfloat16)

    down_grad = lax.psum_scatter(
        contract_tokens(hidden, cot_all).astype(jnp.bfloat16),
        "fsdp",
        scatter_dimension=1,
        tiled=True,
    ).astype(jnp.float32)
    gate_up_part = lax.psum_scatter(
        contract_tokens(normed_two, grad_gate_up).astype(jnp.bfloat16),
        "fsdp",
        scatter_dimension=1,
        tiled=True,
    )
    gate_up_part = lax.all_to_all(
        gate_up_part.reshape(ctx_size, width // ctx_size, -1), "ctx", 0, 0, tiled=True
    )
    core = lax.axis_index("fsdp") % 2
    gate_up_part = gate_up_part.reshape((2, ctx_size // 2) + gate_up_part.shape[1:])
    kept = lax.dynamic_index_in_dim(gate_up_part, core, 0, keepdims=False)
    given = lax.dynamic_index_in_dim(gate_up_part, 1 - core, 0, keepdims=False)
    taken = lax.ppermute(given, "fsdp", [(i, i ^ 1) for i in range(fsdp_size)])
    halves = jnp.where(core == 0, jnp.stack([kept, taken], 2), jnp.stack([taken, kept], 2))
    gate_up_grad = (
        halves.transpose(1, 0, 2, 3).reshape(width // ctx_size, -1).astype(jnp.float32)
    )

    grad_middle_norm, gain_two_term = norm_back_two(grad_normed_two)
    grad_middle = cot_rows.astype(jnp.float32) + grad_middle_norm
    grad_branch = lax.all_gather(grad_middle.astype(jnp.bfloat16), "fsdp", axis=0, tiled=True)
    grad_mixed = collect(contract_rows(grad_branch, out_weight).astype(jnp.bfloat16))
    grad_mixed = grad_mixed.reshape(rows, head_count, HD)

    scores = jnp.einsum("thd,kd->htk", queries, key_rows, preferred_element_type=jnp.float32)
    weights = jnp.where(allowed[None], jnp.exp(scores - log_total), 0.0)
    grad_weights = jnp.einsum(
        "thd,kd->htk", grad_mixed, value_rows, preferred_element_type=jnp.float32
    )
    row_delta = jnp.sum(weights * grad_weights, axis=-1, keepdims=True)
    grad_scores = (weights * (grad_weights - row_delta)).astype(jnp.bfloat16)
    grad_queries = jnp.einsum(
        "htk,kd->thd", grad_scores, key_rows, preferred_element_type=jnp.float32
    )
    grad_keys = jnp.einsum("htk,thd->kd", grad_scores, queries, preferred_element_type=jnp.float32)
    grad_values = jnp.einsum(
        "htk,thd->kd", weights.astype(jnp.bfloat16), grad_mixed, preferred_element_type=jnp.float32
    )
    own_grad = lax.psum_scatter(
        jnp.concatenate([grad_keys, grad_values], axis=1).astype(jnp.bfloat16),
        "ctx",
        scatter_dimension=0,
        tiled=True,
    ).astype(jnp.float32)
    (grad_linear,) = shape_back((grad_queries, own_grad))
    grad_linear = lax.all_gather(grad_linear.astype(jnp.bfloat16), "fsdp", axis=0, tiled=True)
    grad_normed = collect(contract_rows(grad_linear, w_qkv).astype(jnp.bfloat16))
    grad_source_norm, gain_one_term = norm_back_one(grad_normed.astype(jnp.float32))
    input_grad = (grad_middle + grad_source_norm).astype(jnp.bfloat16)

    per_owner = ctx_size // fsdp_size

    def in_blocks(term):
        tall, wide = term.shape
        term = term.astype(jnp.bfloat16)
        term = term.reshape(per_owner, tall // per_owner, fsdp_size, wide // fsdp_size)
        return term.transpose(0, 2, 1, 3).reshape(ctx_size, tall // per_owner, wide // fsdp_size)

    def summed(blocks):
        block = lax.psum_scatter(blocks, "ctx", scatter_dimension=0, tiled=True)[0]
        pairs = [
            ((r * fsdp_size + g) * fsdp_size + f, (per_owner * f + r) * fsdp_size + g)
            for r in range(per_owner)
            for g in range(fsdp_size)
            for f in range(fsdp_size)
        ]
        return lax.ppermute(block, ("ctx", "fsdp"), pairs).astype(jnp.float32)

    out_grad = summed(in_blocks(contract_tokens(mixed, grad_branch)))
    qkv_term = contract_tokens(normed, grad_linear)
    qkv_block = summed(
        jnp.concatenate(
            [in_blocks(qkv_term[:, :inner_width]), in_blocks(qkv_term[:, inner_width:])], axis=2
        )
    )
    query_grad = qkv_block[:, : inner_width // fsdp_size]
    keyval_grad = qkv_block[:, inner_width // fsdp_size :]
    gains = lax.psum_scatter(
        jnp.stack([gain_one_term, gain_two_term]),
        ("ctx", "fsdp"),
        scatter_dimension=1,
        tiled=True,
    )
    return (
        result[None],
        input_grad[None],
        gains[0],
        query_grad,
        keyval_grad,
        out_grad,
        gains[1],
        gate_up_grad,
        down_grad,
    )


def solution(mesh):
    placed = (
        P("fsdp", "ctx", None),
        P("fsdp", None),
        P("fsdp", "ctx", None),
        P(),
        P("fsdp", None),
        P("fsdp", None),
        P("fsdp", None),
        P(),
        P("fsdp", None),
        P("fsdp", None),
    )
    return jax.shard_map(
        per_device,
        mesh=mesh,
        in_specs=placed,
        out_specs=(
            P("fsdp", "ctx", None),
            P("fsdp", "ctx", None),
            P(("ctx", "fsdp")),
            P("ctx", "fsdp"),
            P("ctx", "fsdp"),
            P("ctx", "fsdp"),
            P(("ctx", "fsdp")),
            P("ctx", "fsdp"),
            P("ctx", "fsdp"),
        ),
        check_vma=False,
    )
```

```python
import functools

import jax
import jax.numpy as jnp
from jax import lax
from jax.experimental import pallas as pl
from jax.experimental.pallas import tpu as pltpu
from jax.sharding import PartitionSpec as P

HD = 256
WINDOW = 2048


epsilon = 1e-06
f32 = jnp.float32
bf16 = jnp.bfloat16
VMEM = pltpu.VMEM
DMA = pltpu.SemaphoreType.DMA
vmem_bytes = 58 * 1024 * 1024


def rms_norm(values, gain):
    return values * lax.rsqrt(jnp.mean(values * values, axis=-1, keepdims=True) + epsilon) * gain


def frequencies(quarter):
    return 10000.0 ** (-jnp.arange(quarter, dtype=jnp.float32) / quarter)


def documents(index, bounds):
    return (index >= bounds[0]).astype(jnp.int32) + (index >= bounds[1]).astype(jnp.int32)


def rotary_angles(index, bounds):
    member = documents(index, bounds)
    opening = jnp.where(member == 0, 0, jnp.where(member == 1, bounds[0], bounds[1]))
    return (index - opening).astype(jnp.float32)[:, None] * frequencies(HD // 4)[None, :]


def visible(query_index, key_index, bounds):
    apart = query_index[:, None] - key_index[None, :]
    same_doc = documents(query_index, bounds)[:, None] == documents(key_index, bounds)[None, :]
    return (apart >= 0) & (apart < WINDOW) & (key_index[None, :] >= 0) & same_doc


def contract_rows(left, right):
    return lax.dot_general(
        left, right, (((1,), (1,)), ((), ())), preferred_element_type=jnp.float32
    )


def contract_tokens(left, right):
    return lax.dot_general(
        left, right, (((0,), (0,)), ((), ())), preferred_element_type=jnp.float32
    )


def gelu_product(gate_part, up_part):
    return jax.nn.gelu(gate_part, approximate=True) * up_part


def remote(src, dst, send_sem, recv_sem, device):
    return pltpu.make_async_remote_copy(
        src_ref=src,
        dst_ref=dst,
        send_sem=send_sem,
        recv_sem=recv_sem,
        device_id=device,
        device_id_type=pl.DeviceIdType.MESH,
    )


class Place:
    def __init__(self, lines):
        self.lines = lines
        self.c = lax.axis_index("ctx")
        self.f = lax.axis_index("fsdp")
        self.line = self.c // 2
        self.lane = self.c % 2
        self.chip = self.f // 2
        self.core = self.f % 2
        self.twin_f = self.f + 1 - 2 * self.core
        self.cross_f = (self.f + 2) % 4
        self.diag_f = (self.twin_f + 2) % 4
        self.twin = {"fsdp": self.twin_f}
        self.cross = {"fsdp": self.cross_f}
        self.diag = {"fsdp": self.diag_f}
        self.beside = {"ctx": self.c + 1 - 2 * self.lane}
        self.right = {"ctx": self.c + 2}
        self.left = {"ctx": self.c - 2}
        self.has_right = self.line < lines - 1
        self.has_left = self.line > 0

    def barrier(self, ctx=True, fsdp=True):
        sem = pltpu.get_barrier_semaphore()

        def greet(device):
            pl.semaphore_signal(sem, 1, device_id=device, device_id_type=pl.DeviceIdType.MESH)

        count = 0
        if fsdp:
            for device in (self.twin, self.cross, self.diag):
                greet(device)
            count = 3
        if ctx:
            greet(self.beside)
            pl.when(self.has_right)(lambda: greet(self.right))
            pl.when(self.has_left)(lambda: greet(self.left))
            count = (
                count + 1 + self.has_right.astype(jnp.int32) + self.has_left.astype(jnp.int32)
            )
        pl.semaphore_wait(sem, count)


class LineGather:
    sems = 6

    def __init__(self, place, own, slots, sems):
        self.p, self.own, self.slots, self.s = place, own, slots, sems

    def rightward(self, step):
        at = 2 * (self.p.line - step) + self.p.lane
        src = self.own if step == 0 else self.slots.at[at]
        return remote(src, self.slots.at[at], self.s.at[0, step], self.s.at[1, step], self.p.right)

    def leftward(self, step):
        at = 2 * (self.p.line + step) + self.p.lane
        src = self.own if step == 0 else self.slots.at[at]
        return remote(src, self.slots.at[at], self.s.at[2, step], self.s.at[3, step], self.p.left)

    def across(self, line, own=False):
        at = 2 * line + self.p.lane
        src = self.own if own else self.slots.at[at]
        return remote(
            src, self.slots.at[at], self.s.at[4, line], self.s.at[5, line], self.p.beside
        )

    def from_left(self, step):
        at = 2 * (self.p.line - 1 - step) + self.p.lane
        slot = self.slots.at[at]
        return remote(slot, slot, self.s.at[0, step], self.s.at[1, step], self.p.right)

    def from_right(self, step):
        at = 2 * (self.p.line + 1 + step) + self.p.lane
        slot = self.slots.at[at]
        return remote(slot, slot, self.s.at[2, step], self.s.at[3, step], self.p.left)

    def start(self):
        pl.when(self.p.has_right)(lambda: self.rightward(0).start())
        pl.when(self.p.has_left)(lambda: self.leftward(0).start())
        self.across(self.p.line, True).start()

    def step(self, step):
        p = self.p

        @pl.when(p.line - 1 - step >= 0)
        def _():
            self.from_left(step).wait_recv()
            if step + 1 < p.lines - 1:
                pl.when(p.has_right)(lambda: self.rightward(step + 1).start())
            self.across(p.line - 1 - step).start()

        @pl.when(p.line + 1 + step <= p.lines - 1)
        def _():
            self.from_right(step).wait_recv()
            if step + 1 < p.lines - 1:
                pl.when(p.has_left)(lambda: self.leftward(step + 1).start())
            self.across(p.line + 1 + step).start()

    def steps(self):
        for step in range(self.p.lines - 1):
            self.step(step)

    def arrived_across(self, line):
        at = 2 * line + 1 - self.p.lane
        slot = self.slots.at[at]
        remote(slot, slot, self.s.at[4, line], self.s.at[5, line], self.p.beside).wait_recv()

    def finish(self, arrivals=True):
        p = self.p
        if arrivals:
            for line in range(p.lines):
                self.arrived_across(line)
        for step in range(p.lines - 1):
            pl.when(p.has_right & (p.line - step >= 0))(
                lambda step=step: self.rightward(step).wait_send()
            )
            pl.when(p.has_left & (p.line + step <= p.lines - 1))(
                lambda step=step: self.leftward(step).wait_send()
            )
        for line in range(p.lines):
            self.across(line).wait_send()


class LineSum:
    sems = 6

    def __init__(self, place, parts, side, chain, sems):
        self.p, self.parts, self.side, self.chain, self.s = place, parts, side, chain, sems

    def order(self, turn):
        lines, line = self.p.lines, self.p.line
        value = 0
        for a in range(lines):
            far = sorted(range(lines), key=lambda t: (-abs(t - a), t))
            value = value + jnp.where(line == a, far[turn], 0)
        return value

    def across(self, turn):
        t = self.order(turn)
        at = 2 * t + 1 - self.p.lane
        return remote(
            self.parts.at[at],
            self.side.at[t],
            self.s.at[0, t],
            self.s.at[1, t],
            self.p.beside,
        )

    def rightward(self, t):
        step = self.p.lines - 1 - t
        return remote(
            self.parts.at[2 * t + self.p.lane],
            self.chain.at[0, step],
            self.s.at[2, step],
            self.s.at[3, step],
            self.p.right,
        )

    def leftward(self, t):
        return remote(
            self.parts.at[2 * t + self.p.lane],
            self.chain.at[1, t],
            self.s.at[4, t],
            self.s.at[5, t],
            self.p.left,
        )

    def add(self, at, other):
        self.parts[at] = (self.parts[at].astype(f32) + other.astype(f32)).astype(bf16)

    def start(self):
        for turn in range(min(2, self.p.lines)):
            self.across(turn).start()

    def turn(self, turn):
        p = self.p
        t = self.order(turn)
        at = 2 * t + p.lane
        self.across(turn).wait_recv()
        if turn + 2 < p.lines:
            self.across(turn + 2).start()
        self.add(at, self.side[t])

        @pl.when(t > p.line)
        def _():
            @pl.when(p.has_left)
            def _():
                self.rightward(t).wait_recv()
                self.add(at, self.chain[0, p.lines - 1 - t])

            self.rightward(t).start()

        @pl.when(t < p.line)
        def _():
            @pl.when(p.has_right)
            def _():
                self.leftward(t).wait_recv()
                self.add(at, self.chain[1, t])

            self.leftward(t).start()

    def turns(self):
        for turn in range(self.p.lines):
            self.turn(turn)

    def total(self):
        p = self.p
        at = 2 * p.line + p.lane

        @pl.when(p.has_left)
        def _():
            self.rightward(p.line).wait_recv()
            self.add(at, self.chain[0, p.lines - 1 - p.line])

        @pl.when(p.has_right)
        def _():
            self.leftward(p.line).wait_recv()
            self.add(at, self.chain[1, p.line])

        return self.parts[at].astype(f32)

    def finish(self):
        p = self.p
        for turn in range(p.lines):
            self.across(turn).wait_send()
        for t in range(p.lines):
            pl.when(t > p.line)(lambda t=t: self.rightward(t).wait_send())
            pl.when(t < p.line)(lambda t=t: self.leftward(t).wait_send())


class GroupSum:
    sems = 6

    def __init__(self, place, parts, near, out, far, sems):
        self.p, self.parts, self.near, self.out, self.far, self.s = place, parts, near, out, far, sems

    def to_twin(self, i, which, cols):
        p = self.p
        block = p.diag_f if which == 0 else p.twin_f
        return remote(
            self.parts.at[block, :, cols],
            self.near.at[which, :, cols],
            self.s.at[which, i],
            self.s.at[2 + which, i],
            p.twin,
        )

    def to_cross(self, i, cols):
        return remote(
            self.out.at[:, cols], self.far.at[:, cols], self.s.at[4, i], self.s.at[5, i], self.p.cross
        )

    def give(self, i, cols):
        self.to_twin(i, 0, cols).start()
        self.to_twin(i, 1, cols).start()

    def pass_on(self, i, cols):
        self.to_twin(i, 0, cols).wait_recv()
        mine = self.parts[self.p.cross_f, :, cols].astype(f32)
        self.out[:, cols] = (mine + self.near[0, :, cols].astype(f32)).astype(bf16)
        self.to_cross(i, cols).start()

    def take(self, i, cols):
        self.to_twin(i, 1, cols).wait_recv()
        near = self.parts[self.p.f, :, cols].astype(f32) + self.near[1, :, cols].astype(f32)
        self.to_cross(i, cols).wait_recv()
        return near + self.far[:, cols].astype(f32)

    def finish(self, i, cols):
        self.to_twin(i, 0, cols).wait_send()
        self.to_twin(i, 1, cols).wait_send()
        self.to_cross(i, cols).wait_send()


class GroupTrade:
    sems = 2

    def __init__(self, place, whole, slots, sems, columns):
        self.p, self.whole, self.slots, self.s, self.n = place, whole, slots, sems, columns

    def block(self, g):
        return self.whole.at[:, pl.ds(pl.multiple_of(g * self.n, 128), self.n)]

    def copy(self, d):
        g = (self.p.f + d) % 4
        return remote(
            self.block(g), self.slots.at[self.p.f], self.s.at[0, d], self.s.at[1, d], {"fsdp": g}
        )

    def arrival(self, d):
        slot = self.slots.at[(self.p.f + 4 - d) % 4]
        return remote(slot, slot, self.s.at[0, d], self.s.at[1, d], {"fsdp": (self.p.f + d) % 4})

    def own(self):
        return pltpu.make_async_copy(
            self.block(self.p.f), self.slots.at[self.p.f], self.s.at[1, 0]
        )

    def start(self):
        for d in (2, 3, 1):
            self.copy(d).start()
        self.own().start()

    def wait(self):
        self.own().wait()
        for d in (1, 2, 3):
            self.arrival(d).wait_recv()

    def finish(self):
        for d in (1, 2, 3):
            self.copy(d).wait_send()


def rotated(v, cosine, sine):
    first = v[:, :128]
    return jnp.concatenate(
        [first * cosine + pltpu.roll(first, 64, 1) * sine, v[:, 128:]], axis=1
    )


class WeightColumns:
    sems = 6

    def __init__(self, place, own, whole, sems, own_sem, pieces):
        self.p, self.own, self.whole, self.s, self.own_sem = place, own, whole, sems, own_sem
        self.pieces, self.n = pieces, own.shape[0] // pieces

    def part(self, ref, i):
        return ref.at[pl.ds(i * self.n, self.n)]

    def slot(self, g, i):
        return self.whole.at[g, pl.ds(i * self.n, self.n)]

    def local(self):
        return pltpu.make_async_copy(self.own, self.whole.at[self.p.f], self.own_sem)

    def to_twin(self, i):
        return remote(
            self.part(self.own, i), self.slot(self.p.f, i), self.s.at[0, i], self.s.at[3, i], self.p.twin
        )

    def to_cross(self, i):
        return remote(
            self.part(self.own, i), self.slot(self.p.f, i), self.s.at[1, i], self.s.at[4, i], self.p.cross
        )

    def forward(self, i):
        slot = self.slot(self.p.cross_f, i)
        return remote(slot, slot, self.s.at[2, i], self.s.at[5, i], self.p.twin)

    def give(self, i):
        self.to_cross(i).start()
        self.to_twin(i).start()

    def pass_on(self, i):
        slot = self.slot(self.p.cross_f, i)
        remote(slot, slot, self.s.at[1, i], self.s.at[4, i], self.p.cross).wait_recv()
        self.forward(i).start()

    def finish(self, i):
        twin, diag = self.slot(self.p.twin_f, i), self.slot(self.p.diag_f, i)
        remote(twin, twin, self.s.at[0, i], self.s.at[3, i], self.p.twin).wait_recv()
        remote(diag, diag, self.s.at[2, i], self.s.at[5, i], self.p.twin).wait_recv()
        self.to_twin(i).wait_send()
        self.to_cross(i).wait_send()
        self.forward(i).wait_send()


class WeightRows:
    sems = 3

    def __init__(self, place, held, whole, sems, own_sem, pieces):
        per_owner = place.lines * 2 // 4
        self.p, self.held, self.whole, self.s, self.own_sem = place, held, whole, sems, own_sem
        self.rows = whole.shape[0]
        self.pieces, self.n = pieces, whole.shape[0] // pieces
        self.first = (place.c % per_owner) * self.rows
        owner = place.c // per_owner
        self.is_owner = place.f == owner
        self.is_cross = place.f == (owner + 2) % 4
        self.is_last = (place.f != owner) & (place.f != (owner + 2) % 4)

    def source(self, i):
        return self.held.at[pl.ds(pl.multiple_of(self.first + i * self.n, 16), self.n)]

    def slot(self, i):
        return self.whole.at[pl.ds(i * self.n, self.n)]

    def local(self):
        return pltpu.make_async_copy(
            self.held.at[pl.ds(pl.multiple_of(self.first, 16), self.rows)], self.whole, self.own_sem
        )

    def to_cross(self, i):
        return remote(self.source(i), self.slot(i), self.s.at[0, i], self.s.at[2, i], self.p.cross)

    def to_twin(self, i):
        return remote(self.source(i), self.slot(i), self.s.at[1, i], self.s.at[2, i], self.p.twin)

    def forward(self, i):
        slot = self.slot(i)
        return remote(slot, slot, self.s.at[1, i], self.s.at[2, i], self.p.twin)

    def start(self):
        @pl.when(self.is_owner)
        def _():
            self.local().start()
            for i in range(self.pieces):
                self.to_cross(i).start()
                self.to_twin(i).start()

    def pass_on(self, i):
        @pl.when(self.is_cross)
        def _():
            self.forward(i).wait_recv()
            self.forward(i).start()

    def finish(self):
        @pl.when(self.is_owner)
        def _():
            self.local().wait()
            for i in range(self.pieces):
                self.to_cross(i).wait_send()
                self.to_twin(i).wait_send()

        @pl.when(self.is_cross)
        def _():
            for i in range(self.pieces):
                self.forward(i).wait_send()

        @pl.when(self.is_last)
        def _():
            for i in range(self.pieces):
                self.forward(i).wait_recv()


def tiles_of(first, count, tile):
    tile = tile if count % tile == 0 else 128

    def loop(body):
        def one(i, carry):
            body(pl.ds(pl.multiple_of(first + i * tile, 128), tile))
            return carry

        lax.fori_loop(0, count // tile, one, 0)

    return loop


def front_kernel(
    lines,
    x_ref,
    gain_one,
    gain_two,
    cosine,
    sine,
    bias,
    w_keyval,
    w_query,
    w_out,
    cot,
    w_columns,
    w_rows,
    normed_out,
    query_out,
    keyval_out,
    probs_out,
    mixed_out,
    middle_out,
    normed_two_out,
    cot_all,
    columns_all,
    rows_all,
    whole,
    slots,
    parts,
    near,
    out,
    far,
    keyval,
    mixed,
    trade_sems,
    sum_sems,
    keyval_sems,
    cot_sems,
    column_sems,
    row_sems,
    own_sems,
):
    p = Place(lines)
    rows, width = x_ref.shape
    heads = query_out.shape[0]
    inner = heads * HD
    kv_width = 2 * HD
    p.barrier()

    columns = WeightColumns(p, w_columns, columns_all, column_sems, own_sems.at[0], column_sems.shape[1])
    down = WeightRows(p, w_rows, rows_all, row_sems, own_sems.at[1], row_sems.shape[1])
    cot_gather = LineGather(p, cot, cot_all, cot_sems)
    cot_local = pltpu.make_async_copy(cot, cot_all.at[p.c], own_sems.at[2])

    source = x_ref[...].astype(f32)
    whole[...] = rms_norm(source, gain_one[...]).astype(bf16)
    trade = GroupTrade(p, whole, slots.at[0], trade_sems.at[0], slots.shape[3])
    trade.start()
    columns.local().start()
    cot_local.start()
    cot_gather.start()
    trade.wait()
    normed_out[...] = slots[0]

    half = (heads // 2) * HD
    chunks = [(0, kv_width), (kv_width, half), (kv_width + half, inner - half)]
    group = GroupSum(p, parts, near, out, far, sum_sems.at[0])

    def project(lhs, weight, first, count, to):
        @tiles_of(first, count, 256)
        def _(cols):
            left = lhs[...].reshape(4 * rows, lhs.shape[-1])
            product = jnp.dot(left, weight[:, cols], preferred_element_type=f32)
            if to:
                cols = pl.ds(pl.multiple_of(cols.start + to, 128), cols.size)
            parts[:, :, cols] = product.astype(bf16).reshape(4, rows, cols.size)

    spans = [pl.ds(first, count) for first, count in chunks]
    project(slots.at[0], w_keyval, 0, kv_width, 0)
    group.give(0, spans[0])
    project(slots.at[0], w_query, 0, half, kv_width)
    group.give(1, spans[1])
    group.pass_on(0, spans[0])
    project(slots.at[0], w_query, half, inner - half, kv_width)
    group.give(2, spans[2])
    group.pass_on(1, spans[1])
    group.pass_on(2, spans[2])

    linear = group.take(0, spans[0])
    keyval[p.c] = jnp.concatenate(
        [rotated(linear[:, :HD], cosine[...], sine[...]), linear[:, HD:]], axis=1
    ).astype(bf16)
    kv_gather = LineGather(p, keyval.at[p.c], keyval, keyval_sems)
    kv_gather.start()
    for i in (1, 2):
        linear = group.take(i, spans[i])
        for h in range(linear.shape[1] // HD):
            turned = rotated(linear[:, h * HD : (h + 1) * HD], cosine[...], sine[...])
            at = h if i == 1 else h + heads // 2
            query_out[at] = (turned * HD**-0.5).astype(bf16)
        if i == 1:
            kv_gather.step(0)
    for i in range(columns.pieces):
        columns.give(i)
    for step in range(1, lines - 1):
        kv_gather.step(step)
    kv_gather.finish()
    keyval_out[...] = keyval[...]

    length = bias.shape[1]

    def two_heads(i, carry):
        keys = keyval[:, :, :HD].reshape(length, HD)
        values = keyval[:, :, HD:].reshape(length, HD)
        two = query_out[pl.ds(2 * i, 2)].reshape(2 * rows, HD)
        scores = contract_rows(two, keys).reshape(2, rows, length) + bias[...][None]
        scores = scores.reshape(2 * rows, length)
        weights = jnp.exp(scores - jnp.max(scores, axis=-1, keepdims=True))
        total = jnp.sum(weights, axis=-1, keepdims=True)
        weights = (weights / total).astype(bf16)
        probs_out[pl.ds(2 * i, 2)] = weights.reshape(2, rows, length)
        product = jnp.dot(weights, values, preferred_element_type=f32).astype(bf16)
        at = pl.multiple_of(i * 2 * HD, 128)
        mixed[:, pl.ds(at, HD)] = product[:rows]
        mixed[:, pl.ds(at + HD, HD)] = product[rows:]
        return carry

    lax.fori_loop(0, heads // 2, two_heads, 0)
    trade_two = GroupTrade(p, mixed, slots.at[1], trade_sems.at[1], slots.shape[3])
    trade_two.start()
    for step in range(lines - 1):
        cot_gather.step(step)
    for i in range(len(chunks)):
        group.finish(i, spans[i])
    trade_two.wait()
    mixed_out[...] = slots[1]

    half = width // 2
    spans_two = [pl.ds(0, half), pl.ds(half, half)]
    group_two = GroupSum(p, parts, near, out, far, sum_sems.at[1])
    for i in range(2):
        project(slots.at[1], w_out, i * half, half, 0)
        group_two.give(i, spans_two[i])
    for i in range(2):
        group_two.pass_on(i, spans_two[i])
    for i in range(2):
        middle_out[:, spans_two[i]] = x_ref[:, spans_two[i]].astype(f32) + group_two.take(
            i, spans_two[i]
        )
    normed_two_out[...] = rms_norm(middle_out[...], gain_two[...]).astype(bf16)

    down.start()
    for i in range(columns.pieces):
        columns.pass_on(i)
    for i in range(down.pieces):
        down.pass_on(i)
    for i in range(2):
        group_two.finish(i, spans_two[i])
    trade.finish()
    trade_two.finish()
    columns.local().wait()
    cot_local.wait()
    for i in range(columns.pieces):
        columns.finish(i)
    down.finish()
    cot_gather.finish()


def front(lines, operands, part_width, heads):
    x = operands[0]
    rows, width = x.shape
    places = 2 * lines
    length = places * rows
    inner = heads * HD
    shard = width // 4
    parts_width = inner + 2 * HD
    in_vmem = pl.BlockSpec(memory_space=VMEM)
    anywhere = pl.BlockSpec(memory_space=pl.ANY)
    shape = jax.ShapeDtypeStruct
    pieces = 4
    assert inner == width
    return pl.pallas_call(
        functools.partial(front_kernel, lines),
        out_shape=(
            shape((4, rows, shard), bf16),
            shape((heads, rows, HD), bf16),
            shape((places, rows, 2 * HD), bf16),
            shape((heads, rows, length), bf16),
            shape((4, rows, shard), bf16),
            shape((rows, width), f32),
            shape((rows, width), bf16),
            shape((places, rows, width), bf16),
            shape((4,) + operands[10].shape, bf16),
            shape((part_width, width), bf16),
        ),
        in_specs=[in_vmem] * 9 + [anywhere] * 3,
        out_specs=[in_vmem] * 7 + [anywhere] * 3,
        scratch_shapes=[
            VMEM((rows, width), bf16),
            VMEM((2, 4, rows, shard), bf16),
            VMEM((4, rows, parts_width), bf16),
            VMEM((2, rows, parts_width), bf16),
            VMEM((rows, parts_width), bf16),
            VMEM((rows, parts_width), bf16),
            VMEM((places, rows, 2 * HD), bf16),
            VMEM((rows, inner), bf16),
            DMA((2, GroupTrade.sems, 4)),
            DMA((2, GroupSum.sems, 3)),
            DMA((LineGather.sems, lines)),
            DMA((LineGather.sems, lines)),
            DMA((WeightColumns.sems, pieces)),
            DMA((WeightRows.sems, 3)),
            DMA((3,)),
        ],
        compiler_params=pltpu.CompilerParams(
            collective_id=0, has_side_effects=True, vmem_limit_bytes=vmem_bytes
        ),
        name="front",
    )(*operands)


def per_device(
    tokens,
    doc_bounds,
    cotangent,
    norm_one,
    query_weight,
    keyval_weight,
    out_weight,
    norm_two,
    gate_up_weight,
    down_weight,
):
    ctx_size = lax.axis_size("ctx")
    fsdp_size = lax.axis_size("fsdp")
    lines = ctx_size // 2
    rows = tokens.shape[1]
    width = tokens.shape[2]
    length = rows * ctx_size
    inner_width = query_weight.shape[1]
    head_count = inner_width // HD
    hidden_width = gate_up_weight.shape[1] // 2
    part_width = hidden_width // ctx_size
    padded = -(-part_width // 128) * 128
    ctx_place = lax.axis_index("ctx")
    source = tokens[0].astype(jnp.float32)
    bounds = doc_bounds[0]
    query_index = ctx_place * rows + jnp.arange(rows, dtype=jnp.int32)
    key_index = jnp.arange(length, dtype=jnp.int32)
    allowed = visible(query_index, key_index, bounds)
    bias = jnp.where(allowed, 0.0, -1e30).astype(jnp.float32)
    angles = rotary_angles(query_index, bounds)
    cosine = jnp.cos(angles)
    sine = jnp.sin(angles)
    cosine = jnp.concatenate([cosine, cosine], axis=1)
    sine = jnp.concatenate([-sine, sine], axis=1)

    def own_columns(first):
        cols = lax.dynamic_slice_in_dim(
            gate_up_weight, first + ctx_place * part_width, part_width, 1
        )
        return jnp.pad(cols, ((0, 0), (0, padded - part_width)))

    w_columns = jnp.concatenate([own_columns(0), own_columns(hidden_width)], axis=1)
    cot_rows = cotangent[0]
    (
        normed,
        queries,
        window,
        weights,
        mixed,
        middle,
        normed_two,
        cot_all,
        w_gate_up,
        w_down,
    ) = front(
        lines,
        (
            tokens[0],
            norm_one[None],
            norm_two[None],
            cosine,
            sine,
            bias,
            keyval_weight,
            query_weight,
            out_weight,
            cot_rows,
            w_columns,
            down_weight,
        ),
        part_width,
        head_count,
    )
    normed = normed.reshape(fsdp_size * rows, -1)
    mixed = mixed.reshape(fsdp_size * rows, -1)
    window = window.reshape(length, -1)
    cot_all = cot_all.reshape(length, width)
    w_gate_up = w_gate_up.reshape(width, 2 * padded)
    key_rows = window[:, :HD]
    value_rows = window[:, HD:]
    w_qkv = jnp.concatenate([query_weight, keyval_weight], axis=1)

    def collect(value):
        return lax.all_to_all(value, "fsdp", split_axis=0, concat_axis=1, tiled=True)

    _, norm_back_one = jax.vjp(rms_norm, source, norm_one)
    _, norm_back_two = jax.vjp(rms_norm, middle, norm_two)
    normed_two = lax.all_gather(normed_two, "ctx", axis=0, tiled=True)
    projected = jnp.dot(normed_two, w_gate_up, preferred_element_type=jnp.float32)
    hidden_full, gelu_back = jax.vjp(gelu_product, projected[:, :padded], projected[:, padded:])
    hidden = hidden_full.astype(jnp.bfloat16)[:, :part_width]
    grad_hidden = contract_rows(cot_all, w_down)
    grad_gate, grad_up = gelu_back(jnp.pad(grad_hidden, ((0, 0), (0, padded - part_width))))
    grad_gate_up = jnp.concatenate([grad_gate, grad_up], axis=1).astype(jnp.bfloat16)
    grad_normed_two = lax.psum_scatter(
        contract_rows(grad_gate_up, w_gate_up).astype(jnp.bfloat16),
        "ctx",
        scatter_dimension=0,
        tiled=True,
    ).astype(jnp.float32)
    branch_two = lax.psum_scatter(
        jnp.dot(hidden, w_down, preferred_element_type=jnp.float32).astype(jnp.bfloat16),
        "ctx",
        scatter_dimension=0,
        tiled=True,
    ).astype(jnp.float32)
    result = (middle + branch_two).astype(jnp.bfloat16)

    down_grad = lax.psum_scatter(
        contract_tokens(hidden, cot_all).astype(jnp.bfloat16),
        "fsdp",
        scatter_dimension=1,
        tiled=True,
    ).astype(jnp.float32)
    gate_up_part = lax.psum_scatter(
        contract_tokens(normed_two, grad_gate_up).astype(jnp.bfloat16),
        "fsdp",
        scatter_dimension=1,
        tiled=True,
    )
    gate_up_part = lax.all_to_all(
        gate_up_part.reshape(ctx_size, width // ctx_size, -1), "ctx", 0, 0, tiled=True
    )
    core = lax.axis_index("fsdp") % 2
    gate_up_part = gate_up_part.reshape((2, ctx_size // 2) + gate_up_part.shape[1:])
    kept = lax.dynamic_index_in_dim(gate_up_part, core, 0, keepdims=False)
    given = lax.dynamic_index_in_dim(gate_up_part, 1 - core, 0, keepdims=False)
    taken = lax.ppermute(given, "fsdp", [(i, i ^ 1) for i in range(fsdp_size)])
    halves = jnp.where(core == 0, jnp.stack([kept, taken], 2), jnp.stack([taken, kept], 2))
    halves = halves.reshape(halves.shape[:2] + (-1,))[:, :, :part_width]
    gate_up_grad = (
        halves.transpose(1, 0, 2).reshape(width // ctx_size, -1).astype(jnp.float32)
    )

    grad_middle_norm, gain_two_term = norm_back_two(grad_normed_two)
    grad_middle = cot_rows.astype(jnp.float32) + grad_middle_norm
    grad_branch = lax.all_gather(grad_middle.astype(jnp.bfloat16), "fsdp", axis=0, tiled=True)
    grad_mixed = collect(contract_rows(grad_branch, out_weight).astype(jnp.bfloat16))
    grad_mixed = grad_mixed.reshape(rows, head_count, HD)

    grad_weights = jnp.einsum(
        "thd,kd->htk", grad_mixed, value_rows, preferred_element_type=jnp.float32
    )
    row_delta = jnp.sum(weights * grad_weights, axis=-1, keepdims=True)
    grad_scores = (weights * (grad_weights - row_delta)).astype(jnp.bfloat16)
    grad_queries = jnp.einsum(
        "htk,kd->htd", grad_scores, key_rows, preferred_element_type=jnp.float32
    )
    grad_keys = jnp.einsum("htk,htd->kd", grad_scores, queries, preferred_element_type=jnp.float32)
    grad_values = jnp.einsum(
        "htk,thd->kd", weights, grad_mixed, preferred_element_type=jnp.float32
    )
    own_grad = lax.psum_scatter(
        jnp.concatenate([grad_keys, grad_values], axis=1).astype(jnp.bfloat16),
        "ctx",
        scatter_dimension=0,
        tiled=True,
    ).astype(jnp.float32)

    def turned_back(part):
        first = part[..., :128]
        swapped = jnp.concatenate([first[..., 64:], first[..., :64]], axis=-1)
        return jnp.concatenate([first * cosine - swapped * sine, part[..., 128:]], axis=-1)

    grad_linear = jnp.concatenate(
        [
            (turned_back(grad_queries) * HD**-0.5).transpose(1, 0, 2).reshape(rows, inner_width),
            turned_back(own_grad[:, :HD]),
            own_grad[:, HD:],
        ],
        axis=1,
    )
    grad_linear = lax.all_gather(grad_linear.astype(jnp.bfloat16), "fsdp", axis=0, tiled=True)
    grad_normed = collect(contract_rows(grad_linear, w_qkv).astype(jnp.bfloat16))
    grad_source_norm, gain_one_term = norm_back_one(grad_normed.astype(jnp.float32))
    input_grad = (grad_middle + grad_source_norm).astype(jnp.bfloat16)

    per_owner = ctx_size // fsdp_size

    def in_blocks(term):
        tall, wide = term.shape
        term = term.astype(jnp.bfloat16)
        term = term.reshape(per_owner, tall // per_owner, fsdp_size, wide // fsdp_size)
        return term.transpose(0, 2, 1, 3).reshape(ctx_size, tall // per_owner, wide // fsdp_size)

    def summed(blocks):
        block = lax.psum_scatter(blocks, "ctx", scatter_dimension=0, tiled=True)[0]
        pairs = [
            ((r * fsdp_size + g) * fsdp_size + f, (per_owner * f + r) * fsdp_size + g)
            for r in range(per_owner)
            for g in range(fsdp_size)
            for f in range(fsdp_size)
        ]
        return lax.ppermute(block, ("ctx", "fsdp"), pairs).astype(jnp.float32)

    out_grad = summed(in_blocks(contract_tokens(mixed, grad_branch)))
    qkv_term = contract_tokens(normed, grad_linear)
    qkv_block = summed(
        jnp.concatenate(
            [in_blocks(qkv_term[:, :inner_width]), in_blocks(qkv_term[:, inner_width:])], axis=2
        )
    )
    query_grad = qkv_block[:, : inner_width // fsdp_size]
    keyval_grad = qkv_block[:, inner_width // fsdp_size :]
    gains = lax.psum_scatter(
        jnp.stack([gain_one_term, gain_two_term]),
        ("ctx", "fsdp"),
        scatter_dimension=1,
        tiled=True,
    )
    return (
        result[None],
        input_grad[None],
        gains[0],
        query_grad,
        keyval_grad,
        out_grad,
        gains[1],
        gate_up_grad,
        down_grad,
    )


def solution(mesh):
    placed = (
        P("fsdp", "ctx", None),
        P("fsdp", None),
        P("fsdp", "ctx", None),
        P(),
        P("fsdp", None),
        P("fsdp", None),
        P("fsdp", None),
        P(),
        P("fsdp", None),
        P("fsdp", None),
    )
    return jax.shard_map(
        per_device,
        mesh=mesh,
        in_specs=placed,
        out_specs=(
            P("fsdp", "ctx", None),
            P("fsdp", "ctx", None),
            P(("ctx", "fsdp")),
            P("ctx", "fsdp"),
            P("ctx", "fsdp"),
            P("ctx", "fsdp"),
            P(("ctx", "fsdp")),
            P("ctx", "fsdp"),
            P("ctx", "fsdp"),
        ),
        check_vma=False,
    )
```

```python
import functools

import jax
import jax.numpy as jnp
from jax import lax
from jax.experimental import pallas as pl
from jax.experimental.pallas import tpu as pltpu
from jax.sharding import PartitionSpec as P

HD = 256
WINDOW = 2048


epsilon = 1e-06
f32 = jnp.float32
bf16 = jnp.bfloat16
VMEM = pltpu.VMEM
DMA = pltpu.SemaphoreType.DMA
vmem_bytes = 62 * 1024 * 1024


def rms_norm(values, gain):
    return values * lax.rsqrt(jnp.mean(values * values, axis=-1, keepdims=True) + epsilon) * gain


def frequencies(quarter):
    return 10000.0 ** (-jnp.arange(quarter, dtype=jnp.float32) / quarter)


def documents(index, bounds):
    return (index >= bounds[0]).astype(jnp.int32) + (index >= bounds[1]).astype(jnp.int32)


def rotary_angles(index, bounds):
    member = documents(index, bounds)
    opening = jnp.where(member == 0, 0, jnp.where(member == 1, bounds[0], bounds[1]))
    return (index - opening).astype(jnp.float32)[:, None] * frequencies(HD // 4)[None, :]


def visible(query_index, key_index, bounds):
    apart = query_index[:, None] - key_index[None, :]
    same_doc = documents(query_index, bounds)[:, None] == documents(key_index, bounds)[None, :]
    return (apart >= 0) & (apart < WINDOW) & (key_index[None, :] >= 0) & same_doc


def contract_rows(left, right):
    return lax.dot_general(
        left, right, (((1,), (1,)), ((), ())), preferred_element_type=jnp.float32
    )


def contract_tokens(left, right):
    return lax.dot_general(
        left, right, (((0,), (0,)), ((), ())), preferred_element_type=jnp.float32
    )


def gelu_product(gate_part, up_part):
    return jax.nn.gelu(gate_part, approximate=True) * up_part


def remote(src, dst, send_sem, recv_sem, device):
    return pltpu.make_async_remote_copy(
        src_ref=src,
        dst_ref=dst,
        send_sem=send_sem,
        recv_sem=recv_sem,
        device_id=device,
        device_id_type=pl.DeviceIdType.MESH,
    )


class Place:
    def __init__(self, lines):
        self.lines = lines
        self.c = lax.axis_index("ctx")
        self.f = lax.axis_index("fsdp")
        self.line = self.c // 2
        self.lane = self.c % 2
        self.chip = self.f // 2
        self.core = self.f % 2
        self.twin_f = self.f + 1 - 2 * self.core
        self.cross_f = (self.f + 2) % 4
        self.diag_f = (self.twin_f + 2) % 4
        self.twin = {"fsdp": self.twin_f}
        self.cross = {"fsdp": self.cross_f}
        self.diag = {"fsdp": self.diag_f}
        self.beside = {"ctx": self.c + 1 - 2 * self.lane}
        self.right = {"ctx": self.c + 2}
        self.left = {"ctx": self.c - 2}
        self.has_right = self.line < lines - 1
        self.has_left = self.line > 0

    def barrier(self, ctx=True, fsdp=True):
        sem = pltpu.get_barrier_semaphore()

        def greet(device):
            pl.semaphore_signal(sem, 1, device_id=device, device_id_type=pl.DeviceIdType.MESH)

        count = 0
        if fsdp:
            for device in (self.twin, self.cross, self.diag):
                greet(device)
            count = 3
        if ctx:
            greet(self.beside)
            pl.when(self.has_right)(lambda: greet(self.right))
            pl.when(self.has_left)(lambda: greet(self.left))
            count = (
                count + 1 + self.has_right.astype(jnp.int32) + self.has_left.astype(jnp.int32)
            )
        pl.semaphore_wait(sem, count)


class LineGather:
    sems = 6

    def __init__(self, place, own, slots, sems):
        self.p, self.own, self.slots, self.s = place, own, slots, sems

    def rightward(self, step):
        at = 2 * (self.p.line - step) + self.p.lane
        src = self.own if step == 0 else self.slots.at[at]
        return remote(src, self.slots.at[at], self.s.at[0, step], self.s.at[1, step], self.p.right)

    def leftward(self, step):
        at = 2 * (self.p.line + step) + self.p.lane
        src = self.own if step == 0 else self.slots.at[at]
        return remote(src, self.slots.at[at], self.s.at[2, step], self.s.at[3, step], self.p.left)

    def across(self, line, own=False):
        at = 2 * line + self.p.lane
        src = self.own if own else self.slots.at[at]
        return remote(
            src, self.slots.at[at], self.s.at[4, line], self.s.at[5, line], self.p.beside
        )

    def from_left(self, step):
        at = 2 * (self.p.line - 1 - step) + self.p.lane
        slot = self.slots.at[at]
        return remote(slot, slot, self.s.at[0, step], self.s.at[1, step], self.p.right)

    def from_right(self, step):
        at = 2 * (self.p.line + 1 + step) + self.p.lane
        slot = self.slots.at[at]
        return remote(slot, slot, self.s.at[2, step], self.s.at[3, step], self.p.left)

    def start(self):
        pl.when(self.p.has_right)(lambda: self.rightward(0).start())
        pl.when(self.p.has_left)(lambda: self.leftward(0).start())
        self.across(self.p.line, True).start()

    def step(self, step):
        p = self.p

        @pl.when(p.line - 1 - step >= 0)
        def _():
            self.from_left(step).wait_recv()
            if step + 1 < p.lines - 1:
                pl.when(p.has_right)(lambda: self.rightward(step + 1).start())
            self.across(p.line - 1 - step).start()

        @pl.when(p.line + 1 + step <= p.lines - 1)
        def _():
            self.from_right(step).wait_recv()
            if step + 1 < p.lines - 1:
                pl.when(p.has_left)(lambda: self.leftward(step + 1).start())
            self.across(p.line + 1 + step).start()

    def steps(self):
        for step in range(self.p.lines - 1):
            self.step(step)

    def arrived_across(self, line):
        at = 2 * line + 1 - self.p.lane
        slot = self.slots.at[at]
        remote(slot, slot, self.s.at[4, line], self.s.at[5, line], self.p.beside).wait_recv()

    def finish(self, arrivals=True):
        p = self.p
        if arrivals:
            for line in range(p.lines):
                self.arrived_across(line)
        for step in range(p.lines - 1):
            pl.when(p.has_right & (p.line - step >= 0))(
                lambda step=step: self.rightward(step).wait_send()
            )
            pl.when(p.has_left & (p.line + step <= p.lines - 1))(
                lambda step=step: self.leftward(step).wait_send()
            )
        for line in range(p.lines):
            self.across(line).wait_send()


class LineSum:
    sems = 6

    def __init__(self, place, parts, side, chain, sems):
        self.p, self.parts, self.side, self.chain, self.s = place, parts, side, chain, sems

    def order(self, turn):
        lines, line = self.p.lines, self.p.line
        value = 0
        for a in range(lines):
            far = sorted(range(lines), key=lambda t: (-abs(t - a), t))
            value = value + jnp.where(line == a, far[turn], 0)
        return value

    def across(self, turn):
        t = self.order(turn)
        at = 2 * t + 1 - self.p.lane
        return remote(
            self.parts.at[at],
            self.side.at[t],
            self.s.at[0, t],
            self.s.at[1, t],
            self.p.beside,
        )

    def rightward(self, t):
        step = self.p.lines - 1 - t
        return remote(
            self.parts.at[2 * t + self.p.lane],
            self.chain.at[0, step],
            self.s.at[2, step],
            self.s.at[3, step],
            self.p.right,
        )

    def leftward(self, t):
        return remote(
            self.parts.at[2 * t + self.p.lane],
            self.chain.at[1, t],
            self.s.at[4, t],
            self.s.at[5, t],
            self.p.left,
        )

    def add(self, at, other):
        self.parts[at] = (self.parts[at].astype(f32) + other.astype(f32)).astype(bf16)

    def start(self):
        for turn in range(min(2, self.p.lines)):
            self.across(turn).start()

    def turn(self, turn, ahead=2):
        p = self.p
        t = self.order(turn)
        at = 2 * t + p.lane
        self.across(turn).wait_recv()
        if ahead and turn + ahead < p.lines:
            self.across(turn + ahead).start()
        self.add(at, self.side[t])

        @pl.when(t > p.line)
        def _():
            @pl.when(p.has_left)
            def _():
                self.rightward(t).wait_recv()
                self.add(at, self.chain[0, p.lines - 1 - t])

            self.rightward(t).start()

        @pl.when(t < p.line)
        def _():
            @pl.when(p.has_right)
            def _():
                self.leftward(t).wait_recv()
                self.add(at, self.chain[1, t])

            self.leftward(t).start()

    def turns(self):
        for turn in range(self.p.lines):
            self.turn(turn)

    def total(self):
        p = self.p
        at = 2 * p.line + p.lane

        @pl.when(p.has_left)
        def _():
            self.rightward(p.line).wait_recv()
            self.add(at, self.chain[0, p.lines - 1 - p.line])

        @pl.when(p.has_right)
        def _():
            self.leftward(p.line).wait_recv()
            self.add(at, self.chain[1, p.line])

        return self.parts[at].astype(f32)

    def finish(self):
        p = self.p
        for turn in range(p.lines):
            self.across(turn).wait_send()
        for t in range(p.lines):
            pl.when(t > p.line)(lambda t=t: self.rightward(t).wait_send())
            pl.when(t < p.line)(lambda t=t: self.leftward(t).wait_send())


class GroupSum:
    sems = 6

    def __init__(self, place, parts, near, out, far, sems):
        self.p, self.parts, self.near, self.out, self.far, self.s = place, parts, near, out, far, sems

    def to_twin(self, i, which, cols):
        p = self.p
        block = p.diag_f if which == 0 else p.twin_f
        return remote(
            self.parts.at[block, :, cols],
            self.near.at[which, :, cols],
            self.s.at[which, i],
            self.s.at[2 + which, i],
            p.twin,
        )

    def to_cross(self, i, cols):
        return remote(
            self.out.at[:, cols], self.far.at[:, cols], self.s.at[4, i], self.s.at[5, i], self.p.cross
        )

    def give(self, i, cols):
        self.to_twin(i, 0, cols).start()
        self.to_twin(i, 1, cols).start()

    def pass_on(self, i, cols):
        self.to_twin(i, 0, cols).wait_recv()
        mine = self.parts[self.p.cross_f, :, cols].astype(f32)
        self.out[:, cols] = (mine + self.near[0, :, cols].astype(f32)).astype(bf16)
        self.to_cross(i, cols).start()

    def take(self, i, cols, own=None):
        self.to_twin(i, 1, cols).wait_recv()
        own = self.parts[self.p.f, :, cols] if own is None else own
        near = own.astype(f32) + self.near[1, :, cols].astype(f32)
        self.to_cross(i, cols).wait_recv()
        return near + self.far[:, cols].astype(f32)

    def given(self, i, cols):
        self.to_twin(i, 0, cols).wait_send()
        self.to_twin(i, 1, cols).wait_send()

    def passed(self, i, cols):
        self.to_cross(i, cols).wait_send()

    def finish(self, i, cols):
        self.given(i, cols)
        self.passed(i, cols)


class GroupTrade:
    sems = 2

    def __init__(self, place, whole, slots, sems, columns):
        self.p, self.whole, self.slots, self.s, self.n = place, whole, slots, sems, columns

    def block(self, g):
        return self.whole.at[:, pl.ds(pl.multiple_of(g * self.n, 128), self.n)]

    def copy(self, d):
        g = (self.p.f + d) % 4
        return remote(
            self.block(g), self.slots.at[self.p.f], self.s.at[0, d], self.s.at[1, d], {"fsdp": g}
        )

    def arrival(self, d):
        slot = self.slots.at[(self.p.f + 4 - d) % 4]
        return remote(slot, slot, self.s.at[0, d], self.s.at[1, d], {"fsdp": (self.p.f + d) % 4})

    def own(self):
        return pltpu.make_async_copy(
            self.block(self.p.f), self.slots.at[self.p.f], self.s.at[1, 0]
        )

    def start(self):
        for d in (2, 3, 1):
            self.copy(d).start()
        self.own().start()

    def wait(self):
        self.own().wait()
        for d in (1, 2, 3):
            self.arrival(d).wait_recv()

    def finish(self):
        for d in (1, 2, 3):
            self.copy(d).wait_send()


def rotated(v, cosine, sine):
    first = v[:, :128]
    return jnp.concatenate(
        [first * cosine + pltpu.roll(first, 64, 1) * sine, v[:, 128:]], axis=1
    )


class GroupGather:
    sems = 6

    def __init__(self, place, own, whole, sems, own_sem, pieces):
        self.p, self.own, self.whole, self.s, self.own_sem = place, own, whole, sems, own_sem
        self.pieces, self.n = pieces, own.shape[0] // pieces

    def part(self, ref, i):
        return ref.at[pl.ds(i * self.n, self.n)]

    def slot(self, g, i):
        return self.whole.at[g, pl.ds(i * self.n, self.n)]

    def local(self):
        return pltpu.make_async_copy(self.own, self.whole.at[self.p.f], self.own_sem)

    def to_twin(self, i):
        return remote(
            self.part(self.own, i), self.slot(self.p.f, i), self.s.at[0, i], self.s.at[3, i], self.p.twin
        )

    def to_cross(self, i):
        return remote(
            self.part(self.own, i), self.slot(self.p.f, i), self.s.at[1, i], self.s.at[4, i], self.p.cross
        )

    def forward(self, i):
        slot = self.slot(self.p.cross_f, i)
        return remote(slot, slot, self.s.at[2, i], self.s.at[5, i], self.p.twin)

    def give(self, i):
        self.to_cross(i).start()
        self.to_twin(i).start()

    def pass_on(self, i):
        slot = self.slot(self.p.cross_f, i)
        remote(slot, slot, self.s.at[1, i], self.s.at[4, i], self.p.cross).wait_recv()
        self.forward(i).start()

    def finish(self, i):
        twin, diag = self.slot(self.p.twin_f, i), self.slot(self.p.diag_f, i)
        remote(twin, twin, self.s.at[0, i], self.s.at[3, i], self.p.twin).wait_recv()
        remote(diag, diag, self.s.at[2, i], self.s.at[5, i], self.p.twin).wait_recv()
        self.to_twin(i).wait_send()
        self.to_cross(i).wait_send()
        self.forward(i).wait_send()


def tiles_of(first, count, tile):
    tile = tile if count % tile == 0 else 128

    def loop(body):
        def one(i, carry):
            body(pl.ds(pl.multiple_of(first + i * tile, 128), tile))
            return carry

        lax.fori_loop(0, count // tile, one, 0)

    return loop


def front_kernel(
    lines,
    x_ref,
    gain_one,
    gain_two,
    cosine,
    sine,
    bias,
    w_keyval,
    w_query,
    w_out,
    cot,
    w_rows,
    normed_out,
    query_out,
    keyval_out,
    probs_out,
    mixed_out,
    middle_out,
    normed_two_out,
    cot_all,
    rows_all,
    whole,
    slots,
    parts,
    near,
    out,
    far,
    keyval,
    mixed,
    trade_sems,
    sum_sems,
    keyval_sems,
    cot_sems,
    row_sems,
    own_sems,
):
    p = Place(lines)
    rows, width = x_ref.shape
    heads = query_out.shape[0]
    inner = heads * HD
    kv_width = 2 * HD
    p.barrier()

    down = GroupGather(p, w_rows, rows_all, row_sems, own_sems.at[0], row_sems.shape[1])
    cot_gather = LineGather(p, cot, cot_all, cot_sems)
    cot_local = pltpu.make_async_copy(cot, cot_all.at[p.c], own_sems.at[1])

    source = x_ref[...].astype(f32)
    whole[...] = rms_norm(source, gain_one[...]).astype(bf16)
    trade = GroupTrade(p, whole, slots.at[0], trade_sems.at[0], slots.shape[3])
    trade.start()
    down.local().start()
    cot_local.start()
    cot_gather.start()
    trade.wait()
    normed_out[...] = slots[0]

    half = (heads // 2) * HD
    chunks = [(0, kv_width), (kv_width, half), (kv_width + half, inner - half)]
    group = GroupSum(p, parts, near, out, far, sum_sems.at[0])

    def project(lhs, weight, first, count, to):
        @tiles_of(first, count, 256)
        def _(cols):
            left = lhs[...].reshape(4 * rows, lhs.shape[-1])
            product = jnp.dot(left, weight[:, cols], preferred_element_type=f32)
            if to:
                cols = pl.ds(pl.multiple_of(cols.start + to, 128), cols.size)
            parts[:, :, cols] = product.astype(bf16).reshape(4, rows, cols.size)

    spans = [pl.ds(first, count) for first, count in chunks]
    project(slots.at[0], w_keyval, 0, kv_width, 0)
    group.give(0, spans[0])
    project(slots.at[0], w_query, 0, half, kv_width)
    group.give(1, spans[1])
    group.pass_on(0, spans[0])
    project(slots.at[0], w_query, half, inner - half, kv_width)
    group.give(2, spans[2])
    group.pass_on(1, spans[1])
    group.pass_on(2, spans[2])
    cot_gather.step(0)

    linear = group.take(0, spans[0])
    keyval[p.c] = jnp.concatenate(
        [rotated(linear[:, :HD], cosine[...], sine[...]), linear[:, HD:]], axis=1
    ).astype(bf16)
    kv_gather = LineGather(p, keyval.at[p.c], keyval, keyval_sems)
    kv_gather.start()
    for i in (1, 2):
        linear = group.take(i, spans[i])
        for h in range(linear.shape[1] // HD):
            turned = rotated(linear[:, h * HD : (h + 1) * HD], cosine[...], sine[...])
            at = h if i == 1 else h + heads // 2
            query_out[at] = (turned * HD**-0.5).astype(bf16)
        if i == 1:
            kv_gather.step(0)
    for i in range(down.pieces):
        down.give(i)
    for step in range(1, lines - 1):
        kv_gather.step(step)
    kv_gather.finish()
    if lines > 2:
        cot_gather.step(1)
    keyval_out[...] = keyval[...]

    length = bias.shape[1]

    def two_heads(i, carry):
        keys = keyval[:, :, :HD].reshape(length, HD)
        values = keyval[:, :, HD:].reshape(length, HD)
        two = query_out[pl.ds(2 * i, 2)].reshape(2 * rows, HD)
        scores = contract_rows(two, keys).reshape(2, rows, length) + bias[...][None]
        scores = scores.reshape(2 * rows, length)
        weights = jnp.exp(scores - jnp.max(scores, axis=-1, keepdims=True))
        total = jnp.sum(weights, axis=-1, keepdims=True)
        weights = (weights / total).astype(bf16)
        probs_out[pl.ds(2 * i, 2)] = weights.reshape(2, rows, length)
        product = jnp.dot(weights, values, preferred_element_type=f32).astype(bf16)
        at = pl.multiple_of(i * 2 * HD, 128)
        mixed[:, pl.ds(at, HD)] = product[:rows]
        mixed[:, pl.ds(at + HD, HD)] = product[rows:]
        return carry

    lax.fori_loop(0, heads // 2, two_heads, 0)
    trade_two = GroupTrade(p, mixed, slots.at[1], trade_sems.at[1], slots.shape[3])
    trade_two.start()
    for step in range(2, lines - 1):
        cot_gather.step(step)
    for i in range(len(chunks)):
        group.finish(i, spans[i])
    trade_two.wait()
    mixed_out[...] = slots[1]

    half = width // 2
    spans_two = [pl.ds(0, half), pl.ds(half, half)]
    group_two = GroupSum(p, parts, near, out, far, sum_sems.at[1])
    for i in range(2):
        project(slots.at[1], w_out, i * half, half, 0)
        group_two.give(i, spans_two[i])
    for i in range(2):
        group_two.pass_on(i, spans_two[i])
    for i in range(2):
        middle_out[:, spans_two[i]] = x_ref[:, spans_two[i]].astype(f32) + group_two.take(
            i, spans_two[i]
        )
    normed_two_out[...] = rms_norm(middle_out[...], gain_two[...]).astype(bf16)

    for i in range(down.pieces):
        down.pass_on(i)
    for i in range(2):
        group_two.finish(i, spans_two[i])
    trade.finish()
    trade_two.finish()
    down.local().wait()
    cot_local.wait()
    for i in range(down.pieces):
        down.finish(i)
    cot_gather.finish()


def front(lines, operands, heads):
    x = operands[0]
    rows, width = x.shape
    places = 2 * lines
    length = places * rows
    inner = heads * HD
    shard = width // 4
    parts_width = inner + 2 * HD
    in_vmem = pl.BlockSpec(memory_space=VMEM)
    anywhere = pl.BlockSpec(memory_space=pl.ANY)
    shape = jax.ShapeDtypeStruct
    pieces = 2
    assert inner == width
    return pl.pallas_call(
        functools.partial(front_kernel, lines),
        out_shape=(
            shape((4, rows, shard), bf16),
            shape((heads, rows, HD), bf16),
            shape((places, rows, 2 * HD), bf16),
            shape((heads, rows, length), bf16),
            shape((4, rows, shard), bf16),
            shape((rows, width), f32),
            shape((rows, width), bf16),
            shape((places, rows, width), bf16),
            shape((4,) + operands[10].shape, bf16),
        ),
        in_specs=[in_vmem] * 9 + [anywhere] * 2,
        out_specs=[in_vmem] * 7 + [anywhere] * 2,
        scratch_shapes=[
            VMEM((rows, width), bf16),
            VMEM((2, 4, rows, shard), bf16),
            VMEM((4, rows, parts_width), bf16),
            VMEM((2, rows, parts_width), bf16),
            VMEM((rows, parts_width), bf16),
            VMEM((rows, parts_width), bf16),
            VMEM((places, rows, 2 * HD), bf16),
            VMEM((rows, inner), bf16),
            DMA((2, GroupTrade.sems, 4)),
            DMA((2, GroupSum.sems, 3)),
            DMA((LineGather.sems, lines)),
            DMA((LineGather.sems, lines)),
            DMA((GroupGather.sems, pieces)),
            DMA((2,)),
        ],
        compiler_params=pltpu.CompilerParams(
            collective_id=0, has_side_effects=True, vmem_limit_bytes=vmem_bytes
        ),
        name="front",
    )(*operands)


def gelu_parts(v):
    k = 0.7978845608028654
    square = v * v
    inner = jnp.tanh(k * v * (1.0 + 0.044715 * square))
    half = 0.5 * (1.0 + inner)
    slope = half + 0.5 * v * (1.0 - inner * inner) * (k * (1.0 + 3 * 0.044715 * square))
    return v * half, slope


def norm_back(values, gain, grad):
    r = lax.rsqrt(jnp.mean(values * values, axis=-1, keepdims=True) + epsilon)
    scaled = values * r
    inner = grad * gain
    grad_values = r * (inner - scaled * jnp.mean(inner * scaled, axis=-1, keepdims=True))
    return grad_values, jnp.sum(grad * scaled, axis=0, keepdims=True)


def middle_kernel(
    lines,
    cot_all,
    w_rows,
    gain_two,
    own,
    middle,
    w_columns,
    grad_middle_out,
    gain_out,
    grads_out,
    down_out,
    normed_all_out,
    result_parts,
    normed_all,
    weights,
    grad_hidden,
    hidden,
    parts,
    side,
    chain,
    down_near,
    down_stage,
    down_far,
    gather_sems,
    column_sems,
    sum_sems,
    down_sems,
    own_sems,
):
    p = Place(lines)
    rows, width = own.shape
    two = 2 * rows
    padded = hidden.shape[2]
    shard = width // 4
    tile = 256 if padded % 256 == 0 else 128
    p.barrier()

    columns = GroupGather(p, w_columns, weights, column_sems, own_sems.at[0], column_sems.shape[1])
    gather = LineGather(p, own, normed_all, gather_sems)
    gather.start()
    for i in range(columns.pieces):
        columns.give(i)
    columns.local().start()
    own_local = pltpu.make_async_copy(own, normed_all.at[p.c], own_sems.at[2 + lines])
    own_local.start()
    middle_local = pltpu.make_async_copy(middle, grad_middle_out, own_sems.at[3 + lines])
    middle_local.start()

    def hidden_grad(line):
        def one(i, carry):
            cols = pl.ds(pl.multiple_of(i * tile, 128), tile)
            left = cot_all[pl.ds(2 * line, 2)].reshape(two, width)
            right = w_rows[pl.ds(pl.multiple_of(i * tile, 16), tile)]
            grad_hidden[line, :, cols] = contract_rows(left, right)
            return carry

        lax.fori_loop(0, padded // tile, one, 0)

    done = 0
    for step in range(lines - 1):
        hidden_grad(done)
        done += 1
        gather.step(step)
        if step < columns.pieces:
            columns.pass_on(step)
    for i in range(lines - 1, columns.pieces):
        columns.pass_on(i)
    while done < lines:
        hidden_grad(done)
        done += 1
    gather.finish()
    own_local.wait()
    columns.local().wait()
    for i in range(columns.pieces):
        columns.finish(i)
    normed_local = pltpu.make_async_copy(normed_all, normed_all_out, own_sems.at[1])
    normed_local.start()

    line_sum = LineSum(p, parts, side, chain, sum_sems)

    def feed_forward(line):
        def one(i, carry):
            cols = pl.ds(pl.multiple_of(i * tile, 128), tile)
            up_cols = pl.ds(pl.multiple_of(i * tile + padded, 128), tile)
            left = normed_all[pl.ds(2 * line, 2)].reshape(two, width)
            gate = jnp.dot(
                left, weights[:, :, cols].reshape(width, tile), preferred_element_type=f32
            )
            up = jnp.dot(
                left, weights[:, :, up_cols].reshape(width, tile), preferred_element_type=f32
            )
            gelu, slope = gelu_parts(gate)
            grad = grad_hidden[line, :, cols]
            hidden[line, :, cols] = (gelu * up).astype(bf16)
            grads_out[line, :, cols] = (grad * up * slope).astype(bf16)
            grads_out[line, :, up_cols] = (grad * gelu).astype(bf16)
            return carry

        lax.fori_loop(0, padded // tile, one, 0)

        def back(g, carry):
            product = contract_rows(grads_out[line], weights[g]).astype(bf16)
            cols = pl.ds(pl.multiple_of(g * shard, 128), shard)
            parts[pl.ds(2 * line, 2), :, cols] = product.reshape(2, rows, shard)
            return carry

        lax.fori_loop(0, 4, back, 0)

    result_stage = normed_all

    def result_copy(line):
        blocks = pl.ds(2 * line, 2)
        return pltpu.make_async_copy(
            result_stage.at[blocks], result_parts.at[blocks], own_sems.at[2 + line]
        )

    def result_part(line):
        def one(i, carry):
            cols = pl.ds(pl.multiple_of(i * shard, 128), shard)
            product = jnp.dot(
                hidden[line], w_rows[:, cols], preferred_element_type=f32
            ).astype(bf16)
            result_stage[pl.ds(2 * line, 2), :, cols] = product.reshape(2, rows, shard)
            return carry

        lax.fori_loop(0, 4, one, 0)
        result_copy(line).start()

    quarter = padded // 4
    every = slice(None)
    down_parts = weights.at[:, pl.ds(0, quarter), pl.ds(0, shard)]

    def down_group(i):
        return GroupSum(p, down_parts, down_near.at[i], down_stage.at[i % 2], down_far.at[i], down_sems)

    def down_chunk(i):
        def one(g, carry):
            cols = pl.ds(pl.multiple_of(g * shard, 128), shard)
            left = hidden[:, :, i * quarter : (i + 1) * quarter].reshape(lines * two, quarter)
            right = cot_all[:, :, cols].reshape(lines * two, shard)
            down_parts[g] = contract_tokens(left, right).astype(bf16)
            return carry

        lax.fori_loop(0, 4, one, 0)
        down_out[i] = down_parts[p.f]
        down_group(i).give(i, every)

    for turn in range(lines):
        feed_forward(line_sum.order(turn))
        line_sum.across(turn).start()
        if turn > 0:
            line_sum.turn(turn - 1, 0)
    normed_local.wait()

    for i in range(4):
        if i >= 1:
            down_group(i - 1).given(i - 1, every)
        if i >= 2:
            down_out[i - 2] = down_group(i - 2).take(i - 2, every, down_out[i - 2]).astype(bf16)
            down_group(i - 2).passed(i - 2, every)
        down_chunk(i)
        if i < lines:
            result_part(i)
        down_group(i).pass_on(i, every)
    for line in range(4, lines):
        result_part(line)
    line_sum.turn(lines - 1, 0)
    grad = line_sum.total()
    middle_local.wait()
    grad_values, gain = norm_back(grad_middle_out[...], gain_two[...], grad)
    grad_middle_out[...] = cot_all[p.c].astype(f32) + grad_values
    gain_out[...] = gain
    for i in (2, 3):
        down_out[i] = down_group(i).take(i, every, down_out[i]).astype(bf16)
        down_group(i).passed(i, every)
    down_group(3).given(3, every)
    for line in range(lines):
        result_copy(line).wait()
    line_sum.finish()


def middle_bytes(lines, rows, width, padded):
    length = 2 * lines * rows
    return (
        14 * rows * width
        + 9 * length * width
        + 9 * padded * width
        + 10 * length * padded
    )


def middle_part(lines, operands, padded):
    own = operands[3]
    rows, width = own.shape
    places = 2 * lines
    shard = width // 4
    quarter = padded // 4
    pieces = 4
    in_vmem = pl.BlockSpec(memory_space=VMEM)
    anywhere = pl.BlockSpec(memory_space=pl.ANY)
    shape = jax.ShapeDtypeStruct
    return pl.pallas_call(
        functools.partial(middle_kernel, lines),
        out_shape=(
            shape((rows, width), f32),
            shape((1, width), f32),
            shape((lines, 2 * rows, 2 * padded), bf16),
            shape((4, quarter, shard), bf16),
            shape((places, rows, width), bf16),
            shape((places, rows, width), bf16),
        ),
        in_specs=[in_vmem] * 3 + [anywhere] * 3,
        out_specs=[in_vmem] * 4 + [anywhere] * 2,
        scratch_shapes=[
            VMEM((places, rows, width), bf16),
            VMEM((4, shard, 2 * padded), bf16),
            VMEM((lines, 2 * rows, padded), f32),
            VMEM((lines, 2 * rows, padded), bf16),
            VMEM((places, rows, width), bf16),
            VMEM((lines, rows, width), bf16),
            VMEM((2, lines - 1, rows, width), bf16),
            VMEM((4, 2, quarter, shard), bf16),
            VMEM((2, quarter, shard), bf16),
            VMEM((4, quarter, shard), bf16),
            DMA((LineGather.sems, lines)),
            DMA((GroupGather.sems, pieces)),
            DMA((LineSum.sems, lines)),
            DMA((GroupSum.sems, 4)),
            DMA((4 + lines,)),
        ],
        compiler_params=pltpu.CompilerParams(
            collective_id=1, has_side_effects=True, vmem_limit_bytes=vmem_bytes
        ),
        name="middle",
    )(*operands)


def per_device(
    tokens,
    doc_bounds,
    cotangent,
    norm_one,
    query_weight,
    keyval_weight,
    out_weight,
    norm_two,
    gate_up_weight,
    down_weight,
):
    ctx_size = lax.axis_size("ctx")
    fsdp_size = lax.axis_size("fsdp")
    lines = ctx_size // 2
    rows = tokens.shape[1]
    width = tokens.shape[2]
    length = rows * ctx_size
    inner_width = query_weight.shape[1]
    head_count = inner_width // HD
    hidden_width = gate_up_weight.shape[1] // 2
    piece = hidden_width // (ctx_size * fsdp_size)
    padded_piece = -(-piece // 32) * 32
    padded = padded_piece * fsdp_size
    ctx_place = lax.axis_index("ctx")
    source = tokens[0].astype(jnp.float32)
    bounds = doc_bounds[0]
    query_index = ctx_place * rows + jnp.arange(rows, dtype=jnp.int32)
    key_index = jnp.arange(length, dtype=jnp.int32)
    allowed = visible(query_index, key_index, bounds)
    bias = jnp.where(allowed, 0.0, -1e30).astype(jnp.float32)
    angles = rotary_angles(query_index, bounds)
    cosine = jnp.cos(angles)
    sine = jnp.sin(angles)
    cosine = jnp.concatenate([cosine, cosine], axis=1)
    sine = jnp.concatenate([-sine, sine], axis=1)

    def padded_to(value, axis):
        pads = [(0, 0)] * value.ndim
        pads[axis] = (0, padded_piece - piece)
        return jnp.pad(value, pads)

    shard_width = hidden_width // fsdp_size
    w_columns = jnp.concatenate(
        [
            padded_to(
                lax.dynamic_slice_in_dim(
                    gate_up_weight, q * shard_width + ctx_place * piece, piece, 1
                ),
                1,
            )
            for q in range(2 * fsdp_size)
        ],
        axis=1,
    )
    w_rows = padded_to(lax.dynamic_slice_in_dim(down_weight, ctx_place * piece, piece, 0), 0)
    cot_rows = cotangent[0]
    (
        normed,
        queries,
        window,
        weights,
        mixed,
        middle,
        normed_two,
        cot_all,
        w_down,
    ) = front(
        lines,
        (
            tokens[0],
            norm_one[None],
            norm_two[None],
            cosine,
            sine,
            bias,
            keyval_weight,
            query_weight,
            out_weight,
            cot_rows,
            w_rows,
        ),
        head_count,
    )
    normed = normed.reshape(fsdp_size * rows, -1)
    mixed = mixed.reshape(fsdp_size * rows, -1)
    window = window.reshape(length, -1)
    key_rows = window[:, :HD]
    value_rows = window[:, HD:]
    w_qkv = jnp.concatenate([query_weight, keyval_weight], axis=1)

    def collect(value):
        return lax.all_to_all(value, "fsdp", split_axis=0, concat_axis=1, tiled=True)

    _, norm_back_one = jax.vjp(rms_norm, source, norm_one)
    w_down = w_down.reshape(padded, width)
    if middle_bytes(lines, rows, width, padded) <= vmem_bytes:
        grad_middle, gain_two_term, grad_gate_up, down_part, normed_two, result_parts = middle_part(
            lines, (cot_all, w_down, norm_two[None], normed_two, middle, w_columns), padded
        )
        gain_two_term = gain_two_term[0]
        normed_two = normed_two.reshape(length, width)
        grad_gate_up = grad_gate_up.reshape(length, 2 * padded)
        result_parts = result_parts.reshape(length, width)
    else:
        cot_all = cot_all.reshape(length, width)
        normed_two = lax.all_gather(normed_two, "ctx", axis=0, tiled=True)
        w_gate_up = lax.all_gather(w_columns, "fsdp", axis=0, tiled=True)
        projected = jnp.dot(normed_two, w_gate_up, preferred_element_type=f32)
        gelu, slope = gelu_parts(projected[:, :padded])
        up_part = projected[:, padded:]
        hidden = (gelu * up_part).astype(bf16)
        grad_hidden = contract_rows(cot_all, w_down)
        grad_gate_up = jnp.concatenate(
            [grad_hidden * up_part * slope, grad_hidden * gelu], axis=1
        ).astype(bf16)
        grad_normed_two = lax.psum_scatter(
            contract_rows(grad_gate_up, w_gate_up).astype(bf16),
            "ctx",
            scatter_dimension=0,
            tiled=True,
        ).astype(f32)
        grad_middle_norm, gain_two_term = norm_back(middle, norm_two[None], grad_normed_two)
        gain_two_term = gain_two_term[0]
        grad_middle = cot_rows.astype(f32) + grad_middle_norm
        result_parts = jnp.dot(hidden, w_down, preferred_element_type=f32).astype(bf16)
        down_part = lax.psum_scatter(
            contract_tokens(hidden, cot_all).astype(bf16),
            "fsdp",
            scatter_dimension=1,
            tiled=True,
        ).reshape(fsdp_size, padded_piece, -1)
    branch_two = lax.psum_scatter(result_parts, "ctx", scatter_dimension=0, tiled=True)
    result = (middle + branch_two.astype(f32)).astype(bf16)

    per_owner = ctx_size // fsdp_size
    down_grad = lax.all_to_all(jnp.repeat(down_part, per_owner, axis=0), "ctx", 0, 0, tiled=True)
    first = (ctx_place % per_owner) * fsdp_size
    down_grad = lax.dynamic_slice_in_dim(down_grad, first, fsdp_size, 0)
    down_grad = down_grad[:, :piece].reshape(fsdp_size * piece, -1).astype(f32)

    gate_up_part = lax.psum_scatter(
        contract_tokens(normed_two, grad_gate_up).astype(bf16),
        "fsdp",
        scatter_dimension=1,
        tiled=True,
    )
    gate_up_part = lax.all_to_all(
        gate_up_part.reshape(ctx_size, width // ctx_size, -1), "ctx", 0, 0, tiled=True
    )
    gate_up_part = gate_up_part.reshape(ctx_size, width // ctx_size, 2, padded_piece)[..., :piece]
    gate_up_grad = (
        gate_up_part.transpose(1, 2, 0, 3).reshape(width // ctx_size, -1).astype(f32)
    )

    grad_branch = lax.all_gather(grad_middle.astype(jnp.bfloat16), "fsdp", axis=0, tiled=True)
    grad_mixed = collect(contract_rows(grad_branch, out_weight).astype(jnp.bfloat16))
    grad_mixed = grad_mixed.reshape(rows, head_count, HD)

    grad_weights = jnp.einsum(
        "thd,kd->htk", grad_mixed, value_rows, preferred_element_type=jnp.float32
    )
    row_delta = jnp.sum(weights * grad_weights, axis=-1, keepdims=True)
    grad_scores = (weights * (grad_weights - row_delta)).astype(jnp.bfloat16)
    grad_queries = jnp.einsum(
        "htk,kd->htd", grad_scores, key_rows, preferred_element_type=jnp.float32
    )
    grad_keys = jnp.einsum("htk,htd->kd", grad_scores, queries, preferred_element_type=jnp.float32)
    grad_values = jnp.einsum(
        "htk,thd->kd", weights, grad_mixed, preferred_element_type=jnp.float32
    )
    own_grad = lax.psum_scatter(
        jnp.concatenate([grad_keys, grad_values], axis=1).astype(jnp.bfloat16),
        "ctx",
        scatter_dimension=0,
        tiled=True,
    ).astype(jnp.float32)

    def turned_back(part):
        first = part[..., :128]
        swapped = jnp.concatenate([first[..., 64:], first[..., :64]], axis=-1)
        return jnp.concatenate([first * cosine - swapped * sine, part[..., 128:]], axis=-1)

    grad_linear = jnp.concatenate(
        [
            (turned_back(grad_queries) * HD**-0.5).transpose(1, 0, 2).reshape(rows, inner_width),
            turned_back(own_grad[:, :HD]),
            own_grad[:, HD:],
        ],
        axis=1,
    )
    grad_linear = lax.all_gather(grad_linear.astype(jnp.bfloat16), "fsdp", axis=0, tiled=True)
    grad_normed = collect(contract_rows(grad_linear, w_qkv).astype(jnp.bfloat16))
    grad_source_norm, gain_one_term = norm_back_one(grad_normed.astype(jnp.float32))
    input_grad = (grad_middle + grad_source_norm).astype(jnp.bfloat16)


    def in_blocks(term):
        tall, wide = term.shape
        term = term.astype(jnp.bfloat16)
        term = term.reshape(per_owner, tall // per_owner, fsdp_size, wide // fsdp_size)
        return term.transpose(0, 2, 1, 3).reshape(ctx_size, tall // per_owner, wide // fsdp_size)

    def summed(blocks):
        block = lax.psum_scatter(blocks, "ctx", scatter_dimension=0, tiled=True)[0]
        pairs = [
            ((r * fsdp_size + g) * fsdp_size + f, (per_owner * f + r) * fsdp_size + g)
            for r in range(per_owner)
            for g in range(fsdp_size)
            for f in range(fsdp_size)
        ]
        return lax.ppermute(block, ("ctx", "fsdp"), pairs).astype(jnp.float32)

    out_grad = summed(in_blocks(contract_tokens(mixed, grad_branch)))
    qkv_term = contract_tokens(normed, grad_linear)
    qkv_block = summed(
        jnp.concatenate(
            [in_blocks(qkv_term[:, :inner_width]), in_blocks(qkv_term[:, inner_width:])], axis=2
        )
    )
    query_grad = qkv_block[:, : inner_width // fsdp_size]
    keyval_grad = qkv_block[:, inner_width // fsdp_size :]
    gains = lax.psum_scatter(
        jnp.stack([gain_one_term, gain_two_term]),
        ("ctx", "fsdp"),
        scatter_dimension=1,
        tiled=True,
    )
    return (
        result[None],
        input_grad[None],
        gains[0],
        query_grad,
        keyval_grad,
        out_grad,
        gains[1],
        gate_up_grad,
        down_grad,
    )


def solution(mesh):
    placed = (
        P("fsdp", "ctx", None),
        P("fsdp", None),
        P("fsdp", "ctx", None),
        P(),
        P("fsdp", None),
        P("fsdp", None),
        P("fsdp", None),
        P(),
        P("fsdp", None),
        P("fsdp", None),
    )
    return jax.shard_map(
        per_device,
        mesh=mesh,
        in_specs=placed,
        out_specs=(
            P("fsdp", "ctx", None),
            P("fsdp", "ctx", None),
            P(("ctx", "fsdp")),
            P("ctx", "fsdp"),
            P("ctx", "fsdp"),
            P("ctx", "fsdp"),
            P(("ctx", "fsdp")),
            P("ctx", "fsdp"),
            P("ctx", "fsdp"),
        ),
        check_vma=False,
    )
```

```python
import functools

import jax
import jax.numpy as jnp
from jax import lax
from jax.experimental import pallas as pl
from jax.experimental.pallas import tpu as pltpu
from jax.sharding import PartitionSpec as P

HD = 256
WINDOW = 2048


epsilon = 1e-06
f32 = jnp.float32
bf16 = jnp.bfloat16
VMEM = pltpu.VMEM
DMA = pltpu.SemaphoreType.DMA
vmem_bytes = 62 * 1024 * 1024


def rms_norm(values, gain):
    return values * lax.rsqrt(jnp.mean(values * values, axis=-1, keepdims=True) + epsilon) * gain


def frequencies(quarter):
    return 10000.0 ** (-jnp.arange(quarter, dtype=jnp.float32) / quarter)


def documents(index, bounds):
    return (index >= bounds[0]).astype(jnp.int32) + (index >= bounds[1]).astype(jnp.int32)


def rotary_angles(index, bounds):
    member = documents(index, bounds)
    opening = jnp.where(member == 0, 0, jnp.where(member == 1, bounds[0], bounds[1]))
    return (index - opening).astype(jnp.float32)[:, None] * frequencies(HD // 4)[None, :]


def visible(query_index, key_index, bounds):
    apart = query_index[:, None] - key_index[None, :]
    same_doc = documents(query_index, bounds)[:, None] == documents(key_index, bounds)[None, :]
    return (apart >= 0) & (apart < WINDOW) & (key_index[None, :] >= 0) & same_doc


def contract_rows(left, right):
    return lax.dot_general(
        left, right, (((1,), (1,)), ((), ())), preferred_element_type=jnp.float32
    )


def contract_tokens(left, right):
    return lax.dot_general(
        left, right, (((0,), (0,)), ((), ())), preferred_element_type=jnp.float32
    )


def gelu_product(gate_part, up_part):
    return jax.nn.gelu(gate_part, approximate=True) * up_part


def remote(src, dst, send_sem, recv_sem, device):
    return pltpu.make_async_remote_copy(
        src_ref=src,
        dst_ref=dst,
        send_sem=send_sem,
        recv_sem=recv_sem,
        device_id=device,
        device_id_type=pl.DeviceIdType.MESH,
    )


class Place:
    def __init__(self, lines):
        self.lines = lines
        self.c = lax.axis_index("ctx")
        self.f = lax.axis_index("fsdp")
        self.line = self.c // 2
        self.lane = self.c % 2
        self.chip = self.f // 2
        self.core = self.f % 2
        self.twin_f = self.f + 1 - 2 * self.core
        self.cross_f = (self.f + 2) % 4
        self.diag_f = (self.twin_f + 2) % 4
        self.twin = {"fsdp": self.twin_f}
        self.cross = {"fsdp": self.cross_f}
        self.diag = {"fsdp": self.diag_f}
        self.beside = {"ctx": self.c + 1 - 2 * self.lane}
        self.right = {"ctx": self.c + 2}
        self.left = {"ctx": self.c - 2}
        self.has_right = self.line < lines - 1
        self.has_left = self.line > 0

    def barrier(self, ctx=True, fsdp=True, also=()):
        sem = pltpu.get_barrier_semaphore()

        def greet(device):
            pl.semaphore_signal(sem, 1, device_id=device, device_id_type=pl.DeviceIdType.MESH)

        count = 0
        if fsdp:
            for device in (self.twin, self.cross, self.diag):
                greet(device)
            count = 3
        if ctx:
            greet(self.beside)
            pl.when(self.has_right)(lambda: greet(self.right))
            pl.when(self.has_left)(lambda: greet(self.left))
            count = (
                count + 1 + self.has_right.astype(jnp.int32) + self.has_left.astype(jnp.int32)
            )
        for needed, device in also:
            pl.when(needed)(lambda device=device: greet(device))
            count = count + needed.astype(jnp.int32)
        pl.semaphore_wait(sem, count)


class LineGather:
    sems = 6

    def __init__(self, place, own, slots, sems):
        self.p, self.own, self.slots, self.s = place, own, slots, sems

    def rightward(self, step):
        at = 2 * (self.p.line - step) + self.p.lane
        src = self.own if step == 0 else self.slots.at[at]
        return remote(src, self.slots.at[at], self.s.at[0, step], self.s.at[1, step], self.p.right)

    def leftward(self, step):
        at = 2 * (self.p.line + step) + self.p.lane
        src = self.own if step == 0 else self.slots.at[at]
        return remote(src, self.slots.at[at], self.s.at[2, step], self.s.at[3, step], self.p.left)

    def across(self, line, own=False):
        at = 2 * line + self.p.lane
        src = self.own if own else self.slots.at[at]
        return remote(
            src, self.slots.at[at], self.s.at[4, line], self.s.at[5, line], self.p.beside
        )

    def from_left(self, step):
        at = 2 * (self.p.line - 1 - step) + self.p.lane
        slot = self.slots.at[at]
        return remote(slot, slot, self.s.at[0, step], self.s.at[1, step], self.p.right)

    def from_right(self, step):
        at = 2 * (self.p.line + 1 + step) + self.p.lane
        slot = self.slots.at[at]
        return remote(slot, slot, self.s.at[2, step], self.s.at[3, step], self.p.left)

    def start(self):
        pl.when(self.p.has_right)(lambda: self.rightward(0).start())
        pl.when(self.p.has_left)(lambda: self.leftward(0).start())
        self.across(self.p.line, True).start()

    def step(self, step):
        p = self.p

        @pl.when(p.line - 1 - step >= 0)
        def _():
            self.from_left(step).wait_recv()
            if step + 1 < p.lines - 1:
                pl.when(p.has_right)(lambda: self.rightward(step + 1).start())
            self.across(p.line - 1 - step).start()

        @pl.when(p.line + 1 + step <= p.lines - 1)
        def _():
            self.from_right(step).wait_recv()
            if step + 1 < p.lines - 1:
                pl.when(p.has_left)(lambda: self.leftward(step + 1).start())
            self.across(p.line + 1 + step).start()

    def steps(self):
        for step in range(self.p.lines - 1):
            self.step(step)

    def arrived_across(self, line):
        at = 2 * line + 1 - self.p.lane
        slot = self.slots.at[at]
        remote(slot, slot, self.s.at[4, line], self.s.at[5, line], self.p.beside).wait_recv()

    def finish(self, arrivals=True):
        p = self.p
        if arrivals:
            for line in range(p.lines):
                self.arrived_across(line)
        for step in range(p.lines - 1):
            pl.when(p.has_right & (p.line - step >= 0))(
                lambda step=step: self.rightward(step).wait_send()
            )
            pl.when(p.has_left & (p.line + step <= p.lines - 1))(
                lambda step=step: self.leftward(step).wait_send()
            )
        for line in range(p.lines):
            self.across(line).wait_send()


class LineSum:
    sems = 6

    def __init__(self, place, parts, side, chain, sems):
        self.p, self.parts, self.side, self.chain, self.s = place, parts, side, chain, sems

    def order(self, turn):
        lines, line = self.p.lines, self.p.line
        value = 0
        for a in range(lines):
            far = sorted(range(lines), key=lambda t: (-abs(t - a), t))
            value = value + jnp.where(line == a, far[turn], 0)
        return value

    def across(self, turn):
        t = self.order(turn)
        at = 2 * t + 1 - self.p.lane
        return remote(
            self.parts.at[at],
            self.side.at[t],
            self.s.at[0, t],
            self.s.at[1, t],
            self.p.beside,
        )

    def rightward(self, t):
        step = self.p.lines - 1 - t
        return remote(
            self.parts.at[2 * t + self.p.lane],
            self.chain.at[0, step],
            self.s.at[2, step],
            self.s.at[3, step],
            self.p.right,
        )

    def leftward(self, t):
        return remote(
            self.parts.at[2 * t + self.p.lane],
            self.chain.at[1, t],
            self.s.at[4, t],
            self.s.at[5, t],
            self.p.left,
        )

    def add(self, at, other):
        self.parts[at] = (self.parts[at].astype(f32) + other.astype(f32)).astype(bf16)

    def start(self, ahead=2):
        for turn in range(min(ahead, self.p.lines)):
            self.across(turn).start()

    def near(self, turn, ahead=2):
        p = self.p
        t = self.order(turn)
        at = 2 * t + p.lane
        self.across(turn).wait_recv()
        if ahead and turn + ahead < p.lines:
            self.across(turn + ahead).start()
        self.add(at, self.side[t])
        pl.when((t > p.line) & (p.line == 0))(lambda: self.rightward(t).start())
        pl.when((t < p.line) & (p.line == p.lines - 1))(lambda: self.leftward(t).start())

    def far(self, turn):
        p = self.p
        t = self.order(turn)
        at = 2 * t + p.lane

        @pl.when((t > p.line) & p.has_left)
        def _():
            self.rightward(t).wait_recv()
            self.add(at, self.chain[0, p.lines - 1 - t])
            self.rightward(t).start()

        @pl.when((t < p.line) & p.has_right)
        def _():
            self.leftward(t).wait_recv()
            self.add(at, self.chain[1, t])
            self.leftward(t).start()

    def turns(self, ahead=2):
        for turn in range(self.p.lines):
            self.near(turn, ahead)
            if turn > 0:
                self.far(turn - 1)
        self.far(self.p.lines - 1)

    def total(self):
        p = self.p
        at = 2 * p.line + p.lane

        @pl.when(p.has_left)
        def _():
            self.rightward(p.line).wait_recv()
            self.add(at, self.chain[0, p.lines - 1 - p.line])

        @pl.when(p.has_right)
        def _():
            self.leftward(p.line).wait_recv()
            self.add(at, self.chain[1, p.line])

        return self.parts[at].astype(f32)

    def finish(self):
        p = self.p
        for turn in range(p.lines):
            self.across(turn).wait_send()
        for t in range(p.lines):
            pl.when(t > p.line)(lambda t=t: self.rightward(t).wait_send())
            pl.when(t < p.line)(lambda t=t: self.leftward(t).wait_send())


class GroupSum:
    sems = 6

    def __init__(self, place, parts, near, out, far, sems):
        self.p, self.parts, self.near, self.out, self.far, self.s = place, parts, near, out, far, sems

    def to_twin(self, i, which, cols):
        p = self.p
        block = p.diag_f if which == 0 else p.twin_f
        return remote(
            self.parts.at[block, :, cols],
            self.near.at[which, :, cols],
            self.s.at[which, i],
            self.s.at[2 + which, i],
            p.twin,
        )

    def to_cross(self, i, cols):
        return remote(
            self.out.at[:, cols], self.far.at[:, cols], self.s.at[4, i], self.s.at[5, i], self.p.cross
        )

    def give(self, i, cols):
        self.to_twin(i, 0, cols).start()
        self.to_twin(i, 1, cols).start()

    def pass_on(self, i, cols):
        self.to_twin(i, 0, cols).wait_recv()
        mine = self.parts[self.p.cross_f, :, cols].astype(f32)
        self.out[:, cols] = (mine + self.near[0, :, cols].astype(f32)).astype(bf16)
        self.to_cross(i, cols).start()

    def take(self, i, cols, own=None):
        self.to_twin(i, 1, cols).wait_recv()
        own = self.parts[self.p.f, :, cols] if own is None else own
        near = own.astype(f32) + self.near[1, :, cols].astype(f32)
        self.to_cross(i, cols).wait_recv()
        return near + self.far[:, cols].astype(f32)

    def given(self, i, cols):
        self.to_twin(i, 0, cols).wait_send()
        self.to_twin(i, 1, cols).wait_send()

    def passed(self, i, cols):
        self.to_cross(i, cols).wait_send()

    def finish(self, i, cols):
        self.given(i, cols)
        self.passed(i, cols)


class GroupTrade:
    sems = 2

    def __init__(self, place, whole, slots, sems, columns):
        self.p, self.whole, self.slots, self.s, self.n = place, whole, slots, sems, columns

    def block(self, g):
        return self.whole.at[:, pl.ds(pl.multiple_of(g * self.n, 128), self.n)]

    def send(self, d):
        self.copy(d).start()

    def copy(self, d):
        g = (self.p.f + d) % 4
        return remote(
            self.block(g), self.slots.at[self.p.f], self.s.at[0, d], self.s.at[1, d], {"fsdp": g}
        )

    def arrival(self, d):
        slot = self.slots.at[(self.p.f + 4 - d) % 4]
        return remote(slot, slot, self.s.at[0, d], self.s.at[1, d], {"fsdp": (self.p.f + d) % 4})

    def own(self):
        return pltpu.make_async_copy(
            self.block(self.p.f), self.slots.at[self.p.f], self.s.at[1, 0]
        )

    def start(self):
        for d in (2, 3, 1):
            self.copy(d).start()
        self.own().start()

    def wait(self):
        self.own().wait()
        for d in (1, 2, 3):
            self.arrival(d).wait_recv()

    def finish(self):
        for d in (1, 2, 3):
            self.copy(d).wait_send()


class GroupReturn(GroupTrade):
    def __init__(self, place, whole, slots, sems):
        super().__init__(place, whole, slots, sems, 0)

    def block(self, g):
        return self.whole.at[g]


def rotated(v, cosine, sine):
    first = v[:, :128]
    return jnp.concatenate(
        [first * cosine + pltpu.roll(first, 64, 1) * sine, v[:, 128:]], axis=1
    )


class GroupGather:
    sems = 6

    def __init__(self, place, own, whole, sems, own_sem, pieces, cuts=None):
        self.p, self.own, self.whole, self.s, self.own_sem = place, own, whole, sems, own_sem
        self.pieces, self.n, self.cuts = pieces, own.shape[0] // pieces, cuts

    def span(self, i):
        return (slice(None), self.cuts[i]) if self.cuts else (pl.ds(i * self.n, self.n),)

    def part(self, i):
        return self.own.at[self.span(i)]

    def slot(self, g, i):
        return self.whole.at[(g,) + self.span(i)]

    def local(self):
        return pltpu.make_async_copy(self.own, self.whole.at[self.p.f], self.own_sem)

    def to_twin(self, i):
        return remote(
            self.part(i), self.slot(self.p.f, i), self.s.at[0, i], self.s.at[3, i], self.p.twin
        )

    def to_cross(self, i):
        return remote(
            self.part(i), self.slot(self.p.f, i), self.s.at[1, i], self.s.at[4, i], self.p.cross
        )

    def forward(self, i):
        slot = self.slot(self.p.cross_f, i)
        return remote(slot, slot, self.s.at[2, i], self.s.at[5, i], self.p.twin)

    def give(self, i):
        self.to_cross(i).start()
        self.to_twin(i).start()

    def near(self, i):
        twin = self.slot(self.p.twin_f, i)
        remote(twin, twin, self.s.at[0, i], self.s.at[3, i], self.p.twin).wait_recv()

    def pass_on(self, i):
        slot = self.slot(self.p.cross_f, i)
        remote(slot, slot, self.s.at[1, i], self.s.at[4, i], self.p.cross).wait_recv()
        self.forward(i).start()

    def last(self, i):
        diag = self.slot(self.p.diag_f, i)
        remote(diag, diag, self.s.at[2, i], self.s.at[5, i], self.p.twin).wait_recv()

    def sent(self, i):
        self.to_twin(i).wait_send()
        self.to_cross(i).wait_send()
        self.forward(i).wait_send()

    def finish(self, i):
        self.near(i)
        self.last(i)
        self.sent(i)


def tiles_of(first, count, tile):
    tile = tile if count % tile == 0 else 128

    def loop(body):
        def one(i, carry):
            body(pl.ds(pl.multiple_of(first + i * tile, 128), tile))
            return carry

        lax.fori_loop(0, count // tile, one, 0)

    return loop


def front_kernel(
    lines,
    x_ref,
    gain_one,
    gain_two,
    cosine,
    sine,
    bias,
    w_keyval,
    w_query,
    w_out,
    cot,
    w_rows,
    normed_out,
    query_out,
    keyval_out,
    probs_out,
    mixed_out,
    middle_out,
    normed_two_out,
    cot_all,
    rows_all,
    whole,
    slots,
    parts,
    near,
    out,
    far,
    keyval,
    mixed,
    trade_sems,
    sum_sems,
    keyval_sems,
    cot_sems,
    row_sems,
    own_sems,
):
    p = Place(lines)
    rows, width = x_ref.shape
    heads = query_out.shape[0]
    inner = heads * HD
    kv_width = 2 * HD
    p.barrier()

    down = GroupGather(p, w_rows, rows_all, row_sems, own_sems.at[0], row_sems.shape[1])
    cot_gather = LineGather(p, cot, cot_all, cot_sems)
    cot_local = pltpu.make_async_copy(cot, cot_all.at[p.c], own_sems.at[1])

    source = x_ref[...].astype(f32)
    whole[...] = rms_norm(source, gain_one[...]).astype(bf16)
    trade = GroupTrade(p, whole, slots.at[0], trade_sems.at[0], slots.shape[3])
    trade.start()
    down.local().start()
    cot_local.start()
    cot_gather.start()
    trade.wait()
    normed_out[...] = slots[0]

    half = (heads // 2) * HD
    chunks = [(0, kv_width), (kv_width, half), (kv_width + half, inner - half)]
    group = GroupSum(p, parts, near, out, far, sum_sems.at[0])

    def project(lhs, weight, first, count, to):
        @tiles_of(first, count, 256)
        def _(cols):
            left = lhs[...].reshape(4 * rows, lhs.shape[-1])
            product = jnp.dot(left, weight[:, cols], preferred_element_type=f32)
            if to:
                cols = pl.ds(pl.multiple_of(cols.start + to, 128), cols.size)
            parts[:, :, cols] = product.astype(bf16).reshape(4, rows, cols.size)

    spans = [pl.ds(first, count) for first, count in chunks]
    project(slots.at[0], w_keyval, 0, kv_width, 0)
    group.give(0, spans[0])
    project(slots.at[0], w_query, 0, half, kv_width)
    group.give(1, spans[1])
    group.pass_on(0, spans[0])
    project(slots.at[0], w_query, half, inner - half, kv_width)
    group.give(2, spans[2])
    group.pass_on(1, spans[1])
    group.pass_on(2, spans[2])
    cot_gather.step(0)

    linear = group.take(0, spans[0])
    keyval[p.c] = jnp.concatenate(
        [rotated(linear[:, :HD], cosine[...], sine[...]), linear[:, HD:]], axis=1
    ).astype(bf16)
    kv_gather = LineGather(p, keyval.at[p.c], keyval, keyval_sems)
    kv_gather.start()
    for i in (1, 2):
        linear = group.take(i, spans[i])
        for h in range(linear.shape[1] // HD):
            turned = rotated(linear[:, h * HD : (h + 1) * HD], cosine[...], sine[...])
            at = h if i == 1 else h + heads // 2
            query_out[at] = (turned * HD**-0.5).astype(bf16)
        if i == 1:
            kv_gather.step(0)
    for i in range(down.pieces):
        down.give(i)
    for step in range(1, lines - 1):
        kv_gather.step(step)
    kv_gather.finish()
    if lines > 2:
        cot_gather.step(1)
    keyval_out[...] = keyval[...]

    length = bias.shape[1]

    def two_heads(i, carry):
        keys = keyval[:, :, :HD].reshape(length, HD)
        values = keyval[:, :, HD:].reshape(length, HD)
        two = query_out[pl.ds(2 * i, 2)].reshape(2 * rows, HD)
        scores = contract_rows(two, keys).reshape(2, rows, length) + bias[...][None]
        scores = scores.reshape(2 * rows, length)
        weights = jnp.exp(scores - jnp.max(scores, axis=-1, keepdims=True))
        total = jnp.sum(weights, axis=-1, keepdims=True)
        weights = (weights / total).astype(bf16)
        probs_out[pl.ds(2 * i, 2)] = weights.reshape(2, rows, length)
        product = jnp.dot(weights, values, preferred_element_type=f32).astype(bf16)
        at = pl.multiple_of(i * 2 * HD, 128)
        mixed[:, pl.ds(at, HD)] = product[:rows]
        mixed[:, pl.ds(at + HD, HD)] = product[rows:]
        return carry

    lax.fori_loop(0, heads // 2, two_heads, 0)
    trade_two = GroupTrade(p, mixed, slots.at[1], trade_sems.at[1], slots.shape[3])
    trade_two.start()
    for step in range(2, lines - 1):
        cot_gather.step(step)
    for i in range(len(chunks)):
        group.finish(i, spans[i])
    trade_two.wait()
    mixed_out[...] = slots[1]

    half = width // 2
    spans_two = [pl.ds(0, half), pl.ds(half, half)]
    group_two = GroupSum(p, parts, near, out, far, sum_sems.at[1])
    for i in range(2):
        project(slots.at[1], w_out, i * half, half, 0)
        group_two.give(i, spans_two[i])
    for i in range(2):
        group_two.pass_on(i, spans_two[i])
    for i in range(2):
        middle_out[:, spans_two[i]] = x_ref[:, spans_two[i]].astype(f32) + group_two.take(
            i, spans_two[i]
        )
    normed_two_out[...] = rms_norm(middle_out[...], gain_two[...]).astype(bf16)

    for i in range(down.pieces):
        down.pass_on(i)
    for i in range(2):
        group_two.finish(i, spans_two[i])
    trade.finish()
    trade_two.finish()
    down.local().wait()
    cot_local.wait()
    for i in range(down.pieces):
        down.finish(i)
    cot_gather.finish()


def front(lines, operands, heads):
    x = operands[0]
    rows, width = x.shape
    places = 2 * lines
    length = places * rows
    inner = heads * HD
    shard = width // 4
    parts_width = inner + 2 * HD
    in_vmem = pl.BlockSpec(memory_space=VMEM)
    anywhere = pl.BlockSpec(memory_space=pl.ANY)
    shape = jax.ShapeDtypeStruct
    pieces = 2
    assert inner == width
    return pl.pallas_call(
        functools.partial(front_kernel, lines),
        out_shape=(
            shape((4, rows, shard), bf16),
            shape((heads, rows, HD), bf16),
            shape((places, rows, 2 * HD), bf16),
            shape((heads, rows, length), bf16),
            shape((4, rows, shard), bf16),
            shape((rows, width), f32),
            shape((rows, width), bf16),
            shape((places, rows, width), bf16),
            shape((4,) + operands[10].shape, bf16),
        ),
        in_specs=[in_vmem] * 9 + [anywhere] * 2,
        out_specs=[in_vmem] * 7 + [anywhere] * 2,
        scratch_shapes=[
            VMEM((rows, width), bf16),
            VMEM((2, 4, rows, shard), bf16),
            VMEM((4, rows, parts_width), bf16),
            VMEM((2, rows, parts_width), bf16),
            VMEM((rows, parts_width), bf16),
            VMEM((rows, parts_width), bf16),
            VMEM((places, rows, 2 * HD), bf16),
            VMEM((rows, inner), bf16),
            DMA((2, GroupTrade.sems, 4)),
            DMA((2, GroupSum.sems, 3)),
            DMA((LineGather.sems, lines)),
            DMA((LineGather.sems, lines)),
            DMA((GroupGather.sems, pieces)),
            DMA((2,)),
        ],
        compiler_params=pltpu.CompilerParams(
            collective_id=0, has_side_effects=True, vmem_limit_bytes=vmem_bytes
        ),
        name="front",
    )(*operands)


def gelu_parts(v):
    k = 0.7978845608028654
    square = v * v
    inner = jnp.tanh(k * v * (1.0 + 0.044715 * square))
    half = 0.5 * (1.0 + inner)
    slope = half + 0.5 * v * (1.0 - inner * inner) * (k * (1.0 + 3 * 0.044715 * square))
    return v * half, slope


def norm_back(values, gain, grad):
    r = lax.rsqrt(jnp.mean(values * values, axis=-1, keepdims=True) + epsilon)
    scaled = values * r
    inner = grad * gain
    grad_values = r * (inner - scaled * jnp.mean(inner * scaled, axis=-1, keepdims=True))
    return grad_values, jnp.sum(grad * scaled, axis=0, keepdims=True)


def middle_kernel(
    lines,
    cot_all,
    w_rows,
    gain_two,
    own,
    middle,
    w_columns,
    grad_middle_out,
    gain_out,
    grads_out,
    down_out,
    normed_all_out,
    result_parts,
    normed_all,
    weights,
    grad_hidden,
    hidden,
    parts,
    side,
    chain,
    down_near,
    down_stage,
    down_far,
    gather_sems,
    column_sems,
    sum_sems,
    down_sems,
    own_sems,
):
    p = Place(lines)
    rows, width = own.shape
    two = 2 * rows
    padded = hidden.shape[2]
    shard = width // 4
    tile = 256 if padded % 256 == 0 else 128
    p.barrier()

    columns = GroupGather(p, w_columns, weights, column_sems, own_sems.at[0], column_sems.shape[1])
    gather = LineGather(p, own, normed_all, gather_sems)
    gather.start()
    for i in range(columns.pieces):
        columns.give(i)
    columns.local().start()
    own_local = pltpu.make_async_copy(own, normed_all.at[p.c], own_sems.at[2 + lines])
    own_local.start()
    middle_local = pltpu.make_async_copy(middle, grad_middle_out, own_sems.at[3 + lines])
    middle_local.start()

    def hidden_grad(line):
        def one(i, carry):
            cols = pl.ds(pl.multiple_of(i * tile, 128), tile)
            left = cot_all[pl.ds(2 * line, 2)].reshape(two, width)
            right = w_rows[pl.ds(pl.multiple_of(i * tile, 16), tile)]
            grad_hidden[line, :, cols] = contract_rows(left, right)
            return carry

        lax.fori_loop(0, padded // tile, one, 0)

    done = 0
    for step in range(lines - 1):
        hidden_grad(done)
        done += 1
        gather.step(step)
        if step < columns.pieces:
            columns.pass_on(step)
    for i in range(lines - 1, columns.pieces):
        columns.pass_on(i)
    while done < lines:
        hidden_grad(done)
        done += 1
    gather.finish()
    own_local.wait()
    columns.local().wait()
    for i in range(columns.pieces):
        columns.finish(i)
    normed_local = pltpu.make_async_copy(normed_all, normed_all_out, own_sems.at[1])
    normed_local.start()

    line_sum = LineSum(p, parts, side, chain, sum_sems)

    def feed_forward(line):
        def one(i, carry):
            cols = pl.ds(pl.multiple_of(i * tile, 128), tile)
            up_cols = pl.ds(pl.multiple_of(i * tile + padded, 128), tile)
            left = normed_all[pl.ds(2 * line, 2)].reshape(two, width)
            gate = jnp.dot(
                left, weights[:, :, cols].reshape(width, tile), preferred_element_type=f32
            )
            up = jnp.dot(
                left, weights[:, :, up_cols].reshape(width, tile), preferred_element_type=f32
            )
            gelu, slope = gelu_parts(gate)
            grad = grad_hidden[line, :, cols]
            hidden[line, :, cols] = (gelu * up).astype(bf16)
            grads_out[line, :, cols] = (grad * up * slope).astype(bf16)
            grads_out[line, :, up_cols] = (grad * gelu).astype(bf16)
            return carry

        lax.fori_loop(0, padded // tile, one, 0)

        def back(g, carry):
            product = contract_rows(grads_out[line], weights[g]).astype(bf16)
            cols = pl.ds(pl.multiple_of(g * shard, 128), shard)
            parts[pl.ds(2 * line, 2), :, cols] = product.reshape(2, rows, shard)
            return carry

        lax.fori_loop(0, 4, back, 0)

    result_stage = normed_all

    def result_copy(line):
        blocks = pl.ds(2 * line, 2)
        return pltpu.make_async_copy(
            result_stage.at[blocks], result_parts.at[blocks], own_sems.at[2 + line]
        )

    def result_part(line):
        def one(i, carry):
            cols = pl.ds(pl.multiple_of(i * shard, 128), shard)
            product = jnp.dot(
                hidden[line], w_rows[:, cols], preferred_element_type=f32
            ).astype(bf16)
            result_stage[pl.ds(2 * line, 2), :, cols] = product.reshape(2, rows, shard)
            return carry

        lax.fori_loop(0, 4, one, 0)
        result_copy(line).start()

    quarter = padded // 4
    every = slice(None)
    down_parts = weights.at[:, pl.ds(0, quarter), pl.ds(0, shard)]

    def down_group(i):
        return GroupSum(p, down_parts, down_near.at[i], down_stage.at[i % 2], down_far.at[i], down_sems)

    def down_chunk(i):
        def one(g, carry):
            cols = pl.ds(pl.multiple_of(g * shard, 128), shard)
            left = hidden[:, :, i * quarter : (i + 1) * quarter].reshape(lines * two, quarter)
            right = cot_all[:, :, cols].reshape(lines * two, shard)
            down_parts[g] = contract_tokens(left, right).astype(bf16)
            return carry

        lax.fori_loop(0, 4, one, 0)
        down_out[i] = down_parts[p.f]
        down_group(i).give(i, every)

    for turn in range(lines):
        feed_forward(line_sum.order(turn))
        line_sum.across(turn).start()
        if turn > 0:
            line_sum.near(turn - 1, 0)
        if turn > 1:
            line_sum.far(turn - 2)
    normed_local.wait()

    for i in range(4):
        if i >= 1:
            down_group(i - 1).given(i - 1, every)
        if i >= 2:
            down_out[i - 2] = down_group(i - 2).take(i - 2, every, down_out[i - 2]).astype(bf16)
            down_group(i - 2).passed(i - 2, every)
        down_chunk(i)
        if i < lines:
            result_part(i)
        down_group(i).pass_on(i, every)
        if i == 1:
            line_sum.far(lines - 2)
    for line in range(4, lines):
        result_part(line)
    line_sum.near(lines - 1, 0)
    line_sum.far(lines - 1)
    grad = line_sum.total()
    middle_local.wait()
    grad_values, gain = norm_back(grad_middle_out[...], gain_two[...], grad)
    grad_middle_out[...] = cot_all[p.c].astype(f32) + grad_values
    gain_out[...] = gain
    for i in (2, 3):
        down_out[i] = down_group(i).take(i, every, down_out[i]).astype(bf16)
        down_group(i).passed(i, every)
    down_group(3).given(3, every)
    for line in range(lines):
        result_copy(line).wait()
    line_sum.finish()


def middle_bytes(lines, rows, width, padded):
    length = 2 * lines * rows
    return (
        14 * rows * width
        + 9 * length * width
        + 9 * padded * width
        + 10 * length * padded
    )


def middle_part(lines, operands, padded):
    own = operands[3]
    rows, width = own.shape
    places = 2 * lines
    shard = width // 4
    quarter = padded // 4
    pieces = 4
    in_vmem = pl.BlockSpec(memory_space=VMEM)
    anywhere = pl.BlockSpec(memory_space=pl.ANY)
    shape = jax.ShapeDtypeStruct
    return pl.pallas_call(
        functools.partial(middle_kernel, lines),
        out_shape=(
            shape((rows, width), f32),
            shape((1, width), f32),
            shape((lines, 2 * rows, 2 * padded), bf16),
            shape((4, quarter, shard), bf16),
            shape((places, rows, width), bf16),
            shape((places, rows, width), bf16),
        ),
        in_specs=[in_vmem] * 3 + [anywhere] * 3,
        out_specs=[in_vmem] * 4 + [anywhere] * 2,
        scratch_shapes=[
            VMEM((places, rows, width), bf16),
            VMEM((4, shard, 2 * padded), bf16),
            VMEM((lines, 2 * rows, padded), f32),
            VMEM((lines, 2 * rows, padded), bf16),
            VMEM((places, rows, width), bf16),
            VMEM((lines, rows, width), bf16),
            VMEM((2, lines - 1, rows, width), bf16),
            VMEM((4, 2, quarter, shard), bf16),
            VMEM((2, quarter, shard), bf16),
            VMEM((4, quarter, shard), bf16),
            DMA((LineGather.sems, lines)),
            DMA((GroupGather.sems, pieces)),
            DMA((LineSum.sems, lines)),
            DMA((GroupSum.sems, 4)),
            DMA((4 + lines,)),
        ],
        compiler_params=pltpu.CompilerParams(
            collective_id=1, has_side_effects=True, vmem_limit_bytes=vmem_bytes
        ),
        name="middle",
    )(*operands)


def back_kernel(
    lines,
    with_result,
    grad_middle,
    probs,
    keyval,
    queries,
    tokens,
    gain_one,
    cosine,
    sine,
    w_out,
    w_query,
    w_keyval,
    *rest,
):
    if with_result:
        middle, result_in, result_out, *rest = rest
    (
        input_grad_out,
        gain_out,
        branch_out,
        linear_out,
        branch_all,
        linear_all,
        branch,
        linear,
        trade_parts,
        trade_slots,
        grad_mixed,
        kv_total,
        kv_parts,
        kv_side,
        kv_chain,
        branch_sems,
        linear_sems,
        trade_sems,
        kv_sems,
        own_sems,
        *rest,
    ) = rest
    p = Place(lines)
    rows, width = grad_middle.shape
    heads = queries.shape[0]
    length = probs.shape[2]
    shard = w_out.shape[0]
    kv_width = 2 * HD
    p.barrier()
    if with_result:
        result_parts, result_side, result_chain, result_sems = rest
        result_sum = LineSum(p, result_parts, result_side, result_chain, result_sems)
        result_copy = pltpu.make_async_copy(result_in, result_parts, own_sems.at[2])
        result_copy.start()

    branch[...] = grad_middle[...].astype(bf16)
    group = GroupGather(p, branch, branch_all, branch_sems, own_sems.at[0], 1)
    group.give(0)
    group.local().start()
    if with_result:
        result_copy.wait()
        result_sum.start(1)
    back_trade = GroupReturn(p, trade_parts.at[0], trade_slots.at[0], trade_sems.at[0])

    def mixed_back(g):
        trade_parts[0, g] = contract_rows(branch_all[g], w_out[...]).astype(bf16)

    group.local().wait()
    mixed_back(p.f)
    back_trade.own().start()
    group.near(0)
    mixed_back(p.twin_f)
    group.pass_on(0)
    mixed_back(p.cross_f)
    back_trade.send(2)
    group.last(0)
    mixed_back(p.diag_f)
    back_trade.send(1)
    back_trade.send(3)
    branch_copy = pltpu.make_async_copy(branch_all, branch_out, own_sems.at[3])
    branch_copy.start()
    if with_result:
        result_sum.near(0, 1)
    back_trade.wait()
    for g in range(4):
        grad_mixed[:, g * shard : (g + 1) * shard] = trade_slots[0, g]

    kv_total[...] = jnp.zeros_like(kv_total)
    kv_at, q_at = pl.ds(0, kv_width), pl.ds(kv_width, heads * HD)

    batch = 2 if length <= 2048 else 1

    def some_heads(i, carry):
        keys = keyval[:, :, :HD].reshape(length, HD)
        values = keyval[:, :, HD:].reshape(length, HD)
        at = [pl.multiple_of((i * batch + h) * HD, 128) for h in range(batch)]
        outer = jnp.concatenate([grad_mixed[:, pl.ds(a, HD)] for a in at], axis=0)
        weights = probs[pl.ds(batch * i, batch)].reshape(batch * rows, length)
        wide = weights.astype(f32)
        grad_weights = contract_rows(outer, values)
        delta = jnp.sum(wide * grad_weights, axis=-1, keepdims=True)
        grad_scores = (wide * (grad_weights - delta)).astype(bf16)
        product = jnp.dot(grad_scores, keys, preferred_element_type=f32) * HD**-0.5
        for h in range(batch):
            turned = rotated(product[h * rows : (h + 1) * rows], cosine[...], -sine[...])
            linear[:, pl.ds(kv_width + at[h], HD)] = turned.astype(bf16)
        two = queries[pl.ds(batch * i, batch)].reshape(batch * rows, HD)
        kv_total[:, :HD] += contract_tokens(grad_scores, two)
        kv_total[:, HD:] += contract_tokens(weights, outer)
        return carry

    lax.fori_loop(0, heads // batch, some_heads, 0)
    linear_group = GroupGather(
        p, linear, linear_all, linear_sems, own_sems.at[1], 2, (q_at, kv_at)
    )
    linear_group.give(0)
    if with_result:
        result_sum.far(0)
        result_sum.near(1, 0)
    kv_parts[...] = kv_total[...].astype(bf16).reshape(kv_parts.shape)
    kv_sum = LineSum(p, kv_parts, kv_side, kv_chain, kv_sems)
    kv_sum.start(lines)
    kv_sum.turns(0)
    own = kv_sum.total()
    linear[:, :HD] = rotated(own[:, :HD], cosine[...], -sine[...]).astype(bf16)
    linear[:, pl.ds(HD, HD)] = own[:, HD:].astype(bf16)
    linear_group.give(1)
    linear_group.local().start()
    if with_result:
        for turn in range(2, lines):
            result_sum.across(turn).start()
        result_sum.far(1)
    linear_group.pass_on(0)
    linear_group.pass_on(1)
    linear_group.local().wait()
    for i in range(2):
        linear_group.near(i)
        linear_group.last(i)

    linear_copy = pltpu.make_async_copy(linear_all, linear_out, own_sems.at[4])
    linear_copy.start()

    last_trade = GroupReturn(p, trade_parts.at[1], trade_slots.at[1], trade_sems.at[1])

    def normed_back(g):
        product = contract_rows(linear_all[g, :, kv_at], w_keyval[...])
        product += contract_rows(linear_all[g, :, q_at], w_query[...])
        trade_parts[1, g] = product.astype(bf16)

    normed_back(p.cross_f)
    last_trade.send(2)
    normed_back(p.diag_f)
    normed_back(p.twin_f)
    last_trade.send(1)
    last_trade.send(3)
    normed_back(p.f)
    last_trade.own().start()
    if with_result:
        for turn in range(2, lines):
            result_sum.near(turn, 0)
            result_sum.far(turn)
    last_trade.wait()
    for g in range(4):
        grad_mixed[:, g * shard : (g + 1) * shard] = trade_slots[1, g]
    source = tokens[...].astype(f32)
    grad_values, gain = norm_back(source, gain_one[...], grad_mixed[...].astype(f32))
    input_grad_out[...] = (grad_middle[...] + grad_values).astype(bf16)
    gain_out[...] = gain
    if with_result:
        result_out[...] = (middle[...] + result_sum.total()).astype(bf16)
        result_sum.finish()
    back_trade.finish()
    last_trade.finish()
    group.sent(0)
    linear_group.sent(0)
    linear_group.sent(1)
    kv_sum.finish()
    branch_copy.wait()
    linear_copy.wait()


def back(lines, operands, result_operands):
    rows, width = operands[0].shape
    heads = operands[3].shape[0]
    places = 2 * lines
    length = places * rows
    shard = width // 4
    linear_width = width + 2 * HD
    in_vmem = pl.BlockSpec(memory_space=VMEM)
    anywhere = pl.BlockSpec(memory_space=pl.ANY)
    shape = jax.ShapeDtypeStruct
    with_result = bool(result_operands)
    result_scratch = [
        VMEM((places, rows, width), bf16),
        VMEM((lines, rows, width), bf16),
        VMEM((2, lines - 1, rows, width), bf16),
        DMA((LineSum.sems, lines)),
    ]
    return pl.pallas_call(
        functools.partial(back_kernel, lines, with_result),
        out_shape=((shape((rows, width), bf16),) if with_result else ())
        + (
            shape((rows, width), bf16),
            shape((1, width), f32),
            shape((4, rows, width), bf16),
            shape((4, rows, linear_width), bf16),
        ),
        in_specs=[in_vmem] * 11 + ([in_vmem, anywhere] if with_result else []),
        out_specs=[in_vmem] * (3 if with_result else 2) + [anywhere] * 2,
        scratch_shapes=[
            VMEM((4, rows, width), bf16),
            VMEM((4, rows, linear_width), bf16),
            VMEM((rows, width), bf16),
            VMEM((rows, linear_width), bf16),
            VMEM((2, 4, rows, shard), bf16),
            VMEM((2, 4, rows, shard), bf16),
            VMEM((rows, width), bf16),
            VMEM((length, 2 * HD), f32),
            VMEM((places, rows, 2 * HD), bf16),
            VMEM((lines, rows, 2 * HD), bf16),
            VMEM((2, lines - 1, rows, 2 * HD), bf16),
            DMA((GroupGather.sems, 1)),
            DMA((GroupGather.sems, 2)),
            DMA((2, GroupTrade.sems, 4)),
            DMA((LineSum.sems, lines)),
            DMA((5,)),
        ]
        + (result_scratch if with_result else []),
        compiler_params=pltpu.CompilerParams(
            collective_id=2, has_side_effects=True, vmem_limit_bytes=vmem_bytes
        ),
        name="back",
    )(*operands, *result_operands)


def grads_kernel(lines, with_columns, normed, mixed, branch_all, linear_all, down_in, *rest):
    if with_columns:
        normed_two, hidden_grads, *rest = rest
    projection_out, out_out, down_out, *rest = rest
    if with_columns:
        columns_out, *rest = rest
    (
        parts,
        side,
        chain,
        out_parts,
        out_side,
        out_chain,
        sums,
        projection_sems,
        out_sems,
        down_sems,
        place_sems,
        *rest,
    ) = rest
    if with_columns:
        chunk_parts, near, stage, far, chunks, group_sems, trade_sems, *rest = rest
    p = Place(lines)
    places = 2 * lines
    shard = normed.shape[2]
    tokens = 4 * normed.shape[1]
    per_owner = places // 4
    tall = shard // per_owner
    kv_share = 2 * HD // 4

    to_ctx, to_f = per_owner * p.f + p.c // 4, p.c % 4
    from_ctx, from_f = 4 * (p.c % per_owner) + p.f, p.c // per_owner
    moves = (to_ctx != p.c) | (to_f != p.f)
    others = [
        (jnp.full((), True), {"ctx": (p.c + d) % places}) for d in range(1, places)
    ] + [
        (moves, {"ctx": to_ctx, "fsdp": to_f}),
        (moves, {"ctx": from_ctx, "fsdp": from_f}),
    ]
    p.barrier(ctx=False, also=others)

    def down_copy(q):
        dest = per_owner * q + p.c // 4
        return remote(
            down_in.at[q], down_out.at[p.c % 4], down_sems.at[0, q], down_sems.at[1, p.c % 4], {"ctx": dest}
        )

    def down_own(q):
        return pltpu.make_async_copy(down_in.at[q], down_out.at[p.c % 4], down_sems.at[2, 0])

    def down_arrival(i):
        slot = down_out.at[i]
        return remote(slot, slot, down_sems.at[0, 0], down_sems.at[1, i], p.beside)

    for q in range(4):
        stays = per_owner * q + p.c // 4 == p.c
        pl.when(~stays)(lambda q=q: down_copy(q).start())
        pl.when(stays)(lambda q=q: down_own(q).start())

    projection_sum = LineSum(p, parts, side, chain, projection_sems)
    out_sum = LineSum(p, out_parts, out_side, out_chain, out_sems)

    def out_blocks(g, carry):
        left = mixed[...].reshape(tokens, shard)
        right = branch_all[:, :, pl.ds(pl.multiple_of(g * shard, 128), shard)]
        product = contract_tokens(left, right.reshape(tokens, shard))
        for r in range(per_owner):
            out_parts[4 * r + g] = product[r * tall : (r + 1) * tall].astype(bf16)
        return carry

    def projection_blocks(g, carry):
        left = normed[...].reshape(tokens, shard)
        right = linear_all[:, :, pl.ds(pl.multiple_of(2 * HD + g * shard, 128), shard)]
        product = contract_tokens(left, right.reshape(tokens, shard))
        right = linear_all[:, :, pl.ds(pl.multiple_of(g * kv_share, 128), kv_share)]
        kv_product = contract_tokens(left, right.reshape(tokens, kv_share))
        for r in range(per_owner):
            rows = slice(r * tall, (r + 1) * tall)
            parts[4 * r + g, :, :shard] = product[rows].astype(bf16)
            parts[4 * r + g, :, shard:] = kv_product[rows].astype(bf16)
        return carry

    lax.fori_loop(0, 4, out_blocks, 0)
    out_sum.start(2)
    lax.fori_loop(0, 4, projection_blocks, 0)

    if with_columns:
        block = columns_out.shape[2]
        every = slice(None)

        def chunk_of(k):
            return (p.line + k) % lines

        def group(k):
            return GroupSum(p, chunk_parts, near.at[k], stage.at[k % 2], far.at[k], group_sems)

        def compute(k):
            cols = pl.ds(pl.multiple_of(chunk_of(k) * chunk_parts.shape[1], 128), chunk_parts.shape[1])

            def one(g, carry):
                left = normed_two[:, :, cols].reshape(-1, chunk_parts.shape[1])
                right = hidden_grads[:, :, pl.ds(pl.multiple_of(g * block, 128), block)]
                chunk_parts[g] = contract_tokens(left, right.reshape(-1, block)).astype(bf16)
                return carry

            lax.fori_loop(0, 4, one, 0)
            chunks[k] = chunk_parts[p.f]
            group(k).give(k, every)

        def halves(k):
            half = chunk_parts.shape[1] // 2
            for lane in range(2):
                yield lane, 2 * chunk_of(k) + lane, chunks.at[k, pl.ds(lane * half, half)]

        def place_copy(k, lane, dest, src):
            return remote(
                src,
                columns_out.at[p.c],
                trade_sems.at[0, 2 * k + lane],
                trade_sems.at[1, p.c],
                {"ctx": dest},
            )

        def place_own(src):
            return pltpu.make_async_copy(src, columns_out.at[p.c], trade_sems.at[2, 0])

        def arrival(i):
            slot = columns_out.at[i]
            return remote(slot, slot, trade_sems.at[0, 0], trade_sems.at[1, i], p.beside)

        def complete(k):
            chunks[k] = group(k).take(k, every, chunks[k]).astype(bf16)
            for lane, dest, src in halves(k):
                pl.when(dest != p.c)(
                    lambda k=k, lane=lane, dest=dest, src=src: place_copy(k, lane, dest, src).start()
                )
                pl.when(dest == p.c)(lambda src=src: place_own(src).start())

        for k in range(lines):
            if k >= 1:
                group(k - 1).given(k - 1, every)
            if k >= 2:
                complete(k - 2)
                group(k - 2).passed(k - 2, every)
            compute(k)
            group(k).pass_on(k, every)
            out_sum.near(k, 2)
            if k > 0:
                out_sum.far(k - 1)
        out_sum.far(lines - 1)
    else:
        out_sum.turns(2)

    def to_place(i, src, dst):
        return remote(
            src, dst, place_sems.at[0, i], place_sems.at[1, i], {"ctx": to_ctx, "fsdp": to_f}
        )

    def hand_over(i, line_sum, at, dst):
        src = sums.at[pl.ds(0, tall), at]
        sums[:, at] = line_sum.total().astype(bf16)
        pl.when(moves)(lambda: to_place(i, src, dst).start())
        pl.when(~moves)(lambda: pltpu.make_async_copy(src, dst, place_sems.at[2, i]).start())

    def handed(i, at, dst):
        src = sums.at[pl.ds(0, tall), at]

        @pl.when(moves)
        def _():
            to_place(i, src, dst).wait_send()
            to_place(i, src, dst).wait_recv()

        pl.when(~moves)(lambda: pltpu.make_async_copy(src, dst, place_sems.at[2, i]).wait())

    projection_sum.start(2)
    wide = shard + kv_share
    hand_over(0, out_sum, pl.ds(wide, shard), out_out)
    if with_columns:
        for k in (lines - 2, lines - 1):
            complete(k)
            group(k).passed(k, every)
        group(lines - 1).given(lines - 1, every)
    projection_sum.turns(2)
    hand_over(1, projection_sum, pl.ds(0, wide), projection_out)

    handed(0, pl.ds(wide, shard), out_out)
    for q in range(4):
        stays = per_owner * q + p.c // 4 == p.c
        pl.when(~stays)(lambda q=q: down_copy(q).wait_send())
        pl.when(stays)(lambda q=q: down_own(q).wait())
    for i in range(4):
        source = 4 * (p.c % per_owner) + i
        pl.when(source != p.c)(lambda i=i: down_arrival(i).wait_recv())
    if with_columns:
        for k in range(lines):
            for lane, dest, src in halves(k):
                pl.when(dest != p.c)(
                    lambda k=k, lane=lane, dest=dest, src=src: place_copy(k, lane, dest, src).wait_send()
                )
                pl.when(dest == p.c)(lambda src=src: place_own(src).wait())
        for i in range(places):
            pl.when(p.c != i)(lambda i=i: arrival(i).wait_recv())
    out_sum.finish()
    projection_sum.finish()
    handed(1, pl.ds(0, wide), projection_out)


def weight_grads(lines, operands, column_operands):
    rows, shard = operands[0].shape[1:]
    width = 4 * shard
    places = 2 * lines
    tall = 4 * shard // places
    wide = shard + 2 * HD // 4
    quarter = operands[4].shape[1]
    in_vmem = pl.BlockSpec(memory_space=VMEM)
    anywhere = pl.BlockSpec(memory_space=pl.ANY)
    shape = jax.ShapeDtypeStruct
    with_columns = bool(column_operands)
    column_shapes, column_scratch = (), []
    if with_columns:
        block = column_operands[1].shape[2] // 4
        chunk = width // lines
        column_shapes = (shape((places, chunk // 2, block), bf16),)
        column_scratch = [
            VMEM((4, chunk, block), bf16),
            VMEM((lines, 2, chunk, block), bf16),
            VMEM((2, chunk, block), bf16),
            VMEM((lines, chunk, block), bf16),
            VMEM((lines, chunk, block), bf16),
            DMA((GroupSum.sems, lines)),
            DMA((3, places)),
        ]
    return pl.pallas_call(
        functools.partial(grads_kernel, lines, with_columns),
        out_shape=(
            shape((tall, wide), bf16),
            shape((tall, shard), bf16),
            shape((4, quarter, shard), bf16),
        )
        + column_shapes,
        in_specs=[in_vmem] * 4 + [anywhere] + [in_vmem] * len(column_operands),
        out_specs=[anywhere] * (3 + len(column_shapes)),
        scratch_shapes=[
            VMEM((places, tall, wide), bf16),
            VMEM((lines, tall, wide), bf16),
            VMEM((2, lines - 1, tall, wide), bf16),
            VMEM((places, tall, shard), bf16),
            VMEM((lines, tall, shard), bf16),
            VMEM((2, lines - 1, tall, shard), bf16),
            VMEM((tall, wide + shard), bf16),
            DMA((LineSum.sems, lines)),
            DMA((LineSum.sems, lines)),
            DMA((3, 4)),
            DMA((3, 2)),
        ]
        + column_scratch,
        compiler_params=pltpu.CompilerParams(
            collective_id=3, has_side_effects=True, vmem_limit_bytes=vmem_bytes
        ),
        name="grads",
    )(*operands, *column_operands)


def per_device(
    tokens,
    doc_bounds,
    cotangent,
    norm_one,
    query_weight,
    keyval_weight,
    out_weight,
    norm_two,
    gate_up_weight,
    down_weight,
):
    ctx_size = lax.axis_size("ctx")
    fsdp_size = lax.axis_size("fsdp")
    lines = ctx_size // 2
    rows = tokens.shape[1]
    width = tokens.shape[2]
    length = rows * ctx_size
    inner_width = query_weight.shape[1]
    head_count = inner_width // HD
    hidden_width = gate_up_weight.shape[1] // 2
    piece = hidden_width // (ctx_size * fsdp_size)
    padded_piece = -(-piece // 32) * 32
    padded = padded_piece * fsdp_size
    ctx_place = lax.axis_index("ctx")
    bounds = doc_bounds[0]
    query_index = ctx_place * rows + jnp.arange(rows, dtype=jnp.int32)
    key_index = jnp.arange(length, dtype=jnp.int32)
    allowed = visible(query_index, key_index, bounds)
    bias = jnp.where(allowed, 0.0, -1e30).astype(jnp.float32)
    angles = rotary_angles(query_index, bounds)
    cosine = jnp.cos(angles)
    sine = jnp.sin(angles)
    cosine = jnp.concatenate([cosine, cosine], axis=1)
    sine = jnp.concatenate([-sine, sine], axis=1)

    def padded_to(value, axis):
        pads = [(0, 0)] * value.ndim
        pads[axis] = (0, padded_piece - piece)
        return jnp.pad(value, pads)

    shard_width = hidden_width // fsdp_size
    w_columns = jnp.concatenate(
        [
            padded_to(
                lax.dynamic_slice_in_dim(
                    gate_up_weight, q * shard_width + ctx_place * piece, piece, 1
                ),
                1,
            )
            for q in range(2 * fsdp_size)
        ],
        axis=1,
    )
    w_rows = padded_to(lax.dynamic_slice_in_dim(down_weight, ctx_place * piece, piece, 0), 0)
    cot_rows = cotangent[0]
    (
        normed,
        queries,
        window,
        weights,
        mixed,
        middle,
        normed_two,
        cot_all,
        w_down,
    ) = front(
        lines,
        (
            tokens[0],
            norm_one[None],
            norm_two[None],
            cosine,
            sine,
            bias,
            keyval_weight,
            query_weight,
            out_weight,
            cot_rows,
            w_rows,
        ),
        head_count,
    )
    w_down = w_down.reshape(padded, width)
    fits = middle_bytes(lines, rows, width, padded) <= vmem_bytes
    if fits:
        grad_middle, gain_two_term, grad_gate_up, down_part, normed_two, result_parts = middle_part(
            lines, (cot_all, w_down, norm_two[None], normed_two, middle, w_columns), padded
        )
        gain_two_term = gain_two_term[0]
    else:
        cot_all = cot_all.reshape(length, width)
        normed_two = lax.all_gather(normed_two, "ctx", axis=0, tiled=True)
        w_gate_up = lax.all_gather(w_columns, "fsdp", axis=0, tiled=True)
        projected = jnp.dot(normed_two, w_gate_up, preferred_element_type=f32)
        gelu, slope = gelu_parts(projected[:, :padded])
        up_part = projected[:, padded:]
        hidden = (gelu * up_part).astype(bf16)
        grad_hidden = contract_rows(cot_all, w_down)
        grad_gate_up = jnp.concatenate(
            [grad_hidden * up_part * slope, grad_hidden * gelu], axis=1
        ).astype(bf16)
        grad_normed_two = lax.psum_scatter(
            contract_rows(grad_gate_up, w_gate_up).astype(bf16),
            "ctx",
            scatter_dimension=0,
            tiled=True,
        ).astype(f32)
        grad_middle_norm, gain_two_term = norm_back(middle, norm_two[None], grad_normed_two)
        gain_two_term = gain_two_term[0]
        grad_middle = cot_rows.astype(f32) + grad_middle_norm
        result_parts = jnp.dot(hidden, w_down, preferred_element_type=f32).astype(bf16)
        down_part = lax.psum_scatter(
            contract_tokens(hidden, cot_all).astype(bf16),
            "fsdp",
            scatter_dimension=1,
            tiled=True,
        ).reshape(fsdp_size, padded_piece, -1)
    operands = (
        grad_middle,
        weights,
        window,
        queries,
        tokens[0],
        norm_one[None],
        cosine,
        sine,
        out_weight,
        query_weight,
        keyval_weight,
    )
    if fits:
        result, input_grad, gain_one_term, grad_branch, grad_linear = back(
            lines, operands, (middle, result_parts.reshape(ctx_size, rows, width))
        )
    else:
        input_grad, gain_one_term, grad_branch, grad_linear = back(lines, operands, ())
        branch_two = lax.psum_scatter(result_parts, "ctx", scatter_dimension=0, tiled=True)
        result = (middle + branch_two.astype(f32)).astype(bf16)
    gain_one_term = gain_one_term[0]

    operands = (normed, mixed, grad_branch, grad_linear, down_part)
    if fits:
        projection_grad, out_grad, down_grad, gate_up_part = weight_grads(
            lines, operands, (normed_two, grad_gate_up)
        )
    else:
        projection_grad, out_grad, down_grad = weight_grads(lines, operands, ())
        gate_up_part = lax.psum_scatter(
            contract_tokens(normed_two, grad_gate_up).astype(bf16),
            "fsdp",
            scatter_dimension=1,
            tiled=True,
        )
        gate_up_part = lax.all_to_all(
            gate_up_part.reshape(ctx_size, width // ctx_size, -1), "ctx", 0, 0, tiled=True
        )
    query_grad = projection_grad[:, : inner_width // fsdp_size].astype(f32)
    keyval_grad = projection_grad[:, inner_width // fsdp_size :].astype(f32)
    out_grad = out_grad.astype(f32)
    down_grad = down_grad[:, :piece].reshape(fsdp_size * piece, -1).astype(f32)
    gate_up_part = gate_up_part.reshape(ctx_size, width // ctx_size, 2, padded_piece)[..., :piece]
    gate_up_grad = gate_up_part.transpose(1, 2, 0, 3).reshape(width // ctx_size, -1).astype(f32)
    gains = lax.psum_scatter(
        jnp.stack([gain_one_term, gain_two_term]),
        ("ctx", "fsdp"),
        scatter_dimension=1,
        tiled=True,
    )
    return (
        result[None],
        input_grad[None],
        gains[0],
        query_grad,
        keyval_grad,
        out_grad,
        gains[1],
        gate_up_grad,
        down_grad,
    )


def solution(mesh):
    placed = (
        P("fsdp", "ctx", None),
        P("fsdp", None),
        P("fsdp", "ctx", None),
        P(),
        P("fsdp", None),
        P("fsdp", None),
        P("fsdp", None),
        P(),
        P("fsdp", None),
        P("fsdp", None),
    )
    return jax.shard_map(
        per_device,
        mesh=mesh,
        in_specs=placed,
        out_specs=(
            P("fsdp", "ctx", None),
            P("fsdp", "ctx", None),
            P(("ctx", "fsdp")),
            P("ctx", "fsdp"),
            P("ctx", "fsdp"),
            P("ctx", "fsdp"),
            P(("ctx", "fsdp")),
            P("ctx", "fsdp"),
            P("ctx", "fsdp"),
        ),
        check_vma=False,
    )
```

```python
import functools
import math

import jax
import jax.numpy as jnp
from jax import lax
from jax.experimental import pallas as pl
from jax.experimental.pallas import tpu as pltpu
from jax.sharding import PartitionSpec as P

HD = 256
WINDOW = 2048


epsilon = 1e-06
f32 = jnp.float32
bf16 = jnp.bfloat16
VMEM = pltpu.VMEM
DMA = pltpu.SemaphoreType.DMA
vmem_bytes = 62 * 1024 * 1024


def rms_norm(values, gain):
    return values * lax.rsqrt(jnp.mean(values * values, axis=-1, keepdims=True) + epsilon) * gain


def documents(index, bounds):
    return (index >= bounds[0]).astype(jnp.int32) + (index >= bounds[1]).astype(jnp.int32)


def contract_rows(left, right):
    return lax.dot_general(
        left, right, (((1,), (1,)), ((), ())), preferred_element_type=jnp.float32
    )


def contract_tokens(left, right):
    return lax.dot_general(
        left, right, (((0,), (0,)), ((), ())), preferred_element_type=jnp.float32
    )


def remote(src, dst, send_sem, recv_sem, device):
    return pltpu.make_async_remote_copy(
        src_ref=src,
        dst_ref=dst,
        send_sem=send_sem,
        recv_sem=recv_sem,
        device_id=device,
        device_id_type=pl.DeviceIdType.MESH,
    )


class Place:
    def __init__(self, lines):
        self.lines = lines
        self.c = lax.axis_index("ctx")
        self.f = lax.axis_index("fsdp")
        self.line = self.c // 2
        self.lane = self.c % 2
        self.chip = self.f // 2
        self.core = self.f % 2
        self.twin_f = self.f + 1 - 2 * self.core
        self.cross_f = (self.f + 2) % 4
        self.diag_f = (self.twin_f + 2) % 4
        self.twin = {"fsdp": self.twin_f}
        self.cross = {"fsdp": self.cross_f}
        self.diag = {"fsdp": self.diag_f}
        self.beside = {"ctx": self.c + 1 - 2 * self.lane}
        self.right = {"ctx": self.c + 2}
        self.left = {"ctx": self.c - 2}
        self.has_right = self.line < lines - 1
        self.has_left = self.line > 0

    def barrier(self, ctx=True, fsdp=True, also=()):
        sem = pltpu.get_barrier_semaphore()

        def greet(device):
            pl.semaphore_signal(sem, 1, device_id=device, device_id_type=pl.DeviceIdType.MESH)

        count = 0
        if fsdp:
            for device in (self.twin, self.cross, self.diag):
                greet(device)
            count = 3
        if ctx:
            greet(self.beside)
            pl.when(self.has_right)(lambda: greet(self.right))
            pl.when(self.has_left)(lambda: greet(self.left))
            count = (
                count + 1 + self.has_right.astype(jnp.int32) + self.has_left.astype(jnp.int32)
            )
        for needed, device in also:
            pl.when(needed)(lambda device=device: greet(device))
            count = count + needed.astype(jnp.int32)
        pl.semaphore_wait(sem, count)


class LineGather:
    sems = 6

    def __init__(self, place, own, slots, sems):
        self.p, self.own, self.slots, self.s = place, own, slots, sems

    def rightward(self, step):
        at = 2 * (self.p.line - step) + self.p.lane
        src = self.own if step == 0 else self.slots.at[at]
        return remote(src, self.slots.at[at], self.s.at[0, step], self.s.at[1, step], self.p.right)

    def leftward(self, step):
        at = 2 * (self.p.line + step) + self.p.lane
        src = self.own if step == 0 else self.slots.at[at]
        return remote(src, self.slots.at[at], self.s.at[2, step], self.s.at[3, step], self.p.left)

    def across(self, line, own=False):
        at = 2 * line + self.p.lane
        src = self.own if own else self.slots.at[at]
        return remote(
            src, self.slots.at[at], self.s.at[4, line], self.s.at[5, line], self.p.beside
        )

    def from_left(self, step):
        at = 2 * (self.p.line - 1 - step) + self.p.lane
        slot = self.slots.at[at]
        return remote(slot, slot, self.s.at[0, step], self.s.at[1, step], self.p.right)

    def from_right(self, step):
        at = 2 * (self.p.line + 1 + step) + self.p.lane
        slot = self.slots.at[at]
        return remote(slot, slot, self.s.at[2, step], self.s.at[3, step], self.p.left)

    def start(self):
        pl.when(self.p.has_right)(lambda: self.rightward(0).start())
        pl.when(self.p.has_left)(lambda: self.leftward(0).start())
        self.across(self.p.line, True).start()

    def step(self, step):
        p = self.p

        @pl.when(p.line - 1 - step >= 0)
        def _():
            self.from_left(step).wait_recv()
            if step + 1 < p.lines - 1:
                pl.when(p.has_right)(lambda: self.rightward(step + 1).start())
            self.across(p.line - 1 - step).start()

        @pl.when(p.line + 1 + step <= p.lines - 1)
        def _():
            self.from_right(step).wait_recv()
            if step + 1 < p.lines - 1:
                pl.when(p.has_left)(lambda: self.leftward(step + 1).start())
            self.across(p.line + 1 + step).start()

    def steps(self):
        for step in range(self.p.lines - 1):
            self.step(step)

    def arrived_across(self, line):
        at = 2 * line + 1 - self.p.lane
        slot = self.slots.at[at]
        remote(slot, slot, self.s.at[4, line], self.s.at[5, line], self.p.beside).wait_recv()

    def finish(self, arrivals=True):
        p = self.p
        if arrivals:
            for line in range(p.lines):
                self.arrived_across(line)
        for step in range(p.lines - 1):
            pl.when(p.has_right & (p.line - step >= 0))(
                lambda step=step: self.rightward(step).wait_send()
            )
            pl.when(p.has_left & (p.line + step <= p.lines - 1))(
                lambda step=step: self.leftward(step).wait_send()
            )
        for line in range(p.lines):
            self.across(line).wait_send()


class LineSum:
    sems = 6

    def __init__(self, place, parts, side, chain, sems):
        self.p, self.parts, self.side, self.chain, self.s = place, parts, side, chain, sems

    def order(self, turn):
        lines, line = self.p.lines, self.p.line
        value = 0
        for a in range(lines):
            far = sorted(range(lines), key=lambda t: (-abs(t - a), t))
            value = value + jnp.where(line == a, far[turn], 0)
        return value

    def across(self, turn):
        t = self.order(turn)
        at = 2 * t + 1 - self.p.lane
        return remote(
            self.parts.at[at],
            self.side.at[t],
            self.s.at[0, t],
            self.s.at[1, t],
            self.p.beside,
        )

    def rightward(self, t):
        step = self.p.lines - 1 - t
        return remote(
            self.parts.at[2 * t + self.p.lane],
            self.chain.at[0, step],
            self.s.at[2, step],
            self.s.at[3, step],
            self.p.right,
        )

    def leftward(self, t):
        return remote(
            self.parts.at[2 * t + self.p.lane],
            self.chain.at[1, t],
            self.s.at[4, t],
            self.s.at[5, t],
            self.p.left,
        )

    def add(self, at, other):
        self.parts[at] = (self.parts[at].astype(f32) + other.astype(f32)).astype(self.parts.dtype)

    def start(self, ahead=2):
        for turn in range(min(ahead, self.p.lines)):
            self.across(turn).start()

    def near(self, turn, ahead=2):
        p = self.p
        t = self.order(turn)
        at = 2 * t + p.lane
        self.across(turn).wait_recv()
        if ahead and turn + ahead < p.lines:
            self.across(turn + ahead).start()
        self.add(at, self.side[t])
        pl.when((t > p.line) & (p.line == 0))(lambda: self.rightward(t).start())
        pl.when((t < p.line) & (p.line == p.lines - 1))(lambda: self.leftward(t).start())

    def far(self, turn):
        p = self.p
        t = self.order(turn)
        at = 2 * t + p.lane

        @pl.when((t > p.line) & p.has_left)
        def _():
            self.rightward(t).wait_recv()
            self.add(at, self.chain[0, p.lines - 1 - t])
            self.rightward(t).start()

        @pl.when((t < p.line) & p.has_right)
        def _():
            self.leftward(t).wait_recv()
            self.add(at, self.chain[1, t])
            self.leftward(t).start()

    def turns(self, ahead=2):
        for turn in range(self.p.lines):
            self.near(turn, ahead)
            if turn > 0:
                self.far(turn - 1)
        self.far(self.p.lines - 1)

    def total(self):
        p = self.p
        at = 2 * p.line + p.lane

        @pl.when(p.has_left)
        def _():
            self.rightward(p.line).wait_recv()
            self.add(at, self.chain[0, p.lines - 1 - p.line])

        @pl.when(p.has_right)
        def _():
            self.leftward(p.line).wait_recv()
            self.add(at, self.chain[1, p.line])

        return self.parts[at].astype(f32)

    def finish(self):
        p = self.p
        for turn in range(p.lines):
            self.across(turn).wait_send()
        for t in range(p.lines):
            pl.when(t > p.line)(lambda t=t: self.rightward(t).wait_send())
            pl.when(t < p.line)(lambda t=t: self.leftward(t).wait_send())


class GroupSum:
    sems = 6

    def __init__(self, place, parts, near, out, far, sems):
        self.p, self.parts, self.near, self.out, self.far, self.s = place, parts, near, out, far, sems

    def to_twin(self, i, which, cols):
        p = self.p
        block = p.diag_f if which == 0 else p.twin_f
        return remote(
            self.parts.at[block, :, cols],
            self.near.at[which, :, cols],
            self.s.at[which, i],
            self.s.at[2 + which, i],
            p.twin,
        )

    def to_cross(self, i, cols):
        return remote(
            self.out.at[:, cols], self.far.at[:, cols], self.s.at[4, i], self.s.at[5, i], self.p.cross
        )

    def give(self, i, cols):
        self.to_twin(i, 0, cols).start()
        self.to_twin(i, 1, cols).start()

    def pass_on(self, i, cols):
        self.to_twin(i, 0, cols).wait_recv()
        mine = self.parts[self.p.cross_f, :, cols].astype(f32)
        self.out[:, cols] = (mine + self.near[0, :, cols].astype(f32)).astype(bf16)
        self.to_cross(i, cols).start()

    def take(self, i, cols, own=None):
        self.to_twin(i, 1, cols).wait_recv()
        own = self.parts[self.p.f, :, cols] if own is None else own
        near = own.astype(f32) + self.near[1, :, cols].astype(f32)
        self.to_cross(i, cols).wait_recv()
        return near + self.far[:, cols].astype(f32)

    def given(self, i, cols):
        self.to_twin(i, 0, cols).wait_send()
        self.to_twin(i, 1, cols).wait_send()

    def passed(self, i, cols):
        self.to_cross(i, cols).wait_send()

    def finish(self, i, cols):
        self.given(i, cols)
        self.passed(i, cols)


class GroupTrade:
    sems = 2

    def __init__(self, place, whole, slots, sems, columns):
        self.p, self.whole, self.slots, self.s, self.n = place, whole, slots, sems, columns

    def block(self, g):
        return self.whole.at[:, pl.ds(pl.multiple_of(g * self.n, 128), self.n)]

    def send(self, d):
        self.copy(d).start()

    def copy(self, d):
        g = (self.p.f + d) % 4
        return remote(
            self.block(g), self.slots.at[self.p.f], self.s.at[0, d], self.s.at[1, d], {"fsdp": g}
        )

    def arrival(self, d):
        slot = self.slots.at[(self.p.f + 4 - d) % 4]
        return remote(slot, slot, self.s.at[0, d], self.s.at[1, d], {"fsdp": (self.p.f + d) % 4})

    def own(self):
        return pltpu.make_async_copy(
            self.block(self.p.f), self.slots.at[self.p.f], self.s.at[1, 0]
        )

    def start(self):
        for d in (2, 3, 1):
            self.copy(d).start()
        self.own().start()

    def wait(self):
        self.own().wait()
        for d in (1, 2, 3):
            self.arrival(d).wait_recv()

    def finish(self):
        for d in (1, 2, 3):
            self.copy(d).wait_send()


class BlockMove:
    def __init__(self, place, per_owner, src, dst, sems):
        p = place
        self.src, self.dst, self.s = src, dst, sems
        self.to_ctx, self.to_f = per_owner * p.f + p.c // 4, p.c % 4
        self.from_ctx, self.from_f = 4 * (p.c % per_owner) + p.f, p.c // per_owner
        self.moves = (self.to_ctx != p.c) | (self.to_f != p.f)

    def greets(self):
        return [
            (self.moves, {"ctx": self.to_ctx, "fsdp": self.to_f}),
            (self.moves, {"ctx": self.from_ctx, "fsdp": self.from_f}),
        ]

    def copy(self):
        device = {"ctx": self.to_ctx, "fsdp": self.to_f}
        return remote(self.src, self.dst, self.s.at[0], self.s.at[1], device)

    def stay(self):
        return pltpu.make_async_copy(self.src, self.dst, self.s.at[2])

    def start(self):
        pl.when(self.moves)(lambda: self.copy().start())
        pl.when(~self.moves)(lambda: self.stay().start())

    def finish(self):
        @pl.when(self.moves)
        def _():
            self.copy().wait_send()
            self.copy().wait_recv()

        pl.when(~self.moves)(lambda: self.stay().wait())


class PieceMove:
    def __init__(self, place, per_owner, pieces, slots, sems):
        p = place
        self.p, self.n, self.pieces, self.slots, self.s = p, per_owner, pieces, slots, sems
        self.at = hidden_piece(p.c, p.lines)

    def dest(self, q):
        return self.n * q + self.at // 4

    def copy(self, q):
        return remote(
            self.pieces.at[q],
            self.slots.at[self.at % 4],
            self.s.at[0, q],
            self.s.at[1, self.at % 4],
            {"ctx": self.dest(q)},
        )

    def stay(self, q):
        return pltpu.make_async_copy(self.pieces.at[q], self.slots.at[self.at % 4], self.s.at[2, 0])

    def start(self):
        for q in range(4):
            here = self.dest(q) == self.p.c
            pl.when(~here)(lambda q=q: self.copy(q).start())
            pl.when(here)(lambda q=q: self.stay(q).start())

    def finish(self):
        p = self.p
        for q in range(4):
            here = self.dest(q) == p.c
            pl.when(~here)(lambda q=q: self.copy(q).wait_send())
            pl.when(here)(lambda q=q: self.stay(q).wait())
        for i in range(4):
            source = place_of_piece(4 * (p.c % self.n) + i, p.lines)
            slot = self.slots.at[i]
            arrival = remote(slot, slot, self.s.at[0, 0], self.s.at[1, i], p.beside)
            pl.when(source != p.c)(lambda arrival=arrival: arrival.wait_recv())


def hidden_piece(c, lines):
    return (c % 2) * lines + c // 2


def place_of_piece(piece, lines):
    return (piece % lines) * 2 + piece // lines


class GroupReturn(GroupTrade):
    def __init__(self, place, whole, slots, sems):
        super().__init__(place, whole, slots, sems, 0)

    def block(self, g):
        return self.whole.at[g]


def rotary_tables(first, rows, bounds):
    index = first + lax.broadcasted_iota(jnp.int32, (rows, 128), 0)
    lane = lax.broadcasted_iota(jnp.int32, (rows, 128), 1)
    quarter = HD // 4
    member = documents(index, bounds)
    opening = jnp.where(member == 0, 0, jnp.where(member == 1, bounds[0], bounds[1]))
    frequency = jnp.exp((lane % quarter).astype(f32) * (-math.log(10000.0) / quarter))
    angles = (index - opening).astype(f32) * frequency
    sine = jnp.sin(angles)
    return jnp.cos(angles), jnp.where(lane < quarter, -sine, sine)


def rotated(v, cosine, sine):
    first = v[:, :128]
    return jnp.concatenate(
        [first * cosine + pltpu.roll(first, 64, 1) * sine, v[:, 128:]], axis=1
    )


class GroupGather:
    sems = 6

    def __init__(self, place, own, whole, sems, own_sem, pieces, cuts=None):
        self.p, self.own, self.whole, self.s, self.own_sem = place, own, whole, sems, own_sem
        self.pieces, self.n, self.cuts = pieces, own.shape[0] // pieces, cuts

    def span(self, i):
        return (slice(None), self.cuts[i]) if self.cuts else (pl.ds(i * self.n, self.n),)

    def part(self, i):
        return self.own.at[self.span(i)]

    def slot(self, g, i):
        return self.whole.at[(g,) + self.span(i)]

    def local(self):
        return pltpu.make_async_copy(self.own, self.whole.at[self.p.f], self.own_sem)

    def to_twin(self, i):
        return remote(
            self.part(i), self.slot(self.p.f, i), self.s.at[0, i], self.s.at[3, i], self.p.twin
        )

    def to_cross(self, i):
        return remote(
            self.part(i), self.slot(self.p.f, i), self.s.at[1, i], self.s.at[4, i], self.p.cross
        )

    def forward(self, i):
        slot = self.slot(self.p.cross_f, i)
        return remote(slot, slot, self.s.at[2, i], self.s.at[5, i], self.p.twin)

    def give(self, i):
        self.to_cross(i).start()
        self.to_twin(i).start()

    def near(self, i):
        twin = self.slot(self.p.twin_f, i)
        remote(twin, twin, self.s.at[0, i], self.s.at[3, i], self.p.twin).wait_recv()

    def pass_on(self, i):
        slot = self.slot(self.p.cross_f, i)
        remote(slot, slot, self.s.at[1, i], self.s.at[4, i], self.p.cross).wait_recv()
        self.forward(i).start()

    def last(self, i):
        diag = self.slot(self.p.diag_f, i)
        remote(diag, diag, self.s.at[2, i], self.s.at[5, i], self.p.twin).wait_recv()

    def sent(self, i):
        self.to_twin(i).wait_send()
        self.to_cross(i).wait_send()
        self.forward(i).wait_send()

    def finish(self, i):
        self.near(i)
        self.last(i)
        self.sent(i)


def tiles_of(first, count, tile):
    tile = tile if count % tile == 0 else 128

    def loop(body):
        def one(i, carry):
            body(pl.ds(pl.multiple_of(first + i * tile, 128), tile))
            return carry

        lax.fori_loop(0, count // tile, one, 0)

    return loop


def front_kernel(
    lines,
    bounds_ref,
    x_ref,
    gains,
    w_keyval,
    w_query,
    w_out,
    cot,
    w_down,
    w_gate_up,
    normed_out,
    query_out,
    keyval_out,
    probs_out,
    mixed_out,
    middle_out,
    normed_two_out,
    cosine,
    sine,
    columns_out,
    cot_all,
    rows_all,
    whole,
    slots,
    parts,
    near,
    out,
    far,
    keyval,
    mixed,
    bias,
    w_rows,
    windows,
    trade_sems,
    sum_sems,
    keyval_sems,
    cot_sems,
    row_sems,
    own_sems,
):
    p = Place(lines)
    rows, width = x_ref.shape
    length = bias.shape[1]
    heads = query_out.shape[0]
    inner = heads * HD
    kv_width = 2 * HD
    p.barrier()

    units = w_gate_up.shape[1] // 2
    piece = units // (4 * 2 * lines)
    padded_piece = w_rows.shape[0]
    own_piece = hidden_piece(p.c, lines)
    if w_down.shape[0] == padded_piece:
        rows_copy = pltpu.make_async_copy(w_down, w_rows, own_sems.at[2])
    else:
        rows_copy = pltpu.make_async_copy(
            w_down.at[pl.ds(pl.multiple_of(own_piece * piece, 16), piece)],
            w_rows.at[pl.ds(0, piece)],
            own_sems.at[2],
        )
    rows_copy.start()
    span = windows.shape[2]
    shard = w_gate_up.shape[0]

    def window_first(q):
        first = q * (units // 4) + own_piece * piece
        return jnp.minimum(first // 128 * 128, 2 * units - span), first

    def window(q):
        return pltpu.make_async_copy(
            w_gate_up.at[:, pl.ds(pl.multiple_of(window_first(q)[0], 128), span)],
            windows.at[q % 2],
            own_sems.at[3 + q % 2],
        )

    def pack_columns(q):
        window(q).wait()
        start, first = window_first(q)
        by = first - start
        lane = lax.broadcasted_iota(jnp.int32, (shard, 128), 1)
        tiles = [
            pltpu.roll(windows[q % 2, :, t * 128 : (t + 1) * 128].astype(f32), (128 - by % 128) % 128, 1)
            for t in range(span // 128)
        ]
        late = by >= 128
        turned = []
        for t in range(span // 128 - 1):
            turned.append(jnp.where(lane < 128 - by % 128, tiles[t], tiles[t + 1]))
        turned.append(jnp.where(lane < 128 - by % 128, tiles[-1], 0.0))
        turned = [
            jnp.where(late, turned[t + 1], turned[t]) for t in range(span // 128 - 1)
        ]
        turned = jnp.concatenate(turned, axis=1)[:, :padded_piece]
        lane = lax.broadcasted_iota(jnp.int32, (shard, padded_piece), 1)
        columns_out[:, q * padded_piece : (q + 1) * padded_piece] = jnp.where(
            lane < piece, turned, 0.0
        ).astype(bf16)
        if q + 2 < 8:
            window(q + 2).start()

    window(0).start()
    window(1).start()
    down = GroupGather(p, w_rows, rows_all, row_sems, own_sems.at[0], row_sems.shape[1])
    cot_gather = LineGather(p, cot, cot_all, cot_sems)
    cot_local = pltpu.make_async_copy(cot, cot_all.at[p.c], own_sems.at[1])

    source = x_ref[...].astype(f32)
    whole[...] = rms_norm(source, gains[0:1]).astype(bf16)
    trade = GroupTrade(p, whole, slots.at[0], trade_sems.at[0], slots.shape[3])
    trade.start()
    cot_local.start()
    cot_gather.start()
    bounds = (bounds_ref[0, 0], bounds_ref[0, 1])
    cosine[...], sine[...] = rotary_tables(p.c * rows, rows, bounds)
    query_at = p.c * rows + lax.broadcasted_iota(jnp.int32, (rows, length), 0)
    key_at = lax.broadcasted_iota(jnp.int32, (rows, length), 1)
    allowed = (
        (query_at >= key_at)
        & (query_at - key_at < WINDOW)
        & (documents(query_at, bounds) == documents(key_at, bounds))
    )
    bias[...] = jnp.where(allowed, 0.0, -1e30)
    trade.wait()
    normed_out[...] = slots[0]

    half = (heads // 2) * HD
    chunks = [(0, kv_width), (kv_width, half), (kv_width + half, inner - half)]
    group = GroupSum(p, parts, near, out, far, sum_sems.at[0])

    def project(lhs, weight, first, count, to):
        @tiles_of(first, count, 256)
        def _(cols):
            left = lhs[...].reshape(4 * rows, lhs.shape[-1])
            product = jnp.dot(left, weight[:, cols], preferred_element_type=f32)
            if to:
                cols = pl.ds(pl.multiple_of(cols.start + to, 128), cols.size)
            parts[:, :, cols] = product.astype(bf16).reshape(4, rows, cols.size)

    spans = [pl.ds(first, count) for first, count in chunks]
    project(slots.at[0], w_keyval, 0, kv_width, 0)
    group.give(0, spans[0])
    project(slots.at[0], w_query, 0, half, kv_width)
    group.give(1, spans[1])
    group.pass_on(0, spans[0])
    project(slots.at[0], w_query, half, inner - half, kv_width)
    group.give(2, spans[2])
    group.pass_on(1, spans[1])
    group.pass_on(2, spans[2])
    cot_gather.step(0)

    linear = group.take(0, spans[0])
    keyval[p.c] = jnp.concatenate(
        [rotated(linear[:, :HD], cosine[...], sine[...]), linear[:, HD:]], axis=1
    ).astype(bf16)
    kv_gather = LineGather(p, keyval.at[p.c], keyval, keyval_sems)
    kv_gather.start()
    for i in (1, 2):
        linear = group.take(i, spans[i])
        for h in range(linear.shape[1] // HD):
            turned = rotated(linear[:, h * HD : (h + 1) * HD], cosine[...], sine[...])
            at = h if i == 1 else h + heads // 2
            query_out[at] = (turned * HD**-0.5).astype(bf16)
        if i == 1:
            kv_gather.step(0)
    rows_copy.wait()
    if w_down.shape[0] != padded_piece and piece < padded_piece:
        w_rows[pl.ds(piece, padded_piece - piece)] = jnp.zeros(
            (padded_piece - piece, width), bf16
        )
    down.local().start()
    for i in range(down.pieces):
        down.give(i)
    for step in range(1, lines - 1):
        kv_gather.step(step)
    kv_gather.finish()
    if lines > 2:
        cot_gather.step(1)
    keyval_out[...] = keyval[...]


    def two_heads(i, carry):
        keys = keyval[:, :, :HD].reshape(length, HD)
        values = keyval[:, :, HD:].reshape(length, HD)
        two = query_out[pl.ds(2 * i, 2)].reshape(2 * rows, HD)
        scores = contract_rows(two, keys).reshape(2, rows, length) + bias[...][None]
        scores = scores.reshape(2 * rows, length)
        weights = jnp.exp(scores - jnp.max(scores, axis=-1, keepdims=True))
        total = jnp.sum(weights, axis=-1, keepdims=True)
        weights = (weights / total).astype(bf16)
        probs_out[pl.ds(2 * i, 2)] = weights.reshape(2, rows, length)
        product = jnp.dot(weights, values, preferred_element_type=f32).astype(bf16)
        at = pl.multiple_of(i * 2 * HD, 128)
        mixed[:, pl.ds(at, HD)] = product[:rows]
        mixed[:, pl.ds(at + HD, HD)] = product[rows:]
        return carry

    lax.fori_loop(0, heads // 2, two_heads, 0)
    trade_two = GroupTrade(p, mixed, slots.at[1], trade_sems.at[1], slots.shape[3])
    trade_two.start()
    for q in range(4):
        pack_columns(q)
    for step in range(2, lines - 1):
        cot_gather.step(step)
    for i in range(len(chunks)):
        group.finish(i, spans[i])
    trade_two.wait()
    mixed_out[...] = slots[1]

    half = width // 2
    spans_two = [pl.ds(0, half), pl.ds(half, half)]
    group_two = GroupSum(p, parts, near, out, far, sum_sems.at[1])
    for i in range(2):
        project(slots.at[1], w_out, i * half, half, 0)
        group_two.give(i, spans_two[i])
    for i in range(2):
        group_two.pass_on(i, spans_two[i])
    for q in range(4, 8):
        pack_columns(q)
    for i in range(2):
        middle_out[:, spans_two[i]] = x_ref[:, spans_two[i]].astype(f32) + group_two.take(
            i, spans_two[i]
        )
    normed_two_out[...] = rms_norm(middle_out[...], gains[1:2]).astype(bf16)

    for i in range(down.pieces):
        down.pass_on(i)
    for i in range(2):
        group_two.finish(i, spans_two[i])
    trade.finish()
    trade_two.finish()
    down.local().wait()
    cot_local.wait()
    for i in range(down.pieces):
        down.finish(i)
    cot_gather.finish()


def front(lines, operands, heads, padded_piece):
    x = operands[1]
    rows, width = x.shape
    places = 2 * lines
    length = places * rows
    inner = heads * HD
    shard = width // 4
    parts_width = inner + 2 * HD
    in_vmem = pl.BlockSpec(memory_space=VMEM)
    anywhere = pl.BlockSpec(memory_space=pl.ANY)
    shape = jax.ShapeDtypeStruct
    pieces = 2
    assert inner == width
    return pl.pallas_call(
        functools.partial(front_kernel, lines),
        out_shape=(
            shape((4, rows, shard), bf16),
            shape((heads, rows, HD), bf16),
            shape((places, rows, 2 * HD), bf16),
            shape((heads, rows, length), bf16),
            shape((4, rows, shard), bf16),
            shape((rows, width), f32),
            shape((rows, width), bf16),
            shape((rows, 128), f32),
            shape((rows, 128), f32),
            shape((shard, 8 * padded_piece), bf16),
            shape((places, rows, width), bf16),
            shape((4, padded_piece, width), bf16),
        ),
        in_specs=[pl.BlockSpec(memory_space=pltpu.SMEM)] + [in_vmem] * 5 + [anywhere] * 3,
        out_specs=[in_vmem] * 10 + [anywhere] * 2,
        scratch_shapes=[
            VMEM((rows, width), bf16),
            VMEM((2, 4, rows, shard), bf16),
            VMEM((4, rows, parts_width), bf16),
            VMEM((2, rows, parts_width), bf16),
            VMEM((rows, parts_width), bf16),
            VMEM((rows, parts_width), bf16),
            VMEM((places, rows, 2 * HD), bf16),
            VMEM((rows, inner), bf16),
            VMEM((rows, length), f32),
            VMEM((padded_piece, width), bf16),
            VMEM((2, shard, (padded_piece + 127) // 128 * 128 + 128), bf16),
            DMA((2, GroupTrade.sems, 4)),
            DMA((2, GroupSum.sems, 3)),
            DMA((LineGather.sems, lines)),
            DMA((LineGather.sems, lines)),
            DMA((GroupGather.sems, pieces)),
            DMA((5,)),
        ],
        compiler_params=pltpu.CompilerParams(
            collective_id=0, has_side_effects=True, vmem_limit_bytes=vmem_bytes
        ),
        name="front",
    )(*operands)


def gelu_parts(v):
    k = 0.7978845608028654
    square = v * v
    inner = jnp.tanh(k * v * (1.0 + 0.044715 * square))
    half = 0.5 * (1.0 + inner)
    slope = half + 0.5 * v * (1.0 - inner * inner) * (k * (1.0 + 3 * 0.044715 * square))
    return v * half, slope


def norm_back(values, gain, grad):
    r = lax.rsqrt(jnp.mean(values * values, axis=-1, keepdims=True) + epsilon)
    scaled = values * r
    inner = grad * gain
    grad_values = r * (inner - scaled * jnp.mean(inner * scaled, axis=-1, keepdims=True))
    return grad_values, jnp.sum(grad * scaled, axis=0, keepdims=True)


def middle_kernel(
    lines,
    cot_all,
    w_rows,
    gains,
    own,
    middle,
    w_columns,
    grad_middle_out,
    gain_out,
    grads_out,
    down_out,
    normed_all_out,
    result_parts,
    normed_all,
    weights,
    grad_hidden,
    hidden,
    parts,
    side,
    chain,
    down_near,
    down_stage,
    down_far,
    gather_sems,
    column_sems,
    sum_sems,
    down_sems,
    own_sems,
):
    p = Place(lines)
    rows, width = own.shape
    two = 2 * rows
    padded = hidden.shape[2]
    shard = width // 4
    tile = 256 if padded % 256 == 0 else 128
    p.barrier()

    columns = GroupGather(p, w_columns, weights, column_sems, own_sems.at[0], column_sems.shape[1])
    gather = LineGather(p, own, normed_all, gather_sems)
    gather.start()
    for i in range(columns.pieces):
        columns.give(i)
    columns.local().start()
    own_local = pltpu.make_async_copy(own, normed_all.at[p.c], own_sems.at[2 + lines])
    own_local.start()
    middle_local = pltpu.make_async_copy(middle, grad_middle_out, own_sems.at[3 + lines])
    middle_local.start()

    def hidden_grad(line):
        def one(i, carry):
            cols = pl.ds(pl.multiple_of(i * tile, 128), tile)
            left = cot_all[pl.ds(2 * line, 2)].reshape(two, width)
            right = w_rows[pl.ds(pl.multiple_of(i * tile, 16), tile)]
            grad_hidden[line, :, cols] = contract_rows(left, right)
            return carry

        lax.fori_loop(0, padded // tile, one, 0)

    done = 0
    for step in range(lines - 1):
        hidden_grad(done)
        done += 1
        gather.step(step)
        if step < columns.pieces:
            columns.pass_on(step)
    for i in range(lines - 1, columns.pieces):
        columns.pass_on(i)
    while done < lines:
        hidden_grad(done)
        done += 1
    gather.finish()
    own_local.wait()
    columns.local().wait()
    for i in range(columns.pieces):
        columns.finish(i)
    normed_local = pltpu.make_async_copy(normed_all, normed_all_out, own_sems.at[1])
    normed_local.start()

    line_sum = LineSum(p, parts, side, chain, sum_sems)

    def feed_forward(line):
        def one(i, carry):
            cols = pl.ds(pl.multiple_of(i * tile, 128), tile)
            up_cols = pl.ds(pl.multiple_of(i * tile + padded, 128), tile)
            left = normed_all[pl.ds(2 * line, 2)].reshape(two, width)
            gate = jnp.dot(
                left, weights[:, :, cols].reshape(width, tile), preferred_element_type=f32
            )
            up = jnp.dot(
                left, weights[:, :, up_cols].reshape(width, tile), preferred_element_type=f32
            )
            gelu, slope = gelu_parts(gate)
            grad = grad_hidden[line, :, cols]
            hidden[line, :, cols] = (gelu * up).astype(bf16)
            grads_out[line, :, cols] = (grad * up * slope).astype(bf16)
            grads_out[line, :, up_cols] = (grad * gelu).astype(bf16)
            return carry

        lax.fori_loop(0, padded // tile, one, 0)

        def back(g, carry):
            product = contract_rows(grads_out[line], weights[g]).astype(bf16)
            cols = pl.ds(pl.multiple_of(g * shard, 128), shard)
            parts[pl.ds(2 * line, 2), :, cols] = product.reshape(2, rows, shard)
            return carry

        lax.fori_loop(0, 4, back, 0)

    result_stage = normed_all

    def result_copy(line):
        blocks = pl.ds(2 * line, 2)
        return pltpu.make_async_copy(
            result_stage.at[blocks], result_parts.at[blocks], own_sems.at[2 + line]
        )

    def result_part(line):
        def one(i, carry):
            cols = pl.ds(pl.multiple_of(i * shard, 128), shard)
            product = jnp.dot(
                hidden[line], w_rows[:, cols], preferred_element_type=f32
            ).astype(bf16)
            result_stage[pl.ds(2 * line, 2), :, cols] = product.reshape(2, rows, shard)
            return carry

        lax.fori_loop(0, 4, one, 0)
        result_copy(line).start()

    quarter = padded // 4
    every = slice(None)
    down_parts = weights.at[:, pl.ds(0, quarter), pl.ds(0, shard)]

    def down_group(i):
        return GroupSum(p, down_parts, down_near.at[i], down_stage.at[i % 2], down_far.at[i], down_sems)

    def down_chunk(i):
        def one(g, carry):
            cols = pl.ds(pl.multiple_of(g * shard, 128), shard)
            left = hidden[:, :, i * quarter : (i + 1) * quarter].reshape(lines * two, quarter)
            right = cot_all[:, :, cols].reshape(lines * two, shard)
            down_parts[g] = contract_tokens(left, right).astype(bf16)
            return carry

        lax.fori_loop(0, 4, one, 0)
        down_out[i] = down_parts[p.f]
        down_group(i).give(i, every)

    for turn in range(lines):
        feed_forward(line_sum.order(turn))
        line_sum.across(turn).start()
        if turn > 0:
            line_sum.near(turn - 1, 0)
        if turn > 1:
            line_sum.far(turn - 2)
    normed_local.wait()

    for i in range(4):
        if i >= 1:
            down_group(i - 1).given(i - 1, every)
        if i >= 2:
            down_out[i - 2] = down_group(i - 2).take(i - 2, every, down_out[i - 2]).astype(bf16)
            down_group(i - 2).passed(i - 2, every)
        down_chunk(i)
        if i < lines:
            result_part(i)
        down_group(i).pass_on(i, every)
        if i == 1:
            line_sum.far(lines - 2)
    for line in range(4, lines):
        result_part(line)
    line_sum.near(lines - 1, 0)
    line_sum.far(lines - 1)
    grad = line_sum.total()
    middle_local.wait()
    grad_values, gain = norm_back(grad_middle_out[...], gains[1:2], grad)
    grad_middle_out[...] = cot_all[p.c].astype(f32) + grad_values
    gain_out[...] = gain
    for i in (2, 3):
        down_out[i] = down_group(i).take(i, every, down_out[i]).astype(bf16)
        down_group(i).passed(i, every)
    down_group(3).given(3, every)
    for line in range(lines):
        result_copy(line).wait()
    line_sum.finish()


def middle_bytes(lines, rows, width, padded):
    length = 2 * lines * rows
    return (
        14 * rows * width
        + 9 * length * width
        + 9 * padded * width
        + 10 * length * padded
    )


def middle_part(lines, operands, padded):
    own = operands[3]
    rows, width = own.shape
    places = 2 * lines
    shard = width // 4
    quarter = padded // 4
    pieces = 4
    in_vmem = pl.BlockSpec(memory_space=VMEM)
    anywhere = pl.BlockSpec(memory_space=pl.ANY)
    shape = jax.ShapeDtypeStruct
    return pl.pallas_call(
        functools.partial(middle_kernel, lines),
        out_shape=(
            shape((rows, width), f32),
            shape((1, width), f32),
            shape((lines, 2 * rows, 2 * padded), bf16),
            shape((4, quarter, shard), bf16),
            shape((places, rows, width), bf16),
            shape((places, rows, width), bf16),
        ),
        in_specs=[in_vmem] * 3 + [anywhere] * 3,
        out_specs=[in_vmem] * 4 + [anywhere] * 2,
        scratch_shapes=[
            VMEM((places, rows, width), bf16),
            VMEM((4, shard, 2 * padded), bf16),
            VMEM((lines, 2 * rows, padded), f32),
            VMEM((lines, 2 * rows, padded), bf16),
            VMEM((places, rows, width), bf16),
            VMEM((lines, rows, width), bf16),
            VMEM((2, lines - 1, rows, width), bf16),
            VMEM((4, 2, quarter, shard), bf16),
            VMEM((2, quarter, shard), bf16),
            VMEM((4, quarter, shard), bf16),
            DMA((LineGather.sems, lines)),
            DMA((GroupGather.sems, pieces)),
            DMA((LineSum.sems, lines)),
            DMA((GroupSum.sems, 4)),
            DMA((4 + lines,)),
        ],
        compiler_params=pltpu.CompilerParams(
            collective_id=1, has_side_effects=True, vmem_limit_bytes=vmem_bytes
        ),
        name="middle",
    )(*operands)


def is_long(length):
    return length > 2048


def back_kernel(
    lines,
    with_result,
    grad_middle,
    probs,
    keyval,
    queries,
    mixed,
    tokens,
    gains,
    cosine,
    sine,
    w_out,
    w_query,
    w_keyval,
    down_in,
    *rest,
):
    if with_result:
        middle, result_in, result_out, *rest = rest
    (
        input_grad_out,
        gain_out,
        branch_out,
        linear_out,
        out_out,
        down_out,
        branch_all,
        linear_all,
        branch,
        linear,
        trade_parts,
        trade_slots,
        grad_mixed,
        kv_total,
        kv_parts,
        kv_side,
        kv_chain,
        out_parts,
        out_side,
        out_chain,
        out_stage,
        probs_stage,
        branch_sems,
        linear_sems,
        trade_sems,
        kv_sems,
        out_sems,
        move_sems,
        piece_sems,
        own_sems,
        *rest,
    ) = rest
    p = Place(lines)
    rows, width = grad_middle.shape
    heads = queries.shape[0]
    length = probs.shape[2]
    shard = w_out.shape[0]
    kv_width = 2 * HD
    per_owner = 2 * lines // 4
    tall = shard // per_owner
    out_move = BlockMove(p, per_owner, out_stage, out_out, move_sems)
    others = [(jnp.full((), True), {"ctx": (p.c + d) % (2 * lines)}) for d in range(1, 2 * lines)]
    p.barrier(ctx=False, also=others + out_move.greets())
    if with_result:
        result_parts, result_side, result_chain, result_sems = rest
        result_sum = LineSum(p, result_parts, result_side, result_chain, result_sems)
        result_copy = pltpu.make_async_copy(result_in, result_parts, own_sems.at[2])
        result_copy.start()

    branch[...] = grad_middle[...].astype(bf16)
    group = GroupGather(p, branch, branch_all, branch_sems, own_sems.at[0], 1)
    group.give(0)
    group.local().start()
    down_move = PieceMove(p, per_owner, down_in, down_out, piece_sems)
    down_move.start()
    out_sum = LineSum(p, out_parts, out_side, out_chain, out_sems)
    if with_result:
        result_copy.wait()
        result_sum.start(2)
    back_trade = GroupReturn(p, trade_parts.at[0], trade_slots.at[0], trade_sems.at[0])

    def mixed_back(g):
        trade_parts[0, g] = contract_rows(branch_all[g], w_out[...]).astype(bf16)

    group.local().wait()
    mixed_back(p.f)
    back_trade.own().start()
    group.near(0)
    mixed_back(p.twin_f)
    group.pass_on(0)
    mixed_back(p.cross_f)
    back_trade.send(2)
    group.last(0)
    mixed_back(p.diag_f)
    back_trade.send(1)
    back_trade.send(3)
    branch_copy = pltpu.make_async_copy(branch_all, branch_out, own_sems.at[3])
    branch_copy.start()

    def out_blocks(g, carry):
        left = mixed[...].reshape(4 * rows, shard)
        right = branch_all[:, :, pl.ds(pl.multiple_of(g * shard, 128), shard)]
        product = contract_tokens(left, right.reshape(4 * rows, shard))
        for r in range(per_owner):
            out_parts[4 * r + g] = product[r * tall : (r + 1) * tall].astype(bf16)
        return carry

    lax.fori_loop(0, 4, out_blocks, 0)
    out_sum.start(2)
    if with_result:
        result_sum.near(0, 0)
    back_trade.wait()
    for g in range(4):
        grad_mixed[:, g * shard : (g + 1) * shard] = trade_slots[0, g]

    kv_total[...] = jnp.zeros_like(kv_total)
    kv_at, q_at = pl.ds(0, kv_width), pl.ds(kv_width, heads * HD)

    batch = 1 if is_long(length) else 2

    def some_heads(i, carry):
        keys = keyval[:, :, :HD].reshape(length, HD)
        values = keyval[:, :, HD:].reshape(length, HD)
        at = [pl.multiple_of((i * batch + h) * HD, 128) for h in range(batch)]
        outer = jnp.concatenate([grad_mixed[:, pl.ds(a, HD)] for a in at], axis=0)
        if batch == 1:
            fetch = pltpu.make_async_copy(probs.at[i], probs_stage, own_sems.at[5])
            fetch.start()
            fetch.wait()
            weights = probs_stage[...]
        else:
            weights = probs[pl.ds(batch * i, batch)].reshape(batch * rows, length)
        wide = weights.astype(f32)
        grad_weights = contract_rows(outer, values)
        delta = jnp.sum(wide * grad_weights, axis=-1, keepdims=True)
        grad_scores = (wide * (grad_weights - delta)).astype(bf16)
        product = jnp.dot(grad_scores, keys, preferred_element_type=f32) * HD**-0.5
        for h in range(batch):
            turned = rotated(product[h * rows : (h + 1) * rows], cosine[...], -sine[...])
            linear[:, pl.ds(kv_width + at[h], HD)] = turned.astype(bf16)
        two = queries[pl.ds(batch * i, batch)].reshape(batch * rows, HD)
        kv_total[:, :HD] += contract_tokens(grad_scores, two)
        kv_total[:, HD:] += contract_tokens(weights, outer)
        return carry

    lax.fori_loop(0, heads // batch, some_heads, 0)
    linear_group = GroupGather(
        p, linear, linear_all, linear_sems, own_sems.at[1], 2, (q_at, kv_at)
    )
    linear_group.give(0)
    if with_result:
        result_sum.far(0)
        result_sum.near(1, 0)
    out_sum.near(0, 0)
    kv_parts[...] = kv_total[...].astype(bf16).reshape(kv_parts.shape)
    kv_sum = LineSum(p, kv_parts, kv_side, kv_chain, kv_sems)
    kv_sum.start(lines)
    kv_sum.turns(0)
    own = kv_sum.total()
    linear[:, :HD] = rotated(own[:, :HD], cosine[...], -sine[...]).astype(bf16)
    linear[:, pl.ds(HD, HD)] = own[:, HD:].astype(bf16)
    linear_group.give(1)
    linear_group.local().start()
    if with_result:
        for turn in range(2, lines):
            result_sum.across(turn).start()
        result_sum.far(1)
    for turn in range(2, lines):
        out_sum.across(turn).start()
    out_sum.far(0)
    out_sum.near(1, 0)
    out_sum.far(1)
    linear_group.pass_on(0)
    linear_group.pass_on(1)
    linear_group.local().wait()
    for i in range(2):
        linear_group.near(i)
        linear_group.last(i)

    linear_copy = pltpu.make_async_copy(linear_all, linear_out, own_sems.at[4])
    linear_copy.start()

    last_trade = GroupReturn(p, trade_parts.at[1], trade_slots.at[1], trade_sems.at[1])

    def normed_back(g):
        product = contract_rows(linear_all[g, :, kv_at], w_keyval[...])
        product += contract_rows(linear_all[g, :, q_at], w_query[...])
        trade_parts[1, g] = product.astype(bf16)

    normed_back(p.cross_f)
    last_trade.send(2)
    normed_back(p.diag_f)
    normed_back(p.twin_f)
    last_trade.send(1)
    last_trade.send(3)
    normed_back(p.f)
    last_trade.own().start()
    if with_result:
        for turn in range(2, lines):
            result_sum.near(turn, 0)
            result_sum.far(turn)
    last_trade.wait()
    for g in range(4):
        grad_mixed[:, g * shard : (g + 1) * shard] = trade_slots[1, g]
    source = tokens[...].astype(f32)
    grad_values, gain = norm_back(source, gains[0:1], grad_mixed[...].astype(f32))
    input_grad_out[...] = (grad_middle[...] + grad_values).astype(bf16)
    gain_out[...] = gain
    for turn in range(2, lines):
        out_sum.near(turn, 0)
        out_sum.far(turn)
    out_stage[...] = out_sum.total().astype(bf16)
    out_move.start()
    if with_result:
        result_out[...] = (middle[...] + result_sum.total()).astype(bf16)
        result_sum.finish()
    back_trade.finish()
    last_trade.finish()
    group.sent(0)
    linear_group.sent(0)
    linear_group.sent(1)
    kv_sum.finish()
    branch_copy.wait()
    linear_copy.wait()
    out_sum.finish()
    down_move.finish()
    out_move.finish()


def back(lines, operands, result_operands):
    rows, width = operands[0].shape
    heads = operands[3].shape[0]
    places = 2 * lines
    length = places * rows
    shard = width // 4
    linear_width = width + 2 * HD
    tall = width // places
    pieces = operands[12].shape
    in_vmem = pl.BlockSpec(memory_space=VMEM)
    anywhere = pl.BlockSpec(memory_space=pl.ANY)
    shape = jax.ShapeDtypeStruct
    with_result = bool(result_operands)
    long = is_long(length)
    result_scratch = [
        VMEM((places, rows, width), bf16),
        VMEM((lines, rows, width), bf16),
        VMEM((2, lines - 1, rows, width), bf16),
        DMA((LineSum.sems, lines)),
    ]
    return pl.pallas_call(
        functools.partial(back_kernel, lines, with_result),
        out_shape=((shape((rows, width), bf16),) if with_result else ())
        + (
            shape((rows, width), bf16),
            shape((1, width), f32),
            shape((4, rows, width), bf16),
            shape((4, rows, linear_width), bf16),
            shape((tall, shard), bf16),
            shape(pieces, bf16),
        ),
        in_specs=[in_vmem, anywhere if long else in_vmem] + [in_vmem] * 10 + [anywhere] + ([in_vmem, anywhere] if with_result else []),
        out_specs=[in_vmem] * (3 if with_result else 2) + [anywhere] * 4,
        scratch_shapes=[
            VMEM((4, rows, width), bf16),
            VMEM((4, rows, linear_width), bf16),
            VMEM((rows, width), bf16),
            VMEM((rows, linear_width), bf16),
            VMEM((2, 4, rows, shard), bf16),
            VMEM((2, 4, rows, shard), bf16),
            VMEM((rows, width), bf16),
            VMEM((length, 2 * HD), f32),
            VMEM((places, rows, 2 * HD), bf16),
            VMEM((lines, rows, 2 * HD), bf16),
            VMEM((2, lines - 1, rows, 2 * HD), bf16),
            VMEM((places, tall, shard), bf16),
            VMEM((lines, tall, shard), bf16),
            VMEM((2, lines - 1, tall, shard), bf16),
            VMEM((tall, shard), bf16),
            VMEM((rows, length if long else 128), bf16),
            DMA((GroupGather.sems, 1)),
            DMA((GroupGather.sems, 2)),
            DMA((2, GroupTrade.sems, 4)),
            DMA((LineSum.sems, lines)),
            DMA((LineSum.sems, lines)),
            DMA((3,)),
            DMA((3, 4)),
            DMA((6,)),
        ]
        + (result_scratch if with_result else []),
        compiler_params=pltpu.CompilerParams(
            collective_id=2, has_side_effects=True, vmem_limit_bytes=vmem_bytes
        ),
        name="back",
    )(*operands, *result_operands)


def grads_kernel(lines, with_columns, normed, linear_all, gain_one, gain_two, *rest):
    if with_columns:
        normed_two, hidden_grads, *rest = rest
    projection_out, gains_out, *rest = rest
    if with_columns:
        columns_out, *rest = rest
    (
        parts,
        side,
        chain,
        stage,
        gain_parts,
        gain_side,
        gain_chain,
        gain_slots,
        projection_sems,
        gain_sems,
        slot_sems,
        move_sems,
        *rest,
    ) = rest
    if with_columns:
        chunk_parts, near, passing, far, chunks, group_sems, trade_sems = rest
    p = Place(lines)
    places = 2 * lines
    shard = normed.shape[2]
    tokens = 4 * normed.shape[1]
    per_owner = places // 4
    tall = shard // per_owner
    kv_share = 2 * HD // 4
    move = BlockMove(p, per_owner, stage, projection_out, move_sems)
    others = [(jnp.full((), True), {"ctx": (p.c + d) % places}) for d in range(1, places)]
    p.barrier(ctx=False, also=others + move.greets())

    for c in range(places):
        cols = slice(c * tall, (c + 1) * tall)
        gain_parts[c, 0:1, :tall] = gain_one[:, cols]
        gain_parts[c, 1:2, :tall] = gain_two[:, cols]
    gain_sum = LineSum(p, gain_parts, gain_side, gain_chain, gain_sems)
    gain_sum.start(lines)

    projection_sum = LineSum(p, parts, side, chain, projection_sems)

    def projection_blocks(g, carry):
        left = normed[...].reshape(tokens, shard)
        right = linear_all[:, :, pl.ds(pl.multiple_of(2 * HD + g * shard, 128), shard)]
        product = contract_tokens(left, right.reshape(tokens, shard))
        right = linear_all[:, :, pl.ds(pl.multiple_of(g * kv_share, 128), kv_share)]
        kv_product = contract_tokens(left, right.reshape(tokens, kv_share))
        for r in range(per_owner):
            rows = slice(r * tall, (r + 1) * tall)
            parts[4 * r + g, :, :shard] = product[rows].astype(bf16)
            parts[4 * r + g, :, shard:] = kv_product[rows].astype(bf16)
        return carry

    lax.fori_loop(0, 4, projection_blocks, 0)
    projection_sum.start(2)

    if with_columns:
        block = columns_out.shape[2]
        chunk = chunk_parts.shape[1]
        every = slice(None)

        def chunk_of(k):
            return (p.line + k) % lines

        def group(k):
            return GroupSum(p, chunk_parts, near.at[k], passing.at[k % 2], far.at[k], group_sems)

        def compute(k):
            cols = pl.ds(pl.multiple_of(chunk_of(k) * chunk, 128), chunk)

            def one(g, carry):
                left = normed_two[:, :, cols].reshape(-1, chunk)
                right = hidden_grads[:, :, pl.ds(pl.multiple_of(g * block, 128), block)]
                chunk_parts[g] = contract_tokens(left, right.reshape(-1, block)).astype(bf16)
                return carry

            lax.fori_loop(0, 4, one, 0)
            chunks[k] = chunk_parts[p.f]
            group(k).give(k, every)

        def halves(k):
            half = chunk // 2
            for lane in range(2):
                yield lane, 2 * chunk_of(k) + lane, chunks.at[k, pl.ds(lane * half, half)]

        def place_copy(k, lane, dest, src):
            return remote(
                src,
                columns_out.at[p.c],
                trade_sems.at[0, 2 * k + lane],
                trade_sems.at[1, p.c],
                {"ctx": dest},
            )

        def place_own(src):
            return pltpu.make_async_copy(src, columns_out.at[p.c], trade_sems.at[2, 0])

        def arrival(i):
            slot = columns_out.at[i]
            return remote(slot, slot, trade_sems.at[0, 0], trade_sems.at[1, i], p.beside)

        def complete(k):
            chunks[k] = group(k).take(k, every, chunks[k]).astype(bf16)
            for lane, dest, src in halves(k):
                pl.when(dest != p.c)(
                    lambda k=k, lane=lane, dest=dest, src=src: place_copy(k, lane, dest, src).start()
                )
                pl.when(dest == p.c)(lambda src=src: place_own(src).start())

        for k in range(lines):
            if k >= 1:
                group(k - 1).given(k - 1, every)
            if k >= 2:
                complete(k - 2)
                group(k - 2).passed(k - 2, every)
            compute(k)
            group(k).pass_on(k, every)
            if k == 0:
                gain_sum.turns(0)
            projection_sum.near(k, 2)
            if k > 0:
                projection_sum.far(k - 1)
        for k in (lines - 2, lines - 1):
            complete(k)
            group(k).passed(k, every)
        group(lines - 1).given(lines - 1, every)
        projection_sum.far(lines - 1)
    else:
        gain_sum.turns(0)
        projection_sum.turns(2)

    own = gain_sum.total()
    gain_parts[p.c] = own

    def gain_copy(d):
        return remote(
            gain_parts.at[p.c],
            gain_slots.at[d],
            slot_sems.at[0, d],
            slot_sems.at[1, d],
            {"fsdp": (p.f + d) % 4},
        )

    for d in (1, 2, 3):
        gain_copy(d).start()
    stage[...] = projection_sum.total().astype(bf16)
    move.start()
    for d in (1, 2, 3):
        gain_copy(d).wait_recv()
        own = own + gain_slots[d]
    gains_out[...] = own

    for d in (1, 2, 3):
        gain_copy(d).wait_send()
    if with_columns:
        for k in range(lines):
            for lane, dest, src in halves(k):
                pl.when(dest != p.c)(
                    lambda k=k, lane=lane, dest=dest, src=src: place_copy(k, lane, dest, src).wait_send()
                )
                pl.when(dest == p.c)(lambda src=src: place_own(src).wait())
        for i in range(places):
            pl.when(p.c != i)(lambda i=i: arrival(i).wait_recv())
    gain_sum.finish()
    projection_sum.finish()
    move.finish()


def weight_grads(lines, operands, column_operands):
    rows, shard = operands[0].shape[1:]
    width = 4 * shard
    places = 2 * lines
    tall = width // places
    wide = shard + 2 * HD // 4
    gain_wide = -(-tall // 128) * 128
    in_vmem = pl.BlockSpec(memory_space=VMEM)
    anywhere = pl.BlockSpec(memory_space=pl.ANY)
    shape = jax.ShapeDtypeStruct
    with_columns = bool(column_operands)
    column_shapes, column_scratch = (), []
    if with_columns:
        block = column_operands[1].shape[2] // 4
        chunk = width // lines
        column_shapes = (shape((places, chunk // 2, block), bf16),)
        column_scratch = [
            VMEM((4, chunk, block), bf16),
            VMEM((lines, 2, chunk, block), bf16),
            VMEM((2, chunk, block), bf16),
            VMEM((lines, chunk, block), bf16),
            VMEM((lines, chunk, block), bf16),
            DMA((GroupSum.sems, lines)),
            DMA((3, places)),
        ]
    return pl.pallas_call(
        functools.partial(grads_kernel, lines, with_columns),
        out_shape=(shape((tall, wide), bf16), shape((8, gain_wide), f32)) + column_shapes,
        in_specs=[in_vmem] * (4 + len(column_operands)),
        out_specs=[anywhere, in_vmem] + [anywhere] * len(column_shapes),
        scratch_shapes=[
            VMEM((places, tall, wide), bf16),
            VMEM((lines, tall, wide), bf16),
            VMEM((2, lines - 1, tall, wide), bf16),
            VMEM((tall, wide), bf16),
            VMEM((places, 8, gain_wide), f32),
            VMEM((lines, 8, gain_wide), f32),
            VMEM((2, lines - 1, 8, gain_wide), f32),
            VMEM((4, 8, gain_wide), f32),
            DMA((LineSum.sems, lines)),
            DMA((LineSum.sems, lines)),
            DMA((2, 4)),
            DMA((3,)),
        ]
        + column_scratch,
        compiler_params=pltpu.CompilerParams(
            collective_id=3, has_side_effects=True, vmem_limit_bytes=vmem_bytes
        ),
        name="grads",
    )(*operands, *column_operands)


def assemble_kernel(lines, piece, projection, out, down, columns, *outs):
    query_out, keyval_out, out_out, down_out, columns_out = outs
    shard = out.shape[1]
    padded_piece = columns.shape[2] // 2
    query_out[...] = projection[:, :shard].astype(f32)
    keyval_out[...] = projection[:, shard:].astype(f32)
    out_out[...] = out[...].astype(f32)
    for i in range(down.shape[0]):
        down_out[i * piece : (i + 1) * piece] = down[i, :piece].astype(f32)
    pieces = [
        columns[place_of_piece(n, lines), :, q * padded_piece : q * padded_piece + piece]
        for q in range(2)
        for n in range(2 * lines)
    ]
    columns_out[...] = jnp.concatenate(pieces, axis=1).astype(f32)


def assemble(lines, piece, projection, out, down, columns):
    tall, wide = projection.shape
    shard = out.shape[1]
    places = 2 * lines
    block = columns.shape[2]
    steps = 4 if tall % 64 == 0 else 1
    run = tall // steps
    full = 2 * places * piece

    def flat(rows, cols):
        return pl.BlockSpec((rows, cols), lambda i: (i, 0))

    shape = jax.ShapeDtypeStruct
    return pl.pallas_call(
        functools.partial(assemble_kernel, lines, piece),
        grid=(steps,),
        out_shape=(
            shape((tall, shard), f32),
            shape((tall, wide - shard), f32),
            shape((tall, shard), f32),
            shape((4 * piece, shard), f32),
            shape((tall, full), f32),
        ),
        in_specs=[
            flat(run, wide),
            flat(run, shard),
            pl.BlockSpec((4 // steps, down.shape[1], shard), lambda i: (i, 0, 0)),
            pl.BlockSpec((places, run, block), lambda i: (0, i, 0)),
        ],
        out_specs=[
            flat(run, shard),
            flat(run, wide - shard),
            flat(run, shard),
            flat(4 // steps * piece, shard),
            flat(run, full),
        ],
        compiler_params=pltpu.CompilerParams(vmem_limit_bytes=vmem_bytes),
        name="assemble",
    )(projection, out, down, columns)


def per_device(
    tokens,
    doc_bounds,
    cotangent,
    norm_one,
    query_weight,
    keyval_weight,
    out_weight,
    norm_two,
    gate_up_weight,
    down_weight,
):
    ctx_size = lax.axis_size("ctx")
    fsdp_size = lax.axis_size("fsdp")
    lines = ctx_size // 2
    rows = tokens.shape[1]
    width = tokens.shape[2]
    length = rows * ctx_size
    inner_width = query_weight.shape[1]
    head_count = inner_width // HD
    hidden_width = gate_up_weight.shape[1] // 2
    piece = hidden_width // (ctx_size * fsdp_size)
    padded_piece = -(-piece // 32) * 32
    padded = padded_piece * fsdp_size
    gains = jnp.stack([norm_one, norm_two])
    cot_rows = cotangent[0]
    down_rows = down_weight
    if piece % 16:
        first = hidden_piece(lax.axis_index("ctx"), lines) * piece
        down_rows = lax.dynamic_slice_in_dim(down_weight, first, piece, 0)
        down_rows = jnp.pad(down_rows, ((0, padded_piece - piece), (0, 0)))
    (
        normed,
        queries,
        window,
        weights,
        mixed,
        middle,
        normed_two,
        cosine,
        sine,
        w_columns,
        cot_all,
        w_down,
    ) = front(
        lines,
        (
            doc_bounds,
            tokens[0],
            gains,
            keyval_weight,
            query_weight,
            out_weight,
            cot_rows,
            down_rows,
            gate_up_weight,
        ),
        head_count,
        padded_piece,
    )
    w_down = w_down.reshape(padded, width)
    fits = middle_bytes(lines, rows, width, padded) <= vmem_bytes
    if fits:
        grad_middle, gain_two_term, grad_gate_up, down_part, normed_two, result_parts = middle_part(
            lines, (cot_all, w_down, gains, normed_two, middle, w_columns), padded
        )
    else:
        cot_all = cot_all.reshape(length, width)
        normed_two = lax.all_gather(normed_two, "ctx", axis=0, tiled=True)
        w_gate_up = lax.all_gather(w_columns, "fsdp", axis=0, tiled=True)
        projected = jnp.dot(normed_two, w_gate_up, preferred_element_type=f32)
        gelu, slope = gelu_parts(projected[:, :padded])
        up_part = projected[:, padded:]
        hidden = (gelu * up_part).astype(bf16)
        grad_hidden = contract_rows(cot_all, w_down)
        grad_gate_up = jnp.concatenate(
            [grad_hidden * up_part * slope, grad_hidden * gelu], axis=1
        ).astype(bf16)
        grad_normed_two = lax.psum_scatter(
            contract_rows(grad_gate_up, w_gate_up).astype(bf16),
            "ctx",
            scatter_dimension=0,
            tiled=True,
        ).astype(f32)
        grad_middle_norm, gain_two_term = norm_back(middle, norm_two[None], grad_normed_two)
        grad_middle = cot_rows.astype(f32) + grad_middle_norm
        result_parts = jnp.dot(hidden, w_down, preferred_element_type=f32).astype(bf16)
        down_part = lax.psum_scatter(
            contract_tokens(hidden, cot_all).astype(bf16),
            "fsdp",
            scatter_dimension=1,
            tiled=True,
        ).reshape(fsdp_size, padded_piece, -1)
    operands = (
        grad_middle,
        weights,
        window,
        queries,
        mixed,
        tokens[0],
        gains,
        cosine,
        sine,
        out_weight,
        query_weight,
        keyval_weight,
        down_part,
    )
    if fits:
        result, input_grad, gain_one_term, _, grad_linear, out_grad, down_grad = back(
            lines, operands, (middle, result_parts.reshape(ctx_size, rows, width))
        )
    else:
        input_grad, gain_one_term, _, grad_linear, out_grad, down_grad = back(lines, operands, ())
        branch_two = lax.psum_scatter(result_parts, "ctx", scatter_dimension=0, tiled=True)
        result = (middle + branch_two.astype(f32)).astype(bf16)

    operands = (normed, grad_linear, gain_one_term, gain_two_term)
    if fits:
        projection_grad, gain_grads, gate_up_part = weight_grads(
            lines, operands, (normed_two, grad_gate_up)
        )
    else:
        projection_grad, gain_grads = weight_grads(lines, operands, ())
        gate_up_part = lax.psum_scatter(
            contract_tokens(normed_two, grad_gate_up).astype(bf16),
            "fsdp",
            scatter_dimension=1,
            tiled=True,
        )
        gate_up_part = lax.all_to_all(
            gate_up_part.reshape(ctx_size, width // ctx_size, -1), "ctx", 0, 0, tiled=True
        )
    query_grad, keyval_grad, out_grad, down_grad, gate_up_grad = assemble(
        lines, piece, projection_grad, out_grad, down_grad, gate_up_part
    )
    share = width // (ctx_size * fsdp_size)
    gains = lax.dynamic_slice_in_dim(gain_grads, lax.axis_index("fsdp") * share, share, 1)
    return (
        result[None],
        input_grad[None],
        gains[0],
        query_grad,
        keyval_grad,
        out_grad,
        gains[1],
        gate_up_grad,
        down_grad,
    )


def solution(mesh):
    placed = (
        P("fsdp", "ctx", None),
        P("fsdp", None),
        P("fsdp", "ctx", None),
        P(),
        P("fsdp", None),
        P("fsdp", None),
        P("fsdp", None),
        P(),
        P("fsdp", None),
        P("fsdp", None),
    )
    return jax.shard_map(
        per_device,
        mesh=mesh,
        in_specs=placed,
        out_specs=(
            P("fsdp", "ctx", None),
            P("fsdp", "ctx", None),
            P(("ctx", "fsdp")),
            P("ctx", "fsdp"),
            P("ctx", "fsdp"),
            P("ctx", "fsdp"),
            P(("ctx", "fsdp")),
            P("ctx", "fsdp"),
            P("ctx", "fsdp"),
        ),
        check_vma=False,
    )
```

```python
import functools
import math

import jax
import jax.numpy as jnp
from jax import lax
from jax.experimental import pallas as pl
from jax.experimental.pallas import tpu as pltpu
from jax.sharding import PartitionSpec as P

HD = 256
WINDOW = 2048


epsilon = 1e-06
f32 = jnp.float32
bf16 = jnp.bfloat16
VMEM = pltpu.VMEM
DMA = pltpu.SemaphoreType.DMA
vmem_bytes = 62 * 1024 * 1024


def rms_norm(values, gain):
    return values * lax.rsqrt(jnp.mean(values * values, axis=-1, keepdims=True) + epsilon) * gain


def documents(index, bounds):
    return (index >= bounds[0]).astype(jnp.int32) + (index >= bounds[1]).astype(jnp.int32)


def contract_rows(left, right):
    return lax.dot_general(
        left, right, (((1,), (1,)), ((), ())), preferred_element_type=jnp.float32
    )


def contract_tokens(left, right):
    return lax.dot_general(
        left, right, (((0,), (0,)), ((), ())), preferred_element_type=jnp.float32
    )


def remote(src, dst, send_sem, recv_sem, device):
    return pltpu.make_async_remote_copy(
        src_ref=src,
        dst_ref=dst,
        send_sem=send_sem,
        recv_sem=recv_sem,
        device_id=device,
        device_id_type=pl.DeviceIdType.MESH,
    )


class Place:
    def __init__(self, lines):
        self.lines = lines
        self.c = lax.axis_index("ctx")
        self.f = lax.axis_index("fsdp")
        self.line = self.c // 2
        self.lane = self.c % 2
        self.chip = self.f // 2
        self.core = self.f % 2
        self.twin_f = self.f + 1 - 2 * self.core
        self.cross_f = (self.f + 2) % 4
        self.diag_f = (self.twin_f + 2) % 4
        self.twin = {"fsdp": self.twin_f}
        self.cross = {"fsdp": self.cross_f}
        self.diag = {"fsdp": self.diag_f}
        self.beside = {"ctx": self.c + 1 - 2 * self.lane}
        self.right = {"ctx": self.c + 2}
        self.left = {"ctx": self.c - 2}
        self.has_right = self.line < lines - 1
        self.has_left = self.line > 0

    def barrier(self, ctx=True, fsdp=True, also=()):
        sem = pltpu.get_barrier_semaphore()

        def greet(device):
            pl.semaphore_signal(sem, 1, device_id=device, device_id_type=pl.DeviceIdType.MESH)

        count = 0
        if fsdp:
            for device in (self.twin, self.cross, self.diag):
                greet(device)
            count = 3
        if ctx:
            greet(self.beside)
            pl.when(self.has_right)(lambda: greet(self.right))
            pl.when(self.has_left)(lambda: greet(self.left))
            count = (
                count + 1 + self.has_right.astype(jnp.int32) + self.has_left.astype(jnp.int32)
            )
        for needed, device in also:
            pl.when(needed)(lambda device=device: greet(device))
            count = count + needed.astype(jnp.int32)
        pl.semaphore_wait(sem, count)


class Fetch:
    def __init__(self, pairs, sems):
        self.copies = [
            pltpu.make_async_copy(src, dst, sems.at[i]) for i, (src, dst) in enumerate(pairs)
        ]
        for copy in self.copies:
            copy.start()

    def wait(self, *which):
        for i in which:
            self.copies[i].wait()


def held(operands):
    return [VMEM(operand.shape, operand.dtype) for operand in operands]


class LineGather:
    sems = 6

    def __init__(self, place, own, slots, sems):
        self.p, self.own, self.slots, self.s = place, own, slots, sems

    def rightward(self, step):
        at = 2 * (self.p.line - step) + self.p.lane
        src = self.own if step == 0 else self.slots.at[at]
        return remote(src, self.slots.at[at], self.s.at[0, step], self.s.at[1, step], self.p.right)

    def leftward(self, step):
        at = 2 * (self.p.line + step) + self.p.lane
        src = self.own if step == 0 else self.slots.at[at]
        return remote(src, self.slots.at[at], self.s.at[2, step], self.s.at[3, step], self.p.left)

    def across(self, line, own=False):
        at = 2 * line + self.p.lane
        src = self.own if own else self.slots.at[at]
        return remote(
            src, self.slots.at[at], self.s.at[4, line], self.s.at[5, line], self.p.beside
        )

    def from_left(self, step):
        at = 2 * (self.p.line - 1 - step) + self.p.lane
        slot = self.slots.at[at]
        return remote(slot, slot, self.s.at[0, step], self.s.at[1, step], self.p.right)

    def from_right(self, step):
        at = 2 * (self.p.line + 1 + step) + self.p.lane
        slot = self.slots.at[at]
        return remote(slot, slot, self.s.at[2, step], self.s.at[3, step], self.p.left)

    def start(self):
        pl.when(self.p.has_right)(lambda: self.rightward(0).start())
        pl.when(self.p.has_left)(lambda: self.leftward(0).start())
        self.across(self.p.line, True).start()

    def step(self, step):
        p = self.p

        @pl.when(p.line - 1 - step >= 0)
        def _():
            self.from_left(step).wait_recv()
            if step + 1 < p.lines - 1:
                pl.when(p.has_right)(lambda: self.rightward(step + 1).start())
            self.across(p.line - 1 - step).start()

        @pl.when(p.line + 1 + step <= p.lines - 1)
        def _():
            self.from_right(step).wait_recv()
            if step + 1 < p.lines - 1:
                pl.when(p.has_left)(lambda: self.leftward(step + 1).start())
            self.across(p.line + 1 + step).start()

    def steps(self):
        for step in range(self.p.lines - 1):
            self.step(step)

    def arrived_across(self, line):
        at = 2 * line + 1 - self.p.lane
        slot = self.slots.at[at]
        remote(slot, slot, self.s.at[4, line], self.s.at[5, line], self.p.beside).wait_recv()

    def finish(self, arrivals=True):
        p = self.p
        if arrivals:
            for line in range(p.lines):
                self.arrived_across(line)
        for step in range(p.lines - 1):
            pl.when(p.has_right & (p.line - step >= 0))(
                lambda step=step: self.rightward(step).wait_send()
            )
            pl.when(p.has_left & (p.line + step <= p.lines - 1))(
                lambda step=step: self.leftward(step).wait_send()
            )
        for line in range(p.lines):
            self.across(line).wait_send()


class LineSum:
    sems = 6

    def __init__(self, place, parts, side, chain, sems):
        self.p, self.parts, self.side, self.chain, self.s = place, parts, side, chain, sems

    def order(self, turn):
        lines, line = self.p.lines, self.p.line
        value = 0
        for a in range(lines):
            far = sorted(range(lines), key=lambda t: (-abs(t - a), t))
            value = value + jnp.where(line == a, far[turn], 0)
        return value

    def across(self, turn):
        t = self.order(turn)
        at = 2 * t + 1 - self.p.lane
        return remote(
            self.parts.at[at],
            self.side.at[t],
            self.s.at[0, t],
            self.s.at[1, t],
            self.p.beside,
        )

    def rightward(self, t):
        step = self.p.lines - 1 - t
        return remote(
            self.parts.at[2 * t + self.p.lane],
            self.chain.at[0, step],
            self.s.at[2, step],
            self.s.at[3, step],
            self.p.right,
        )

    def leftward(self, t):
        return remote(
            self.parts.at[2 * t + self.p.lane],
            self.chain.at[1, t],
            self.s.at[4, t],
            self.s.at[5, t],
            self.p.left,
        )

    def add(self, at, other):
        self.parts[at] = (self.parts[at].astype(f32) + other.astype(f32)).astype(self.parts.dtype)

    def start(self, ahead=2):
        for turn in range(min(ahead, self.p.lines)):
            self.across(turn).start()

    def near(self, turn, ahead=2):
        p = self.p
        t = self.order(turn)
        at = 2 * t + p.lane
        self.across(turn).wait_recv()
        if ahead and turn + ahead < p.lines:
            self.across(turn + ahead).start()
        self.add(at, self.side[t])
        pl.when((t > p.line) & (p.line == 0))(lambda: self.rightward(t).start())
        pl.when((t < p.line) & (p.line == p.lines - 1))(lambda: self.leftward(t).start())

    def far(self, turn):
        p = self.p
        t = self.order(turn)
        at = 2 * t + p.lane

        @pl.when((t > p.line) & p.has_left)
        def _():
            self.rightward(t).wait_recv()
            self.add(at, self.chain[0, p.lines - 1 - t])
            self.rightward(t).start()

        @pl.when((t < p.line) & p.has_right)
        def _():
            self.leftward(t).wait_recv()
            self.add(at, self.chain[1, t])
            self.leftward(t).start()

    def turns(self, ahead=2):
        for turn in range(self.p.lines):
            self.near(turn, ahead)
            if turn > 0:
                self.far(turn - 1)
        self.far(self.p.lines - 1)

    def total(self):
        p = self.p
        at = 2 * p.line + p.lane

        @pl.when(p.has_left)
        def _():
            self.rightward(p.line).wait_recv()
            self.add(at, self.chain[0, p.lines - 1 - p.line])

        @pl.when(p.has_right)
        def _():
            self.leftward(p.line).wait_recv()
            self.add(at, self.chain[1, p.line])

        return self.parts[at].astype(f32)

    def finish(self):
        p = self.p
        for turn in range(p.lines):
            self.across(turn).wait_send()
        for t in range(p.lines):
            pl.when(t > p.line)(lambda t=t: self.rightward(t).wait_send())
            pl.when(t < p.line)(lambda t=t: self.leftward(t).wait_send())


class GroupSum:
    sems = 6

    def __init__(self, place, parts, near, out, far, sems):
        self.p, self.parts, self.near, self.out, self.far, self.s = place, parts, near, out, far, sems

    def to_twin(self, i, which, cols):
        p = self.p
        block = p.diag_f if which == 0 else p.twin_f
        return remote(
            self.parts.at[block, :, cols],
            self.near.at[which, :, cols],
            self.s.at[which, i],
            self.s.at[2 + which, i],
            p.twin,
        )

    def to_cross(self, i, cols):
        return remote(
            self.out.at[:, cols], self.far.at[:, cols], self.s.at[4, i], self.s.at[5, i], self.p.cross
        )

    def give(self, i, cols):
        self.to_twin(i, 0, cols).start()
        self.to_twin(i, 1, cols).start()

    def pass_on(self, i, cols):
        self.to_twin(i, 0, cols).wait_recv()
        mine = self.parts[self.p.cross_f, :, cols].astype(f32)
        self.out[:, cols] = (mine + self.near[0, :, cols].astype(f32)).astype(bf16)
        self.to_cross(i, cols).start()

    def take(self, i, cols, own=None):
        self.to_twin(i, 1, cols).wait_recv()
        own = self.parts[self.p.f, :, cols] if own is None else own
        near = own.astype(f32) + self.near[1, :, cols].astype(f32)
        self.to_cross(i, cols).wait_recv()
        return near + self.far[:, cols].astype(f32)

    def given(self, i, cols):
        self.to_twin(i, 0, cols).wait_send()
        self.to_twin(i, 1, cols).wait_send()

    def passed(self, i, cols):
        self.to_cross(i, cols).wait_send()

    def finish(self, i, cols):
        self.given(i, cols)
        self.passed(i, cols)


class GroupTrade:
    sems = 2

    def __init__(self, place, whole, slots, sems, columns):
        self.p, self.whole, self.slots, self.s, self.n = place, whole, slots, sems, columns

    def block(self, g):
        return self.whole.at[:, pl.ds(pl.multiple_of(g * self.n, 128), self.n)]

    def send(self, d):
        self.copy(d).start()

    def copy(self, d):
        g = (self.p.f + d) % 4
        return remote(
            self.block(g), self.slots.at[self.p.f], self.s.at[0, d], self.s.at[1, d], {"fsdp": g}
        )

    def arrival(self, d):
        slot = self.slots.at[(self.p.f + 4 - d) % 4]
        return remote(slot, slot, self.s.at[0, d], self.s.at[1, d], {"fsdp": (self.p.f + d) % 4})

    def own(self):
        return pltpu.make_async_copy(
            self.block(self.p.f), self.slots.at[self.p.f], self.s.at[1, 0]
        )

    def start(self):
        for d in (2, 3, 1):
            self.copy(d).start()
        self.own().start()

    def wait(self):
        self.own().wait()
        for d in (1, 2, 3):
            self.arrival(d).wait_recv()

    def finish(self):
        for d in (1, 2, 3):
            self.copy(d).wait_send()


class BlockMove:
    def __init__(self, place, per_owner, src, dst, sems):
        p = place
        self.src, self.dst, self.s = src, dst, sems
        self.to_ctx, self.to_f = per_owner * p.f + p.c // 4, p.c % 4
        self.from_ctx, self.from_f = 4 * (p.c % per_owner) + p.f, p.c // per_owner
        self.moves = (self.to_ctx != p.c) | (self.to_f != p.f)

    def greets(self):
        return [
            (self.moves, {"ctx": self.to_ctx, "fsdp": self.to_f}),
            (self.moves, {"ctx": self.from_ctx, "fsdp": self.from_f}),
        ]

    def copy(self):
        device = {"ctx": self.to_ctx, "fsdp": self.to_f}
        return remote(self.src, self.dst, self.s.at[0], self.s.at[1], device)

    def stay(self):
        return pltpu.make_async_copy(self.src, self.dst, self.s.at[2])

    def start(self):
        pl.when(self.moves)(lambda: self.copy().start())
        pl.when(~self.moves)(lambda: self.stay().start())

    def finish(self):
        @pl.when(self.moves)
        def _():
            self.copy().wait_send()
            self.copy().wait_recv()

        pl.when(~self.moves)(lambda: self.stay().wait())


class PieceMove:
    def __init__(self, place, per_owner, pieces, slots, sems):
        p = place
        self.p, self.n, self.pieces, self.slots, self.s = p, per_owner, pieces, slots, sems
        self.at = hidden_piece(p.c, p.lines)

    def dest(self, q):
        return self.n * q + self.at // 4

    def copy(self, q):
        return remote(
            self.pieces.at[q],
            self.slots.at[self.at % 4],
            self.s.at[0, q],
            self.s.at[1, self.at % 4],
            {"ctx": self.dest(q)},
        )

    def stay(self, q):
        return pltpu.make_async_copy(self.pieces.at[q], self.slots.at[self.at % 4], self.s.at[2, 0])

    def start(self):
        for q in range(4):
            here = self.dest(q) == self.p.c
            pl.when(~here)(lambda q=q: self.copy(q).start())
            pl.when(here)(lambda q=q: self.stay(q).start())

    def finish(self):
        p = self.p
        for q in range(4):
            here = self.dest(q) == p.c
            pl.when(~here)(lambda q=q: self.copy(q).wait_send())
            pl.when(here)(lambda q=q: self.stay(q).wait())
        for i in range(4):
            source = place_of_piece(4 * (p.c % self.n) + i, p.lines)
            slot = self.slots.at[i]
            arrival = remote(slot, slot, self.s.at[0, 0], self.s.at[1, i], p.beside)
            pl.when(source != p.c)(lambda arrival=arrival: arrival.wait_recv())


def hidden_piece(c, lines):
    return (c % 2) * lines + c // 2


def place_of_piece(piece, lines):
    return (piece % lines) * 2 + piece // lines


class GroupReturn(GroupTrade):
    def __init__(self, place, whole, slots, sems):
        super().__init__(place, whole, slots, sems, 0)

    def block(self, g):
        return self.whole.at[g]


def rotary_tables(first, rows, bounds):
    index = first + lax.broadcasted_iota(jnp.int32, (rows, 128), 0)
    lane = lax.broadcasted_iota(jnp.int32, (rows, 128), 1)
    quarter = HD // 4
    member = documents(index, bounds)
    opening = jnp.where(member == 0, 0, jnp.where(member == 1, bounds[0], bounds[1]))
    frequency = jnp.exp((lane % quarter).astype(f32) * (-math.log(10000.0) / quarter))
    angles = (index - opening).astype(f32) * frequency
    sine = jnp.sin(angles)
    return jnp.cos(angles), jnp.where(lane < quarter, -sine, sine)


def rotated(v, cosine, sine):
    first = v[:, :128]
    return jnp.concatenate(
        [first * cosine + pltpu.roll(first, 64, 1) * sine, v[:, 128:]], axis=1
    )


class GroupGather:
    sems = 6

    def __init__(self, place, own, whole, sems, own_sem, pieces, cuts=None):
        self.p, self.own, self.whole, self.s, self.own_sem = place, own, whole, sems, own_sem
        self.pieces, self.n, self.cuts = pieces, own.shape[0] // pieces, cuts

    def span(self, i):
        return (slice(None), self.cuts[i]) if self.cuts else (pl.ds(i * self.n, self.n),)

    def part(self, i):
        return self.own.at[self.span(i)]

    def slot(self, g, i):
        return self.whole.at[(g,) + self.span(i)]

    def local(self):
        return pltpu.make_async_copy(self.own, self.whole.at[self.p.f], self.own_sem)

    def to_twin(self, i):
        return remote(
            self.part(i), self.slot(self.p.f, i), self.s.at[0, i], self.s.at[3, i], self.p.twin
        )

    def to_cross(self, i):
        return remote(
            self.part(i), self.slot(self.p.f, i), self.s.at[1, i], self.s.at[4, i], self.p.cross
        )

    def forward(self, i):
        slot = self.slot(self.p.cross_f, i)
        return remote(slot, slot, self.s.at[2, i], self.s.at[5, i], self.p.twin)

    def give(self, i):
        self.to_cross(i).start()
        self.to_twin(i).start()

    def near(self, i):
        twin = self.slot(self.p.twin_f, i)
        remote(twin, twin, self.s.at[0, i], self.s.at[3, i], self.p.twin).wait_recv()

    def pass_on(self, i):
        slot = self.slot(self.p.cross_f, i)
        remote(slot, slot, self.s.at[1, i], self.s.at[4, i], self.p.cross).wait_recv()
        self.forward(i).start()

    def last(self, i):
        diag = self.slot(self.p.diag_f, i)
        remote(diag, diag, self.s.at[2, i], self.s.at[5, i], self.p.twin).wait_recv()

    def sent(self, i):
        self.to_twin(i).wait_send()
        self.to_cross(i).wait_send()
        self.forward(i).wait_send()

    def finish(self, i):
        self.near(i)
        self.last(i)
        self.sent(i)


def tiles_of(first, count, tile):
    tile = tile if count % tile == 0 else 128

    def loop(body):
        def one(i, carry):
            body(pl.ds(pl.multiple_of(first + i * tile, 128), tile))
            return carry

        lax.fori_loop(0, count // tile, one, 0)

    return loop


def front_kernel(
    lines,
    bounds_ref,
    x_ref,
    gains,
    w_keyval_in,
    w_query_in,
    w_out_in,
    cot,
    w_down,
    w_gate_up,
    normed_out,
    query_out,
    keyval_out,
    probs_out,
    mixed_out,
    middle_out,
    normed_two_out,
    cosine,
    sine,
    columns_out,
    cot_all,
    rows_all,
    whole,
    slots,
    parts,
    near,
    out,
    far,
    keyval,
    mixed,
    bias,
    w_rows,
    windows,
    w_keyval,
    w_query,
    w_out,
    fetch_sems,
    trade_sems,
    sum_sems,
    keyval_sems,
    cot_sems,
    row_sems,
    own_sems,
):
    p = Place(lines)
    rows, width = x_ref.shape
    length = bias.shape[1]
    heads = query_out.shape[0]
    inner = heads * HD
    kv_width = 2 * HD
    fetch = Fetch(
        ((w_keyval_in, w_keyval), (w_query_in, w_query), (w_out_in, w_out)), fetch_sems
    )
    p.barrier()

    units = w_gate_up.shape[1] // 2
    piece = units // (4 * 2 * lines)
    padded_piece = w_rows.shape[0]
    own_piece = hidden_piece(p.c, lines)
    if w_down.shape[0] == padded_piece:
        rows_copy = pltpu.make_async_copy(w_down, w_rows, own_sems.at[2])
    else:
        rows_copy = pltpu.make_async_copy(
            w_down.at[pl.ds(pl.multiple_of(own_piece * piece, 16), piece)],
            w_rows.at[pl.ds(0, piece)],
            own_sems.at[2],
        )
    rows_copy.start()
    span = windows.shape[2]
    shard = w_gate_up.shape[0]

    def window_first(q):
        first = q * (units // 4) + own_piece * piece
        return jnp.minimum(first // 128 * 128, 2 * units - span), first

    def window(q):
        return pltpu.make_async_copy(
            w_gate_up.at[:, pl.ds(pl.multiple_of(window_first(q)[0], 128), span)],
            windows.at[q % 2],
            own_sems.at[3 + q % 2],
        )

    def pack_columns(q):
        window(q).wait()
        start, first = window_first(q)
        by = first - start
        lane = lax.broadcasted_iota(jnp.int32, (shard, 128), 1)
        tiles = [
            pltpu.roll(windows[q % 2, :, t * 128 : (t + 1) * 128].astype(f32), (128 - by % 128) % 128, 1)
            for t in range(span // 128)
        ]
        late = by >= 128
        turned = []
        for t in range(span // 128 - 1):
            turned.append(jnp.where(lane < 128 - by % 128, tiles[t], tiles[t + 1]))
        turned.append(jnp.where(lane < 128 - by % 128, tiles[-1], 0.0))
        turned = [
            jnp.where(late, turned[t + 1], turned[t]) for t in range(span // 128 - 1)
        ]
        turned = jnp.concatenate(turned, axis=1)[:, :padded_piece]
        lane = lax.broadcasted_iota(jnp.int32, (shard, padded_piece), 1)
        columns_out[:, q * padded_piece : (q + 1) * padded_piece] = jnp.where(
            lane < piece, turned, 0.0
        ).astype(bf16)
        if q + 2 < 8:
            window(q + 2).start()

    window(0).start()
    window(1).start()
    down = GroupGather(p, w_rows, rows_all, row_sems, own_sems.at[0], row_sems.shape[1])
    cot_gather = LineGather(p, cot, cot_all, cot_sems)
    cot_local = pltpu.make_async_copy(cot, cot_all.at[p.c], own_sems.at[1])

    def give(first, last):
        for i in range(first, min(last, down.pieces)):
            down.give(i)

    def pass_on(first, last):
        for i in range(first, min(last, down.pieces)):
            down.pass_on(i)

    source = x_ref[...].astype(f32)
    whole[...] = rms_norm(source, gains[0:1]).astype(bf16)
    trade = GroupTrade(p, whole, slots.at[0], trade_sems.at[0], slots.shape[3])
    trade.start()
    cot_local.start()
    cot_gather.start()
    bounds = (bounds_ref[0, 0], bounds_ref[0, 1])
    cosine[...], sine[...] = rotary_tables(p.c * rows, rows, bounds)
    query_at = p.c * rows + lax.broadcasted_iota(jnp.int32, (rows, length), 0)
    key_at = lax.broadcasted_iota(jnp.int32, (rows, length), 1)
    allowed = (
        (query_at >= key_at)
        & (query_at - key_at < WINDOW)
        & (documents(query_at, bounds) == documents(key_at, bounds))
    )
    bias[...] = jnp.where(allowed, 0.0, -1e30)
    rows_copy.wait()
    if w_down.shape[0] != padded_piece and piece < padded_piece:
        w_rows[pl.ds(piece, padded_piece - piece)] = jnp.zeros(
            (padded_piece - piece, width), bf16
        )
    down.local().start()
    give(0, 1)
    trade.wait()
    normed_out[...] = slots[0]

    half = (heads // 2) * HD
    chunks = [(0, kv_width), (kv_width, half), (kv_width + half, inner - half)]
    group = GroupSum(p, parts, near, out, far, sum_sems.at[0])

    def project(lhs, weight, first, count, to):
        @tiles_of(first, count, 256)
        def _(cols):
            left = lhs[...].reshape(4 * rows, lhs.shape[-1])
            product = jnp.dot(left, weight[:, cols], preferred_element_type=f32)
            if to:
                cols = pl.ds(pl.multiple_of(cols.start + to, 128), cols.size)
            parts[:, :, cols] = product.astype(bf16).reshape(4, rows, cols.size)

    spans = [pl.ds(first, count) for first, count in chunks]
    fetch.wait(0, 1)
    project(slots.at[0], w_keyval, 0, kv_width, 0)
    group.give(0, spans[0])
    project(slots.at[0], w_query, 0, half, kv_width)
    group.give(1, spans[1])
    group.pass_on(0, spans[0])
    project(slots.at[0], w_query, half, inner - half, kv_width)
    group.give(2, spans[2])
    group.pass_on(1, spans[1])
    group.pass_on(2, spans[2])

    linear = group.take(0, spans[0])
    keyval[p.c] = jnp.concatenate(
        [rotated(linear[:, :HD], cosine[...], sine[...]), linear[:, HD:]], axis=1
    ).astype(bf16)
    kv_gather = LineGather(p, keyval.at[p.c], keyval, keyval_sems)
    kv_gather.start()
    kv_gather.step(0)

    def take_queries(i):
        linear = group.take(i, spans[i])
        for h in range(linear.shape[1] // HD):
            turned = rotated(linear[:, h * HD : (h + 1) * HD], cosine[...], sine[...])
            at = h if i == 1 else h + heads // 2
            query_out[at] = (turned * HD**-0.5).astype(bf16)

    take_queries(1)
    for step in range(1, lines - 1):
        kv_gather.step(step)
    cot_gather.step(0)
    take_queries(2)
    give(1, 4)
    kv_gather.finish()
    keyval_out[...] = keyval[...]


    def two_heads(i, carry):
        keys = keyval[:, :, :HD].reshape(length, HD)
        values = keyval[:, :, HD:].reshape(length, HD)
        two = query_out[pl.ds(2 * i, 2)].reshape(2 * rows, HD)
        scores = contract_rows(two, keys).reshape(2, rows, length) + bias[...][None]
        scores = scores.reshape(2 * rows, length)
        weights = jnp.exp(scores - jnp.max(scores, axis=-1, keepdims=True))
        total = jnp.sum(weights, axis=-1, keepdims=True)
        weights = (weights / total).astype(bf16)
        probs_out[pl.ds(2 * i, 2)] = weights.reshape(2, rows, length)
        product = jnp.dot(weights, values, preferred_element_type=f32).astype(bf16)
        at = pl.multiple_of(i * 2 * HD, 128)
        mixed[:, pl.ds(at, HD)] = product[:rows]
        mixed[:, pl.ds(at + HD, HD)] = product[rows:]
        return carry

    lax.fori_loop(0, heads // 2, two_heads, 0)
    trade_two = GroupTrade(p, mixed, slots.at[1], trade_sems.at[1], slots.shape[3])
    trade_two.start()
    for q in range(4):
        pack_columns(q)
    for i in range(len(chunks)):
        group.finish(i, spans[i])
    give(4, 6)
    trade_two.wait()
    mixed_out[...] = slots[1]
    if lines > 2:
        cot_gather.step(1)
    fetch.wait(2)

    half = width // 2
    spans_two = [pl.ds(0, half), pl.ds(half, half)]
    group_two = GroupSum(p, parts, near, out, far, sum_sems.at[1])
    for i in range(2):
        project(slots.at[1], w_out, i * half, half, 0)
        group_two.give(i, spans_two[i])
    for i in range(2):
        group_two.pass_on(i, spans_two[i])
    give(6, 8)
    for q in range(4, 8):
        pack_columns(q)
    pass_on(0, 6)
    for step in range(2, lines - 1):
        cot_gather.step(step)
    for i in range(2):
        middle_out[:, spans_two[i]] = x_ref[:, spans_two[i]].astype(f32) + group_two.take(
            i, spans_two[i]
        )
    normed_two_out[...] = rms_norm(middle_out[...], gains[1:2]).astype(bf16)

    pass_on(6, 8)
    for i in range(2):
        group_two.finish(i, spans_two[i])
    trade.finish()
    trade_two.finish()
    down.local().wait()
    cot_local.wait()
    for i in range(down.pieces):
        down.finish(i)
    cot_gather.finish()


def front(lines, operands, heads, padded_piece):
    x = operands[1]
    rows, width = x.shape
    places = 2 * lines
    length = places * rows
    inner = heads * HD
    shard = width // 4
    parts_width = inner + 2 * HD
    in_vmem = pl.BlockSpec(memory_space=VMEM)
    anywhere = pl.BlockSpec(memory_space=pl.ANY)
    shape = jax.ShapeDtypeStruct
    pieces = 8 if padded_piece % 128 == 0 else 1
    assert inner == width
    return pl.pallas_call(
        functools.partial(front_kernel, lines),
        out_shape=(
            shape((4, rows, shard), bf16),
            shape((heads, rows, HD), bf16),
            shape((places, rows, 2 * HD), bf16),
            shape((heads, rows, length), bf16),
            shape((4, rows, shard), bf16),
            shape((rows, width), f32),
            shape((rows, width), bf16),
            shape((rows, 128), f32),
            shape((rows, 128), f32),
            shape((shard, 8 * padded_piece), bf16),
            shape((places, rows, width), bf16),
            shape((4, padded_piece, width), bf16),
        ),
        in_specs=[pl.BlockSpec(memory_space=pltpu.SMEM)] + [in_vmem] * 2 + [anywhere] * 6,
        out_specs=[in_vmem] * 10 + [anywhere] * 2,
        scratch_shapes=[
            VMEM((rows, width), bf16),
            VMEM((2, 4, rows, shard), bf16),
            VMEM((4, rows, parts_width), bf16),
            VMEM((2, rows, parts_width), bf16),
            VMEM((rows, parts_width), bf16),
            VMEM((rows, parts_width), bf16),
            VMEM((places, rows, 2 * HD), bf16),
            VMEM((rows, inner), bf16),
            VMEM((rows, length), f32),
            VMEM((padded_piece, width), bf16),
            VMEM((2, shard, (padded_piece + 127) // 128 * 128 + 128), bf16),
            *held(operands[3:6]),
            DMA((3,)),
            DMA((2, GroupTrade.sems, 4)),
            DMA((2, GroupSum.sems, 3)),
            DMA((LineGather.sems, lines)),
            DMA((LineGather.sems, lines)),
            DMA((GroupGather.sems, pieces)),
            DMA((5,)),
        ],
        compiler_params=pltpu.CompilerParams(
            collective_id=0, has_side_effects=True, vmem_limit_bytes=vmem_bytes
        ),
        name="front",
    )(*operands)


def gelu_parts(v):
    k = 0.7978845608028654
    square = v * v
    inner = jnp.tanh(k * v * (1.0 + 0.044715 * square))
    half = 0.5 * (1.0 + inner)
    slope = half + 0.5 * v * (1.0 - inner * inner) * (k * (1.0 + 3 * 0.044715 * square))
    return v * half, slope


def norm_back(values, gain, grad):
    r = lax.rsqrt(jnp.mean(values * values, axis=-1, keepdims=True) + epsilon)
    scaled = values * r
    inner = grad * gain
    grad_values = r * (inner - scaled * jnp.mean(inner * scaled, axis=-1, keepdims=True))
    return grad_values, jnp.sum(grad * scaled, axis=0, keepdims=True)


def middle_kernel(
    lines,
    gains,
    cot_in,
    w_rows_in,
    own,
    middle,
    w_columns,
    grad_middle_out,
    gain_out,
    grads_out,
    down_out,
    normed_all_out,
    result_parts,
    normed_all,
    weights,
    grad_hidden,
    hidden,
    parts,
    side,
    chain,
    down_near,
    down_stage,
    down_far,
    cot_all,
    w_rows,
    fetch_sems,
    gather_sems,
    column_sems,
    sum_sems,
    down_sems,
    own_sems,
):
    p = Place(lines)
    rows, width = own.shape
    two = 2 * rows
    padded = hidden.shape[2]
    shard = width // 4
    tile = 256 if padded % 256 == 0 else 128
    fetch = Fetch(((cot_in, cot_all), (w_rows_in, w_rows)), fetch_sems)
    p.barrier()

    columns = GroupGather(p, w_columns, weights, column_sems, own_sems.at[0], column_sems.shape[1])
    gather = LineGather(p, own, normed_all, gather_sems)
    gather.start()
    for i in range(columns.pieces):
        columns.give(i)
    columns.local().start()
    own_local = pltpu.make_async_copy(own, normed_all.at[p.c], own_sems.at[2 + lines])
    own_local.start()
    middle_local = pltpu.make_async_copy(middle, grad_middle_out, own_sems.at[3 + lines])
    middle_local.start()

    def hidden_grad(line):
        def one(i, carry):
            cols = pl.ds(pl.multiple_of(i * tile, 128), tile)
            left = cot_all[pl.ds(2 * line, 2)].reshape(two, width)
            right = w_rows[pl.ds(pl.multiple_of(i * tile, 16), tile)]
            grad_hidden[line, :, cols] = contract_rows(left, right)
            return carry

        lax.fori_loop(0, padded // tile, one, 0)

    fetch.wait(0, 1)
    done = 0
    for step in range(lines - 1):
        hidden_grad(done)
        done += 1
        gather.step(step)
        if step < columns.pieces:
            columns.pass_on(step)
    for i in range(lines - 1, columns.pieces):
        columns.pass_on(i)
    while done < lines:
        hidden_grad(done)
        done += 1
    gather.finish()
    own_local.wait()
    columns.local().wait()
    for i in range(columns.pieces):
        columns.finish(i)
    normed_local = pltpu.make_async_copy(normed_all, normed_all_out, own_sems.at[1])
    normed_local.start()

    line_sum = LineSum(p, parts, side, chain, sum_sems)

    def feed_forward(line):
        def one(i, carry):
            cols = pl.ds(pl.multiple_of(i * tile, 128), tile)
            up_cols = pl.ds(pl.multiple_of(i * tile + padded, 128), tile)
            left = normed_all[pl.ds(2 * line, 2)].reshape(two, width)
            gate = jnp.dot(
                left, weights[:, :, cols].reshape(width, tile), preferred_element_type=f32
            )
            up = jnp.dot(
                left, weights[:, :, up_cols].reshape(width, tile), preferred_element_type=f32
            )
            gelu, slope = gelu_parts(gate)
            grad = grad_hidden[line, :, cols]
            hidden[line, :, cols] = (gelu * up).astype(bf16)
            grads_out[line, :, cols] = (grad * up * slope).astype(bf16)
            grads_out[line, :, up_cols] = (grad * gelu).astype(bf16)
            return carry

        lax.fori_loop(0, padded // tile, one, 0)

        def back(g, carry):
            product = contract_rows(grads_out[line], weights[g]).astype(bf16)
            cols = pl.ds(pl.multiple_of(g * shard, 128), shard)
            parts[pl.ds(2 * line, 2), :, cols] = product.reshape(2, rows, shard)
            return carry

        lax.fori_loop(0, 4, back, 0)

    result_stage = normed_all

    def result_copy(line):
        blocks = pl.ds(2 * line, 2)
        return pltpu.make_async_copy(
            result_stage.at[blocks], result_parts.at[blocks], own_sems.at[2 + line]
        )

    def result_part(line):
        def one(i, carry):
            cols = pl.ds(pl.multiple_of(i * shard, 128), shard)
            product = jnp.dot(
                hidden[line], w_rows[:, cols], preferred_element_type=f32
            ).astype(bf16)
            result_stage[pl.ds(2 * line, 2), :, cols] = product.reshape(2, rows, shard)
            return carry

        lax.fori_loop(0, 4, one, 0)
        result_copy(line).start()

    quarter = padded // 4
    every = slice(None)
    down_parts = weights.at[:, pl.ds(0, quarter), pl.ds(0, shard)]

    def down_group(i):
        return GroupSum(p, down_parts, down_near.at[i], down_stage.at[i % 2], down_far.at[i], down_sems)

    def down_chunk(i):
        def one(g, carry):
            cols = pl.ds(pl.multiple_of(g * shard, 128), shard)
            left = hidden[:, :, i * quarter : (i + 1) * quarter].reshape(lines * two, quarter)
            right = cot_all[:, :, cols].reshape(lines * two, shard)
            down_parts[g] = contract_tokens(left, right).astype(bf16)
            return carry

        lax.fori_loop(0, 4, one, 0)
        down_out[i] = down_parts[p.f]
        down_group(i).give(i, every)

    for turn in range(lines):
        feed_forward(line_sum.order(turn))
        line_sum.across(turn).start()
        if turn == lines - 2:
            line_sum.near(0, 0)
    normed_local.wait()

    for i in range(4):
        if i >= 1:
            down_group(i - 1).given(i - 1, every)
        if i >= 2:
            down_out[i - 2] = down_group(i - 2).take(i - 2, every, down_out[i - 2]).astype(bf16)
            down_group(i - 2).passed(i - 2, every)
        down_chunk(i)
        down_group(i).pass_on(i, every)
        if i < 2:
            if i + 1 < lines - 1:
                line_sum.near(i + 1, 0)
            line_sum.far(i)
        if i < lines:
            result_part(i)
    for turn in range(2, lines - 1):
        if turn > 2:
            line_sum.near(turn, 0)
        line_sum.far(turn)
    for line in range(4, lines):
        result_part(line)
    line_sum.near(lines - 1, 0)
    line_sum.far(lines - 1)
    grad = line_sum.total()
    middle_local.wait()
    grad_values, gain = norm_back(grad_middle_out[...], gains[1:2], grad)
    grad_middle_out[...] = cot_all[p.c].astype(f32) + grad_values
    gain_out[...] = gain
    for i in (2, 3):
        down_out[i] = down_group(i).take(i, every, down_out[i]).astype(bf16)
        down_group(i).passed(i, every)
    down_group(3).given(3, every)
    for line in range(lines):
        result_copy(line).wait()
    line_sum.finish()


def middle_bytes(lines, rows, width, padded):
    length = 2 * lines * rows
    return (
        14 * rows * width
        + 9 * length * width
        + 9 * padded * width
        + 10 * length * padded
    )


def middle_part(lines, operands, padded):
    own = operands[3]
    rows, width = own.shape
    places = 2 * lines
    shard = width // 4
    quarter = padded // 4
    pieces = 4
    in_vmem = pl.BlockSpec(memory_space=VMEM)
    anywhere = pl.BlockSpec(memory_space=pl.ANY)
    shape = jax.ShapeDtypeStruct
    return pl.pallas_call(
        functools.partial(middle_kernel, lines),
        out_shape=(
            shape((rows, width), f32),
            shape((1, width), f32),
            shape((lines, 2 * rows, 2 * padded), bf16),
            shape((4, quarter, shard), bf16),
            shape((places, rows, width), bf16),
            shape((places, rows, width), bf16),
        ),
        in_specs=[in_vmem] + [anywhere] * 5,
        out_specs=[in_vmem] * 4 + [anywhere] * 2,
        scratch_shapes=[
            VMEM((places, rows, width), bf16),
            VMEM((4, shard, 2 * padded), bf16),
            VMEM((lines, 2 * rows, padded), f32),
            VMEM((lines, 2 * rows, padded), bf16),
            VMEM((places, rows, width), bf16),
            VMEM((lines, rows, width), bf16),
            VMEM((2, lines - 1, rows, width), bf16),
            VMEM((4, 2, quarter, shard), bf16),
            VMEM((2, quarter, shard), bf16),
            VMEM((4, quarter, shard), bf16),
            *held(operands[1:3]),
            DMA((2,)),
            DMA((LineGather.sems, lines)),
            DMA((GroupGather.sems, pieces)),
            DMA((LineSum.sems, lines)),
            DMA((GroupSum.sems, 4)),
            DMA((4 + lines,)),
        ],
        compiler_params=pltpu.CompilerParams(
            collective_id=1, has_side_effects=True, vmem_limit_bytes=vmem_bytes
        ),
        name="middle",
    )(*operands)


def is_long(length):
    return length > 2048


def back_kernel(
    lines,
    with_result,
    grad_middle,
    tokens,
    gains,
    cosine,
    sine,
    w_out_in,
    probs_in,
    keyval_in,
    queries_in,
    mixed_in,
    w_query_in,
    w_keyval_in,
    down_in,
    *rest,
):
    if with_result:
        middle, result_in, result_out, *rest = rest
    (
        input_grad_out,
        gain_out,
        branch_out,
        linear_out,
        out_out,
        down_out,
        branch_all,
        linear_all,
        branch,
        linear,
        trade_parts,
        trade_slots,
        grad_mixed,
        kv_total,
        kv_parts,
        kv_side,
        kv_chain,
        out_parts,
        out_side,
        out_chain,
        w_out,
        probs,
        keyval,
        queries,
        mixed,
        w_query,
        w_keyval,
        fetch_sems,
        branch_sems,
        linear_sems,
        trade_sems,
        kv_sems,
        out_sems,
        piece_sems,
        own_sems,
        *rest,
    ) = rest
    p = Place(lines)
    rows, width = grad_middle.shape
    heads = queries.shape[0]
    length = probs_in.shape[2]
    long = is_long(length)
    operands = [
        (w_out_in, w_out),
        (keyval_in, keyval),
        (queries_in, queries),
        (mixed_in, mixed),
        (w_query_in, w_query),
        (w_keyval_in, w_keyval),
    ]
    fetch = Fetch(operands if long else operands + [(probs_in, probs)], fetch_sems)
    shard = w_out.shape[0]
    kv_width = 2 * HD
    per_owner = 2 * lines // 4
    tall = shard // per_owner
    others = [(jnp.full((), True), {"ctx": (p.c + d) % (2 * lines)}) for d in range(1, 2 * lines)]
    p.barrier(ctx=False, also=others)
    if with_result:
        result_parts, result_side, result_chain, result_sems = rest
        result_sum = LineSum(p, result_parts, result_side, result_chain, result_sems)
        result_copy = pltpu.make_async_copy(result_in, result_parts, own_sems.at[2])
        result_copy.start()

    branch[...] = grad_middle[...].astype(bf16)
    group = GroupGather(p, branch, branch_all, branch_sems, own_sems.at[0], 1)
    group.give(0)
    group.local().start()
    down_move = PieceMove(p, per_owner, down_in, down_out, piece_sems)
    down_move.start()
    out_sum = LineSum(p, out_parts, out_side, out_chain, out_sems)
    if with_result:
        result_copy.wait()
        result_sum.start(2)
    back_trade = GroupReturn(p, trade_parts.at[0], trade_slots.at[0], trade_sems.at[0])

    def mixed_back(g):
        trade_parts[0, g] = contract_rows(branch_all[g], w_out[...]).astype(bf16)

    group.local().wait()
    fetch.wait(0)
    mixed_back(p.f)
    back_trade.own().start()
    group.near(0)
    mixed_back(p.twin_f)
    group.pass_on(0)
    mixed_back(p.cross_f)
    back_trade.send(2)
    group.last(0)
    mixed_back(p.diag_f)
    back_trade.send(1)
    back_trade.send(3)
    branch_copy = pltpu.make_async_copy(branch_all, branch_out, own_sems.at[3])
    branch_copy.start()

    def out_blocks(g, carry):
        left = mixed[...].reshape(4 * rows, shard)
        right = branch_all[:, :, pl.ds(pl.multiple_of(g * shard, 128), shard)]
        product = contract_tokens(left, right.reshape(4 * rows, shard))
        for r in range(per_owner):
            out_parts[4 * r + g] = product[r * tall : (r + 1) * tall].astype(bf16)
        return carry

    fetch.wait(3)
    lax.fori_loop(0, 4, out_blocks, 0)
    if with_result:
        result_sum.near(0, 0)
    back_trade.wait()
    for g in range(4):
        grad_mixed[:, g * shard : (g + 1) * shard] = trade_slots[0, g]

    kv_total[...] = jnp.zeros_like(kv_total)
    kv_at, q_at = pl.ds(0, kv_width), pl.ds(kv_width, heads * HD)

    batch = 1 if long else 2
    fetch.wait(1, 2)
    if not long:
        fetch.wait(6)

    def some_heads(i, carry):
        keys = keyval[:, :, :HD].reshape(length, HD)
        values = keyval[:, :, HD:].reshape(length, HD)
        at = [pl.multiple_of((i * batch + h) * HD, 128) for h in range(batch)]
        outer = jnp.concatenate([grad_mixed[:, pl.ds(a, HD)] for a in at], axis=0)
        if batch == 1:
            one = pltpu.make_async_copy(probs_in.at[i], probs, own_sems.at[5])
            one.start()
            one.wait()
            weights = probs[...]
        else:
            weights = probs[pl.ds(batch * i, batch)].reshape(batch * rows, length)
        wide = weights.astype(f32)
        grad_weights = contract_rows(outer, values)
        delta = jnp.sum(wide * grad_weights, axis=-1, keepdims=True)
        grad_scores = (wide * (grad_weights - delta)).astype(bf16)
        product = jnp.dot(grad_scores, keys, preferred_element_type=f32) * HD**-0.5
        for h in range(batch):
            turned = rotated(product[h * rows : (h + 1) * rows], cosine[...], -sine[...])
            linear[:, pl.ds(kv_width + at[h], HD)] = turned.astype(bf16)
        two = queries[pl.ds(batch * i, batch)].reshape(batch * rows, HD)
        kv_total[:, :HD] += contract_tokens(grad_scores, two)
        kv_total[:, HD:] += contract_tokens(weights, outer)
        return carry

    lax.fori_loop(0, heads // batch, some_heads, 0)
    linear_group = GroupGather(
        p, linear, linear_all, linear_sems, own_sems.at[1], 2, (q_at, kv_at)
    )
    linear_group.give(0)
    kv_parts[...] = kv_total[...].astype(bf16).reshape(kv_parts.shape)
    kv_sum = LineSum(p, kv_parts, kv_side, kv_chain, kv_sems)
    kv_sum.start(lines)
    kv_sum.turns(0)
    own = kv_sum.total()
    linear[:, :HD] = rotated(own[:, :HD], cosine[...], -sine[...]).astype(bf16)
    linear[:, pl.ds(HD, HD)] = own[:, HD:].astype(bf16)
    linear_group.give(1)
    linear_group.local().start()
    if with_result:
        for turn in range(2, lines):
            result_sum.across(turn).start()
        result_sum.near(1, 0)
        result_sum.far(0)
    out_sum.start(lines)
    fetch.wait(4, 5)
    linear_group.pass_on(0)
    linear_group.pass_on(1)
    linear_group.local().wait()
    for i in range(2):
        linear_group.near(i)
        linear_group.last(i)

    linear_copy = pltpu.make_async_copy(linear_all, linear_out, own_sems.at[4])
    linear_copy.start()

    last_trade = GroupReturn(p, trade_parts.at[1], trade_slots.at[1], trade_sems.at[1])

    def normed_back(g):
        product = contract_rows(linear_all[g, :, kv_at], w_keyval[...])
        product += contract_rows(linear_all[g, :, q_at], w_query[...])
        trade_parts[1, g] = product.astype(bf16)

    normed_back(p.cross_f)
    last_trade.send(2)
    normed_back(p.diag_f)
    normed_back(p.twin_f)
    last_trade.send(1)
    last_trade.send(3)
    normed_back(p.f)
    last_trade.own().start()
    last_trade.wait()
    for g in range(4):
        grad_mixed[:, g * shard : (g + 1) * shard] = trade_slots[1, g]
    source = tokens[...].astype(f32)
    grad_values, gain = norm_back(source, gains[0:1], grad_mixed[...].astype(f32))
    input_grad_out[...] = (grad_middle[...] + grad_values).astype(bf16)
    gain_out[...] = gain
    if with_result:
        result_sum.far(1)
        for turn in range(2, lines):
            result_sum.near(turn, 0)
            result_sum.far(turn)
    out_sum.turns(0)
    out_out[...] = out_sum.total().astype(bf16)
    if with_result:
        result_out[...] = (middle[...] + result_sum.total()).astype(bf16)
        result_sum.finish()
    back_trade.finish()
    last_trade.finish()
    group.sent(0)
    linear_group.sent(0)
    linear_group.sent(1)
    kv_sum.finish()
    branch_copy.wait()
    linear_copy.wait()
    out_sum.finish()
    down_move.finish()


def back(lines, operands, result_operands):
    rows, width = operands[0].shape
    heads = operands[8].shape[0]
    places = 2 * lines
    length = places * rows
    shard = width // 4
    linear_width = width + 2 * HD
    tall = width // places
    pieces = operands[12].shape
    in_vmem = pl.BlockSpec(memory_space=VMEM)
    anywhere = pl.BlockSpec(memory_space=pl.ANY)
    shape = jax.ShapeDtypeStruct
    with_result = bool(result_operands)
    long = is_long(length)
    scratch = held(operands[5:12])
    if long:
        scratch[1] = VMEM((rows, length), bf16)
    result_scratch = [
        VMEM((places, rows, width), bf16),
        VMEM((lines, rows, width), bf16),
        VMEM((2, lines - 1, rows, width), bf16),
        DMA((LineSum.sems, lines)),
    ]
    return pl.pallas_call(
        functools.partial(back_kernel, lines, with_result),
        out_shape=((shape((rows, width), bf16),) if with_result else ())
        + (
            shape((rows, width), bf16),
            shape((1, width), f32),
            shape((4, rows, width), bf16),
            shape((4, rows, linear_width), bf16),
            shape((tall, shard), bf16),
            shape(pieces, bf16),
        ),
        in_specs=[in_vmem] * 5 + [anywhere] * 8 + ([in_vmem, anywhere] if with_result else []),
        out_specs=[in_vmem] * (3 if with_result else 2) + [anywhere] * 2 + [in_vmem, anywhere],
        scratch_shapes=[
            VMEM((4, rows, width), bf16),
            VMEM((4, rows, linear_width), bf16),
            VMEM((rows, width), bf16),
            VMEM((rows, linear_width), bf16),
            VMEM((2, 4, rows, shard), bf16),
            VMEM((2, 4, rows, shard), bf16),
            VMEM((rows, width), bf16),
            VMEM((length, 2 * HD), f32),
            VMEM((places, rows, 2 * HD), bf16),
            VMEM((lines, rows, 2 * HD), bf16),
            VMEM((2, lines - 1, rows, 2 * HD), bf16),
            VMEM((places, tall, shard), bf16),
            VMEM((lines, tall, shard), bf16),
            VMEM((2, lines - 1, tall, shard), bf16),
            *scratch,
            DMA((7,)),
            DMA((GroupGather.sems, 1)),
            DMA((GroupGather.sems, 2)),
            DMA((2, GroupTrade.sems, 4)),
            DMA((LineSum.sems, lines)),
            DMA((LineSum.sems, lines)),
            DMA((3, 4)),
            DMA((6,)),
        ]
        + (result_scratch if with_result else []),
        compiler_params=pltpu.CompilerParams(
            collective_id=2, has_side_effects=True, vmem_limit_bytes=vmem_bytes
        ),
        name="back",
    )(*operands, *result_operands)


def grads_kernel(lines, with_columns, gain_one, gain_two, out_in, normed_in, linear_in, *rest):
    if with_columns:
        normed_two_in, hidden_grads_in, *rest = rest
    projection_out, gains_out, out_out, *rest = rest
    if with_columns:
        columns_out, *rest = rest
    (
        parts,
        side,
        chain,
        stage,
        gain_parts,
        gain_side,
        gain_chain,
        gain_slots,
        normed,
        linear_all,
        fetch_sems,
        projection_sems,
        gain_sems,
        slot_sems,
        move_sems,
        out_move_sems,
        *rest,
    ) = rest
    if with_columns:
        chunk_parts, near, passing, far, chunks, group_sems, trade_sems, normed_two, hidden_grads = rest
    operands = [(normed_in, normed), (linear_in, linear_all)]
    if with_columns:
        operands += [(normed_two_in, normed_two), (hidden_grads_in, hidden_grads)]
    fetch = Fetch(operands, fetch_sems)
    p = Place(lines)
    places = 2 * lines
    shard = normed.shape[2]
    tokens = 4 * normed.shape[1]
    per_owner = places // 4
    tall = shard // per_owner
    kv_share = 2 * HD // 4
    move = BlockMove(p, per_owner, stage, projection_out, move_sems)
    others = [(jnp.full((), True), {"ctx": (p.c + d) % places}) for d in range(1, places)]
    p.barrier(ctx=False, also=others + move.greets())
    out_move = BlockMove(p, per_owner, out_in, out_out, out_move_sems)
    out_move.start()

    for c in range(places):
        cols = slice(c * tall, (c + 1) * tall)
        gain_parts[c, 0:1, :tall] = gain_one[:, cols]
        gain_parts[c, 1:2, :tall] = gain_two[:, cols]
    gain_sum = LineSum(p, gain_parts, gain_side, gain_chain, gain_sems)
    gain_sum.start(lines)

    projection_sum = LineSum(p, parts, side, chain, projection_sems)

    def projection_blocks(g, carry):
        left = normed[...].reshape(tokens, shard)
        right = linear_all[:, :, pl.ds(pl.multiple_of(2 * HD + g * shard, 128), shard)]
        product = contract_tokens(left, right.reshape(tokens, shard))
        right = linear_all[:, :, pl.ds(pl.multiple_of(g * kv_share, 128), kv_share)]
        kv_product = contract_tokens(left, right.reshape(tokens, kv_share))
        for r in range(per_owner):
            rows = slice(r * tall, (r + 1) * tall)
            parts[4 * r + g, :, :shard] = product[rows].astype(bf16)
            parts[4 * r + g, :, shard:] = kv_product[rows].astype(bf16)
        return carry

    def start_projections():
        fetch.wait(0, 1)
        lax.fori_loop(0, 4, projection_blocks, 0)
        projection_sum.start(2)

    if not with_columns:
        start_projections()

    if with_columns:
        fetch.wait(2, 3)
        block = columns_out.shape[2]
        chunk = chunk_parts.shape[1]
        every = slice(None)

        def chunk_of(k):
            return (p.line + (k + 1) % lines) % lines

        def group(k):
            return GroupSum(p, chunk_parts, near.at[k], passing.at[k % 2], far.at[k], group_sems)

        def compute(k):
            cols = pl.ds(pl.multiple_of(chunk_of(k) * chunk, 128), chunk)

            def one(g, carry):
                left = normed_two[:, :, cols].reshape(-1, chunk)
                right = hidden_grads[:, :, pl.ds(pl.multiple_of(g * block, 128), block)]
                chunk_parts[g] = contract_tokens(left, right.reshape(-1, block)).astype(bf16)
                return carry

            lax.fori_loop(0, 4, one, 0)
            chunks[k] = chunk_parts[p.f]
            group(k).give(k, every)

        def halves(k):
            half = chunk // 2
            for lane in range(2):
                yield lane, 2 * chunk_of(k) + lane, chunks.at[k, pl.ds(lane * half, half)]

        def place_copy(k, lane, dest, src):
            return remote(
                src,
                columns_out.at[p.c],
                trade_sems.at[0, 2 * k + lane],
                trade_sems.at[1, p.c],
                {"ctx": dest},
            )

        def place_own(src):
            return pltpu.make_async_copy(src, columns_out.at[p.c], trade_sems.at[2, 0])

        def arrival(i):
            slot = columns_out.at[i]
            return remote(slot, slot, trade_sems.at[0, 0], trade_sems.at[1, i], p.beside)

        def complete(k):
            chunks[k] = group(k).take(k, every, chunks[k]).astype(bf16)
            for lane, dest, src in halves(k):
                pl.when(dest != p.c)(
                    lambda k=k, lane=lane, dest=dest, src=src: place_copy(k, lane, dest, src).start()
                )
                pl.when(dest == p.c)(lambda src=src: place_own(src).start())

        for k in range(lines):
            if k >= 1:
                group(k - 1).given(k - 1, every)
            compute(k)
            if k >= 2:
                group(k - 2).passed(k - 2, every)
            group(k).pass_on(k, every)
            if k == 0:
                start_projections()
                gain_sum.turns(0)
            if k >= 1:
                complete(k - 1)
                projection_sum.near(k - 1, 2)
            if k >= 2:
                projection_sum.far(k - 2)
        complete(lines - 1)
        for k in (lines - 2, lines - 1):
            group(k).passed(k, every)
        group(lines - 1).given(lines - 1, every)
        projection_sum.near(lines - 1, 2)
        projection_sum.far(lines - 2)
        projection_sum.far(lines - 1)
    else:
        gain_sum.turns(0)
        projection_sum.turns(2)

    own = gain_sum.total()
    gain_parts[p.c] = own

    def gain_copy(d):
        return remote(
            gain_parts.at[p.c],
            gain_slots.at[d],
            slot_sems.at[0, d],
            slot_sems.at[1, d],
            {"fsdp": (p.f + d) % 4},
        )

    for d in (1, 2, 3):
        gain_copy(d).start()
    stage[...] = projection_sum.total().astype(bf16)
    move.start()
    for d in (1, 2, 3):
        gain_copy(d).wait_recv()
        own = own + gain_slots[d]
    gains_out[...] = own

    for d in (1, 2, 3):
        gain_copy(d).wait_send()
    if with_columns:
        for k in range(lines):
            for lane, dest, src in halves(k):
                pl.when(dest != p.c)(
                    lambda k=k, lane=lane, dest=dest, src=src: place_copy(k, lane, dest, src).wait_send()
                )
                pl.when(dest == p.c)(lambda src=src: place_own(src).wait())
        for i in range(places):
            pl.when(p.c != i)(lambda i=i: arrival(i).wait_recv())
    gain_sum.finish()
    projection_sum.finish()
    out_move.finish()
    move.finish()


def weight_grads(lines, operands, column_operands):
    rows, shard = operands[3].shape[1:]
    width = 4 * shard
    places = 2 * lines
    tall = width // places
    wide = shard + 2 * HD // 4
    gain_wide = -(-tall // 128) * 128
    in_vmem = pl.BlockSpec(memory_space=VMEM)
    anywhere = pl.BlockSpec(memory_space=pl.ANY)
    shape = jax.ShapeDtypeStruct
    with_columns = bool(column_operands)
    column_shapes, column_scratch = (), []
    if with_columns:
        block = column_operands[1].shape[2] // 4
        chunk = width // lines
        column_shapes = (shape((places, chunk // 2, block), bf16),)
        column_scratch = [
            VMEM((4, chunk, block), bf16),
            VMEM((lines, 2, chunk, block), bf16),
            VMEM((2, chunk, block), bf16),
            VMEM((lines, chunk, block), bf16),
            VMEM((lines, chunk, block), bf16),
            DMA((GroupSum.sems, lines)),
            DMA((3, places)),
            *held(column_operands),
        ]
    return pl.pallas_call(
        functools.partial(grads_kernel, lines, with_columns),
        out_shape=(shape((tall, wide), bf16), shape((8, gain_wide), f32), shape((tall, shard), bf16)) + column_shapes,
        in_specs=[in_vmem] * 2 + [anywhere] * (3 + len(column_operands)),
        out_specs=[anywhere, in_vmem, anywhere] + [anywhere] * len(column_shapes),
        scratch_shapes=[
            VMEM((places, tall, wide), bf16),
            VMEM((lines, tall, wide), bf16),
            VMEM((2, lines - 1, tall, wide), bf16),
            VMEM((tall, wide), bf16),
            VMEM((places, 8, gain_wide), f32),
            VMEM((lines, 8, gain_wide), f32),
            VMEM((2, lines - 1, 8, gain_wide), f32),
            VMEM((4, 8, gain_wide), f32),
            *held(operands[3:5]),
            DMA((4,)),
            DMA((LineSum.sems, lines)),
            DMA((LineSum.sems, lines)),
            DMA((2, 4)),
            DMA((3,)),
            DMA((3,)),
        ]
        + column_scratch,
        compiler_params=pltpu.CompilerParams(
            collective_id=3, has_side_effects=True, vmem_limit_bytes=vmem_bytes
        ),
        name="grads",
    )(*operands, *column_operands)


def assemble_kernel(lines, piece, projection, out, down, columns, *outs):
    query_out, keyval_out, out_out, down_out, columns_out = outs
    shard = out.shape[1]
    padded_piece = columns.shape[2] // 2
    query_out[...] = projection[:, :shard].astype(f32)
    keyval_out[...] = projection[:, shard:].astype(f32)
    out_out[...] = out[...].astype(f32)
    for i in range(down.shape[0]):
        down_out[i * piece : (i + 1) * piece] = down[i, :piece].astype(f32)
    pieces = [
        columns[place_of_piece(n, lines), :, q * padded_piece : q * padded_piece + piece]
        for q in range(2)
        for n in range(2 * lines)
    ]
    columns_out[...] = jnp.concatenate(pieces, axis=1).astype(f32)


def assemble(lines, piece, projection, out, down, columns):
    tall, wide = projection.shape
    shard = out.shape[1]
    places = 2 * lines
    block = columns.shape[2]
    steps = 4 if tall % 64 == 0 else 1
    run = tall // steps
    full = 2 * places * piece

    def flat(rows, cols):
        return pl.BlockSpec((rows, cols), lambda i: (i, 0))

    shape = jax.ShapeDtypeStruct
    return pl.pallas_call(
        functools.partial(assemble_kernel, lines, piece),
        grid=(steps,),
        out_shape=(
            shape((tall, shard), f32),
            shape((tall, wide - shard), f32),
            shape((tall, shard), f32),
            shape((4 * piece, shard), f32),
            shape((tall, full), f32),
        ),
        in_specs=[
            flat(run, wide),
            flat(run, shard),
            pl.BlockSpec((4 // steps, down.shape[1], shard), lambda i: (i, 0, 0)),
            pl.BlockSpec((places, run, block), lambda i: (0, i, 0)),
        ],
        out_specs=[
            flat(run, shard),
            flat(run, wide - shard),
            flat(run, shard),
            flat(4 // steps * piece, shard),
            flat(run, full),
        ],
        compiler_params=pltpu.CompilerParams(vmem_limit_bytes=vmem_bytes),
        name="assemble",
    )(projection, out, down, columns)


def per_device(
    tokens,
    doc_bounds,
    cotangent,
    norm_one,
    query_weight,
    keyval_weight,
    out_weight,
    norm_two,
    gate_up_weight,
    down_weight,
):
    ctx_size = lax.axis_size("ctx")
    fsdp_size = lax.axis_size("fsdp")
    lines = ctx_size // 2
    rows = tokens.shape[1]
    width = tokens.shape[2]
    length = rows * ctx_size
    inner_width = query_weight.shape[1]
    head_count = inner_width // HD
    hidden_width = gate_up_weight.shape[1] // 2
    piece = hidden_width // (ctx_size * fsdp_size)
    padded_piece = -(-piece // 32) * 32
    padded = padded_piece * fsdp_size
    gains = jnp.stack([norm_one, norm_two])
    cot_rows = cotangent[0]
    down_rows = down_weight
    if piece % 16:
        first = hidden_piece(lax.axis_index("ctx"), lines) * piece
        down_rows = lax.dynamic_slice_in_dim(down_weight, first, piece, 0)
        down_rows = jnp.pad(down_rows, ((0, padded_piece - piece), (0, 0)))
    (
        normed,
        queries,
        window,
        weights,
        mixed,
        middle,
        normed_two,
        cosine,
        sine,
        w_columns,
        cot_all,
        w_down,
    ) = front(
        lines,
        (
            doc_bounds,
            tokens[0],
            gains,
            keyval_weight,
            query_weight,
            out_weight,
            cot_rows,
            down_rows,
            gate_up_weight,
        ),
        head_count,
        padded_piece,
    )
    w_down = w_down.reshape(padded, width)
    fits = middle_bytes(lines, rows, width, padded) <= vmem_bytes
    if fits:
        grad_middle, gain_two_term, grad_gate_up, down_part, normed_two, result_parts = middle_part(
            lines, (gains, cot_all, w_down, normed_two, middle, w_columns), padded
        )
    else:
        cot_all = cot_all.reshape(length, width)
        normed_two = lax.all_gather(normed_two, "ctx", axis=0, tiled=True)
        w_gate_up = lax.all_gather(w_columns, "fsdp", axis=0, tiled=True)
        projected = jnp.dot(normed_two, w_gate_up, preferred_element_type=f32)
        gelu, slope = gelu_parts(projected[:, :padded])
        up_part = projected[:, padded:]
        hidden = (gelu * up_part).astype(bf16)
        grad_hidden = contract_rows(cot_all, w_down)
        grad_gate_up = jnp.concatenate(
            [grad_hidden * up_part * slope, grad_hidden * gelu], axis=1
        ).astype(bf16)
        grad_normed_two = lax.psum_scatter(
            contract_rows(grad_gate_up, w_gate_up).astype(bf16),
            "ctx",
            scatter_dimension=0,
            tiled=True,
        ).astype(f32)
        grad_middle_norm, gain_two_term = norm_back(middle, norm_two[None], grad_normed_two)
        grad_middle = cot_rows.astype(f32) + grad_middle_norm
        result_parts = jnp.dot(hidden, w_down, preferred_element_type=f32).astype(bf16)
        down_part = lax.psum_scatter(
            contract_tokens(hidden, cot_all).astype(bf16),
            "fsdp",
            scatter_dimension=1,
            tiled=True,
        ).reshape(fsdp_size, padded_piece, -1)
    operands = (
        grad_middle,
        tokens[0],
        gains,
        cosine,
        sine,
        out_weight,
        weights,
        window,
        queries,
        mixed,
        query_weight,
        keyval_weight,
        down_part,
    )
    if fits:
        result, input_grad, gain_one_term, _, grad_linear, out_grad, down_grad = back(
            lines, operands, (middle, result_parts.reshape(ctx_size, rows, width))
        )
    else:
        input_grad, gain_one_term, _, grad_linear, out_grad, down_grad = back(lines, operands, ())
        branch_two = lax.psum_scatter(result_parts, "ctx", scatter_dimension=0, tiled=True)
        result = (middle + branch_two.astype(f32)).astype(bf16)

    operands = (gain_one_term, gain_two_term, out_grad, normed, grad_linear)
    if fits:
        projection_grad, gain_grads, out_grad, gate_up_part = weight_grads(
            lines, operands, (normed_two, grad_gate_up)
        )
    else:
        projection_grad, gain_grads, out_grad = weight_grads(lines, operands, ())
        gate_up_part = lax.psum_scatter(
            contract_tokens(normed_two, grad_gate_up).astype(bf16),
            "fsdp",
            scatter_dimension=1,
            tiled=True,
        )
        gate_up_part = lax.all_to_all(
            gate_up_part.reshape(ctx_size, width // ctx_size, -1), "ctx", 0, 0, tiled=True
        )
    query_grad, keyval_grad, out_grad, down_grad, gate_up_grad = assemble(
        lines, piece, projection_grad, out_grad, down_grad, gate_up_part
    )
    share = width // (ctx_size * fsdp_size)
    gains = lax.dynamic_slice_in_dim(gain_grads, lax.axis_index("fsdp") * share, share, 1)
    return (
        result[None],
        input_grad[None],
        gains[0],
        query_grad,
        keyval_grad,
        out_grad,
        gains[1],
        gate_up_grad,
        down_grad,
    )


def solution(mesh):
    placed = (
        P("fsdp", "ctx", None),
        P("fsdp", None),
        P("fsdp", "ctx", None),
        P(),
        P("fsdp", None),
        P("fsdp", None),
        P("fsdp", None),
        P(),
        P("fsdp", None),
        P("fsdp", None),
    )
    return jax.shard_map(
        per_device,
        mesh=mesh,
        in_specs=placed,
        out_specs=(
            P("fsdp", "ctx", None),
            P("fsdp", "ctx", None),
            P(("ctx", "fsdp")),
            P("ctx", "fsdp"),
            P("ctx", "fsdp"),
            P("ctx", "fsdp"),
            P(("ctx", "fsdp")),
            P("ctx", "fsdp"),
            P("ctx", "fsdp"),
        ),
        check_vma=False,
    )
```

```python
import functools
import math

import jax
import jax.numpy as jnp
from jax import lax
from jax.experimental import pallas as pl
from jax.experimental.pallas import tpu as pltpu
from jax.sharding import PartitionSpec as P

HD = 256
WINDOW = 2048


epsilon = 1e-06
f32 = jnp.float32
bf16 = jnp.bfloat16
VMEM = pltpu.VMEM
DMA = pltpu.SemaphoreType.DMA
vmem_bytes = 62 * 1024 * 1024


def rms_norm(values, gain):
    return values * lax.rsqrt(jnp.mean(values * values, axis=-1, keepdims=True) + epsilon) * gain


def documents(index, bounds):
    return (index >= bounds[0]).astype(jnp.int32) + (index >= bounds[1]).astype(jnp.int32)


def contract_rows(left, right):
    return lax.dot_general(
        left, right, (((1,), (1,)), ((), ())), preferred_element_type=jnp.float32
    )


def contract_tokens(left, right):
    return lax.dot_general(
        left, right, (((0,), (0,)), ((), ())), preferred_element_type=jnp.float32
    )


def remote(src, dst, send_sem, recv_sem, device):
    return pltpu.make_async_remote_copy(
        src_ref=src,
        dst_ref=dst,
        send_sem=send_sem,
        recv_sem=recv_sem,
        device_id=device,
        device_id_type=pl.DeviceIdType.MESH,
    )


class Place:
    def __init__(self, lines):
        self.lines = lines
        self.c = lax.axis_index("ctx")
        self.f = lax.axis_index("fsdp")
        self.line = self.c // 2
        self.lane = self.c % 2
        self.chip = self.f // 2
        self.core = self.f % 2
        self.twin_f = self.f + 1 - 2 * self.core
        self.cross_f = (self.f + 2) % 4
        self.diag_f = (self.twin_f + 2) % 4
        self.twin = {"fsdp": self.twin_f}
        self.cross = {"fsdp": self.cross_f}
        self.diag = {"fsdp": self.diag_f}
        self.beside = {"ctx": self.c + 1 - 2 * self.lane}
        self.right = {"ctx": self.c + 2}
        self.left = {"ctx": self.c - 2}
        self.has_right = self.line < lines - 1
        self.has_left = self.line > 0

    def barrier(self, ctx=True, fsdp=True, also=()):
        sem = pltpu.get_barrier_semaphore()

        def greet(device):
            pl.semaphore_signal(sem, 1, device_id=device, device_id_type=pl.DeviceIdType.MESH)

        count = 0
        if fsdp:
            for device in (self.twin, self.cross, self.diag):
                greet(device)
            count = 3
        if ctx:
            greet(self.beside)
            pl.when(self.has_right)(lambda: greet(self.right))
            pl.when(self.has_left)(lambda: greet(self.left))
            count = (
                count + 1 + self.has_right.astype(jnp.int32) + self.has_left.astype(jnp.int32)
            )
        for needed, device in also:
            pl.when(needed)(lambda device=device: greet(device))
            count = count + needed.astype(jnp.int32)
        pl.semaphore_wait(sem, count)


class Fetch:
    def __init__(self, pairs, sems):
        self.copies = [
            pltpu.make_async_copy(src, dst, sems.at[i]) for i, (src, dst) in enumerate(pairs)
        ]
        for copy in self.copies:
            copy.start()

    def wait(self, *which):
        for i in which:
            self.copies[i].wait()


def held(operands):
    return [VMEM(operand.shape, operand.dtype) for operand in operands]


class LineGather:
    sems = 6

    def __init__(self, place, own, slots, sems):
        self.p, self.own, self.slots, self.s = place, own, slots, sems

    def rightward(self, step):
        at = 2 * (self.p.line - step) + self.p.lane
        src = self.own if step == 0 else self.slots.at[at]
        return remote(src, self.slots.at[at], self.s.at[0, step], self.s.at[1, step], self.p.right)

    def leftward(self, step):
        at = 2 * (self.p.line + step) + self.p.lane
        src = self.own if step == 0 else self.slots.at[at]
        return remote(src, self.slots.at[at], self.s.at[2, step], self.s.at[3, step], self.p.left)

    def across(self, line, own=False):
        at = 2 * line + self.p.lane
        src = self.own if own else self.slots.at[at]
        return remote(
            src, self.slots.at[at], self.s.at[4, line], self.s.at[5, line], self.p.beside
        )

    def from_left(self, step):
        at = 2 * (self.p.line - 1 - step) + self.p.lane
        slot = self.slots.at[at]
        return remote(slot, slot, self.s.at[0, step], self.s.at[1, step], self.p.right)

    def from_right(self, step):
        at = 2 * (self.p.line + 1 + step) + self.p.lane
        slot = self.slots.at[at]
        return remote(slot, slot, self.s.at[2, step], self.s.at[3, step], self.p.left)

    def start(self):
        pl.when(self.p.has_right)(lambda: self.rightward(0).start())
        pl.when(self.p.has_left)(lambda: self.leftward(0).start())
        self.across(self.p.line, True).start()

    def step(self, step):
        p = self.p

        @pl.when(p.line - 1 - step >= 0)
        def _():
            self.from_left(step).wait_recv()
            if step + 1 < p.lines - 1:
                pl.when(p.has_right)(lambda: self.rightward(step + 1).start())
            self.across(p.line - 1 - step).start()

        @pl.when(p.line + 1 + step <= p.lines - 1)
        def _():
            self.from_right(step).wait_recv()
            if step + 1 < p.lines - 1:
                pl.when(p.has_left)(lambda: self.leftward(step + 1).start())
            self.across(p.line + 1 + step).start()

    def steps(self):
        for step in range(self.p.lines - 1):
            self.step(step)

    def arrived_across(self, line):
        at = 2 * line + 1 - self.p.lane
        slot = self.slots.at[at]
        remote(slot, slot, self.s.at[4, line], self.s.at[5, line], self.p.beside).wait_recv()

    def finish(self, arrivals=True):
        p = self.p
        if arrivals:
            for line in range(p.lines):
                self.arrived_across(line)
        for step in range(p.lines - 1):
            pl.when(p.has_right & (p.line - step >= 0))(
                lambda step=step: self.rightward(step).wait_send()
            )
            pl.when(p.has_left & (p.line + step <= p.lines - 1))(
                lambda step=step: self.leftward(step).wait_send()
            )
        for line in range(p.lines):
            self.across(line).wait_send()


class LineSum:
    sems = 6

    def __init__(self, place, parts, side, chain, sems):
        self.p, self.parts, self.side, self.chain, self.s = place, parts, side, chain, sems

    def order(self, turn):
        lines, line = self.p.lines, self.p.line
        value = 0
        for a in range(lines):
            far = sorted(range(lines), key=lambda t: (-abs(t - a), t))
            value = value + jnp.where(line == a, far[turn], 0)
        return value

    def across(self, turn):
        t = self.order(turn)
        at = 2 * t + 1 - self.p.lane
        return remote(
            self.parts.at[at],
            self.side.at[t],
            self.s.at[0, t],
            self.s.at[1, t],
            self.p.beside,
        )

    def rightward(self, t):
        step = self.p.lines - 1 - t
        return remote(
            self.parts.at[2 * t + self.p.lane],
            self.chain.at[0, step],
            self.s.at[2, step],
            self.s.at[3, step],
            self.p.right,
        )

    def leftward(self, t):
        return remote(
            self.parts.at[2 * t + self.p.lane],
            self.chain.at[1, t],
            self.s.at[4, t],
            self.s.at[5, t],
            self.p.left,
        )

    def add(self, at, other):
        self.parts[at] = (self.parts[at].astype(f32) + other.astype(f32)).astype(self.parts.dtype)

    def start(self, ahead=2):
        for turn in range(min(ahead, self.p.lines)):
            self.across(turn).start()

    def near(self, turn, ahead=2):
        p = self.p
        t = self.order(turn)
        at = 2 * t + p.lane
        self.across(turn).wait_recv()
        if ahead and turn + ahead < p.lines:
            self.across(turn + ahead).start()
        self.add(at, self.side[t])
        pl.when((t > p.line) & (p.line == 0))(lambda: self.rightward(t).start())
        pl.when((t < p.line) & (p.line == p.lines - 1))(lambda: self.leftward(t).start())

    def far(self, turn):
        p = self.p
        t = self.order(turn)
        at = 2 * t + p.lane

        @pl.when((t > p.line) & p.has_left)
        def _():
            self.rightward(t).wait_recv()
            self.add(at, self.chain[0, p.lines - 1 - t])
            self.rightward(t).start()

        @pl.when((t < p.line) & p.has_right)
        def _():
            self.leftward(t).wait_recv()
            self.add(at, self.chain[1, t])
            self.leftward(t).start()

    def turns(self, ahead=2):
        for turn in range(self.p.lines):
            self.near(turn, ahead)
            if turn > 0:
                self.far(turn - 1)
        self.far(self.p.lines - 1)

    def total(self):
        p = self.p
        at = 2 * p.line + p.lane

        @pl.when(p.has_left)
        def _():
            self.rightward(p.line).wait_recv()
            self.add(at, self.chain[0, p.lines - 1 - p.line])

        @pl.when(p.has_right)
        def _():
            self.leftward(p.line).wait_recv()
            self.add(at, self.chain[1, p.line])

        return self.parts[at].astype(f32)

    def finish(self):
        p = self.p
        for turn in range(p.lines):
            self.across(turn).wait_send()
        for t in range(p.lines):
            pl.when(t > p.line)(lambda t=t: self.rightward(t).wait_send())
            pl.when(t < p.line)(lambda t=t: self.leftward(t).wait_send())


class Turns:
    def __init__(self, line_sum, ahead=2):
        self.sum, self.ahead, self.nears, self.fars = line_sum, ahead, 0, 0

    def start(self):
        self.sum.start(self.ahead)

    def near(self, upto):
        while self.nears < min(upto, self.sum.p.lines):
            self.sum.near(self.nears, self.ahead)
            self.nears += 1

    def far(self, upto):
        while self.fars < min(upto, self.sum.p.lines):
            self.near(self.fars + 1)
            self.sum.far(self.fars)
            self.fars += 1

    def total(self):
        self.far(self.sum.p.lines)
        return self.sum.total()


class GroupSum:
    sems = 6

    def __init__(self, place, parts, near, out, far, sems):
        self.p, self.parts, self.near, self.out, self.far, self.s = place, parts, near, out, far, sems

    def to_twin(self, i, which, cols):
        p = self.p
        block = p.diag_f if which == 0 else p.twin_f
        return remote(
            self.parts.at[block, :, cols],
            self.near.at[which, :, cols],
            self.s.at[which, i],
            self.s.at[2 + which, i],
            p.twin,
        )

    def to_cross(self, i, cols):
        return remote(
            self.out.at[:, cols], self.far.at[:, cols], self.s.at[4, i], self.s.at[5, i], self.p.cross
        )

    def give(self, i, cols):
        self.to_twin(i, 0, cols).start()
        self.to_twin(i, 1, cols).start()

    def pass_on(self, i, cols):
        self.to_twin(i, 0, cols).wait_recv()
        mine = self.parts[self.p.cross_f, :, cols].astype(f32)
        self.out[:, cols] = (mine + self.near[0, :, cols].astype(f32)).astype(bf16)
        self.to_cross(i, cols).start()

    def take(self, i, cols, own=None):
        self.to_twin(i, 1, cols).wait_recv()
        own = self.parts[self.p.f, :, cols] if own is None else own
        near = own.astype(f32) + self.near[1, :, cols].astype(f32)
        self.to_cross(i, cols).wait_recv()
        return near + self.far[:, cols].astype(f32)

    def given(self, i, cols):
        self.to_twin(i, 0, cols).wait_send()
        self.to_twin(i, 1, cols).wait_send()

    def passed(self, i, cols):
        self.to_cross(i, cols).wait_send()

    def finish(self, i, cols):
        self.given(i, cols)
        self.passed(i, cols)


class GroupTrade:
    sems = 2

    def __init__(self, place, whole, slots, sems, columns):
        self.p, self.whole, self.slots, self.s, self.n = place, whole, slots, sems, columns

    def block(self, g):
        return self.whole.at[:, pl.ds(pl.multiple_of(g * self.n, 128), self.n)]

    def send(self, d):
        self.copy(d).start()

    def copy(self, d):
        g = (self.p.f + d) % 4
        return remote(
            self.block(g), self.slots.at[self.p.f], self.s.at[0, d], self.s.at[1, d], {"fsdp": g}
        )

    def arrival(self, d):
        slot = self.slots.at[(self.p.f + 4 - d) % 4]
        return remote(slot, slot, self.s.at[0, d], self.s.at[1, d], {"fsdp": (self.p.f + d) % 4})

    def own(self):
        return pltpu.make_async_copy(
            self.block(self.p.f), self.slots.at[self.p.f], self.s.at[1, 0]
        )

    def start(self):
        for d in (2, 3, 1):
            self.copy(d).start()
        self.own().start()

    def wait(self):
        self.own().wait()
        for d in (1, 2, 3):
            self.arrival(d).wait_recv()

    def finish(self):
        for d in (1, 2, 3):
            self.copy(d).wait_send()


class GroupScatter:
    sems = 4

    def __init__(self, place, per_owner, stage, slots, sems):
        self.p, self.half, self.stage, self.slots, self.s = place, per_owner // 2, stage, slots, sems
        self.places = (place.twin_f, place.cross_f, place.diag_f)
        self.devices = (place.twin, place.cross, place.diag)

    def slot(self, f, half):
        return self.slots.at[pl.ds((2 * f + half) * self.half, self.half)]

    def own(self):
        return self.slots.at[pl.ds(2 * self.p.f * self.half, 2 * self.half)]

    def copy(self, kind, half):
        return remote(
            self.stage.at[kind, pl.ds(half * self.half, self.half)],
            self.slot(self.p.f, half),
            self.s.at[half, kind],
            self.s.at[2 + half, kind],
            self.devices[kind],
        )

    def arrived(self, kind):
        for half in range(2):
            slot = self.slot(self.places[kind], half)
            remote(
                slot, slot, self.s.at[half, kind], self.s.at[2 + half, kind], self.devices[kind]
            ).wait_recv()

    def send(self, kind):
        for half in range(2):
            self.copy(kind, half).start()

    def sent(self):
        for kind in range(3):
            for half in range(2):
                self.copy(kind, half).wait_send()


class PieceMove:
    def __init__(self, place, per_owner, pieces, slots, sems):
        p = place
        self.p, self.n, self.pieces, self.slots, self.s = p, per_owner, pieces, slots, sems
        self.at = hidden_piece(p.c, p.lines)

    def dest(self, q):
        return self.n * q + self.at // 4

    def copy(self, q):
        return remote(
            self.pieces.at[q],
            self.slots.at[self.at % 4],
            self.s.at[0, q],
            self.s.at[1, self.at % 4],
            {"ctx": self.dest(q)},
        )

    def stay(self, q):
        return pltpu.make_async_copy(self.pieces.at[q], self.slots.at[self.at % 4], self.s.at[2, 0])

    def start(self):
        for q in range(4):
            here = self.dest(q) == self.p.c
            pl.when(~here)(lambda q=q: self.copy(q).start())
            pl.when(here)(lambda q=q: self.stay(q).start())

    def finish(self):
        p = self.p
        for q in range(4):
            here = self.dest(q) == p.c
            pl.when(~here)(lambda q=q: self.copy(q).wait_send())
            pl.when(here)(lambda q=q: self.stay(q).wait())
        for i in range(4):
            source = place_of_piece(4 * (p.c % self.n) + i, p.lines)
            slot = self.slots.at[i]
            arrival = remote(slot, slot, self.s.at[0, 0], self.s.at[1, i], p.beside)
            pl.when(source != p.c)(lambda arrival=arrival: arrival.wait_recv())


def hidden_piece(c, lines):
    return (c % 2) * lines + c // 2


def place_of_piece(piece, lines):
    return (piece % lines) * 2 + piece // lines


class GroupReturn(GroupTrade):
    def __init__(self, place, whole, slots, sems):
        super().__init__(place, whole, slots, sems, 0)

    def block(self, g):
        return self.whole.at[g]


def rotary_tables(first, rows, bounds):
    index = first + lax.broadcasted_iota(jnp.int32, (rows, 128), 0)
    lane = lax.broadcasted_iota(jnp.int32, (rows, 128), 1)
    quarter = HD // 4
    member = documents(index, bounds)
    opening = jnp.where(member == 0, 0, jnp.where(member == 1, bounds[0], bounds[1]))
    frequency = jnp.exp((lane % quarter).astype(f32) * (-math.log(10000.0) / quarter))
    angles = (index - opening).astype(f32) * frequency
    sine = jnp.sin(angles)
    return jnp.cos(angles), jnp.where(lane < quarter, -sine, sine)


def rotated(v, cosine, sine):
    first = v[:, :128]
    return jnp.concatenate(
        [first * cosine + pltpu.roll(first, 64, 1) * sine, v[:, 128:]], axis=1
    )


class GroupGather:
    sems = 6

    def __init__(self, place, own, whole, sems, own_sem, pieces, cuts=None):
        self.p, self.own, self.whole, self.s, self.own_sem = place, own, whole, sems, own_sem
        self.pieces, self.n, self.cuts = pieces, own.shape[0] // pieces, cuts

    def span(self, i):
        return (slice(None), self.cuts[i]) if self.cuts else (pl.ds(i * self.n, self.n),)

    def part(self, i):
        return self.own.at[self.span(i)]

    def slot(self, g, i):
        return self.whole.at[(g,) + self.span(i)]

    def local(self):
        return pltpu.make_async_copy(self.own, self.whole.at[self.p.f], self.own_sem)

    def to_twin(self, i):
        return remote(
            self.part(i), self.slot(self.p.f, i), self.s.at[0, i], self.s.at[3, i], self.p.twin
        )

    def to_cross(self, i):
        return remote(
            self.part(i), self.slot(self.p.f, i), self.s.at[1, i], self.s.at[4, i], self.p.cross
        )

    def forward(self, i):
        slot = self.slot(self.p.cross_f, i)
        return remote(slot, slot, self.s.at[2, i], self.s.at[5, i], self.p.twin)

    def give(self, i):
        self.to_cross(i).start()
        self.to_twin(i).start()

    def near(self, i):
        twin = self.slot(self.p.twin_f, i)
        remote(twin, twin, self.s.at[0, i], self.s.at[3, i], self.p.twin).wait_recv()

    def pass_on(self, i):
        slot = self.slot(self.p.cross_f, i)
        remote(slot, slot, self.s.at[1, i], self.s.at[4, i], self.p.cross).wait_recv()
        self.forward(i).start()

    def last(self, i):
        diag = self.slot(self.p.diag_f, i)
        remote(diag, diag, self.s.at[2, i], self.s.at[5, i], self.p.twin).wait_recv()

    def sent(self, i):
        self.to_twin(i).wait_send()
        self.to_cross(i).wait_send()
        self.forward(i).wait_send()

    def finish(self, i):
        self.near(i)
        self.last(i)
        self.sent(i)


def tiles_of(first, count, tile):
    tile = tile if count % tile == 0 else 128

    def loop(body):
        def one(i, carry):
            body(pl.ds(pl.multiple_of(first + i * tile, 128), tile))
            return carry

        lax.fori_loop(0, count // tile, one, 0)

    return loop


def front_kernel(
    lines,
    bounds_ref,
    x_ref,
    gains,
    w_keyval_in,
    w_query_in,
    w_out_in,
    cot,
    w_down,
    w_gate_up,
    normed_out,
    query_out,
    keyval_out,
    probs_out,
    mixed_out,
    middle_out,
    normed_two_out,
    cosine,
    sine,
    columns_out,
    cot_all,
    rows_all,
    whole,
    slots,
    parts,
    near,
    out,
    far,
    keyval,
    mixed,
    bias,
    w_rows,
    windows,
    w_keyval,
    w_query,
    w_out,
    fetch_sems,
    trade_sems,
    sum_sems,
    keyval_sems,
    cot_sems,
    row_sems,
    own_sems,
):
    p = Place(lines)
    rows, width = x_ref.shape
    length = bias.shape[1]
    heads = query_out.shape[0]
    inner = heads * HD
    kv_width = 2 * HD
    fetch = Fetch(
        ((w_keyval_in, w_keyval), (w_query_in, w_query), (w_out_in, w_out)), fetch_sems
    )
    p.barrier()

    units = w_gate_up.shape[1] // 2
    piece = units // (4 * 2 * lines)
    padded_piece = w_rows.shape[0]
    own_piece = hidden_piece(p.c, lines)
    if w_down.shape[0] == padded_piece:
        rows_copy = pltpu.make_async_copy(w_down, w_rows, own_sems.at[2])
    else:
        rows_copy = pltpu.make_async_copy(
            w_down.at[pl.ds(pl.multiple_of(own_piece * piece, 16), piece)],
            w_rows.at[pl.ds(0, piece)],
            own_sems.at[2],
        )
    rows_copy.start()
    span = windows.shape[2]
    shard = w_gate_up.shape[0]

    def window_first(q):
        first = q * (units // 4) + own_piece * piece
        return jnp.minimum(first // 128 * 128, 2 * units - span), first

    def window(q):
        return pltpu.make_async_copy(
            w_gate_up.at[:, pl.ds(pl.multiple_of(window_first(q)[0], 128), span)],
            windows.at[q % 2],
            own_sems.at[3 + q % 2],
        )

    def pack_columns(q):
        window(q).wait()
        start, first = window_first(q)
        by = first - start
        lane = lax.broadcasted_iota(jnp.int32, (shard, 128), 1)
        tiles = [
            pltpu.roll(windows[q % 2, :, t * 128 : (t + 1) * 128].astype(f32), (128 - by % 128) % 128, 1)
            for t in range(span // 128)
        ]
        late = by >= 128
        turned = []
        for t in range(span // 128 - 1):
            turned.append(jnp.where(lane < 128 - by % 128, tiles[t], tiles[t + 1]))
        turned.append(jnp.where(lane < 128 - by % 128, tiles[-1], 0.0))
        turned = [
            jnp.where(late, turned[t + 1], turned[t]) for t in range(span // 128 - 1)
        ]
        turned = jnp.concatenate(turned, axis=1)[:, :padded_piece]
        lane = lax.broadcasted_iota(jnp.int32, (shard, padded_piece), 1)
        columns_out[:, q * padded_piece : (q + 1) * padded_piece] = jnp.where(
            lane < piece, turned, 0.0
        ).astype(bf16)
        if q + 2 < 8:
            window(q + 2).start()

    window(0).start()
    window(1).start()
    down = GroupGather(p, w_rows, rows_all, row_sems, own_sems.at[0], row_sems.shape[1])
    cot_gather = LineGather(p, cot, cot_all, cot_sems)
    cot_local = pltpu.make_async_copy(cot, cot_all.at[p.c], own_sems.at[1])

    def give(first, last):
        for i in range(first, min(last, down.pieces)):
            down.give(i)

    def pass_on(first, last):
        for i in range(first, min(last, down.pieces)):
            down.pass_on(i)

    source = x_ref[...].astype(f32)
    whole[...] = rms_norm(source, gains[0:1]).astype(bf16)
    trade = GroupTrade(p, whole, slots.at[0], trade_sems.at[0], slots.shape[3])
    trade.start()
    cot_local.start()
    cot_gather.start()
    bounds = (bounds_ref[0, 0], bounds_ref[0, 1])
    cosine[...], sine[...] = rotary_tables(p.c * rows, rows, bounds)
    query_at = p.c * rows + lax.broadcasted_iota(jnp.int32, (rows, length), 0)
    key_at = lax.broadcasted_iota(jnp.int32, (rows, length), 1)
    allowed = (
        (query_at >= key_at)
        & (query_at - key_at < WINDOW)
        & (documents(query_at, bounds) == documents(key_at, bounds))
    )
    bias[...] = jnp.where(allowed, 0.0, -1e30)
    rows_copy.wait()
    if w_down.shape[0] != padded_piece and piece < padded_piece:
        w_rows[pl.ds(piece, padded_piece - piece)] = jnp.zeros(
            (padded_piece - piece, width), bf16
        )
    down.local().start()
    give(0, 1)
    trade.wait()
    normed_out[...] = slots[0]

    half = (heads // 2) * HD
    chunks = [(0, kv_width), (kv_width, half), (kv_width + half, inner - half)]
    group = GroupSum(p, parts, near, out, far, sum_sems.at[0])

    def project(lhs, weight, first, count, to):
        @tiles_of(first, count, 256)
        def _(cols):
            left = lhs[...].reshape(4 * rows, lhs.shape[-1])
            product = jnp.dot(left, weight[:, cols], preferred_element_type=f32)
            if to:
                cols = pl.ds(pl.multiple_of(cols.start + to, 128), cols.size)
            parts[:, :, cols] = product.astype(bf16).reshape(4, rows, cols.size)

    spans = [pl.ds(first, count) for first, count in chunks]
    fetch.wait(0, 1)
    project(slots.at[0], w_keyval, 0, kv_width, 0)
    group.give(0, spans[0])
    project(slots.at[0], w_query, 0, half, kv_width)
    group.give(1, spans[1])
    group.pass_on(0, spans[0])
    project(slots.at[0], w_query, half, inner - half, kv_width)
    group.give(2, spans[2])
    group.pass_on(1, spans[1])
    group.pass_on(2, spans[2])

    linear = group.take(0, spans[0])
    keyval[0, p.c] = rotated(linear[:, :HD], cosine[...], sine[...]).astype(bf16)
    keyval[1, p.c] = linear[:, HD:].astype(bf16)
    kv_gathers = [
        LineGather(p, keyval.at[i, p.c], keyval.at[i], keyval_sems.at[i]) for i in range(2)
    ]
    for gather in kv_gathers:
        gather.start()
    for gather in kv_gathers:
        gather.step(0)

    def take_queries(i):
        linear = group.take(i, spans[i])
        for h in range(linear.shape[1] // HD):
            turned = rotated(linear[:, h * HD : (h + 1) * HD], cosine[...], sine[...])
            at = h if i == 1 else h + heads // 2
            query_out[at] = (turned * HD**-0.5).astype(bf16)

    give(1, 5)
    take_queries(1)
    for step in range(1, lines - 1):
        for gather in kv_gathers:
            gather.step(step)
    cot_gather.step(0)
    take_queries(2)
    for gather in kv_gathers:
        gather.finish()
    keyval_out[...] = keyval[...]


    def two_heads(i, carry):
        keys = keyval[0].reshape(length, HD)
        values = keyval[1].reshape(length, HD)
        two = query_out[pl.ds(2 * i, 2)].reshape(2 * rows, HD)
        scores = contract_rows(two, keys).reshape(2, rows, length) + bias[...][None]
        scores = scores.reshape(2 * rows, length)
        weights = jnp.exp(scores - jnp.max(scores, axis=-1, keepdims=True))
        total = jnp.sum(weights, axis=-1, keepdims=True)
        weights = (weights / total).astype(bf16)
        probs_out[pl.ds(2 * i, 2)] = weights.reshape(2, rows, length)
        product = jnp.dot(weights, values, preferred_element_type=f32).astype(bf16)
        at = pl.multiple_of(i * 2 * HD, 128)
        mixed[:, pl.ds(at, HD)] = product[:rows]
        mixed[:, pl.ds(at + HD, HD)] = product[rows:]
        return carry

    lax.fori_loop(0, heads // 2, two_heads, 0)
    trade_two = GroupTrade(p, mixed, slots.at[1], trade_sems.at[1], slots.shape[3])
    trade_two.start()
    give(5, 7)
    for q in range(4):
        pack_columns(q)
    if lines > 2:
        cot_gather.step(1)
    for i in range(len(chunks)):
        group.finish(i, spans[i])
    trade_two.wait()
    mixed_out[...] = slots[1]
    fetch.wait(2)

    half = width // 2
    spans_two = [pl.ds(0, half), pl.ds(half, half)]
    group_two = GroupSum(p, parts, near, out, far, sum_sems.at[1])
    for i in range(2):
        project(slots.at[1], w_out, i * half, half, 0)
        group_two.give(i, spans_two[i])
    for i in range(2):
        group_two.pass_on(i, spans_two[i])
    give(7, 8)
    for q in range(4, 8):
        pack_columns(q)
    pass_on(0, 7)
    for step in range(2, lines - 1):
        cot_gather.step(step)
    for i in range(2):
        middle_out[:, spans_two[i]] = x_ref[:, spans_two[i]].astype(f32) + group_two.take(
            i, spans_two[i]
        )
    normed_two_out[...] = rms_norm(middle_out[...], gains[1:2]).astype(bf16)

    pass_on(7, 8)
    for i in range(2):
        group_two.finish(i, spans_two[i])
    trade.finish()
    trade_two.finish()
    down.local().wait()
    cot_local.wait()
    for i in range(down.pieces):
        down.finish(i)
    cot_gather.finish()


def front(lines, operands, heads, padded_piece):
    x = operands[1]
    rows, width = x.shape
    places = 2 * lines
    length = places * rows
    inner = heads * HD
    shard = width // 4
    parts_width = inner + 2 * HD
    in_vmem = pl.BlockSpec(memory_space=VMEM)
    anywhere = pl.BlockSpec(memory_space=pl.ANY)
    shape = jax.ShapeDtypeStruct
    pieces = 8 if padded_piece % 128 == 0 else 1
    assert inner == width
    return pl.pallas_call(
        functools.partial(front_kernel, lines),
        out_shape=(
            shape((4, rows, shard), bf16),
            shape((heads, rows, HD), bf16),
            shape((2, places, rows, HD), bf16),
            shape((heads, rows, length), bf16),
            shape((4, rows, shard), bf16),
            shape((rows, width), f32),
            shape((rows, width), bf16),
            shape((rows, 128), f32),
            shape((rows, 128), f32),
            shape((shard, 8 * padded_piece), bf16),
            shape((places, rows, width), bf16),
            shape((4, padded_piece, width), bf16),
        ),
        in_specs=[pl.BlockSpec(memory_space=pltpu.SMEM)] + [in_vmem] * 2 + [anywhere] * 6,
        out_specs=[in_vmem] * 10 + [anywhere] * 2,
        scratch_shapes=[
            VMEM((rows, width), bf16),
            VMEM((2, 4, rows, shard), bf16),
            VMEM((4, rows, parts_width), bf16),
            VMEM((2, rows, parts_width), bf16),
            VMEM((rows, parts_width), bf16),
            VMEM((rows, parts_width), bf16),
            VMEM((2, places, rows, HD), bf16),
            VMEM((rows, inner), bf16),
            VMEM((rows, length), f32),
            VMEM((padded_piece, width), bf16),
            VMEM((2, shard, (padded_piece + 127) // 128 * 128 + 128), bf16),
            *held(operands[3:6]),
            DMA((3,)),
            DMA((2, GroupTrade.sems, 4)),
            DMA((2, GroupSum.sems, 3)),
            DMA((2, LineGather.sems, lines)),
            DMA((LineGather.sems, lines)),
            DMA((GroupGather.sems, pieces)),
            DMA((5,)),
        ],
        compiler_params=pltpu.CompilerParams(
            collective_id=0, has_side_effects=True, vmem_limit_bytes=vmem_bytes
        ),
        name="front",
    )(*operands)


def gelu_parts(v):
    k = 0.7978845608028654
    square = v * v
    inner = jnp.tanh(k * v * (1.0 + 0.044715 * square))
    half = 0.5 * (1.0 + inner)
    slope = half + 0.5 * v * (1.0 - inner * inner) * (k * (1.0 + 3 * 0.044715 * square))
    return v * half, slope


def norm_back(values, gain, grad):
    r = lax.rsqrt(jnp.mean(values * values, axis=-1, keepdims=True) + epsilon)
    scaled = values * r
    inner = grad * gain
    grad_values = r * (inner - scaled * jnp.mean(inner * scaled, axis=-1, keepdims=True))
    return grad_values, jnp.sum(grad * scaled, axis=0, keepdims=True)


def middle_kernel(
    lines,
    gains,
    cot_in,
    w_rows_in,
    own,
    middle,
    w_columns,
    grad_middle_out,
    gain_out,
    grads_out,
    down_out,
    normed_all_out,
    result_parts,
    normed_all,
    weights,
    grad_hidden,
    hidden,
    parts,
    side,
    chain,
    down_near,
    down_stage,
    down_far,
    cot_all,
    w_rows,
    fetch_sems,
    gather_sems,
    column_sems,
    sum_sems,
    down_sems,
    own_sems,
):
    p = Place(lines)
    rows, width = own.shape
    two = 2 * rows
    padded = hidden.shape[2]
    shard = width // 4
    tile = 256 if padded % 256 == 0 else 128
    fetch = Fetch(((cot_in, cot_all), (w_rows_in, w_rows)), fetch_sems)
    p.barrier()

    columns = GroupGather(p, w_columns, weights, column_sems, own_sems.at[0], column_sems.shape[1])
    gather = LineGather(p, own, normed_all, gather_sems)
    gather.start()
    for i in range(columns.pieces):
        columns.give(i)
    columns.local().start()
    own_local = pltpu.make_async_copy(own, normed_all.at[p.c], own_sems.at[2 + lines])
    own_local.start()
    middle_local = pltpu.make_async_copy(middle, grad_middle_out, own_sems.at[3 + lines])
    middle_local.start()

    def hidden_grad(line):
        def one(i, carry):
            cols = pl.ds(pl.multiple_of(i * tile, 128), tile)
            left = cot_all[pl.ds(2 * line, 2)].reshape(two, width)
            right = w_rows[pl.ds(pl.multiple_of(i * tile, 16), tile)]
            grad_hidden[line, :, cols] = contract_rows(left, right)
            return carry

        lax.fori_loop(0, padded // tile, one, 0)

    fetch.wait(0, 1)
    done = 0
    for step in range(lines - 1):
        hidden_grad(done)
        done += 1
        gather.step(step)
        if step < columns.pieces:
            columns.pass_on(step)
    for i in range(lines - 1, columns.pieces):
        columns.pass_on(i)
    while done < lines:
        hidden_grad(done)
        done += 1
    gather.finish()
    own_local.wait()
    columns.local().wait()
    for i in range(columns.pieces):
        columns.finish(i)
    normed_local = pltpu.make_async_copy(normed_all, normed_all_out, own_sems.at[1])
    normed_local.start()

    line_sums = [
        LineSum(p, parts.at[i], side.at[i], chain.at[i], sum_sems.at[i]) for i in range(2)
    ]

    def near(turn):
        for line_sum in line_sums:
            line_sum.near(turn, 0)

    def far(turn):
        for line_sum in line_sums:
            line_sum.far(turn)

    def feed_forward(line):
        def one(i, carry):
            cols = pl.ds(pl.multiple_of(i * tile, 128), tile)
            up_cols = pl.ds(pl.multiple_of(i * tile + padded, 128), tile)
            left = normed_all[pl.ds(2 * line, 2)].reshape(two, width)
            gate = jnp.dot(
                left, weights[:, :, cols].reshape(width, tile), preferred_element_type=f32
            )
            up = jnp.dot(
                left, weights[:, :, up_cols].reshape(width, tile), preferred_element_type=f32
            )
            gelu, slope = gelu_parts(gate)
            grad = grad_hidden[line, :, cols]
            hidden[line, :, cols] = (gelu * up).astype(bf16)
            grads_out[line, :, cols] = (grad * up * slope).astype(bf16)
            grads_out[line, :, up_cols] = (grad * gelu).astype(bf16)
            return carry

        lax.fori_loop(0, padded // tile, one, 0)

        def back(g, carry):
            product = contract_rows(grads_out[line], weights[g]).astype(bf16)
            cols = pl.ds(pl.multiple_of(g % 2 * shard, 128), shard)
            parts[g // 2, pl.ds(2 * line, 2), :, cols] = product.reshape(2, rows, shard)
            return carry

        lax.fori_loop(0, 4, back, 0)

    result_stage = normed_all

    def result_copy(line):
        blocks = pl.ds(2 * line, 2)
        return pltpu.make_async_copy(
            result_stage.at[blocks], result_parts.at[blocks], own_sems.at[2 + line]
        )

    def result_part(line):
        def one(i, carry):
            cols = pl.ds(pl.multiple_of(i * shard, 128), shard)
            product = jnp.dot(
                hidden[line], w_rows[:, cols], preferred_element_type=f32
            ).astype(bf16)
            result_stage[pl.ds(2 * line, 2), :, cols] = product.reshape(2, rows, shard)
            return carry

        lax.fori_loop(0, 4, one, 0)
        result_copy(line).start()

    quarter = padded // 4
    every = slice(None)
    down_parts = weights.at[:, pl.ds(0, quarter), pl.ds(0, shard)]

    def down_group(i):
        return GroupSum(p, down_parts, down_near.at[i], down_stage.at[i % 2], down_far.at[i], down_sems)

    def down_chunk(i):
        def one(g, carry):
            cols = pl.ds(pl.multiple_of(g * shard, 128), shard)
            left = hidden[:, :, i * quarter : (i + 1) * quarter].reshape(lines * two, quarter)
            right = cot_all[:, :, cols].reshape(lines * two, shard)
            down_parts[g] = contract_tokens(left, right).astype(bf16)
            return carry

        lax.fori_loop(0, 4, one, 0)
        down_out[i] = down_parts[p.f]
        down_group(i).give(i, every)

    for turn in range(lines):
        feed_forward(line_sums[0].order(turn))
        for line_sum in line_sums:
            line_sum.across(turn).start()
        if turn == lines - 2:
            near(0)
    normed_local.wait()

    for i in range(4):
        if i >= 1:
            down_group(i - 1).given(i - 1, every)
        if i >= 2:
            down_group(i - 2).passed(i - 2, every)
        down_chunk(i)
        down_group(i).pass_on(i, every)
        if i == 1:
            if lines > 2:
                near(1)
            far(0)
        if i == 2 and lines > 3:
            near(2)
            far(1)
            far(2)
    for line in range(lines):
        result_part(line)
    for turn in range(3, lines - 1):
        near(turn)
        far(turn)
    near(lines - 1)
    far(lines - 1)
    grad = jnp.concatenate([line_sum.total() for line_sum in line_sums], axis=1)
    middle_local.wait()
    grad_values, gain = norm_back(grad_middle_out[...], gains[1:2], grad)
    grad_middle_out[...] = cot_all[p.c].astype(f32) + grad_values
    gain_out[...] = gain
    for i in range(2):
        down_out[i] = down_group(i).take(i, every, down_out[i]).astype(bf16)
    for i in (2, 3):
        down_out[i] = down_group(i).take(i, every, down_out[i]).astype(bf16)
        down_group(i).passed(i, every)
    down_group(3).given(3, every)
    for line in range(lines):
        result_copy(line).wait()
    for line_sum in line_sums:
        line_sum.finish()


def middle_bytes(lines, rows, width, padded):
    length = 2 * lines * rows
    return (
        14 * rows * width
        + 9 * length * width
        + 9 * padded * width
        + 10 * length * padded
    )


def middle_part(lines, operands, padded):
    own = operands[3]
    rows, width = own.shape
    places = 2 * lines
    shard = width // 4
    quarter = padded // 4
    pieces = 4
    in_vmem = pl.BlockSpec(memory_space=VMEM)
    anywhere = pl.BlockSpec(memory_space=pl.ANY)
    shape = jax.ShapeDtypeStruct
    return pl.pallas_call(
        functools.partial(middle_kernel, lines),
        out_shape=(
            shape((rows, width), f32),
            shape((1, width), f32),
            shape((lines, 2 * rows, 2 * padded), bf16),
            shape((4, quarter, shard), bf16),
            shape((places, rows, width), bf16),
            shape((places, rows, width), bf16),
        ),
        in_specs=[in_vmem] + [anywhere] * 5,
        out_specs=[in_vmem] * 4 + [anywhere] * 2,
        scratch_shapes=[
            VMEM((places, rows, width), bf16),
            VMEM((4, shard, 2 * padded), bf16),
            VMEM((lines, 2 * rows, padded), f32),
            VMEM((lines, 2 * rows, padded), bf16),
            VMEM((2, places, rows, width // 2), bf16),
            VMEM((2, lines, rows, width // 2), bf16),
            VMEM((2, 2, lines - 1, rows, width // 2), bf16),
            VMEM((4, 2, quarter, shard), bf16),
            VMEM((2, quarter, shard), bf16),
            VMEM((4, quarter, shard), bf16),
            *held(operands[1:3]),
            DMA((2,)),
            DMA((LineGather.sems, lines)),
            DMA((GroupGather.sems, pieces)),
            DMA((2, LineSum.sems, lines)),
            DMA((GroupSum.sems, 4)),
            DMA((4 + lines,)),
        ],
        compiler_params=pltpu.CompilerParams(
            collective_id=1, has_side_effects=True, vmem_limit_bytes=vmem_bytes
        ),
        name="middle",
    )(*operands)


def is_long(length):
    return length > 2048


def back_kernel(
    lines,
    with_result,
    grad_middle,
    tokens,
    gains,
    cosine,
    sine,
    w_out_in,
    probs_in,
    keyval_in,
    queries_in,
    mixed_in,
    w_query_in,
    w_keyval_in,
    down_in,
    *rest,
):
    if with_result:
        middle, result_in, result_out, *rest = rest
    (
        input_grad_out,
        gain_out,
        linear_out,
        out_slots,
        down_out,
        branch_all,
        linear_all,
        branch,
        linear,
        trade_parts,
        trade_slots,
        grad_mixed,
        kv_total,
        kv_parts,
        kv_side,
        kv_chain,
        out_stage,
        w_out,
        probs,
        keyval,
        queries,
        mixed,
        w_query,
        w_keyval,
        fetch_sems,
        branch_sems,
        linear_sems,
        trade_sems,
        kv_sems,
        out_sems,
        piece_sems,
        own_sems,
        *rest,
    ) = rest
    p = Place(lines)
    rows, width = grad_middle.shape
    heads = queries.shape[0]
    length = probs_in.shape[2]
    long = is_long(length)
    operands = [
        (w_out_in, w_out),
        (keyval_in, keyval),
        (queries_in, queries),
        (mixed_in, mixed),
        (w_query_in, w_query),
        (w_keyval_in, w_keyval),
    ]
    fetch = Fetch(operands if long else operands + [(probs_in, probs)], fetch_sems)
    shard = w_out.shape[0]
    kv_width = 2 * HD
    per_owner = 2 * lines // 4
    others = [(jnp.full((), True), {"ctx": (p.c + d) % (2 * lines)}) for d in range(1, 2 * lines)]
    p.barrier(ctx=False, also=others)
    if with_result:
        result_parts, result_side, result_chain, result_sems = rest
        result_sum = Turns(
            LineSum(p, result_parts, result_side, result_chain, result_sems), lines
        )
        half = width // 2
        result_copies = [
            pltpu.make_async_copy(
                result_in.at[:, :, pl.ds(i * half, half)], result_parts.at[i], own_sems.at[2 + i]
            )
            for i in range(2)
        ]
        for copy in result_copies:
            copy.start()
        result_sums = [
            Turns(
                LineSum(
                    p, result_parts.at[i], result_side.at[i], result_chain.at[i], result_sems.at[i]
                ),
                lines,
            )
            for i in range(2)
        ]
    out_scatter = GroupScatter(p, per_owner, out_stage, out_slots, out_sems)

    branch[...] = grad_middle[...].astype(bf16)
    group = GroupGather(p, branch, branch_all, branch_sems, own_sems.at[0], 1)
    group.give(0)
    group.local().start()
    down_move = PieceMove(p, per_owner, down_in, down_out, piece_sems)
    down_move.start()
    if with_result:
        result_copies[0].wait()
        result_sums[0].start()
    back_trade = GroupReturn(p, trade_parts.at[0], trade_slots.at[0], trade_sems.at[0])

    def mixed_back(g):
        trade_parts[0, g] = contract_rows(branch_all[g], w_out[...]).astype(bf16)

    group.local().wait()
    fetch.wait(0)
    mixed_back(p.f)
    back_trade.own().start()
    group.near(0)
    mixed_back(p.twin_f)
    group.pass_on(0)
    mixed_back(p.cross_f)
    back_trade.send(2)
    group.last(0)
    mixed_back(p.diag_f)
    back_trade.send(1)
    back_trade.send(3)

    def out_block(i, g):
        left = mixed[...].reshape(4 * rows, shard)
        right = branch_all[:, :, pl.ds(pl.multiple_of(g * shard, 128), shard)]
        product = contract_tokens(left, right.reshape(4 * rows, shard)).astype(bf16)
        out_stage[i] = product.reshape(out_stage.shape[1:])

    fetch.wait(3)
    out_block(1, p.cross_f)
    out_scatter.copy(1, 0).start()
    out_block(0, p.twin_f)
    out_scatter.send(0)
    out_block(2, p.diag_f)
    out_block(3, p.f)
    out_own = pltpu.make_async_copy(out_stage.at[3], out_scatter.own(), own_sems.at[7])
    out_own.start()
    if with_result:
        result_sums[0].near(2)
    back_trade.wait()
    for g in range(4):
        grad_mixed[:, g * shard : (g + 1) * shard] = trade_slots[0, g]

    kv_total[...] = jnp.zeros_like(kv_total)
    kv_at, q_at = pl.ds(0, kv_width), pl.ds(kv_width, heads * HD)

    batch = 1 if long else 2
    fetch.wait(1, 2)
    if not long:
        fetch.wait(6)

    def some_heads(i, carry):
        keys = keyval[0].reshape(length, HD)
        values = keyval[1].reshape(length, HD)
        at = [pl.multiple_of((i * batch + h) * HD, 128) for h in range(batch)]
        outer = jnp.concatenate([grad_mixed[:, pl.ds(a, HD)] for a in at], axis=0)
        if batch == 1:
            one = pltpu.make_async_copy(probs_in.at[i], probs, own_sems.at[5])
            one.start()
            one.wait()
            weights = probs[...]
        else:
            weights = probs[pl.ds(batch * i, batch)].reshape(batch * rows, length)
        wide = weights.astype(f32)
        grad_weights = contract_rows(outer, values)
        delta = jnp.sum(wide * grad_weights, axis=-1, keepdims=True)
        grad_scores = (wide * (grad_weights - delta)).astype(bf16)
        product = jnp.dot(grad_scores, keys, preferred_element_type=f32) * HD**-0.5
        for h in range(batch):
            turned = rotated(product[h * rows : (h + 1) * rows], cosine[...], -sine[...])
            linear[:, pl.ds(kv_width + at[h], HD)] = turned.astype(bf16)
        two = queries[pl.ds(batch * i, batch)].reshape(batch * rows, HD)
        kv_total[:, :HD] += contract_tokens(grad_scores, two)
        kv_total[:, HD:] += contract_tokens(weights, outer)
        return carry

    lax.fori_loop(0, heads // batch, some_heads, 0)
    linear_group = GroupGather(
        p, linear, linear_all, linear_sems, own_sems.at[1], 2, (q_at, kv_at)
    )
    linear_group.give(0)
    kv_parts[...] = kv_total[...].astype(bf16).reshape(kv_parts.shape)
    kv_sum = LineSum(p, kv_parts, kv_side, kv_chain, kv_sems)
    kv_sum.start(lines)
    if with_result:
        result_copies[1].wait()
        result_sums[1].start()
        result_sums[0].near(lines)
        result_sums[0].far(1)
    kv_sum.turns(0)
    own = kv_sum.total()
    linear[:, :HD] = rotated(own[:, :HD], cosine[...], -sine[...]).astype(bf16)
    linear[:, pl.ds(HD, HD)] = own[:, HD:].astype(bf16)
    linear_group.give(1)
    out_scatter.copy(1, 1).start()
    linear_group.local().start()
    if with_result:
        result_sums[0].far(2)
        result_sums[1].near(2)
    fetch.wait(4, 5)
    linear_group.pass_on(0)
    linear_group.pass_on(1)
    linear_group.local().wait()
    for i in range(2):
        linear_group.near(i)
        linear_group.last(i)

    linear_copy = pltpu.make_async_copy(linear_all, linear_out, own_sems.at[4])
    linear_copy.start()

    last_trade = GroupReturn(p, trade_parts.at[1], trade_slots.at[1], trade_sems.at[1])

    def normed_back(g):
        product = contract_rows(linear_all[g, :, kv_at], w_keyval[...])
        product += contract_rows(linear_all[g, :, q_at], w_query[...])
        trade_parts[1, g] = product.astype(bf16)

    normed_back(p.cross_f)
    last_trade.send(2)
    normed_back(p.diag_f)
    normed_back(p.twin_f)
    last_trade.send(1)
    last_trade.send(3)
    out_scatter.send(2)
    normed_back(p.f)
    last_trade.own().start()
    if with_result:
        result_sums[0].far(3)
        result_sums[1].far(2)
    last_trade.wait()
    for g in range(4):
        grad_mixed[:, g * shard : (g + 1) * shard] = trade_slots[1, g]
    source = tokens[...].astype(f32)
    grad_values, gain = norm_back(source, gains[0:1], grad_mixed[...].astype(f32))
    input_grad_out[...] = (grad_middle[...] + grad_values).astype(bf16)
    gain_out[...] = gain
    if with_result:
        for i in range(2):
            cols = pl.ds(i * half, half)
            result_out[:, cols] = (middle[:, cols] + result_sums[i].total()).astype(bf16)
            result_sums[i].sum.finish()
    back_trade.finish()
    last_trade.finish()
    group.sent(0)
    linear_group.sent(0)
    linear_group.sent(1)
    kv_sum.finish()
    out_own.wait()
    for kind in range(3):
        out_scatter.arrived(kind)
    out_scatter.sent()
    linear_copy.wait()
    down_move.finish()


def back(lines, operands, result_operands):
    rows, width = operands[0].shape
    heads = operands[8].shape[0]
    places = 2 * lines
    length = places * rows
    shard = width // 4
    linear_width = width + 2 * HD
    tall = width // places
    pieces = operands[12].shape
    in_vmem = pl.BlockSpec(memory_space=VMEM)
    anywhere = pl.BlockSpec(memory_space=pl.ANY)
    shape = jax.ShapeDtypeStruct
    with_result = bool(result_operands)
    long = is_long(length)
    scratch = held(operands[5:12])
    if long:
        scratch[1] = VMEM((rows, length), bf16)
    result_scratch = [
        VMEM((2, places, rows, width // 2), bf16),
        VMEM((2, lines, rows, width // 2), bf16),
        VMEM((2, 2, lines - 1, rows, width // 2), bf16),
        DMA((2, LineSum.sems, lines)),
    ]
    return pl.pallas_call(
        functools.partial(back_kernel, lines, with_result),
        out_shape=((shape((rows, width), bf16),) if with_result else ())
        + (
            shape((rows, width), bf16),
            shape((1, width), f32),
            shape((4, rows, linear_width), bf16),
            shape((places, tall, shard), bf16),
            shape(pieces, bf16),
        ),
        in_specs=[in_vmem] * 5 + [anywhere] * 8 + ([in_vmem, anywhere] if with_result else []),
        out_specs=[in_vmem] * (3 if with_result else 2) + [anywhere] * 3,
        scratch_shapes=[
            VMEM((4, rows, width), bf16),
            VMEM((4, rows, linear_width), bf16),
            VMEM((rows, width), bf16),
            VMEM((rows, linear_width), bf16),
            VMEM((2, 4, rows, shard), bf16),
            VMEM((2, 4, rows, shard), bf16),
            VMEM((rows, width), bf16),
            VMEM((length, 2 * HD), f32),
            VMEM((places, rows, 2 * HD), bf16),
            VMEM((lines, rows, 2 * HD), bf16),
            VMEM((2, lines - 1, rows, 2 * HD), bf16),
            VMEM((4, places // 4, tall, shard), bf16),
            *scratch,
            DMA((7,)),
            DMA((GroupGather.sems, 1)),
            DMA((GroupGather.sems, 2)),
            DMA((2, GroupTrade.sems, 4)),
            DMA((LineSum.sems, lines)),
            DMA((GroupScatter.sems, 3)),
            DMA((3, 4)),
            DMA((8,)),
        ]
        + (result_scratch if with_result else []),
        compiler_params=pltpu.CompilerParams(
            collective_id=2, has_side_effects=True, vmem_limit_bytes=vmem_bytes
        ),
        name="back",
    )(*operands, *result_operands)


def grads_kernel(lines, with_columns, gain_one, gain_two, out_in, normed_in, linear_in, *rest):
    if with_columns:
        normed_two_in, hidden_grads_in, *rest = rest
    projection_out, gains_out, out_out, *rest = rest
    if with_columns:
        columns_out, *rest = rest
    (
        parts,
        side,
        chain,
        stage,
        out_parts,
        out_side,
        out_chain,
        gain_parts,
        gain_side,
        gain_chain,
        gain_slots,
        normed,
        linear_all,
        fetch_sems,
        projection_sems,
        out_sems,
        gain_sems,
        slot_sems,
        scatter_sems,
        *rest,
    ) = rest
    p = Place(lines)
    operands = [(out_in, out_parts)]
    if with_columns:
        (
            chunk_parts,
            near,
            passing,
            far,
            chunks,
            group_sems,
            trade_sems,
            normed_two,
            hidden_grads,
        ) = rest
    if with_columns:
        operands += [(normed_two_in, normed_two), (hidden_grads_in, hidden_grads)]
    operands += [(normed_in, normed), (linear_in, linear_all)]
    fetch = Fetch(operands, fetch_sems)
    places = 2 * lines
    shard = normed.shape[2]
    tokens = 4 * normed.shape[1]
    per_owner = places // 4
    tall = shard // per_owner
    kv_share = 2 * HD // 4
    others = [(jnp.full((), True), {"ctx": (p.c + d) % places}) for d in range(1, places)]
    p.barrier(ctx=False, also=others)

    for c in range(places):
        cols = slice(c * tall, (c + 1) * tall)
        gain_parts[c, 0:1, :tall] = gain_one[:, cols]
        gain_parts[c, 1:2, :tall] = gain_two[:, cols]
    gain_sum = LineSum(p, gain_parts, gain_side, gain_chain, gain_sems)
    gain_sum.start(lines)

    projection_sums = [
        Turns(LineSum(p, parts.at[i], side.at[i], chain.at[i], projection_sems.at[i]))
        for i in range(2)
    ]
    out_sum = Turns(LineSum(p, out_parts, out_side, out_chain, out_sems))
    fetch.wait(0)
    out_sum.start()

    if with_columns:
        fetch.wait(1, 2)
        block = columns_out.shape[2]
        chunk = chunk_parts.shape[1]
        every = slice(None)

        def chunk_of(k):
            order = sorted(range(lines), key=lambda d: (d == 0, abs(d - lines // 2), d))
            return (p.line + order[k]) % lines

        def group(k):
            return GroupSum(p, chunk_parts, near.at[k], passing.at[k % 2], far.at[k], group_sems)

        def compute(k):
            cols = pl.ds(pl.multiple_of(chunk_of(k) * chunk, 128), chunk)

            def one(g, carry):
                left = normed_two[:, :, cols].reshape(-1, chunk)
                right = hidden_grads[:, :, pl.ds(pl.multiple_of(g * block, 128), block)]
                chunk_parts[g] = contract_tokens(left, right.reshape(-1, block)).astype(bf16)
                return carry

            lax.fori_loop(0, 4, one, 0)
            chunks[k] = chunk_parts[p.f]
            group(k).give(k, every)

        def halves(k):
            half = chunk // 2
            for lane in range(2):
                yield lane, 2 * chunk_of(k) + lane, chunks.at[k, pl.ds(lane * half, half)]

        def place_copy(k, lane, dest, src):
            return remote(
                src,
                columns_out.at[p.c],
                trade_sems.at[0, 2 * k + lane],
                trade_sems.at[1, p.c],
                {"ctx": dest},
            )

        def place_own(src):
            return pltpu.make_async_copy(src, columns_out.at[p.c], trade_sems.at[2, 0])

        def arrival(i):
            slot = columns_out.at[i]
            return remote(slot, slot, trade_sems.at[0, 0], trade_sems.at[1, i], p.beside)

        def complete(k):
            chunks[k] = group(k).take(k, every, chunks[k]).astype(bf16)
            for lane, dest, src in halves(k):
                pl.when(dest != p.c)(
                    lambda k=k, lane=lane, dest=dest, src=src: place_copy(k, lane, dest, src).start()
                )
                pl.when(dest == p.c)(lambda src=src: place_own(src).start())

        def chunk_step(k):
            if k >= 1:
                group(k - 1).given(k - 1, every)
            compute(k)
            if k >= 2:
                group(k - 2).passed(k - 2, every)
            group(k).pass_on(k, every)

        chunk_step(0)

    scatters = [
        GroupScatter(p, per_owner, stage.at[i], parts.at[i], scatter_sems.at[i]) for i in range(2)
    ]

    def projection_block(first, second, g):
        left = normed[...].reshape(tokens, shard)
        right = linear_all[:, :, pl.ds(pl.multiple_of(2 * HD + g * shard, 128), shard)]
        product = contract_tokens(left, right.reshape(tokens, shard)).astype(bf16)
        right = linear_all[:, :, pl.ds(pl.multiple_of(g * kv_share, 128), kv_share)]
        kv_product = contract_tokens(left, right.reshape(tokens, kv_share)).astype(bf16)
        first[...] = product[:, :half].reshape(per_owner, tall, half)
        if half < shard:
            kv_product = jnp.concatenate([product[:, half:], kv_product], axis=1)
        second[...] = kv_product.reshape(per_owner, tall, half)

    half = (shard + kv_share) // 2
    fetch.wait(*((3, 4) if with_columns else (1, 2)))
    for kind in (1, 2, 0):
        projection_block(stage.at[0, kind], stage.at[1, kind], scatters[0].places[kind])
        scatters[0].send(kind)
    for kind in (1, 2, 0):
        scatters[1].send(kind)
    projection_block(scatters[0].own(), scatters[1].own(), p.f)

    first, second = projection_sums
    if with_columns:
        chunk_step(1)
    out_sum.near(2)
    out_sum.far(1)
    if with_columns:
        complete(0)
        if lines > 2:
            chunk_step(2)
    out_sum.near(lines)
    for k in range(lines):
        gain_sum.near(k, 0)
    for kind in range(3):
        scatters[0].arrived(kind)
    first.start()
    out_sum.far(2)
    first.near(2)
    out_sum.far(3)
    first.near(lines)
    for kind in range(3):
        scatters[1].arrived(kind)
    second.start()
    first.far(1)
    for k in range(lines):
        gain_sum.far(k)
    out_out[...] = out_sum.total().astype(bf16)
    first.far(2)
    if with_columns:
        for k in range(1, lines):
            second.near(k)
            complete(k)
            if k + 2 < lines:
                chunk_step(k + 2)
            first.far(k + 2)
            second.near(k + 1)
            second.far(k)
        for k in (lines - 2, lines - 1):
            group(k).passed(k, every)
        group(lines - 1).given(lines - 1, every)

    own = gain_sum.total()
    gain_parts[p.c] = own

    def gain_copy(d):
        return remote(
            gain_parts.at[p.c],
            gain_slots.at[d],
            slot_sems.at[0, d],
            slot_sems.at[1, d],
            {"fsdp": (p.f + d) % 4},
        )

    for d in (1, 2, 3):
        gain_copy(d).start()
    for i in range(2):
        projection_out[:, i * half : (i + 1) * half] = projection_sums[i].total().astype(bf16)
    for d in (1, 2, 3):
        gain_copy(d).wait_recv()
        own = own + gain_slots[d]
    gains_out[...] = own

    for d in (1, 2, 3):
        gain_copy(d).wait_send()
    if with_columns:
        for k in range(lines):
            for lane, dest, src in halves(k):
                pl.when(dest != p.c)(
                    lambda k=k, lane=lane, dest=dest, src=src: place_copy(k, lane, dest, src).wait_send()
                )
                pl.when(dest == p.c)(lambda src=src: place_own(src).wait())
        for i in range(places):
            pl.when(p.c != i)(lambda i=i: arrival(i).wait_recv())
    gain_sum.finish()
    for projection_sum in projection_sums:
        projection_sum.sum.finish()
    out_sum.sum.finish()
    for scatter in scatters:
        scatter.sent()


def weight_grads(lines, operands, column_operands):
    rows, shard = operands[3].shape[1:]
    width = 4 * shard
    places = 2 * lines
    tall = width // places
    wide = shard + 2 * HD // 4
    gain_wide = -(-tall // 128) * 128
    in_vmem = pl.BlockSpec(memory_space=VMEM)
    anywhere = pl.BlockSpec(memory_space=pl.ANY)
    shape = jax.ShapeDtypeStruct
    with_columns = bool(column_operands)
    column_shapes, column_scratch = (), []
    if with_columns:
        block = column_operands[1].shape[2] // 4
        chunk = width // lines
        column_shapes = (shape((places, chunk // 2, block), bf16),)
        column_scratch = [
            VMEM((4, chunk, block), bf16),
            VMEM((lines, 2, chunk, block), bf16),
            VMEM((2, chunk, block), bf16),
            VMEM((lines, chunk, block), bf16),
            VMEM((lines, chunk, block), bf16),
            DMA((GroupSum.sems, lines)),
            DMA((3, places)),
            *held(column_operands),
        ]
    return pl.pallas_call(
        functools.partial(grads_kernel, lines, with_columns),
        out_shape=(shape((tall, wide), bf16), shape((8, gain_wide), f32), shape((tall, shard), bf16)) + column_shapes,
        in_specs=[in_vmem] * 2 + [anywhere] * (3 + len(column_operands)),
        out_specs=[in_vmem] * 3 + [anywhere] * len(column_shapes),
        scratch_shapes=[
            VMEM((2, places, tall, wide // 2), bf16),
            VMEM((2, lines, tall, wide // 2), bf16),
            VMEM((2, 2, lines - 1, tall, wide // 2), bf16),
            VMEM((2, 3, places // 4, tall, wide // 2), bf16),
            VMEM((places, tall, shard), bf16),
            VMEM((lines, tall, shard), bf16),
            VMEM((2, lines - 1, tall, shard), bf16),
            VMEM((places, 8, gain_wide), f32),
            VMEM((lines, 8, gain_wide), f32),
            VMEM((2, lines - 1, 8, gain_wide), f32),
            VMEM((4, 8, gain_wide), f32),
            *held(operands[3:5]),
            DMA((5,)),
            DMA((2, LineSum.sems, lines)),
            DMA((LineSum.sems, lines)),
            DMA((LineSum.sems, lines)),
            DMA((2, 4)),
            DMA((2, GroupScatter.sems, 3)),
        ]
        + column_scratch,
        compiler_params=pltpu.CompilerParams(
            collective_id=3, has_side_effects=True, vmem_limit_bytes=vmem_bytes
        ),
        name="grads",
    )(*operands, *column_operands)


def assemble_kernel(lines, piece, projection, out, down, columns, *outs):
    query_out, keyval_out, out_out, down_out, columns_out = outs
    shard = out.shape[1]
    padded_piece = columns.shape[2] // 2
    query_out[...] = projection[:, :shard].astype(f32)
    keyval_out[...] = projection[:, shard:].astype(f32)
    out_out[...] = out[...].astype(f32)
    for i in range(down.shape[0]):
        down_out[i * piece : (i + 1) * piece] = down[i, :piece].astype(f32)
    pieces = [
        columns[place_of_piece(n, lines), :, q * padded_piece : q * padded_piece + piece]
        for q in range(2)
        for n in range(2 * lines)
    ]
    columns_out[...] = jnp.concatenate(pieces, axis=1).astype(f32)


def assemble(lines, piece, projection, out, down, columns):
    tall, wide = projection.shape
    shard = out.shape[1]
    places = 2 * lines
    block = columns.shape[2]
    steps = 4 if tall % 64 == 0 else 1
    run = tall // steps
    full = 2 * places * piece

    def flat(rows, cols):
        return pl.BlockSpec((rows, cols), lambda i: (i, 0))

    shape = jax.ShapeDtypeStruct
    return pl.pallas_call(
        functools.partial(assemble_kernel, lines, piece),
        grid=(steps,),
        out_shape=(
            shape((tall, shard), f32),
            shape((tall, wide - shard), f32),
            shape((tall, shard), f32),
            shape((4 * piece, shard), f32),
            shape((tall, full), f32),
        ),
        in_specs=[
            flat(run, wide),
            flat(run, shard),
            pl.BlockSpec((4 // steps, down.shape[1], shard), lambda i: (i, 0, 0)),
            pl.BlockSpec((places, run, block), lambda i: (0, i, 0)),
        ],
        out_specs=[
            flat(run, shard),
            flat(run, wide - shard),
            flat(run, shard),
            flat(4 // steps * piece, shard),
            flat(run, full),
        ],
        compiler_params=pltpu.CompilerParams(vmem_limit_bytes=vmem_bytes),
        name="assemble",
    )(projection, out, down, columns)


def per_device(
    tokens,
    doc_bounds,
    cotangent,
    norm_one,
    query_weight,
    keyval_weight,
    out_weight,
    norm_two,
    gate_up_weight,
    down_weight,
):
    ctx_size = lax.axis_size("ctx")
    fsdp_size = lax.axis_size("fsdp")
    lines = ctx_size // 2
    rows = tokens.shape[1]
    width = tokens.shape[2]
    length = rows * ctx_size
    inner_width = query_weight.shape[1]
    head_count = inner_width // HD
    hidden_width = gate_up_weight.shape[1] // 2
    piece = hidden_width // (ctx_size * fsdp_size)
    padded_piece = -(-piece // 32) * 32
    padded = padded_piece * fsdp_size
    gains = jnp.stack([norm_one, norm_two])
    cot_rows = cotangent[0]
    down_rows = down_weight
    if piece % 16:
        first = hidden_piece(lax.axis_index("ctx"), lines) * piece
        down_rows = lax.dynamic_slice_in_dim(down_weight, first, piece, 0)
        down_rows = jnp.pad(down_rows, ((0, padded_piece - piece), (0, 0)))
    (
        normed,
        queries,
        window,
        weights,
        mixed,
        middle,
        normed_two,
        cosine,
        sine,
        w_columns,
        cot_all,
        w_down,
    ) = front(
        lines,
        (
            doc_bounds,
            tokens[0],
            gains,
            keyval_weight,
            query_weight,
            out_weight,
            cot_rows,
            down_rows,
            gate_up_weight,
        ),
        head_count,
        padded_piece,
    )
    w_down = w_down.reshape(padded, width)
    fits = middle_bytes(lines, rows, width, padded) <= vmem_bytes
    if fits:
        grad_middle, gain_two_term, grad_gate_up, down_part, normed_two, result_parts = middle_part(
            lines, (gains, cot_all, w_down, normed_two, middle, w_columns), padded
        )
    else:
        cot_all = cot_all.reshape(length, width)
        normed_two = lax.all_gather(normed_two, "ctx", axis=0, tiled=True)
        w_gate_up = lax.all_gather(w_columns, "fsdp", axis=0, tiled=True)
        projected = jnp.dot(normed_two, w_gate_up, preferred_element_type=f32)
        gelu, slope = gelu_parts(projected[:, :padded])
        up_part = projected[:, padded:]
        hidden = (gelu * up_part).astype(bf16)
        grad_hidden = contract_rows(cot_all, w_down)
        grad_gate_up = jnp.concatenate(
            [grad_hidden * up_part * slope, grad_hidden * gelu], axis=1
        ).astype(bf16)
        grad_normed_two = lax.psum_scatter(
            contract_rows(grad_gate_up, w_gate_up).astype(bf16),
            "ctx",
            scatter_dimension=0,
            tiled=True,
        ).astype(f32)
        grad_middle_norm, gain_two_term = norm_back(middle, norm_two[None], grad_normed_two)
        grad_middle = cot_rows.astype(f32) + grad_middle_norm
        result_parts = jnp.dot(hidden, w_down, preferred_element_type=f32).astype(bf16)
        down_part = lax.psum_scatter(
            contract_tokens(hidden, cot_all).astype(bf16),
            "fsdp",
            scatter_dimension=1,
            tiled=True,
        ).reshape(fsdp_size, padded_piece, -1)
    operands = (
        grad_middle,
        tokens[0],
        gains,
        cosine,
        sine,
        out_weight,
        weights,
        window,
        queries,
        mixed,
        query_weight,
        keyval_weight,
        down_part,
    )
    if fits:
        result, input_grad, gain_one_term, grad_linear, out_parts, down_grad = back(
            lines, operands, (middle, result_parts)
        )
    else:
        input_grad, gain_one_term, grad_linear, out_parts, down_grad = back(lines, operands, ())
        branch_two = lax.psum_scatter(result_parts, "ctx", scatter_dimension=0, tiled=True)
        result = (middle + branch_two.astype(f32)).astype(bf16)

    operands = (gain_one_term, gain_two_term, out_parts, normed, grad_linear)
    if fits:
        projection_grad, gain_grads, out_grad, gate_up_part = weight_grads(
            lines, operands, (normed_two, grad_gate_up)
        )
    else:
        projection_grad, gain_grads, out_grad = weight_grads(lines, operands, ())
        gate_up_part = lax.psum_scatter(
            contract_tokens(normed_two, grad_gate_up).astype(bf16),
            "fsdp",
            scatter_dimension=1,
            tiled=True,
        )
        gate_up_part = lax.all_to_all(
            gate_up_part.reshape(ctx_size, width // ctx_size, -1), "ctx", 0, 0, tiled=True
        )
    query_grad, keyval_grad, out_grad, down_grad, gate_up_grad = assemble(
        lines, piece, projection_grad, out_grad, down_grad, gate_up_part
    )
    share = width // (ctx_size * fsdp_size)
    gains = lax.dynamic_slice_in_dim(gain_grads, lax.axis_index("fsdp") * share, share, 1)
    return (
        result[None],
        input_grad[None],
        gains[0],
        query_grad,
        keyval_grad,
        out_grad,
        gains[1],
        gate_up_grad,
        down_grad,
    )


def solution(mesh):
    placed = (
        P("fsdp", "ctx", None),
        P("fsdp", None),
        P("fsdp", "ctx", None),
        P(),
        P("fsdp", None),
        P("fsdp", None),
        P("fsdp", None),
        P(),
        P("fsdp", None),
        P("fsdp", None),
    )
    return jax.shard_map(
        per_device,
        mesh=mesh,
        in_specs=placed,
        out_specs=(
            P("fsdp", "ctx", None),
            P("fsdp", "ctx", None),
            P(("ctx", "fsdp")),
            P("ctx", "fsdp"),
            P("ctx", "fsdp"),
            P("ctx", "fsdp"),
            P(("ctx", "fsdp")),
            P("ctx", "fsdp"),
            P("ctx", "fsdp"),
        ),
        check_vma=False,
    )
```

```python
import functools
import math

import jax
import jax.numpy as jnp
from jax import lax
from jax.experimental import pallas as pl
from jax.experimental.pallas import tpu as pltpu
from jax.sharding import PartitionSpec as P

HD = 256
WINDOW = 2048


epsilon = 1e-06
f32 = jnp.float32
bf16 = jnp.bfloat16
VMEM = pltpu.VMEM
DMA = pltpu.SemaphoreType.DMA
vmem_bytes = 62 * 1024 * 1024


def rms_norm(values, gain):
    return values * lax.rsqrt(jnp.mean(values * values, axis=-1, keepdims=True) + epsilon) * gain


def documents(index, bounds):
    return (index >= bounds[0]).astype(jnp.int32) + (index >= bounds[1]).astype(jnp.int32)


def contract_rows(left, right):
    return lax.dot_general(
        left, right, (((1,), (1,)), ((), ())), preferred_element_type=jnp.float32
    )


def contract_tokens(left, right):
    return lax.dot_general(
        left, right, (((0,), (0,)), ((), ())), preferred_element_type=jnp.float32
    )


def remote(src, dst, send_sem, recv_sem, device):
    return pltpu.make_async_remote_copy(
        src_ref=src,
        dst_ref=dst,
        send_sem=send_sem,
        recv_sem=recv_sem,
        device_id=device,
        device_id_type=pl.DeviceIdType.MESH,
    )


class Place:
    def __init__(self, lines):
        self.lines = lines
        self.c = lax.axis_index("ctx")
        self.f = lax.axis_index("fsdp")
        self.line = self.c // 2
        self.lane = self.c % 2
        self.chip = self.f // 2
        self.core = self.f % 2
        self.twin_f = self.f + 1 - 2 * self.core
        self.cross_f = (self.f + 2) % 4
        self.diag_f = (self.twin_f + 2) % 4
        self.twin = {"fsdp": self.twin_f}
        self.cross = {"fsdp": self.cross_f}
        self.diag = {"fsdp": self.diag_f}
        self.beside = {"ctx": self.c + 1 - 2 * self.lane}
        self.right = {"ctx": self.c + 2}
        self.left = {"ctx": self.c - 2}
        self.has_right = self.line < lines - 1
        self.has_left = self.line > 0

    def barrier(self, ctx=True, fsdp=True, also=()):
        sem = pltpu.get_barrier_semaphore()

        def greet(device):
            pl.semaphore_signal(sem, 1, device_id=device, device_id_type=pl.DeviceIdType.MESH)

        count = 0
        if fsdp:
            for device in (self.twin, self.cross, self.diag):
                greet(device)
            count = 3
        if ctx:
            greet(self.beside)
            pl.when(self.has_right)(lambda: greet(self.right))
            pl.when(self.has_left)(lambda: greet(self.left))
            count = (
                count + 1 + self.has_right.astype(jnp.int32) + self.has_left.astype(jnp.int32)
            )
        for needed, device in also:
            pl.when(needed)(lambda device=device: greet(device))
            count = count + needed.astype(jnp.int32)
        pl.semaphore_wait(sem, count)


class Fetch:
    def __init__(self, pairs, sems):
        self.copies = [
            pltpu.make_async_copy(src, dst, sems.at[i]) for i, (src, dst) in enumerate(pairs)
        ]
        for copy in self.copies:
            copy.start()

    def wait(self, *which):
        for i in which:
            self.copies[i].wait()


def held(operands):
    return [VMEM(operand.shape, operand.dtype) for operand in operands]


class LineGather:
    sems = 6

    def __init__(self, place, own, slots, sems):
        self.p, self.own, self.slots, self.s = place, own, slots, sems

    def rightward(self, step):
        at = 2 * (self.p.line - step) + self.p.lane
        src = self.own if step == 0 else self.slots.at[at]
        return remote(src, self.slots.at[at], self.s.at[0, step], self.s.at[1, step], self.p.right)

    def leftward(self, step):
        at = 2 * (self.p.line + step) + self.p.lane
        src = self.own if step == 0 else self.slots.at[at]
        return remote(src, self.slots.at[at], self.s.at[2, step], self.s.at[3, step], self.p.left)

    def across(self, line, own=False):
        at = 2 * line + self.p.lane
        src = self.own if own else self.slots.at[at]
        return remote(
            src, self.slots.at[at], self.s.at[4, line], self.s.at[5, line], self.p.beside
        )

    def from_left(self, step):
        at = 2 * (self.p.line - 1 - step) + self.p.lane
        slot = self.slots.at[at]
        return remote(slot, slot, self.s.at[0, step], self.s.at[1, step], self.p.right)

    def from_right(self, step):
        at = 2 * (self.p.line + 1 + step) + self.p.lane
        slot = self.slots.at[at]
        return remote(slot, slot, self.s.at[2, step], self.s.at[3, step], self.p.left)

    def start(self):
        pl.when(self.p.has_right)(lambda: self.rightward(0).start())
        pl.when(self.p.has_left)(lambda: self.leftward(0).start())
        self.across(self.p.line, True).start()

    def step(self, step):
        p = self.p

        @pl.when(p.line - 1 - step >= 0)
        def _():
            self.from_left(step).wait_recv()
            if step + 1 < p.lines - 1:
                pl.when(p.has_right)(lambda: self.rightward(step + 1).start())
            self.across(p.line - 1 - step).start()

        @pl.when(p.line + 1 + step <= p.lines - 1)
        def _():
            self.from_right(step).wait_recv()
            if step + 1 < p.lines - 1:
                pl.when(p.has_left)(lambda: self.leftward(step + 1).start())
            self.across(p.line + 1 + step).start()

    def steps(self):
        for step in range(self.p.lines - 1):
            self.step(step)

    def arrived_across(self, line):
        at = 2 * line + 1 - self.p.lane
        slot = self.slots.at[at]
        remote(slot, slot, self.s.at[4, line], self.s.at[5, line], self.p.beside).wait_recv()

    def finish(self, arrivals=True):
        p = self.p
        if arrivals:
            for line in range(p.lines):
                self.arrived_across(line)
        for step in range(p.lines - 1):
            pl.when(p.has_right & (p.line - step >= 0))(
                lambda step=step: self.rightward(step).wait_send()
            )
            pl.when(p.has_left & (p.line + step <= p.lines - 1))(
                lambda step=step: self.leftward(step).wait_send()
            )
        for line in range(p.lines):
            self.across(line).wait_send()


class LineSum:
    sems = 6

    def __init__(self, place, parts, side, chain, sems):
        self.p, self.parts, self.side, self.chain, self.s = place, parts, side, chain, sems

    def order(self, turn):
        lines, line = self.p.lines, self.p.line
        value = 0
        for a in range(lines):
            far = sorted(range(lines), key=lambda t: (-abs(t - a), t))
            value = value + jnp.where(line == a, far[turn], 0)
        return value

    def across(self, turn):
        t = self.order(turn)
        at = 2 * t + 1 - self.p.lane
        return remote(
            self.parts.at[at],
            self.side.at[t],
            self.s.at[0, t],
            self.s.at[1, t],
            self.p.beside,
        )

    def rightward(self, t):
        step = self.p.lines - 1 - t
        return remote(
            self.parts.at[2 * t + self.p.lane],
            self.chain.at[0, step],
            self.s.at[2, step],
            self.s.at[3, step],
            self.p.right,
        )

    def leftward(self, t):
        return remote(
            self.parts.at[2 * t + self.p.lane],
            self.chain.at[1, t],
            self.s.at[4, t],
            self.s.at[5, t],
            self.p.left,
        )

    def add(self, at, other):
        self.parts[at] = (self.parts[at].astype(f32) + other.astype(f32)).astype(self.parts.dtype)

    def start(self, ahead=2):
        for turn in range(min(ahead, self.p.lines)):
            self.across(turn).start()

    def near(self, turn, ahead=2):
        p = self.p
        t = self.order(turn)
        at = 2 * t + p.lane
        self.across(turn).wait_recv()
        if ahead and turn + ahead < p.lines:
            self.across(turn + ahead).start()
        self.add(at, self.side[t])
        pl.when((t > p.line) & (p.line == 0))(lambda: self.rightward(t).start())
        pl.when((t < p.line) & (p.line == p.lines - 1))(lambda: self.leftward(t).start())

    def far(self, turn):
        p = self.p
        t = self.order(turn)
        at = 2 * t + p.lane

        @pl.when((t > p.line) & p.has_left)
        def _():
            self.rightward(t).wait_recv()
            self.add(at, self.chain[0, p.lines - 1 - t])
            self.rightward(t).start()

        @pl.when((t < p.line) & p.has_right)
        def _():
            self.leftward(t).wait_recv()
            self.add(at, self.chain[1, t])
            self.leftward(t).start()

    def turns(self, ahead=2):
        for turn in range(self.p.lines):
            self.near(turn, ahead)
            if turn > 0:
                self.far(turn - 1)
        self.far(self.p.lines - 1)

    def total(self):
        p = self.p
        at = 2 * p.line + p.lane

        @pl.when(p.has_left)
        def _():
            self.rightward(p.line).wait_recv()
            self.add(at, self.chain[0, p.lines - 1 - p.line])

        @pl.when(p.has_right)
        def _():
            self.leftward(p.line).wait_recv()
            self.add(at, self.chain[1, p.line])

        return self.parts[at].astype(f32)

    def finish(self):
        p = self.p
        for turn in range(p.lines):
            self.across(turn).wait_send()
        for t in range(p.lines):
            pl.when(t > p.line)(lambda t=t: self.rightward(t).wait_send())
            pl.when(t < p.line)(lambda t=t: self.leftward(t).wait_send())


class Turns:
    def __init__(self, line_sum, ahead=2):
        self.sum, self.ahead, self.nears, self.fars = line_sum, ahead, 0, 0

    def start(self):
        self.sum.start(self.ahead)

    def near(self, upto):
        while self.nears < min(upto, self.sum.p.lines):
            self.sum.near(self.nears, self.ahead)
            self.nears += 1

    def far(self, upto):
        while self.fars < min(upto, self.sum.p.lines):
            self.near(self.fars + 1)
            self.sum.far(self.fars)
            self.fars += 1

    def total(self):
        self.far(self.sum.p.lines)
        return self.sum.total()


class GroupSum:
    sems = 6

    def __init__(self, place, parts, near, out, far, sems):
        self.p, self.parts, self.near, self.out, self.far, self.s = place, parts, near, out, far, sems

    def to_twin(self, i, which, cols):
        p = self.p
        block = p.diag_f if which == 0 else p.twin_f
        return remote(
            self.parts.at[block, :, cols],
            self.near.at[which, :, cols],
            self.s.at[which, i],
            self.s.at[2 + which, i],
            p.twin,
        )

    def to_cross(self, i, cols):
        return remote(
            self.out.at[:, cols], self.far.at[:, cols], self.s.at[4, i], self.s.at[5, i], self.p.cross
        )

    def give(self, i, cols):
        self.to_twin(i, 0, cols).start()
        self.to_twin(i, 1, cols).start()

    def pass_on(self, i, cols):
        self.to_twin(i, 0, cols).wait_recv()
        mine = self.parts[self.p.cross_f, :, cols].astype(f32)
        self.out[:, cols] = (mine + self.near[0, :, cols].astype(f32)).astype(bf16)
        self.to_cross(i, cols).start()

    def take(self, i, cols, own=None):
        self.to_twin(i, 1, cols).wait_recv()
        own = self.parts[self.p.f, :, cols] if own is None else own
        near = own.astype(f32) + self.near[1, :, cols].astype(f32)
        self.to_cross(i, cols).wait_recv()
        return near + self.far[:, cols].astype(f32)

    def given(self, i, cols):
        self.to_twin(i, 0, cols).wait_send()
        self.to_twin(i, 1, cols).wait_send()

    def passed(self, i, cols):
        self.to_cross(i, cols).wait_send()

    def finish(self, i, cols):
        self.given(i, cols)
        self.passed(i, cols)


class GroupTrade:
    sems = 2

    def __init__(self, place, whole, slots, sems, columns):
        self.p, self.whole, self.slots, self.s, self.n = place, whole, slots, sems, columns

    def block(self, g):
        return self.whole.at[:, pl.ds(pl.multiple_of(g * self.n, 128), self.n)]

    def send(self, d):
        self.copy(d).start()

    def copy(self, d):
        g = (self.p.f + d) % 4
        return remote(
            self.block(g), self.slots.at[self.p.f], self.s.at[0, d], self.s.at[1, d], {"fsdp": g}
        )

    def arrival(self, d):
        slot = self.slots.at[(self.p.f + 4 - d) % 4]
        return remote(slot, slot, self.s.at[0, d], self.s.at[1, d], {"fsdp": (self.p.f + d) % 4})

    def own(self):
        return pltpu.make_async_copy(
            self.block(self.p.f), self.slots.at[self.p.f], self.s.at[1, 0]
        )

    def start(self):
        for d in (2, 3, 1):
            self.copy(d).start()
        self.own().start()

    def wait(self):
        self.own().wait()
        for d in (1, 2, 3):
            self.arrival(d).wait_recv()

    def finish(self):
        for d in (1, 2, 3):
            self.copy(d).wait_send()


class GroupScatter:
    sems = 4

    def __init__(self, place, per_owner, stage, slots, sems):
        self.p, self.half, self.stage, self.slots, self.s = place, per_owner // 2, stage, slots, sems
        self.places = (place.twin_f, place.cross_f, place.diag_f)
        self.devices = (place.twin, place.cross, place.diag)

    def slot(self, f, half):
        return self.slots.at[pl.ds((2 * f + half) * self.half, self.half)]

    def own(self):
        return self.slots.at[pl.ds(2 * self.p.f * self.half, 2 * self.half)]

    def copy(self, kind, half):
        return remote(
            self.stage.at[kind, pl.ds(half * self.half, self.half)],
            self.slot(self.p.f, half),
            self.s.at[half, kind],
            self.s.at[2 + half, kind],
            self.devices[kind],
        )

    def arrived(self, kind):
        for half in range(2):
            slot = self.slot(self.places[kind], half)
            remote(
                slot, slot, self.s.at[half, kind], self.s.at[2 + half, kind], self.devices[kind]
            ).wait_recv()

    def send(self, kind):
        for half in range(2):
            self.copy(kind, half).start()

    def sent(self):
        for kind in range(3):
            for half in range(2):
                self.copy(kind, half).wait_send()


class PieceMove:
    def __init__(self, place, per_owner, pieces, slots, sems):
        p = place
        self.p, self.n, self.pieces, self.slots, self.s = p, per_owner, pieces, slots, sems
        self.at = hidden_piece(p.c, p.lines)

    def dest(self, q):
        return self.n * q + self.at // 4

    def copy(self, q):
        return remote(
            self.pieces.at[q],
            self.slots.at[self.at % 4],
            self.s.at[0, q],
            self.s.at[1, self.at % 4],
            {"ctx": self.dest(q)},
        )

    def stay(self, q):
        return pltpu.make_async_copy(self.pieces.at[q], self.slots.at[self.at % 4], self.s.at[2, 0])

    def start(self):
        for q in range(4):
            here = self.dest(q) == self.p.c
            pl.when(~here)(lambda q=q: self.copy(q).start())
            pl.when(here)(lambda q=q: self.stay(q).start())

    def finish(self):
        p = self.p
        for q in range(4):
            here = self.dest(q) == p.c
            pl.when(~here)(lambda q=q: self.copy(q).wait_send())
            pl.when(here)(lambda q=q: self.stay(q).wait())
        for i in range(4):
            source = place_of_piece(4 * (p.c % self.n) + i, p.lines)
            slot = self.slots.at[i]
            arrival = remote(slot, slot, self.s.at[0, 0], self.s.at[1, i], p.beside)
            pl.when(source != p.c)(lambda arrival=arrival: arrival.wait_recv())


def hidden_piece(c, lines):
    return (c % 2) * lines + c // 2


def place_of_piece(piece, lines):
    return (piece % lines) * 2 + piece // lines


class GroupReturn(GroupTrade):
    def __init__(self, place, whole, slots, sems):
        super().__init__(place, whole, slots, sems, 0)

    def block(self, g):
        return self.whole.at[g]


def rotary_tables(first, rows, bounds):
    index = first + lax.broadcasted_iota(jnp.int32, (rows, 128), 0)
    lane = lax.broadcasted_iota(jnp.int32, (rows, 128), 1)
    quarter = HD // 4
    member = documents(index, bounds)
    opening = jnp.where(member == 0, 0, jnp.where(member == 1, bounds[0], bounds[1]))
    frequency = jnp.exp((lane % quarter).astype(f32) * (-math.log(10000.0) / quarter))
    angles = (index - opening).astype(f32) * frequency
    sine = jnp.sin(angles)
    return jnp.cos(angles), jnp.where(lane < quarter, -sine, sine)


def rotated(v, cosine, sine):
    first = v[:, :128]
    return jnp.concatenate(
        [first * cosine + pltpu.roll(first, 64, 1) * sine, v[:, 128:]], axis=1
    )


class GroupGather:
    sems = 6

    def __init__(self, place, own, whole, sems, own_sem, pieces, cuts=None):
        self.p, self.own, self.whole, self.s, self.own_sem = place, own, whole, sems, own_sem
        self.pieces, self.n, self.cuts = pieces, own.shape[0] // pieces, cuts

    def span(self, i):
        return (slice(None), self.cuts[i]) if self.cuts else (pl.ds(i * self.n, self.n),)

    def part(self, i):
        return self.own.at[self.span(i)]

    def slot(self, g, i):
        return self.whole.at[(g,) + self.span(i)]

    def local(self):
        return pltpu.make_async_copy(self.own, self.whole.at[self.p.f], self.own_sem)

    def to_twin(self, i):
        return remote(
            self.part(i), self.slot(self.p.f, i), self.s.at[0, i], self.s.at[3, i], self.p.twin
        )

    def to_cross(self, i):
        return remote(
            self.part(i), self.slot(self.p.f, i), self.s.at[1, i], self.s.at[4, i], self.p.cross
        )

    def forward(self, i):
        slot = self.slot(self.p.cross_f, i)
        return remote(slot, slot, self.s.at[2, i], self.s.at[5, i], self.p.twin)

    def give(self, i):
        self.to_cross(i).start()
        self.to_twin(i).start()

    def near(self, i):
        twin = self.slot(self.p.twin_f, i)
        remote(twin, twin, self.s.at[0, i], self.s.at[3, i], self.p.twin).wait_recv()

    def pass_on(self, i):
        slot = self.slot(self.p.cross_f, i)
        remote(slot, slot, self.s.at[1, i], self.s.at[4, i], self.p.cross).wait_recv()
        self.forward(i).start()

    def last(self, i):
        diag = self.slot(self.p.diag_f, i)
        remote(diag, diag, self.s.at[2, i], self.s.at[5, i], self.p.twin).wait_recv()

    def sent(self, i):
        self.to_twin(i).wait_send()
        self.to_cross(i).wait_send()
        self.forward(i).wait_send()

    def finish(self, i):
        self.near(i)
        self.last(i)
        self.sent(i)


def tiles_of(first, count, tile):
    tile = tile if count % tile == 0 else 128

    def loop(body):
        def one(i, carry):
            body(pl.ds(pl.multiple_of(first + i * tile, 128), tile))
            return carry

        lax.fori_loop(0, count // tile, one, 0)

    return loop


def front_kernel(
    lines,
    bounds_ref,
    x_ref,
    gains,
    w_keyval_in,
    w_query_in,
    w_out_in,
    cot,
    w_down,
    w_gate_up,
    normed_dst,
    query_dst,
    keyval_dst,
    probs_dst,
    mixed_dst,
    middle_out,
    normed_two_out,
    cosine,
    sine,
    columns_dst,
    cot_all,
    rows_all,
    whole,
    slots,
    parts,
    near,
    out,
    far,
    keyval,
    mixed,
    bias,
    w_rows,
    windows,
    normed_out,
    query_out,
    keyval_out,
    probs_out,
    mixed_out,
    columns_out,
    put_sems,
    w_keyval,
    w_query,
    w_out,
    fetch_sems,
    trade_sems,
    sum_sems,
    keyval_sems,
    cot_sems,
    row_sems,
    own_sems,
):
    p = Place(lines)
    rows, width = x_ref.shape
    length = bias.shape[1]
    heads = query_out.shape[0]
    inner = heads * HD
    kv_width = 2 * HD
    fetch = Fetch(
        ((w_keyval_in, w_keyval), (w_query_in, w_query), (w_out_in, w_out)), fetch_sems
    )
    p.barrier()
    puts = []

    def put(src, dst):
        puts.append(pltpu.make_async_copy(src, dst, put_sems.at[len(puts)]))
        puts[-1].start()


    units = w_gate_up.shape[1] // 2
    piece = units // (4 * 2 * lines)
    padded_piece = w_rows.shape[0]
    own_piece = hidden_piece(p.c, lines)
    if w_down.shape[0] == padded_piece:
        rows_copy = pltpu.make_async_copy(w_down, w_rows, own_sems.at[2])
    else:
        rows_copy = pltpu.make_async_copy(
            w_down.at[pl.ds(pl.multiple_of(own_piece * piece, 16), piece)],
            w_rows.at[pl.ds(0, piece)],
            own_sems.at[2],
        )
    rows_copy.start()
    span = windows.shape[2]
    shard = w_gate_up.shape[0]

    def window_first(q):
        first = q * (units // 4) + own_piece * piece
        return jnp.minimum(first // 128 * 128, 2 * units - span), first

    def window(q):
        return pltpu.make_async_copy(
            w_gate_up.at[:, pl.ds(pl.multiple_of(window_first(q)[0], 128), span)],
            windows.at[q % 2],
            own_sems.at[3 + q % 2],
        )

    def pack_columns(q):
        window(q).wait()
        start, first = window_first(q)
        by = first - start
        lane = lax.broadcasted_iota(jnp.int32, (shard, 128), 1)
        tiles = [
            pltpu.roll(windows[q % 2, :, t * 128 : (t + 1) * 128].astype(f32), (128 - by % 128) % 128, 1)
            for t in range(span // 128)
        ]
        late = by >= 128
        turned = []
        for t in range(span // 128 - 1):
            turned.append(jnp.where(lane < 128 - by % 128, tiles[t], tiles[t + 1]))
        turned.append(jnp.where(lane < 128 - by % 128, tiles[-1], 0.0))
        turned = [
            jnp.where(late, turned[t + 1], turned[t]) for t in range(span // 128 - 1)
        ]
        turned = jnp.concatenate(turned, axis=1)[:, :padded_piece]
        lane = lax.broadcasted_iota(jnp.int32, (shard, padded_piece), 1)
        columns_out[:, q * padded_piece : (q + 1) * padded_piece] = jnp.where(
            lane < piece, turned, 0.0
        ).astype(bf16)
        if q + 2 < 8:
            window(q + 2).start()

    window(0).start()
    window(1).start()
    down = GroupGather(p, w_rows, rows_all, row_sems, own_sems.at[0], row_sems.shape[1])
    cot_gather = LineGather(p, cot, cot_all, cot_sems)
    cot_local = pltpu.make_async_copy(cot, cot_all.at[p.c], own_sems.at[1])

    def give(first, last):
        for i in range(first, min(last, down.pieces)):
            down.give(i)

    def pass_on(first, last):
        for i in range(first, min(last, down.pieces)):
            down.pass_on(i)

    source = x_ref[...].astype(f32)
    whole[...] = rms_norm(source, gains[0:1]).astype(bf16)
    trade = GroupTrade(p, whole, slots.at[0], trade_sems.at[0], slots.shape[3])
    trade.start()
    cot_local.start()
    cot_gather.start()
    bounds = (bounds_ref[0, 0], bounds_ref[0, 1])
    cosine[...], sine[...] = rotary_tables(p.c * rows, rows, bounds)
    query_at = p.c * rows + lax.broadcasted_iota(jnp.int32, (rows, length), 0)
    key_at = lax.broadcasted_iota(jnp.int32, (rows, length), 1)
    allowed = (
        (query_at >= key_at)
        & (query_at - key_at < WINDOW)
        & (documents(query_at, bounds) == documents(key_at, bounds))
    )
    bias[...] = jnp.where(allowed, 0.0, -1e30)
    rows_copy.wait()
    if w_down.shape[0] != padded_piece and piece < padded_piece:
        w_rows[pl.ds(piece, padded_piece - piece)] = jnp.zeros(
            (padded_piece - piece, width), bf16
        )
    down.local().start()
    give(0, 1)
    trade.wait()
    normed_out[...] = slots[0]
    put(normed_out, normed_dst)

    half = (heads // 2) * HD
    chunks = [(0, kv_width), (kv_width, half), (kv_width + half, inner - half)]
    group = GroupSum(p, parts, near, out, far, sum_sems.at[0])

    def project(lhs, weight, first, count, to):
        @tiles_of(first, count, 256)
        def _(cols):
            left = lhs[...].reshape(4 * rows, lhs.shape[-1])
            product = jnp.dot(left, weight[:, cols], preferred_element_type=f32)
            if to:
                cols = pl.ds(pl.multiple_of(cols.start + to, 128), cols.size)
            parts[:, :, cols] = product.astype(bf16).reshape(4, rows, cols.size)

    spans = [pl.ds(first, count) for first, count in chunks]
    fetch.wait(0, 1)
    project(slots.at[0], w_keyval, 0, kv_width, 0)
    group.give(0, spans[0])
    project(slots.at[0], w_query, 0, half, kv_width)
    group.give(1, spans[1])
    group.pass_on(0, spans[0])
    project(slots.at[0], w_query, half, inner - half, kv_width)
    group.give(2, spans[2])
    group.pass_on(1, spans[1])
    group.pass_on(2, spans[2])

    linear = group.take(0, spans[0])
    keyval[0, p.c] = rotated(linear[:, :HD], cosine[...], sine[...]).astype(bf16)
    keyval[1, p.c] = linear[:, HD:].astype(bf16)
    kv_gathers = [
        LineGather(p, keyval.at[i, p.c], keyval.at[i], keyval_sems.at[i]) for i in range(2)
    ]
    for gather in kv_gathers:
        gather.start()
    for gather in kv_gathers:
        gather.step(0)

    def take_queries(i):
        linear = group.take(i, spans[i])
        for h in range(linear.shape[1] // HD):
            turned = rotated(linear[:, h * HD : (h + 1) * HD], cosine[...], sine[...])
            at = h if i == 1 else h + heads // 2
            query_out[at] = (turned * HD**-0.5).astype(bf16)

    give(1, 4)
    take_queries(1)
    for step in range(1, lines - 1):
        for gather in kv_gathers:
            gather.step(step)
    cot_gather.step(0)
    take_queries(2)
    for gather in kv_gathers:
        gather.finish()
    keyval_out[...] = keyval[...]
    put(keyval_out, keyval_dst)
    put(query_out, query_dst)


    def two_heads(i, carry):
        keys = keyval[0].reshape(length, HD)
        values = keyval[1].reshape(length, HD)
        two = query_out[pl.ds(2 * i, 2)].reshape(2 * rows, HD)
        scores = contract_rows(two, keys).reshape(2, rows, length) + bias[...][None]
        scores = scores.reshape(2 * rows, length)
        weights = jnp.exp(scores - jnp.max(scores, axis=-1, keepdims=True))
        total = jnp.sum(weights, axis=-1, keepdims=True)
        weights = (weights / total).astype(bf16)
        probs_out[pl.ds(2 * i, 2)] = weights.reshape(2, rows, length)
        product = jnp.dot(weights, values, preferred_element_type=f32).astype(bf16)
        at = pl.multiple_of(i * 2 * HD, 128)
        mixed[:, pl.ds(at, HD)] = product[:rows]
        mixed[:, pl.ds(at + HD, HD)] = product[rows:]
        return carry

    lax.fori_loop(0, heads // 2, two_heads, 0)
    trade_two = GroupTrade(p, mixed, slots.at[1], trade_sems.at[1], slots.shape[3])
    trade_two.start()
    give(4, 6)
    put(probs_out, probs_dst)
    for q in range(4):
        pack_columns(q)
    if lines > 2:
        cot_gather.step(1)
    for i in range(len(chunks)):
        group.finish(i, spans[i])
    trade_two.wait()
    mixed_out[...] = slots[1]
    put(mixed_out, mixed_dst)
    fetch.wait(2)

    half = width // 2
    spans_two = [pl.ds(0, half), pl.ds(half, half)]
    group_two = GroupSum(p, parts, near, out, far, sum_sems.at[1])
    for i in range(2):
        project(slots.at[1], w_out, i * half, half, 0)
        group_two.give(i, spans_two[i])
    for i in range(2):
        group_two.pass_on(i, spans_two[i])
    give(6, 8)
    for q in range(4, 8):
        pack_columns(q)
    put(columns_out, columns_dst)
    pass_on(0, 6)
    for step in range(2, lines - 1):
        cot_gather.step(step)
    for i in range(2):
        middle_out[:, spans_two[i]] = x_ref[:, spans_two[i]].astype(f32) + group_two.take(
            i, spans_two[i]
        )
    normed_two_out[...] = rms_norm(middle_out[...], gains[1:2]).astype(bf16)

    pass_on(6, 8)
    for i in range(2):
        group_two.finish(i, spans_two[i])
    trade.finish()
    trade_two.finish()
    for copy in puts:
        copy.wait()
    down.local().wait()
    cot_local.wait()
    for i in range(down.pieces):
        down.finish(i)
    cot_gather.finish()


def front(lines, operands, heads, padded_piece):
    x = operands[1]
    rows, width = x.shape
    places = 2 * lines
    length = places * rows
    inner = heads * HD
    shard = width // 4
    parts_width = inner + 2 * HD
    in_vmem = pl.BlockSpec(memory_space=VMEM)
    anywhere = pl.BlockSpec(memory_space=pl.ANY)
    shape = jax.ShapeDtypeStruct
    pieces = 8 if padded_piece % 128 == 0 else 1
    assert inner == width
    copied = [
        shape((4, rows, shard), bf16),
        shape((heads, rows, HD), bf16),
        shape((2, places, rows, HD), bf16),
        shape((heads, rows, length), bf16),
        shape((4, rows, shard), bf16),
        shape((shard, 8 * padded_piece), bf16),
    ]
    outs = (
        *copied[:5],
        shape((rows, width), f32),
        shape((rows, width), bf16),
        shape((rows, 128), f32),
        shape((rows, 128), f32),
        copied[5],
        shape((places, rows, width), bf16),
        shape((4, padded_piece, width), bf16),
    )
    return pl.pallas_call(
        functools.partial(front_kernel, lines),
        out_shape=outs,
        in_specs=[pl.BlockSpec(memory_space=pltpu.SMEM)] + [in_vmem] * 2 + [anywhere] * 6,
        out_specs=[anywhere] * 5 + [in_vmem] * 4 + [anywhere] * 3,
        scratch_shapes=[
            VMEM((rows, width), bf16),
            VMEM((2, 4, rows, shard), bf16),
            VMEM((4, rows, parts_width), bf16),
            VMEM((2, rows, parts_width), bf16),
            VMEM((rows, parts_width), bf16),
            VMEM((rows, parts_width), bf16),
            VMEM((2, places, rows, HD), bf16),
            VMEM((rows, inner), bf16),
            VMEM((rows, length), f32),
            VMEM((padded_piece, width), bf16),
            VMEM((2, shard, (padded_piece + 127) // 128 * 128 + 128), bf16),
            *held(copied),
            DMA((6,)),
            *held(operands[3:6]),
            DMA((3,)),
            DMA((2, GroupTrade.sems, 4)),
            DMA((2, GroupSum.sems, 3)),
            DMA((2, LineGather.sems, lines)),
            DMA((LineGather.sems, lines)),
            DMA((GroupGather.sems, pieces)),
            DMA((5,)),
        ],
        compiler_params=pltpu.CompilerParams(
            collective_id=0, has_side_effects=True, vmem_limit_bytes=vmem_bytes
        ),
        name="front",
    )(*operands)


def gelu_parts(v):
    k = 0.7978845608028654
    square = v * v
    inner = jnp.tanh(k * v * (1.0 + 0.044715 * square))
    half = 0.5 * (1.0 + inner)
    slope = half + 0.5 * v * (1.0 - inner * inner) * (k * (1.0 + 3 * 0.044715 * square))
    return v * half, slope


def norm_back(values, gain, grad):
    r = lax.rsqrt(jnp.mean(values * values, axis=-1, keepdims=True) + epsilon)
    scaled = values * r
    inner = grad * gain
    grad_values = r * (inner - scaled * jnp.mean(inner * scaled, axis=-1, keepdims=True))
    return grad_values, jnp.sum(grad * scaled, axis=0, keepdims=True)


def middle_kernel(
    lines,
    gains,
    cot_in,
    w_rows_in,
    own,
    middle,
    w_columns,
    grad_middle_out,
    gain_out,
    grads_dst,
    down_out,
    normed_all_out,
    result_parts,
    normed_all,
    weights,
    grad_hidden,
    hidden,
    parts,
    side,
    chain,
    down_near,
    down_stage,
    down_far,
    cot_all,
    w_rows,
    grads_out,
    put_sems,
    fetch_sems,
    gather_sems,
    column_sems,
    sum_sems,
    down_sems,
    own_sems,
):
    p = Place(lines)
    rows, width = own.shape
    two = 2 * rows
    padded = hidden.shape[2]
    shard = width // 4
    tile = 256 if padded % 256 == 0 else 128
    fetch = Fetch(((cot_in, cot_all), (w_rows_in, w_rows)), fetch_sems)
    p.barrier()

    columns = GroupGather(p, w_columns, weights, column_sems, own_sems.at[0], column_sems.shape[1])
    gather = LineGather(p, own, normed_all, gather_sems)
    gather.start()
    for i in range(columns.pieces):
        columns.give(i)
    columns.local().start()
    own_local = pltpu.make_async_copy(own, normed_all.at[p.c], own_sems.at[2 + lines])
    own_local.start()
    middle_local = pltpu.make_async_copy(middle, grad_middle_out, own_sems.at[3 + lines])
    middle_local.start()

    def hidden_grad(line):
        def one(i, carry):
            cols = pl.ds(pl.multiple_of(i * tile, 128), tile)
            left = cot_all[pl.ds(2 * line, 2)].reshape(two, width)
            right = w_rows[pl.ds(pl.multiple_of(i * tile, 16), tile)]
            grad_hidden[line, :, cols] = contract_rows(left, right)
            return carry

        lax.fori_loop(0, padded // tile, one, 0)

    fetch.wait(0, 1)
    done = 0
    for step in range(lines - 1):
        hidden_grad(done)
        done += 1
        gather.step(step)
        if step < columns.pieces:
            columns.pass_on(step)
    for i in range(lines - 1, columns.pieces):
        columns.pass_on(i)
    while done < lines:
        hidden_grad(done)
        done += 1
    gather.finish()
    own_local.wait()
    columns.local().wait()
    for i in range(columns.pieces):
        columns.finish(i)
    normed_local = pltpu.make_async_copy(normed_all, normed_all_out, own_sems.at[1])
    normed_local.start()

    line_sums = [
        LineSum(p, parts.at[i], side.at[i], chain.at[i], sum_sems.at[i]) for i in range(2)
    ]

    def near(turn):
        for line_sum in line_sums:
            line_sum.near(turn, 0)

    def far(turn):
        for line_sum in line_sums:
            line_sum.far(turn)

    def feed_forward(turn):
        line = line_sums[0].order(turn)

        def one(i, carry):
            cols = pl.ds(pl.multiple_of(i * tile, 128), tile)
            up_cols = pl.ds(pl.multiple_of(i * tile + padded, 128), tile)
            left = normed_all[pl.ds(2 * line, 2)].reshape(two, width)
            gate = jnp.dot(
                left, weights[:, :, cols].reshape(width, tile), preferred_element_type=f32
            )
            up = jnp.dot(
                left, weights[:, :, up_cols].reshape(width, tile), preferred_element_type=f32
            )
            gelu, slope = gelu_parts(gate)
            grad = grad_hidden[line, :, cols]
            hidden[line, :, cols] = (gelu * up).astype(bf16)
            grads_out[line, :, cols] = (grad * up * slope).astype(bf16)
            grads_out[line, :, up_cols] = (grad * gelu).astype(bf16)
            return carry

        lax.fori_loop(0, padded // tile, one, 0, unroll=True)

        def back(g, carry):
            product = contract_rows(grads_out[line], weights[g]).astype(bf16)
            cols = pl.ds(pl.multiple_of(g % 2 * shard, 128), shard)
            parts[g // 2, pl.ds(2 * line, 2), :, cols] = product.reshape(2, rows, shard)
            return carry

        pltpu.make_async_copy(grads_out.at[line], grads_dst.at[line], put_sems.at[turn]).start()
        for half in range(2):
            lax.fori_loop(2 * half, 2 * half + 2, back, 0, unroll=True)
            line_sums[half].across(turn).start()

    result_stage = normed_all

    def result_copy(line):
        blocks = pl.ds(2 * line, 2)
        return pltpu.make_async_copy(
            result_stage.at[blocks], result_parts.at[blocks], own_sems.at[2 + line]
        )

    def result_part(line):
        def one(i, carry):
            cols = pl.ds(pl.multiple_of(i * shard, 128), shard)
            product = jnp.dot(
                hidden[line], w_rows[:, cols], preferred_element_type=f32
            ).astype(bf16)
            result_stage[pl.ds(2 * line, 2), :, cols] = product.reshape(2, rows, shard)
            return carry

        lax.fori_loop(0, 4, one, 0, unroll=True)
        result_copy(line).start()

    quarter = padded // 4
    every = slice(None)
    down_parts = weights.at[:, pl.ds(0, quarter), pl.ds(0, shard)]

    def down_group(i):
        return GroupSum(p, down_parts, down_near.at[i], down_stage.at[i % 2], down_far.at[i], down_sems)

    def down_chunk(i):
        def one(g, carry):
            cols = pl.ds(pl.multiple_of(g * shard, 128), shard)
            left = hidden[:, :, i * quarter : (i + 1) * quarter].reshape(lines * two, quarter)
            right = cot_all[:, :, cols].reshape(lines * two, shard)
            down_parts[g] = contract_tokens(left, right).astype(bf16)
            return carry

        lax.fori_loop(0, 4, one, 0, unroll=True)
        down_out[i] = down_parts[p.f]
        down_group(i).give(i, every)

    for turn in range(lines):
        feed_forward(turn)
        if turn == lines - 2:
            near(0)
    normed_local.wait()
    for turn in range(lines):
        line = line_sums[0].order(turn)
        pltpu.make_async_copy(grads_out.at[line], grads_dst.at[line], put_sems.at[turn]).wait()

    for i in range(4):
        if i >= 1:
            down_group(i - 1).given(i - 1, every)
        if i >= 2:
            down_group(i - 2).passed(i - 2, every)
        down_chunk(i)
        down_group(i).pass_on(i, every)
        if i == 1:
            if lines > 2:
                near(1)
            far(0)
        if i == 2 and lines > 3:
            near(2)
            far(1)
            far(2)
    for line in range(lines):
        result_part(line)
    for turn in range(3, lines - 1):
        near(turn)
        far(turn)
    near(lines - 1)
    far(lines - 1)
    grad = jnp.concatenate([line_sum.total() for line_sum in line_sums], axis=1)
    middle_local.wait()
    grad_values, gain = norm_back(grad_middle_out[...], gains[1:2], grad)
    grad_middle_out[...] = cot_all[p.c].astype(f32) + grad_values
    gain_out[...] = gain
    for i in range(2):
        down_out[i] = down_group(i).take(i, every, down_out[i]).astype(bf16)
    for i in (2, 3):
        down_out[i] = down_group(i).take(i, every, down_out[i]).astype(bf16)
        down_group(i).passed(i, every)
    down_group(3).given(3, every)
    for line in range(lines):
        result_copy(line).wait()
    for line_sum in line_sums:
        line_sum.finish()


def middle_bytes(lines, rows, width, padded):
    length = 2 * lines * rows
    return (
        14 * rows * width
        + 9 * length * width
        + 9 * padded * width
        + 10 * length * padded
    )


def middle_part(lines, operands, padded):
    own = operands[3]
    rows, width = own.shape
    places = 2 * lines
    shard = width // 4
    quarter = padded // 4
    pieces = 4
    in_vmem = pl.BlockSpec(memory_space=VMEM)
    anywhere = pl.BlockSpec(memory_space=pl.ANY)
    shape = jax.ShapeDtypeStruct
    return pl.pallas_call(
        functools.partial(middle_kernel, lines),
        out_shape=(
            shape((rows, width), f32),
            shape((1, width), f32),
            shape((lines, 2 * rows, 2 * padded), bf16),
            shape((4, quarter, shard), bf16),
            shape((places, rows, width), bf16),
            shape((places, rows, width), bf16),
        ),
        in_specs=[in_vmem] + [anywhere] * 5,
        out_specs=[in_vmem] * 2 + [anywhere, in_vmem] + [anywhere] * 2,
        scratch_shapes=[
            VMEM((places, rows, width), bf16),
            VMEM((4, shard, 2 * padded), bf16),
            VMEM((lines, 2 * rows, padded), f32),
            VMEM((lines, 2 * rows, padded), bf16),
            VMEM((2, places, rows, width // 2), bf16),
            VMEM((2, lines, rows, width // 2), bf16),
            VMEM((2, 2, lines - 1, rows, width // 2), bf16),
            VMEM((4, 2, quarter, shard), bf16),
            VMEM((2, quarter, shard), bf16),
            VMEM((4, quarter, shard), bf16),
            *held(operands[1:3]),
            VMEM((lines, 2 * rows, 2 * padded), bf16),
            DMA((lines,)),
            DMA((2,)),
            DMA((LineGather.sems, lines)),
            DMA((GroupGather.sems, pieces)),
            DMA((2, LineSum.sems, lines)),
            DMA((GroupSum.sems, 4)),
            DMA((4 + lines,)),
        ],
        compiler_params=pltpu.CompilerParams(
            collective_id=1, has_side_effects=True, vmem_limit_bytes=vmem_bytes
        ),
        name="middle",
    )(*operands)


def is_long(length):
    return length > 2048


def back_kernel(
    lines,
    with_result,
    grad_middle,
    tokens,
    gains,
    cosine,
    sine,
    w_out_in,
    probs_in,
    keyval_in,
    queries_in,
    mixed_in,
    w_query_in,
    w_keyval_in,
    down_in,
    *rest,
):
    if with_result:
        middle, result_in, result_out, *rest = rest
    (
        input_grad_out,
        gain_out,
        linear_out,
        out_slots,
        down_out,
        branch_all,
        linear_all,
        branch,
        linear,
        trade_parts,
        trade_slots,
        grad_mixed,
        kv_total,
        kv_parts,
        kv_side,
        kv_chain,
        out_stage,
        w_out,
        probs,
        keyval,
        queries,
        mixed,
        w_query,
        w_keyval,
        fetch_sems,
        branch_sems,
        linear_sems,
        trade_sems,
        kv_sems,
        out_sems,
        piece_sems,
        own_sems,
        *rest,
    ) = rest
    p = Place(lines)
    rows, width = grad_middle.shape
    heads = queries.shape[0]
    length = probs_in.shape[2]
    long = is_long(length)
    operands = [
        (w_out_in, w_out),
        (keyval_in, keyval),
        (queries_in, queries),
        (mixed_in, mixed),
        (w_query_in, w_query),
        (w_keyval_in, w_keyval),
    ]
    fetch = Fetch(operands if long else operands + [(probs_in, probs)], fetch_sems)
    shard = w_out.shape[0]
    kv_width = 2 * HD
    per_owner = 2 * lines // 4
    others = [(jnp.full((), True), {"ctx": (p.c + d) % (2 * lines)}) for d in range(1, 2 * lines)]
    p.barrier(ctx=False, also=others)
    if with_result:
        result_parts, result_side, result_chain, result_sems = rest
        result_sum = Turns(
            LineSum(p, result_parts, result_side, result_chain, result_sems), lines
        )
        half = width // 2
        result_copies = [
            pltpu.make_async_copy(
                result_in.at[:, :, pl.ds(i * half, half)], result_parts.at[i], own_sems.at[2 + i]
            )
            for i in range(2)
        ]
        for copy in result_copies:
            copy.start()
        result_sums = [
            Turns(
                LineSum(
                    p, result_parts.at[i], result_side.at[i], result_chain.at[i], result_sems.at[i]
                ),
                lines,
            )
            for i in range(2)
        ]
    out_scatter = GroupScatter(p, per_owner, out_stage, out_slots, out_sems)

    branch[...] = grad_middle[...].astype(bf16)
    group = GroupGather(p, branch, branch_all, branch_sems, own_sems.at[0], 1)
    group.give(0)
    group.local().start()
    down_move = PieceMove(p, per_owner, down_in, down_out, piece_sems)
    down_move.start()
    if with_result:
        result_copies[0].wait()
        result_sums[0].start()
    back_trade = GroupReturn(p, trade_parts.at[0], trade_slots.at[0], trade_sems.at[0])

    def mixed_back(g):
        trade_parts[0, g] = contract_rows(branch_all[g], w_out[...]).astype(bf16)

    group.local().wait()
    fetch.wait(0)
    mixed_back(p.f)
    back_trade.own().start()
    group.near(0)
    mixed_back(p.twin_f)
    group.pass_on(0)
    mixed_back(p.cross_f)
    back_trade.send(2)
    group.last(0)
    mixed_back(p.diag_f)
    back_trade.send(1)
    back_trade.send(3)

    def out_block(i, g):
        left = mixed[...].reshape(4 * rows, shard)
        right = branch_all[:, :, pl.ds(pl.multiple_of(g * shard, 128), shard)]
        product = contract_tokens(left, right.reshape(4 * rows, shard)).astype(bf16)
        out_stage[i] = product.reshape(out_stage.shape[1:])

    fetch.wait(3)
    out_block(1, p.cross_f)
    out_scatter.copy(1, 0).start()
    out_block(0, p.twin_f)
    out_scatter.send(0)
    out_block(2, p.diag_f)
    out_block(3, p.f)
    out_own = pltpu.make_async_copy(out_stage.at[3], out_scatter.own(), own_sems.at[7])
    out_own.start()
    if with_result:
        result_sums[0].near(2)
        result_copies[1].wait()
        result_sums[1].sum.start(1)
    back_trade.wait()
    for g in range(4):
        grad_mixed[:, g * shard : (g + 1) * shard] = trade_slots[0, g]

    kv_total[...] = jnp.zeros_like(kv_total)
    kv_at, q_at = pl.ds(0, kv_width), pl.ds(kv_width, heads * HD)

    batch = 1 if long else 2
    fetch.wait(1, 2)
    if not long:
        fetch.wait(6)

    def some_heads(i, carry):
        keys = keyval[0].reshape(length, HD)
        values = keyval[1].reshape(length, HD)
        at = [pl.multiple_of((i * batch + h) * HD, 128) for h in range(batch)]
        outer = jnp.concatenate([grad_mixed[:, pl.ds(a, HD)] for a in at], axis=0)
        if batch == 1:
            one = pltpu.make_async_copy(probs_in.at[i], probs, own_sems.at[5])
            one.start()
            one.wait()
            weights = probs[...]
        else:
            weights = probs[pl.ds(batch * i, batch)].reshape(batch * rows, length)
        wide = weights.astype(f32)
        grad_weights = contract_rows(outer, values)
        delta = jnp.sum(wide * grad_weights, axis=-1, keepdims=True)
        grad_scores = (wide * (grad_weights - delta)).astype(bf16)
        product = jnp.dot(grad_scores, keys, preferred_element_type=f32) * HD**-0.5
        for h in range(batch):
            turned = rotated(product[h * rows : (h + 1) * rows], cosine[...], -sine[...])
            linear[:, pl.ds(kv_width + at[h], HD)] = turned.astype(bf16)
        two = queries[pl.ds(batch * i, batch)].reshape(batch * rows, HD)
        kv_total[:, :HD] += contract_tokens(grad_scores, two)
        kv_total[:, HD:] += contract_tokens(weights, outer)
        return carry

    lax.fori_loop(0, heads // batch, some_heads, 0)
    linear_group = GroupGather(
        p, linear, linear_all, linear_sems, own_sems.at[1], 2, (q_at, kv_at)
    )
    linear_group.give(0)
    out_scatter.copy(1, 1).start()
    kv_parts[...] = kv_total[...].astype(bf16).reshape(kv_parts.shape)
    kv_sum = LineSum(p, kv_parts, kv_side, kv_chain, kv_sems)
    kv_sum.start(lines)
    if with_result:
        for turn in range(1, lines):
            result_sums[1].sum.across(turn).start()
        result_sums[0].near(lines)
        result_sums[0].far(1)
    kv_sum.turns(0)
    own = kv_sum.total()
    linear[:, :HD] = rotated(own[:, :HD], cosine[...], -sine[...]).astype(bf16)
    linear[:, pl.ds(HD, HD)] = own[:, HD:].astype(bf16)
    linear_group.give(1)
    out_scatter.copy(2, 0).start()
    linear_group.local().start()
    if with_result:
        result_sums[0].far(2)
        result_sums[1].near(2)
    fetch.wait(4, 5)
    linear_group.pass_on(0)
    linear_group.pass_on(1)
    linear_group.local().wait()
    for i in range(2):
        linear_group.near(i)
        linear_group.last(i)

    linear_copy = pltpu.make_async_copy(linear_all, linear_out, own_sems.at[4])
    linear_copy.start()

    last_trade = GroupReturn(p, trade_parts.at[1], trade_slots.at[1], trade_sems.at[1])

    def normed_back(g):
        product = contract_rows(linear_all[g, :, kv_at], w_keyval[...])
        product += contract_rows(linear_all[g, :, q_at], w_query[...])
        trade_parts[1, g] = product.astype(bf16)

    normed_back(p.cross_f)
    last_trade.send(2)
    normed_back(p.diag_f)
    normed_back(p.twin_f)
    last_trade.send(1)
    last_trade.send(3)
    out_scatter.copy(2, 1).start()
    normed_back(p.f)
    last_trade.own().start()
    if with_result:
        result_sums[0].far(3)
        result_sums[1].far(2)
    last_trade.wait()
    for g in range(4):
        grad_mixed[:, g * shard : (g + 1) * shard] = trade_slots[1, g]
    source = tokens[...].astype(f32)
    grad_values, gain = norm_back(source, gains[0:1], grad_mixed[...].astype(f32))
    input_grad_out[...] = (grad_middle[...] + grad_values).astype(bf16)
    gain_out[...] = gain
    if with_result:
        for i in range(2):
            cols = pl.ds(i * half, half)
            result_out[:, cols] = (middle[:, cols] + result_sums[i].total()).astype(bf16)
            result_sums[i].sum.finish()
    back_trade.finish()
    last_trade.finish()
    group.sent(0)
    linear_group.sent(0)
    linear_group.sent(1)
    kv_sum.finish()
    out_own.wait()
    for kind in range(3):
        out_scatter.arrived(kind)
    out_scatter.sent()
    linear_copy.wait()
    down_move.finish()


def back(lines, operands, result_operands):
    rows, width = operands[0].shape
    heads = operands[8].shape[0]
    places = 2 * lines
    length = places * rows
    shard = width // 4
    linear_width = width + 2 * HD
    tall = width // places
    pieces = operands[12].shape
    in_vmem = pl.BlockSpec(memory_space=VMEM)
    anywhere = pl.BlockSpec(memory_space=pl.ANY)
    shape = jax.ShapeDtypeStruct
    with_result = bool(result_operands)
    long = is_long(length)
    scratch = held(operands[5:12])
    if long:
        scratch[1] = VMEM((rows, length), bf16)
    result_scratch = [
        VMEM((2, places, rows, width // 2), bf16),
        VMEM((2, lines, rows, width // 2), bf16),
        VMEM((2, 2, lines - 1, rows, width // 2), bf16),
        DMA((2, LineSum.sems, lines)),
    ]
    return pl.pallas_call(
        functools.partial(back_kernel, lines, with_result),
        out_shape=((shape((rows, width), bf16),) if with_result else ())
        + (
            shape((rows, width), bf16),
            shape((1, width), f32),
            shape((4, rows, linear_width), bf16),
            shape((places, tall, shard), bf16),
            shape(pieces, bf16),
        ),
        in_specs=[in_vmem] * 5 + [anywhere] * 8 + ([in_vmem, anywhere] if with_result else []),
        out_specs=[in_vmem] * (3 if with_result else 2) + [anywhere] * 3,
        scratch_shapes=[
            VMEM((4, rows, width), bf16),
            VMEM((4, rows, linear_width), bf16),
            VMEM((rows, width), bf16),
            VMEM((rows, linear_width), bf16),
            VMEM((2, 4, rows, shard), bf16),
            VMEM((2, 4, rows, shard), bf16),
            VMEM((rows, width), bf16),
            VMEM((length, 2 * HD), f32),
            VMEM((places, rows, 2 * HD), bf16),
            VMEM((lines, rows, 2 * HD), bf16),
            VMEM((2, lines - 1, rows, 2 * HD), bf16),
            VMEM((4, places // 4, tall, shard), bf16),
            *scratch,
            DMA((7,)),
            DMA((GroupGather.sems, 1)),
            DMA((GroupGather.sems, 2)),
            DMA((2, GroupTrade.sems, 4)),
            DMA((LineSum.sems, lines)),
            DMA((GroupScatter.sems, 3)),
            DMA((3, 4)),
            DMA((8,)),
        ]
        + (result_scratch if with_result else []),
        compiler_params=pltpu.CompilerParams(
            collective_id=2, has_side_effects=True, vmem_limit_bytes=vmem_bytes
        ),
        name="back",
    )(*operands, *result_operands)


def grads_kernel(lines, with_columns, gain_one, gain_two, out_in, normed_in, linear_in, *rest):
    if with_columns:
        normed_two_in, hidden_grads_in, *rest = rest
    projection_out, gains_out, out_out, *rest = rest
    if with_columns:
        columns_out, *rest = rest
    (
        parts,
        side,
        chain,
        stage,
        out_parts,
        out_side,
        out_chain,
        gain_parts,
        gain_side,
        gain_chain,
        gain_slots,
        normed,
        linear_all,
        fetch_sems,
        projection_sems,
        out_sems,
        gain_sems,
        slot_sems,
        scatter_sems,
        *rest,
    ) = rest
    p = Place(lines)
    operands = [(out_in, out_parts)]
    if with_columns:
        (
            chunk_parts,
            near,
            passing,
            far,
            chunks,
            group_sems,
            trade_sems,
            normed_two,
            hidden_grads,
        ) = rest
    if with_columns:
        operands += [(normed_two_in, normed_two), (hidden_grads_in, hidden_grads)]
    operands += [(normed_in, normed), (linear_in, linear_all)]
    fetch = Fetch(operands, fetch_sems)
    places = 2 * lines
    shard = normed.shape[2]
    tokens = 4 * normed.shape[1]
    per_owner = places // 4
    tall = shard // per_owner
    kv_share = 2 * HD // 4
    others = [(jnp.full((), True), {"ctx": (p.c + d) % places}) for d in range(1, places)]
    p.barrier(ctx=False, also=others)

    for c in range(places):
        cols = slice(c * tall, (c + 1) * tall)
        gain_parts[c, 0:1, :tall] = gain_one[:, cols]
        gain_parts[c, 1:2, :tall] = gain_two[:, cols]
    gain_sum = LineSum(p, gain_parts, gain_side, gain_chain, gain_sems)
    gain_sum.start(lines)

    projection_sums = [
        Turns(
            LineSum(p, parts.at[i], side.at[i], chain.at[i], projection_sems.at[i]), lines
        )
        for i in range(2)
    ]
    out_sum = Turns(LineSum(p, out_parts, out_side, out_chain, out_sems))
    fetch.wait(0)
    out_sum.start()

    if with_columns:
        fetch.wait(1, 2)
        block = columns_out.shape[2]
        chunk = chunk_parts.shape[1]
        every = slice(None)

        def chunk_of(k):
            order = sorted(range(lines), key=lambda d: (d == 0, abs(d - lines // 2), d))
            return (p.line + order[k]) % lines

        def group(k):
            return GroupSum(p, chunk_parts, near.at[k], passing.at[k % 2], far.at[k], group_sems)

        def compute(k):
            cols = pl.ds(pl.multiple_of(chunk_of(k) * chunk, 128), chunk)

            def one(g, carry):
                left = normed_two[:, :, cols].reshape(-1, chunk)
                right = hidden_grads[:, :, pl.ds(pl.multiple_of(g * block, 128), block)]
                chunk_parts[g] = contract_tokens(left, right.reshape(-1, block)).astype(bf16)
                return carry

            lax.fori_loop(0, 4, one, 0)
            chunks[k] = chunk_parts[p.f]
            group(k).give(k, every)

        def halves(k):
            half = chunk // 2
            for lane in range(2):
                yield lane, 2 * chunk_of(k) + lane, chunks.at[k, pl.ds(lane * half, half)]

        def place_copy(k, lane, dest, src):
            return remote(
                src,
                columns_out.at[p.c],
                trade_sems.at[0, 2 * k + lane],
                trade_sems.at[1, p.c],
                {"ctx": dest},
            )

        def place_own(src):
            return pltpu.make_async_copy(src, columns_out.at[p.c], trade_sems.at[2, 0])

        def arrival(i):
            slot = columns_out.at[i]
            return remote(slot, slot, trade_sems.at[0, 0], trade_sems.at[1, i], p.beside)

        def complete(k):
            chunks[k] = group(k).take(k, every, chunks[k]).astype(bf16)
            for lane, dest, src in halves(k):
                pl.when(dest != p.c)(
                    lambda k=k, lane=lane, dest=dest, src=src: place_copy(k, lane, dest, src).start()
                )
                pl.when(dest == p.c)(lambda src=src: place_own(src).start())

        def chunk_step(k):
            if k >= 1:
                group(k - 1).given(k - 1, every)
            compute(k)
            if k >= 2:
                group(k - 2).passed(k - 2, every)
            group(k).pass_on(k, every)

        chunk_step(0)

    scatters = [
        GroupScatter(p, per_owner, stage.at[i], parts.at[i], scatter_sems.at[i]) for i in range(2)
    ]

    def projection_block(first, second, g):
        left = normed[...].reshape(tokens, shard)
        right = linear_all[:, :, pl.ds(pl.multiple_of(2 * HD + g * shard, 128), shard)]
        product = contract_tokens(left, right.reshape(tokens, shard)).astype(bf16)
        right = linear_all[:, :, pl.ds(pl.multiple_of(g * kv_share, 128), kv_share)]
        kv_product = contract_tokens(left, right.reshape(tokens, kv_share)).astype(bf16)
        first[...] = product[:, :half].reshape(per_owner, tall, half)
        if half < shard:
            kv_product = jnp.concatenate([product[:, half:], kv_product], axis=1)
        second[...] = kv_product.reshape(per_owner, tall, half)

    half = (shard + kv_share) // 2
    fetch.wait(*((3, 4) if with_columns else (1, 2)))
    for kind in (1, 2, 0):
        projection_block(stage.at[0, kind], stage.at[1, kind], scatters[0].places[kind])
        scatters[0].send(kind)
    for kind in (1, 2, 0):
        scatters[1].send(kind)
    projection_block(scatters[0].own(), scatters[1].own(), p.f)

    first, second = projection_sums
    if with_columns:
        chunk_step(1)
    out_sum.near(2)
    out_sum.far(1)
    if with_columns:
        complete(0)
        if lines > 2:
            chunk_step(2)
    out_sum.near(lines)
    for k in range(lines):
        gain_sum.near(k, 0)
    for kind in range(3):
        scatters[0].arrived(kind)
    first.start()
    out_sum.far(2)
    first.near(2)
    out_sum.far(3)
    first.near(lines)
    for kind in range(3):
        scatters[1].arrived(kind)
    second.start()
    first.far(1)
    for k in range(lines):
        gain_sum.far(k)
    out_out[...] = out_sum.total().astype(bf16)
    first.far(2)
    if with_columns:
        second.near(1)
        for k in range(1, lines):
            complete(k)
            if k + 2 < lines:
                chunk_step(k + 2)
            if k == 1:
                first.far(lines)
                second.near(lines)
            second.far(k + 1)
        for k in (lines - 2, lines - 1):
            group(k).passed(k, every)
        group(lines - 1).given(lines - 1, every)

    own = gain_sum.total()
    gain_parts[p.c] = own

    def gain_copy(d):
        return remote(
            gain_parts.at[p.c],
            gain_slots.at[d],
            slot_sems.at[0, d],
            slot_sems.at[1, d],
            {"fsdp": (p.f + d) % 4},
        )

    for d in (1, 2, 3):
        gain_copy(d).start()
    for i in range(2):
        projection_out[:, i * half : (i + 1) * half] = projection_sums[i].total().astype(bf16)
    for d in (1, 2, 3):
        gain_copy(d).wait_recv()
        own = own + gain_slots[d]
    gains_out[...] = own

    for d in (1, 2, 3):
        gain_copy(d).wait_send()
    if with_columns:
        for k in range(lines):
            for lane, dest, src in halves(k):
                pl.when(dest != p.c)(
                    lambda k=k, lane=lane, dest=dest, src=src: place_copy(k, lane, dest, src).wait_send()
                )
                pl.when(dest == p.c)(lambda src=src: place_own(src).wait())
        for i in range(places):
            pl.when(p.c != i)(lambda i=i: arrival(i).wait_recv())
    gain_sum.finish()
    for projection_sum in projection_sums:
        projection_sum.sum.finish()
    out_sum.sum.finish()
    for scatter in scatters:
        scatter.sent()


def weight_grads(lines, operands, column_operands):
    rows, shard = operands[3].shape[1:]
    width = 4 * shard
    places = 2 * lines
    tall = width // places
    wide = shard + 2 * HD // 4
    gain_wide = -(-tall // 128) * 128
    in_vmem = pl.BlockSpec(memory_space=VMEM)
    anywhere = pl.BlockSpec(memory_space=pl.ANY)
    shape = jax.ShapeDtypeStruct
    with_columns = bool(column_operands)
    column_shapes, column_scratch = (), []
    if with_columns:
        block = column_operands[1].shape[2] // 4
        chunk = width // lines
        column_shapes = (shape((places, chunk // 2, block), bf16),)
        column_scratch = [
            VMEM((4, chunk, block), bf16),
            VMEM((lines, 2, chunk, block), bf16),
            VMEM((2, chunk, block), bf16),
            VMEM((lines, chunk, block), bf16),
            VMEM((lines, chunk, block), bf16),
            DMA((GroupSum.sems, lines)),
            DMA((3, places)),
            *held(column_operands),
        ]
    return pl.pallas_call(
        functools.partial(grads_kernel, lines, with_columns),
        out_shape=(shape((tall, wide), bf16), shape((8, gain_wide), f32), shape((tall, shard), bf16)) + column_shapes,
        in_specs=[in_vmem] * 2 + [anywhere] * (3 + len(column_operands)),
        out_specs=[in_vmem] * 3 + [anywhere] * len(column_shapes),
        scratch_shapes=[
            VMEM((2, places, tall, wide // 2), bf16),
            VMEM((2, lines, tall, wide // 2), bf16),
            VMEM((2, 2, lines - 1, tall, wide // 2), bf16),
            VMEM((2, 3, places // 4, tall, wide // 2), bf16),
            VMEM((places, tall, shard), bf16),
            VMEM((lines, tall, shard), bf16),
            VMEM((2, lines - 1, tall, shard), bf16),
            VMEM((places, 8, gain_wide), f32),
            VMEM((lines, 8, gain_wide), f32),
            VMEM((2, lines - 1, 8, gain_wide), f32),
            VMEM((4, 8, gain_wide), f32),
            *held(operands[3:5]),
            DMA((5,)),
            DMA((2, LineSum.sems, lines)),
            DMA((LineSum.sems, lines)),
            DMA((LineSum.sems, lines)),
            DMA((2, 4)),
            DMA((2, GroupScatter.sems, 3)),
        ]
        + column_scratch,
        compiler_params=pltpu.CompilerParams(
            collective_id=3, has_side_effects=True, vmem_limit_bytes=vmem_bytes
        ),
        name="grads",
    )(*operands, *column_operands)


def assemble_kernel(lines, piece, projection, out, down, columns, *outs):
    query_out, keyval_out, out_out, down_out, columns_out = outs
    shard = out.shape[1]
    padded_piece = columns.shape[2] // 2
    query_out[...] = projection[:, :shard].astype(f32)
    keyval_out[...] = projection[:, shard:].astype(f32)
    out_out[...] = out[...].astype(f32)
    for i in range(down.shape[0]):
        down_out[i * piece : (i + 1) * piece] = down[i, :piece].astype(f32)
    pieces = [
        columns[place_of_piece(n, lines), :, q * padded_piece : q * padded_piece + piece]
        for q in range(2)
        for n in range(2 * lines)
    ]
    columns_out[...] = jnp.concatenate(pieces, axis=1).astype(f32)


def assemble(lines, piece, projection, out, down, columns):
    tall, wide = projection.shape
    shard = out.shape[1]
    places = 2 * lines
    block = columns.shape[2]
    steps = 4 if tall % 64 == 0 else 1
    run = tall // steps
    full = 2 * places * piece

    def flat(rows, cols):
        return pl.BlockSpec((rows, cols), lambda i: (i, 0))

    shape = jax.ShapeDtypeStruct
    return pl.pallas_call(
        functools.partial(assemble_kernel, lines, piece),
        grid=(steps,),
        out_shape=(
            shape((tall, shard), f32),
            shape((tall, wide - shard), f32),
            shape((tall, shard), f32),
            shape((4 * piece, shard), f32),
            shape((tall, full), f32),
        ),
        in_specs=[
            flat(run, wide),
            flat(run, shard),
            pl.BlockSpec((4 // steps, down.shape[1], shard), lambda i: (i, 0, 0)),
            pl.BlockSpec((places, run, block), lambda i: (0, i, 0)),
        ],
        out_specs=[
            flat(run, shard),
            flat(run, wide - shard),
            flat(run, shard),
            flat(4 // steps * piece, shard),
            flat(run, full),
        ],
        compiler_params=pltpu.CompilerParams(vmem_limit_bytes=vmem_bytes),
        name="assemble",
    )(projection, out, down, columns)


def per_device(
    tokens,
    doc_bounds,
    cotangent,
    norm_one,
    query_weight,
    keyval_weight,
    out_weight,
    norm_two,
    gate_up_weight,
    down_weight,
):
    ctx_size = lax.axis_size("ctx")
    fsdp_size = lax.axis_size("fsdp")
    lines = ctx_size // 2
    rows = tokens.shape[1]
    width = tokens.shape[2]
    length = rows * ctx_size
    inner_width = query_weight.shape[1]
    head_count = inner_width // HD
    hidden_width = gate_up_weight.shape[1] // 2
    piece = hidden_width // (ctx_size * fsdp_size)
    padded_piece = -(-piece // 32) * 32
    padded = padded_piece * fsdp_size
    gains = jnp.stack([norm_one, norm_two])
    cot_rows = cotangent[0]
    down_rows = down_weight
    if piece % 16:
        first = hidden_piece(lax.axis_index("ctx"), lines) * piece
        down_rows = lax.dynamic_slice_in_dim(down_weight, first, piece, 0)
        down_rows = jnp.pad(down_rows, ((0, padded_piece - piece), (0, 0)))
    (
        normed,
        queries,
        window,
        weights,
        mixed,
        middle,
        normed_two,
        cosine,
        sine,
        w_columns,
        cot_all,
        w_down,
    ) = front(
        lines,
        (
            doc_bounds,
            tokens[0],
            gains,
            keyval_weight,
            query_weight,
            out_weight,
            cot_rows,
            down_rows,
            gate_up_weight,
        ),
        head_count,
        padded_piece,
    )
    w_down = w_down.reshape(padded, width)
    fits = middle_bytes(lines, rows, width, padded) <= vmem_bytes
    if fits:
        grad_middle, gain_two_term, grad_gate_up, down_part, normed_two, result_parts = middle_part(
            lines, (gains, cot_all, w_down, normed_two, middle, w_columns), padded
        )
    else:
        cot_all = cot_all.reshape(length, width)
        normed_two = lax.all_gather(normed_two, "ctx", axis=0, tiled=True)
        w_gate_up = lax.all_gather(w_columns, "fsdp", axis=0, tiled=True)
        projected = jnp.dot(normed_two, w_gate_up, preferred_element_type=f32)
        gelu, slope = gelu_parts(projected[:, :padded])
        up_part = projected[:, padded:]
        hidden = (gelu * up_part).astype(bf16)
        grad_hidden = contract_rows(cot_all, w_down)
        grad_gate_up = jnp.concatenate(
            [grad_hidden * up_part * slope, grad_hidden * gelu], axis=1
        ).astype(bf16)
        grad_normed_two = lax.psum_scatter(
            contract_rows(grad_gate_up, w_gate_up).astype(bf16),
            "ctx",
            scatter_dimension=0,
            tiled=True,
        ).astype(f32)
        grad_middle_norm, gain_two_term = norm_back(middle, norm_two[None], grad_normed_two)
        grad_middle = cot_rows.astype(f32) + grad_middle_norm
        result_parts = jnp.dot(hidden, w_down, preferred_element_type=f32).astype(bf16)
        down_part = lax.psum_scatter(
            contract_tokens(hidden, cot_all).astype(bf16),
            "fsdp",
            scatter_dimension=1,
            tiled=True,
        ).reshape(fsdp_size, padded_piece, -1)
    operands = (
        grad_middle,
        tokens[0],
        gains,
        cosine,
        sine,
        out_weight,
        weights,
        window,
        queries,
        mixed,
        query_weight,
        keyval_weight,
        down_part,
    )
    if fits:
        result, input_grad, gain_one_term, grad_linear, out_parts, down_grad = back(
            lines, operands, (middle, result_parts)
        )
    else:
        input_grad, gain_one_term, grad_linear, out_parts, down_grad = back(lines, operands, ())
        branch_two = lax.psum_scatter(result_parts, "ctx", scatter_dimension=0, tiled=True)
        result = (middle + branch_two.astype(f32)).astype(bf16)

    operands = (gain_one_term, gain_two_term, out_parts, normed, grad_linear)
    if fits:
        projection_grad, gain_grads, out_grad, gate_up_part = weight_grads(
            lines, operands, (normed_two, grad_gate_up)
        )
    else:
        projection_grad, gain_grads, out_grad = weight_grads(lines, operands, ())
        gate_up_part = lax.psum_scatter(
            contract_tokens(normed_two, grad_gate_up).astype(bf16),
            "fsdp",
            scatter_dimension=1,
            tiled=True,
        )
        gate_up_part = lax.all_to_all(
            gate_up_part.reshape(ctx_size, width // ctx_size, -1), "ctx", 0, 0, tiled=True
        )
    query_grad, keyval_grad, out_grad, down_grad, gate_up_grad = assemble(
        lines, piece, projection_grad, out_grad, down_grad, gate_up_part
    )
    share = width // (ctx_size * fsdp_size)
    gains = lax.dynamic_slice_in_dim(gain_grads, lax.axis_index("fsdp") * share, share, 1)
    return (
        result[None],
        input_grad[None],
        gains[0],
        query_grad,
        keyval_grad,
        out_grad,
        gains[1],
        gate_up_grad,
        down_grad,
    )


def solution(mesh):
    placed = (
        P("fsdp", "ctx", None),
        P("fsdp", None),
        P("fsdp", "ctx", None),
        P(),
        P("fsdp", None),
        P("fsdp", None),
        P("fsdp", None),
        P(),
        P("fsdp", None),
        P("fsdp", None),
    )
    return jax.shard_map(
        per_device,
        mesh=mesh,
        in_specs=placed,
        out_specs=(
            P("fsdp", "ctx", None),
            P("fsdp", "ctx", None),
            P(("ctx", "fsdp")),
            P("ctx", "fsdp"),
            P("ctx", "fsdp"),
            P("ctx", "fsdp"),
            P(("ctx", "fsdp")),
            P("ctx", "fsdp"),
            P("ctx", "fsdp"),
        ),
        check_vma=False,
    )
```

```python
import functools
import math

import jax
import jax.numpy as jnp
from jax import lax
from jax.experimental import pallas as pl
from jax.experimental.pallas import tpu as pltpu
from jax.sharding import PartitionSpec as P

HD = 256
WINDOW = 2048


epsilon = 1e-06
f32 = jnp.float32
bf16 = jnp.bfloat16
VMEM = pltpu.VMEM
DMA = pltpu.SemaphoreType.DMA
vmem_bytes = 62 * 1024 * 1024


def rms_norm(values, gain):
    return values * lax.rsqrt(jnp.mean(values * values, axis=-1, keepdims=True) + epsilon) * gain


def documents(index, bounds):
    return (index >= bounds[0]).astype(jnp.int32) + (index >= bounds[1]).astype(jnp.int32)


def contract_rows(left, right):
    return lax.dot_general(
        left, right, (((1,), (1,)), ((), ())), preferred_element_type=jnp.float32
    )


def contract_tokens(left, right):
    return lax.dot_general(
        left, right, (((0,), (0,)), ((), ())), preferred_element_type=jnp.float32
    )


def remote(src, dst, send_sem, recv_sem, device):
    return pltpu.make_async_remote_copy(
        src_ref=src,
        dst_ref=dst,
        send_sem=send_sem,
        recv_sem=recv_sem,
        device_id=device,
        device_id_type=pl.DeviceIdType.MESH,
    )


class Place:
    def __init__(self, lines):
        self.lines = lines
        self.c = lax.axis_index("ctx")
        self.f = lax.axis_index("fsdp")
        self.line = self.c // 2
        self.lane = self.c % 2
        self.chip = self.f // 2
        self.core = self.f % 2
        self.twin_f = self.f + 1 - 2 * self.core
        self.cross_f = (self.f + 2) % 4
        self.diag_f = (self.twin_f + 2) % 4
        self.twin = {"fsdp": self.twin_f}
        self.cross = {"fsdp": self.cross_f}
        self.diag = {"fsdp": self.diag_f}
        self.beside = {"ctx": self.c + 1 - 2 * self.lane}
        self.right = {"ctx": self.c + 2}
        self.left = {"ctx": self.c - 2}
        self.has_right = self.line < lines - 1
        self.has_left = self.line > 0

    def barrier(self, ctx=True, fsdp=True, also=()):
        sem = pltpu.get_barrier_semaphore()

        def greet(device):
            pl.semaphore_signal(sem, 1, device_id=device, device_id_type=pl.DeviceIdType.MESH)

        count = 0
        if fsdp:
            for device in (self.twin, self.cross, self.diag):
                greet(device)
            count = 3
        if ctx:
            greet(self.beside)
            pl.when(self.has_right)(lambda: greet(self.right))
            pl.when(self.has_left)(lambda: greet(self.left))
            count = (
                count + 1 + self.has_right.astype(jnp.int32) + self.has_left.astype(jnp.int32)
            )
        for needed, device in also:
            pl.when(needed)(lambda device=device: greet(device))
            count = count + needed.astype(jnp.int32)
        pl.semaphore_wait(sem, count)


class Fetch:
    def __init__(self, pairs, sems):
        self.copies = [
            pltpu.make_async_copy(src, dst, sems.at[i]) for i, (src, dst) in enumerate(pairs)
        ]
        for copy in self.copies:
            copy.start()

    def wait(self, *which):
        for i in which:
            self.copies[i].wait()


def held(operands):
    return [VMEM(operand.shape, operand.dtype) for operand in operands]


class LineGather:
    sems = 6

    def __init__(self, place, own, slots, sems):
        self.p, self.own, self.slots, self.s = place, own, slots, sems

    def rightward(self, step):
        at = 2 * (self.p.line - step) + self.p.lane
        src = self.own if step == 0 else self.slots.at[at]
        return remote(src, self.slots.at[at], self.s.at[0, step], self.s.at[1, step], self.p.right)

    def leftward(self, step):
        at = 2 * (self.p.line + step) + self.p.lane
        src = self.own if step == 0 else self.slots.at[at]
        return remote(src, self.slots.at[at], self.s.at[2, step], self.s.at[3, step], self.p.left)

    def across(self, line, own=False):
        at = 2 * line + self.p.lane
        src = self.own if own else self.slots.at[at]
        return remote(
            src, self.slots.at[at], self.s.at[4, line], self.s.at[5, line], self.p.beside
        )

    def from_left(self, step):
        at = 2 * (self.p.line - 1 - step) + self.p.lane
        slot = self.slots.at[at]
        return remote(slot, slot, self.s.at[0, step], self.s.at[1, step], self.p.right)

    def from_right(self, step):
        at = 2 * (self.p.line + 1 + step) + self.p.lane
        slot = self.slots.at[at]
        return remote(slot, slot, self.s.at[2, step], self.s.at[3, step], self.p.left)

    def start(self):
        pl.when(self.p.has_right)(lambda: self.rightward(0).start())
        pl.when(self.p.has_left)(lambda: self.leftward(0).start())
        self.across(self.p.line, True).start()

    def step(self, step):
        p = self.p

        @pl.when(p.line - 1 - step >= 0)
        def _():
            self.from_left(step).wait_recv()
            if step + 1 < p.lines - 1:
                pl.when(p.has_right)(lambda: self.rightward(step + 1).start())
            self.across(p.line - 1 - step).start()

        @pl.when(p.line + 1 + step <= p.lines - 1)
        def _():
            self.from_right(step).wait_recv()
            if step + 1 < p.lines - 1:
                pl.when(p.has_left)(lambda: self.leftward(step + 1).start())
            self.across(p.line + 1 + step).start()

    def steps(self):
        for step in range(self.p.lines - 1):
            self.step(step)

    def arrived_across(self, line):
        at = 2 * line + 1 - self.p.lane
        slot = self.slots.at[at]
        remote(slot, slot, self.s.at[4, line], self.s.at[5, line], self.p.beside).wait_recv()

    def finish(self, arrivals=True):
        p = self.p
        if arrivals:
            for line in range(p.lines):
                self.arrived_across(line)
        for step in range(p.lines - 1):
            pl.when(p.has_right & (p.line - step >= 0))(
                lambda step=step: self.rightward(step).wait_send()
            )
            pl.when(p.has_left & (p.line + step <= p.lines - 1))(
                lambda step=step: self.leftward(step).wait_send()
            )
        for line in range(p.lines):
            self.across(line).wait_send()


class LineSum:
    sems = 6

    def __init__(self, place, parts, side, chain, sems):
        self.p, self.parts, self.side, self.chain, self.s = place, parts, side, chain, sems

    def order(self, turn):
        lines, line = self.p.lines, self.p.line
        value = 0
        for a in range(lines):
            far = sorted(range(lines), key=lambda t: (-abs(t - a), t))
            value = value + jnp.where(line == a, far[turn], 0)
        return value

    def across(self, turn):
        t = self.order(turn)
        at = 2 * t + 1 - self.p.lane
        return remote(
            self.parts.at[at],
            self.side.at[t],
            self.s.at[0, t],
            self.s.at[1, t],
            self.p.beside,
        )

    def rightward(self, t):
        step = self.p.lines - 1 - t
        return remote(
            self.parts.at[2 * t + self.p.lane],
            self.chain.at[0, step],
            self.s.at[2, step],
            self.s.at[3, step],
            self.p.right,
        )

    def leftward(self, t):
        return remote(
            self.parts.at[2 * t + self.p.lane],
            self.chain.at[1, t],
            self.s.at[4, t],
            self.s.at[5, t],
            self.p.left,
        )

    def add(self, at, other):
        self.parts[at] = (self.parts[at].astype(f32) + other.astype(f32)).astype(self.parts.dtype)

    def start(self, ahead=2):
        for turn in range(min(ahead, self.p.lines)):
            self.across(turn).start()

    def near(self, turn, ahead=2):
        p = self.p
        t = self.order(turn)
        at = 2 * t + p.lane
        self.across(turn).wait_recv()
        if ahead and turn + ahead < p.lines:
            self.across(turn + ahead).start()
        self.add(at, self.side[t])
        pl.when((t > p.line) & (p.line == 0))(lambda: self.rightward(t).start())
        pl.when((t < p.line) & (p.line == p.lines - 1))(lambda: self.leftward(t).start())

    def far(self, turn):
        p = self.p
        t = self.order(turn)
        at = 2 * t + p.lane

        @pl.when((t > p.line) & p.has_left)
        def _():
            self.rightward(t).wait_recv()
            self.add(at, self.chain[0, p.lines - 1 - t])
            self.rightward(t).start()

        @pl.when((t < p.line) & p.has_right)
        def _():
            self.leftward(t).wait_recv()
            self.add(at, self.chain[1, t])
            self.leftward(t).start()

    def turns(self, ahead=2):
        for turn in range(self.p.lines):
            self.near(turn, ahead)
            if turn > 0:
                self.far(turn - 1)
        self.far(self.p.lines - 1)

    def total(self):
        p = self.p
        at = 2 * p.line + p.lane

        @pl.when(p.has_left)
        def _():
            self.rightward(p.line).wait_recv()
            self.add(at, self.chain[0, p.lines - 1 - p.line])

        @pl.when(p.has_right)
        def _():
            self.leftward(p.line).wait_recv()
            self.add(at, self.chain[1, p.line])

        return self.parts[at].astype(f32)

    def finish(self):
        p = self.p
        for turn in range(p.lines):
            self.across(turn).wait_send()
        for t in range(p.lines):
            pl.when(t > p.line)(lambda t=t: self.rightward(t).wait_send())
            pl.when(t < p.line)(lambda t=t: self.leftward(t).wait_send())


class Turns:
    def __init__(self, line_sum, ahead=2):
        self.sum, self.ahead, self.nears, self.fars = line_sum, ahead, 0, 0

    def start(self):
        self.sum.start(self.ahead)

    def near(self, upto):
        while self.nears < min(upto, self.sum.p.lines):
            self.sum.near(self.nears, self.ahead)
            self.nears += 1

    def far(self, upto):
        while self.fars < min(upto, self.sum.p.lines):
            self.near(self.fars + 1)
            self.sum.far(self.fars)
            self.fars += 1

    def total(self):
        self.far(self.sum.p.lines)
        return self.sum.total()


class GroupSum:
    sems = 6

    def __init__(self, place, parts, near, out, far, sems):
        self.p, self.parts, self.near, self.out, self.far, self.s = place, parts, near, out, far, sems

    def to_twin(self, i, which, cols):
        p = self.p
        block = p.diag_f if which == 0 else p.twin_f
        return remote(
            self.parts.at[block, :, cols],
            self.near.at[which, :, cols],
            self.s.at[which, i],
            self.s.at[2 + which, i],
            p.twin,
        )

    def to_cross(self, i, cols):
        return remote(
            self.out.at[:, cols], self.far.at[:, cols], self.s.at[4, i], self.s.at[5, i], self.p.cross
        )

    def give(self, i, cols):
        self.to_twin(i, 0, cols).start()
        self.to_twin(i, 1, cols).start()

    def pass_on(self, i, cols):
        self.to_twin(i, 0, cols).wait_recv()
        mine = self.parts[self.p.cross_f, :, cols].astype(f32)
        self.out[:, cols] = (mine + self.near[0, :, cols].astype(f32)).astype(bf16)
        self.to_cross(i, cols).start()

    def take(self, i, cols, own=None):
        self.to_twin(i, 1, cols).wait_recv()
        own = self.parts[self.p.f, :, cols] if own is None else own
        near = own.astype(f32) + self.near[1, :, cols].astype(f32)
        self.to_cross(i, cols).wait_recv()
        return near + self.far[:, cols].astype(f32)

    def given(self, i, cols):
        self.to_twin(i, 0, cols).wait_send()
        self.to_twin(i, 1, cols).wait_send()

    def passed(self, i, cols):
        self.to_cross(i, cols).wait_send()

    def finish(self, i, cols):
        self.given(i, cols)
        self.passed(i, cols)


class GroupTrade:
    sems = 2

    def __init__(self, place, whole, slots, sems, columns):
        self.p, self.whole, self.slots, self.s, self.n = place, whole, slots, sems, columns

    def block(self, g):
        return self.whole.at[:, pl.ds(pl.multiple_of(g * self.n, 128), self.n)]

    def send(self, d):
        self.copy(d).start()

    def copy(self, d):
        g = (self.p.f + d) % 4
        return remote(
            self.block(g), self.slots.at[self.p.f], self.s.at[0, d], self.s.at[1, d], {"fsdp": g}
        )

    def arrival(self, d):
        slot = self.slots.at[(self.p.f + 4 - d) % 4]
        return remote(slot, slot, self.s.at[0, d], self.s.at[1, d], {"fsdp": (self.p.f + d) % 4})

    def own(self):
        return pltpu.make_async_copy(
            self.block(self.p.f), self.slots.at[self.p.f], self.s.at[1, 0]
        )

    def start(self):
        for d in (2, 3, 1):
            self.copy(d).start()
        self.own().start()

    def wait(self):
        self.own().wait()
        for d in (1, 2, 3):
            self.arrival(d).wait_recv()

    def finish(self):
        for d in (1, 2, 3):
            self.copy(d).wait_send()


class GroupScatter:
    sems = 4

    def __init__(self, place, per_owner, stage, slots, sems):
        self.p, self.half, self.stage, self.slots, self.s = place, per_owner // 2, stage, slots, sems
        self.places = (place.twin_f, place.cross_f, place.diag_f)
        self.devices = (place.twin, place.cross, place.diag)

    def slot(self, f, half):
        return self.slots.at[pl.ds((2 * f + half) * self.half, self.half)]

    def own(self):
        return self.slots.at[pl.ds(2 * self.p.f * self.half, 2 * self.half)]

    def copy(self, kind, half):
        return remote(
            self.stage.at[kind, pl.ds(half * self.half, self.half)],
            self.slot(self.p.f, half),
            self.s.at[half, kind],
            self.s.at[2 + half, kind],
            self.devices[kind],
        )

    def arrived(self, kind):
        for half in range(2):
            slot = self.slot(self.places[kind], half)
            remote(
                slot, slot, self.s.at[half, kind], self.s.at[2 + half, kind], self.devices[kind]
            ).wait_recv()

    def send(self, kind):
        for half in range(2):
            self.copy(kind, half).start()

    def sent(self):
        for kind in range(3):
            for half in range(2):
                self.copy(kind, half).wait_send()


class PieceMove:
    def __init__(self, place, per_owner, pieces, slots, sems):
        p = place
        self.p, self.n, self.pieces, self.slots, self.s = p, per_owner, pieces, slots, sems
        self.at = hidden_piece(p.c, p.lines)

    def dest(self, q):
        return self.n * q + self.at // 4

    def copy(self, q):
        return remote(
            self.pieces.at[q],
            self.slots.at[self.at % 4],
            self.s.at[0, q],
            self.s.at[1, self.at % 4],
            {"ctx": self.dest(q)},
        )

    def stay(self, q):
        return pltpu.make_async_copy(self.pieces.at[q], self.slots.at[self.at % 4], self.s.at[2, 0])

    def start(self):
        for q in range(4):
            here = self.dest(q) == self.p.c
            pl.when(~here)(lambda q=q: self.copy(q).start())
            pl.when(here)(lambda q=q: self.stay(q).start())

    def finish(self):
        p = self.p
        for q in range(4):
            here = self.dest(q) == p.c
            pl.when(~here)(lambda q=q: self.copy(q).wait_send())
            pl.when(here)(lambda q=q: self.stay(q).wait())
        for i in range(4):
            source = place_of_piece(4 * (p.c % self.n) + i, p.lines)
            slot = self.slots.at[i]
            arrival = remote(slot, slot, self.s.at[0, 0], self.s.at[1, i], p.beside)
            pl.when(source != p.c)(lambda arrival=arrival: arrival.wait_recv())


def hidden_piece(c, lines):
    return (c % 2) * lines + c // 2


def place_of_piece(piece, lines):
    return (piece % lines) * 2 + piece // lines


class GroupReturn(GroupTrade):
    def __init__(self, place, whole, slots, sems):
        super().__init__(place, whole, slots, sems, 0)

    def block(self, g):
        return self.whole.at[g]


def rotary_tables(first, rows, bounds):
    index = first + lax.broadcasted_iota(jnp.int32, (rows, 128), 0)
    lane = lax.broadcasted_iota(jnp.int32, (rows, 128), 1)
    quarter = HD // 4
    member = documents(index, bounds)
    opening = jnp.where(member == 0, 0, jnp.where(member == 1, bounds[0], bounds[1]))
    frequency = jnp.exp((lane % quarter).astype(f32) * (-math.log(10000.0) / quarter))
    angles = (index - opening).astype(f32) * frequency
    sine = jnp.sin(angles)
    return jnp.cos(angles), jnp.where(lane < quarter, -sine, sine)


def rotated(v, cosine, sine):
    first = v[:, :128]
    return jnp.concatenate(
        [first * cosine + pltpu.roll(first, 64, 1) * sine, v[:, 128:]], axis=1
    )


class GroupGather:
    sems = 6

    def __init__(self, place, own, whole, sems, own_sem, pieces, cuts=None):
        self.p, self.own, self.whole, self.s, self.own_sem = place, own, whole, sems, own_sem
        self.pieces, self.n, self.cuts = pieces, own.shape[0] // pieces, cuts

    def span(self, i):
        return (slice(None), self.cuts[i]) if self.cuts else (pl.ds(i * self.n, self.n),)

    def part(self, i):
        return self.own.at[self.span(i)]

    def slot(self, g, i):
        return self.whole.at[(g,) + self.span(i)]

    def local(self):
        return pltpu.make_async_copy(self.own, self.whole.at[self.p.f], self.own_sem)

    def to_twin(self, i):
        return remote(
            self.part(i), self.slot(self.p.f, i), self.s.at[0, i], self.s.at[3, i], self.p.twin
        )

    def to_cross(self, i):
        return remote(
            self.part(i), self.slot(self.p.f, i), self.s.at[1, i], self.s.at[4, i], self.p.cross
        )

    def forward(self, i):
        slot = self.slot(self.p.cross_f, i)
        return remote(slot, slot, self.s.at[2, i], self.s.at[5, i], self.p.twin)

    def give(self, i):
        self.to_cross(i).start()
        self.to_twin(i).start()

    def near(self, i):
        twin = self.slot(self.p.twin_f, i)
        remote(twin, twin, self.s.at[0, i], self.s.at[3, i], self.p.twin).wait_recv()

    def pass_on(self, i):
        slot = self.slot(self.p.cross_f, i)
        remote(slot, slot, self.s.at[1, i], self.s.at[4, i], self.p.cross).wait_recv()
        self.forward(i).start()

    def last(self, i):
        diag = self.slot(self.p.diag_f, i)
        remote(diag, diag, self.s.at[2, i], self.s.at[5, i], self.p.twin).wait_recv()

    def sent(self, i):
        self.to_twin(i).wait_send()
        self.to_cross(i).wait_send()
        self.forward(i).wait_send()

    def finish(self, i):
        self.near(i)
        self.last(i)
        self.sent(i)


def is_long(length):
    return length > 2048


def tiles_of(first, count, tile):
    tile = tile if count % tile == 0 else 128

    def loop(body):
        def one(i, carry):
            body(pl.ds(pl.multiple_of(first + i * tile, 128), tile))
            return carry

        lax.fori_loop(0, count // tile, one, 0, unroll=True)

    return loop


def front_kernel(
    lines,
    bounds_ref,
    x_ref,
    gains,
    w_keyval_in,
    w_query_in,
    w_out_in,
    cot,
    w_down,
    w_gate_up,
    normed_dst,
    query_dst,
    keyval_dst,
    probs_dst,
    mixed_dst,
    middle_out,
    normed_two_out,
    cosine,
    sine,
    columns_dst,
    cot_all,
    rows_all,
    whole,
    slots,
    parts,
    near,
    out,
    far,
    keyval,
    mixed,
    bias,
    w_rows,
    windows,
    normed_out,
    query_out,
    keyval_out,
    probs_out,
    mixed_out,
    columns_out,
    put_sems,
    w_keyval,
    w_query,
    w_out,
    fetch_sems,
    trade_sems,
    sum_sems,
    keyval_sems,
    cot_sems,
    row_sems,
    own_sems,
):
    p = Place(lines)
    rows, width = x_ref.shape
    length = bias.shape[1]
    heads = query_out.shape[0]
    inner = heads * HD
    kv_width = 2 * HD
    fetch = Fetch(
        ((w_keyval_in, w_keyval), (w_query_in, w_query), (w_out_in, w_out)), fetch_sems
    )
    p.barrier()
    puts = []

    def put(src, dst):
        puts.append(pltpu.make_async_copy(src, dst, put_sems.at[len(puts)]))
        puts[-1].start()


    units = w_gate_up.shape[1] // 2
    piece = units // (4 * 2 * lines)
    padded_piece = w_rows.shape[0]
    own_piece = hidden_piece(p.c, lines)
    if w_down.shape[0] == padded_piece:
        rows_copy = pltpu.make_async_copy(w_down, w_rows, own_sems.at[2])
    else:
        rows_copy = pltpu.make_async_copy(
            w_down.at[pl.ds(pl.multiple_of(own_piece * piece, 16), piece)],
            w_rows.at[pl.ds(0, piece)],
            own_sems.at[2],
        )
    rows_copy.start()
    span = windows.shape[2]
    shard = w_gate_up.shape[0]

    def window_first(q):
        first = q * (units // 4) + own_piece * piece
        return jnp.minimum(first // 128 * 128, 2 * units - span), first

    def window(q):
        return pltpu.make_async_copy(
            w_gate_up.at[:, pl.ds(pl.multiple_of(window_first(q)[0], 128), span)],
            windows.at[q % 2],
            own_sems.at[3 + q % 2],
        )

    def pack_columns(q):
        window(q).wait()
        start, first = window_first(q)
        by = first - start
        lane = lax.broadcasted_iota(jnp.int32, (shard, 128), 1)
        tiles = [
            pltpu.roll(windows[q % 2, :, t * 128 : (t + 1) * 128].astype(f32), (128 - by % 128) % 128, 1)
            for t in range(span // 128)
        ]
        late = by >= 128
        turned = []
        for t in range(span // 128 - 1):
            turned.append(jnp.where(lane < 128 - by % 128, tiles[t], tiles[t + 1]))
        turned.append(jnp.where(lane < 128 - by % 128, tiles[-1], 0.0))
        turned = [
            jnp.where(late, turned[t + 1], turned[t]) for t in range(span // 128 - 1)
        ]
        turned = jnp.concatenate(turned, axis=1)[:, :padded_piece]
        lane = lax.broadcasted_iota(jnp.int32, (shard, padded_piece), 1)
        columns_out[:, q * padded_piece : (q + 1) * padded_piece] = jnp.where(
            lane < piece, turned, 0.0
        ).astype(bf16)
        if q + 2 < 8:
            window(q + 2).start()

    window(0).start()
    window(1).start()
    down = GroupGather(p, w_rows, rows_all, row_sems, own_sems.at[0], row_sems.shape[1])
    cot_gather = LineGather(p, cot, cot_all, cot_sems)
    cot_local = pltpu.make_async_copy(cot, cot_all.at[p.c], own_sems.at[1])

    def give(first, last):
        for i in range(first, min(last, down.pieces)):
            down.give(i)

    def pass_on(first, last):
        for i in range(first, min(last, down.pieces)):
            down.pass_on(i)

    source = x_ref[...].astype(f32)
    whole[...] = rms_norm(source, gains[0:1]).astype(bf16)
    trade = GroupTrade(p, whole, slots.at[0], trade_sems.at[0], slots.shape[3])
    trade.start()
    cot_local.start()
    cot_gather.start()
    bounds = (bounds_ref[0, 0], bounds_ref[0, 1])
    cosine[...], sine[...] = rotary_tables(p.c * rows, rows, bounds)
    query_at = p.c * rows + lax.broadcasted_iota(jnp.int32, (rows, length), 0)
    key_at = lax.broadcasted_iota(jnp.int32, (rows, length), 1)
    allowed = (
        (query_at >= key_at)
        & (query_at - key_at < WINDOW)
        & (documents(query_at, bounds) == documents(key_at, bounds))
    )
    bias[...] = jnp.where(allowed, 0.0, -1e30)
    rows_copy.wait()
    if w_down.shape[0] != padded_piece and piece < padded_piece:
        w_rows[pl.ds(piece, padded_piece - piece)] = jnp.zeros(
            (padded_piece - piece, width), bf16
        )
    down.local().start()
    give(0, 1)
    trade.wait()
    normed_out[...] = slots[0]
    put(normed_out, normed_dst)

    half = (heads // 2) * HD
    chunks = [(0, kv_width), (kv_width, half), (kv_width + half, inner - half)]
    group = GroupSum(p, parts, near, out, far, sum_sems.at[0])

    def project(lhs, weight, first, count, to):
        @tiles_of(first, count, 256)
        def _(cols):
            left = lhs[...].reshape(4 * rows, lhs.shape[-1])
            product = jnp.dot(left, weight[:, cols], preferred_element_type=f32)
            if to:
                cols = pl.ds(pl.multiple_of(cols.start + to, 128), cols.size)
            parts[:, :, cols] = product.astype(bf16).reshape(4, rows, cols.size)

    spans = [pl.ds(first, count) for first, count in chunks]
    fetch.wait(0, 1)
    project(slots.at[0], w_keyval, 0, kv_width, 0)
    group.give(0, spans[0])
    project(slots.at[0], w_query, 0, half, kv_width)
    group.give(1, spans[1])
    group.pass_on(0, spans[0])
    project(slots.at[0], w_query, half, inner - half, kv_width)
    group.give(2, spans[2])
    group.pass_on(1, spans[1])
    group.pass_on(2, spans[2])

    linear = group.take(0, spans[0])
    keyval[0, p.c] = rotated(linear[:, :HD], cosine[...], sine[...]).astype(bf16)
    keyval[1, p.c] = linear[:, HD:].astype(bf16)
    kv_gathers = [
        LineGather(p, keyval.at[i, p.c], keyval.at[i], keyval_sems.at[i]) for i in range(2)
    ]
    for gather in kv_gathers:
        gather.start()
    for gather in kv_gathers:
        gather.step(0)

    def take_queries(i):
        linear = group.take(i, spans[i])
        for h in range(linear.shape[1] // HD):
            turned = rotated(linear[:, h * HD : (h + 1) * HD], cosine[...], sine[...])
            at = h if i == 1 else h + heads // 2
            query_out[at] = (turned * HD**-0.5).astype(bf16)

    give(1, 4)
    take_queries(1)
    for step in range(1, lines - 1):
        for gather in kv_gathers:
            gather.step(step)
    cot_gather.step(0)
    take_queries(2)
    for gather in kv_gathers:
        gather.finish()
    keyval_out[...] = keyval[...]
    put(keyval_out, keyval_dst)
    put(query_out, query_dst)


    def two_heads(i, carry):
        keys = keyval[0].reshape(length, HD)
        values = keyval[1].reshape(length, HD)
        two = query_out[pl.ds(2 * i, 2)].reshape(2 * rows, HD)
        scores = contract_rows(two, keys).reshape(2, rows, length) + bias[...][None]
        scores = scores.reshape(2 * rows, length)
        weights = jnp.exp(scores - jnp.max(scores, axis=-1, keepdims=True))
        total = jnp.sum(weights, axis=-1, keepdims=True)
        weights = (weights / total).astype(bf16)
        probs_out[pl.ds(2 * i, 2)] = weights.reshape(2, rows, length)
        product = jnp.dot(weights, values, preferred_element_type=f32).astype(bf16)
        at = pl.multiple_of(i * 2 * HD, 128)
        mixed[:, pl.ds(at, HD)] = product[:rows]
        mixed[:, pl.ds(at + HD, HD)] = product[rows:]
        return carry

    lax.fori_loop(0, heads // 2, two_heads, 0, unroll=not is_long(length))
    trade_two = GroupTrade(p, mixed, slots.at[1], trade_sems.at[1], slots.shape[3])
    trade_two.start()
    give(4, 6)
    put(probs_out, probs_dst)
    for q in range(4):
        pack_columns(q)
    if lines > 2:
        cot_gather.step(1)
    for i in range(len(chunks)):
        group.finish(i, spans[i])
    trade_two.wait()
    mixed_out[...] = slots[1]
    put(mixed_out, mixed_dst)
    fetch.wait(2)

    half = width // 2
    spans_two = [pl.ds(0, half), pl.ds(half, half)]
    group_two = GroupSum(p, parts, near, out, far, sum_sems.at[1])
    for i in range(2):
        project(slots.at[1], w_out, i * half, half, 0)
        group_two.give(i, spans_two[i])
    for i in range(2):
        group_two.pass_on(i, spans_two[i])
    give(6, 8)
    for q in range(4, 8):
        pack_columns(q)
    put(columns_out, columns_dst)
    pass_on(0, 6)
    for step in range(2, lines - 1):
        cot_gather.step(step)
    for i in range(2):
        middle_out[:, spans_two[i]] = x_ref[:, spans_two[i]].astype(f32) + group_two.take(
            i, spans_two[i]
        )
    normed_two_out[...] = rms_norm(middle_out[...], gains[1:2]).astype(bf16)

    pass_on(6, 8)
    for i in range(2):
        group_two.finish(i, spans_two[i])
    trade.finish()
    trade_two.finish()
    for copy in puts:
        copy.wait()
    down.local().wait()
    cot_local.wait()
    for i in range(down.pieces):
        down.finish(i)
    cot_gather.finish()


def front(lines, operands, heads, padded_piece):
    x = operands[1]
    rows, width = x.shape
    places = 2 * lines
    length = places * rows
    inner = heads * HD
    shard = width // 4
    parts_width = inner + 2 * HD
    in_vmem = pl.BlockSpec(memory_space=VMEM)
    anywhere = pl.BlockSpec(memory_space=pl.ANY)
    shape = jax.ShapeDtypeStruct
    pieces = 8 if padded_piece % 128 == 0 else 1
    assert inner == width
    copied = [
        shape((4, rows, shard), bf16),
        shape((heads, rows, HD), bf16),
        shape((2, places, rows, HD), bf16),
        shape((heads, rows, length), bf16),
        shape((4, rows, shard), bf16),
        shape((shard, 8 * padded_piece), bf16),
    ]
    outs = (
        *copied[:5],
        shape((rows, width), f32),
        shape((rows, width), bf16),
        shape((rows, 128), f32),
        shape((rows, 128), f32),
        copied[5],
        shape((places, rows, width), bf16),
        shape((4, padded_piece, width), bf16),
    )
    return pl.pallas_call(
        functools.partial(front_kernel, lines),
        out_shape=outs,
        in_specs=[pl.BlockSpec(memory_space=pltpu.SMEM)] + [in_vmem] * 2 + [anywhere] * 6,
        out_specs=[anywhere] * 5 + [in_vmem] * 4 + [anywhere] * 3,
        scratch_shapes=[
            VMEM((rows, width), bf16),
            VMEM((2, 4, rows, shard), bf16),
            VMEM((4, rows, parts_width), bf16),
            VMEM((2, rows, parts_width), bf16),
            VMEM((rows, parts_width), bf16),
            VMEM((rows, parts_width), bf16),
            VMEM((2, places, rows, HD), bf16),
            VMEM((rows, inner), bf16),
            VMEM((rows, length), f32),
            VMEM((padded_piece, width), bf16),
            VMEM((2, shard, (padded_piece + 127) // 128 * 128 + 128), bf16),
            *held(copied),
            DMA((6,)),
            *held(operands[3:6]),
            DMA((3,)),
            DMA((2, GroupTrade.sems, 4)),
            DMA((2, GroupSum.sems, 3)),
            DMA((2, LineGather.sems, lines)),
            DMA((LineGather.sems, lines)),
            DMA((GroupGather.sems, pieces)),
            DMA((5,)),
        ],
        compiler_params=pltpu.CompilerParams(
            collective_id=0, has_side_effects=True, vmem_limit_bytes=vmem_bytes
        ),
        name="front",
    )(*operands)


def gelu_parts(v):
    k = 0.7978845608028654
    square = v * v
    inner = jnp.tanh(k * v * (1.0 + 0.044715 * square))
    half = 0.5 * (1.0 + inner)
    slope = half + 0.5 * v * (1.0 - inner * inner) * (k * (1.0 + 3 * 0.044715 * square))
    return v * half, slope


def norm_back(values, gain, grad):
    r = lax.rsqrt(jnp.mean(values * values, axis=-1, keepdims=True) + epsilon)
    scaled = values * r
    inner = grad * gain
    grad_values = r * (inner - scaled * jnp.mean(inner * scaled, axis=-1, keepdims=True))
    return grad_values, jnp.sum(grad * scaled, axis=0, keepdims=True)


def middle_kernel(
    lines,
    gains,
    cot_in,
    w_rows_in,
    own,
    middle,
    w_columns,
    grad_middle_out,
    gain_out,
    grads_dst,
    down_out,
    normed_all_out,
    result_parts,
    normed_all,
    weights,
    grad_hidden,
    hidden,
    parts,
    side,
    chain,
    down_near,
    down_stage,
    down_far,
    cot_all,
    w_rows,
    grads_out,
    put_sems,
    fetch_sems,
    gather_sems,
    column_sems,
    sum_sems,
    down_sems,
    own_sems,
):
    p = Place(lines)
    rows, width = own.shape
    two = 2 * rows
    padded = hidden.shape[2]
    shard = width // 4
    tile = 256 if padded % 256 == 0 else 128
    fetch = Fetch(((cot_in, cot_all), (w_rows_in, w_rows)), fetch_sems)
    p.barrier()

    columns = GroupGather(p, w_columns, weights, column_sems, own_sems.at[0], column_sems.shape[1])
    gather = LineGather(p, own, normed_all, gather_sems)
    gather.start()
    for i in range(columns.pieces):
        columns.give(i)
    columns.local().start()
    own_local = pltpu.make_async_copy(own, normed_all.at[p.c], own_sems.at[2 + lines])
    own_local.start()
    middle_local = pltpu.make_async_copy(middle, grad_middle_out, own_sems.at[3 + lines])
    middle_local.start()

    def hidden_grad(line):
        def one(i, carry):
            cols = pl.ds(pl.multiple_of(i * tile, 128), tile)
            left = cot_all[pl.ds(2 * line, 2)].reshape(two, width)
            right = w_rows[pl.ds(pl.multiple_of(i * tile, 16), tile)]
            grad_hidden[line, :, cols] = contract_rows(left, right)
            return carry

        lax.fori_loop(0, padded // tile, one, 0)

    fetch.wait(0, 1)
    done = 0
    for step in range(lines - 1):
        hidden_grad(done)
        done += 1
        gather.step(step)
        if step < columns.pieces:
            columns.pass_on(step)
    for i in range(lines - 1, columns.pieces):
        columns.pass_on(i)
    while done < lines:
        hidden_grad(done)
        done += 1
    gather.finish()
    own_local.wait()
    columns.local().wait()
    for i in range(columns.pieces):
        columns.finish(i)
    normed_local = pltpu.make_async_copy(normed_all, normed_all_out, own_sems.at[1])
    normed_local.start()

    line_sums = [
        LineSum(p, parts.at[i], side.at[i], chain.at[i], sum_sems.at[i]) for i in range(2)
    ]

    def near(turn):
        for line_sum in line_sums:
            line_sum.near(turn, 0)

    def far(turn):
        for line_sum in line_sums:
            line_sum.far(turn)

    def feed_forward(turn):
        line = line_sums[0].order(turn)

        def one(i, carry):
            cols = pl.ds(pl.multiple_of(i * tile, 128), tile)
            up_cols = pl.ds(pl.multiple_of(i * tile + padded, 128), tile)
            left = normed_all[pl.ds(2 * line, 2)].reshape(two, width)
            gate = jnp.dot(
                left, weights[:, :, cols].reshape(width, tile), preferred_element_type=f32
            )
            up = jnp.dot(
                left, weights[:, :, up_cols].reshape(width, tile), preferred_element_type=f32
            )
            gelu, slope = gelu_parts(gate)
            grad = grad_hidden[line, :, cols]
            hidden[line, :, cols] = (gelu * up).astype(bf16)
            grads_out[line, :, cols] = (grad * up * slope).astype(bf16)
            grads_out[line, :, up_cols] = (grad * gelu).astype(bf16)
            return carry

        lax.fori_loop(0, padded // tile, one, 0, unroll=True)

        def back(g, carry):
            product = contract_rows(grads_out[line], weights[g]).astype(bf16)
            cols = pl.ds(pl.multiple_of(g % 2 * shard, 128), shard)
            parts[g // 2, pl.ds(2 * line, 2), :, cols] = product.reshape(2, rows, shard)
            return carry

        pltpu.make_async_copy(grads_out.at[line], grads_dst.at[line], put_sems.at[turn]).start()
        for half in range(2):
            lax.fori_loop(2 * half, 2 * half + 2, back, 0, unroll=True)
            line_sums[half].across(turn).start()

    result_stage = normed_all

    def result_copy(line):
        blocks = pl.ds(2 * line, 2)
        return pltpu.make_async_copy(
            result_stage.at[blocks], result_parts.at[blocks], own_sems.at[2 + line]
        )

    def result_part(line):
        def one(i, carry):
            cols = pl.ds(pl.multiple_of(i * shard, 128), shard)
            product = jnp.dot(
                hidden[line], w_rows[:, cols], preferred_element_type=f32
            ).astype(bf16)
            result_stage[pl.ds(2 * line, 2), :, cols] = product.reshape(2, rows, shard)
            return carry

        lax.fori_loop(0, 4, one, 0, unroll=True)
        result_copy(line).start()

    quarter = padded // 4
    every = slice(None)
    down_parts = weights.at[:, pl.ds(0, quarter), pl.ds(0, shard)]

    def down_group(i):
        return GroupSum(p, down_parts, down_near.at[i], down_stage.at[i % 2], down_far.at[i], down_sems)

    def down_chunk(i):
        def one(g, carry):
            cols = pl.ds(pl.multiple_of(g * shard, 128), shard)
            left = hidden[:, :, i * quarter : (i + 1) * quarter].reshape(lines * two, quarter)
            right = cot_all[:, :, cols].reshape(lines * two, shard)
            down_parts[g] = contract_tokens(left, right).astype(bf16)
            return carry

        lax.fori_loop(0, 4, one, 0, unroll=True)
        down_out[i] = down_parts[p.f]
        down_group(i).give(i, every)

    for turn in range(lines):
        feed_forward(turn)
        if turn == lines - 2:
            near(0)
    normed_local.wait()
    for turn in range(lines):
        line = line_sums[0].order(turn)
        pltpu.make_async_copy(grads_out.at[line], grads_dst.at[line], put_sems.at[turn]).wait()

    for i in range(4):
        if i >= 1:
            down_group(i - 1).given(i - 1, every)
        if i >= 2:
            down_group(i - 2).passed(i - 2, every)
        down_chunk(i)
        down_group(i).pass_on(i, every)
        if i == 1:
            if lines > 2:
                near(1)
            far(0)
        if i == 2 and lines > 3:
            near(2)
            far(1)
            far(2)
    for line in range(lines):
        result_part(line)
    for turn in range(3, lines - 1):
        near(turn)
        far(turn)
    near(lines - 1)
    far(lines - 1)
    grad = jnp.concatenate([line_sum.total() for line_sum in line_sums], axis=1)
    middle_local.wait()
    grad_values, gain = norm_back(grad_middle_out[...], gains[1:2], grad)
    grad_middle_out[...] = cot_all[p.c].astype(f32) + grad_values
    gain_out[...] = gain
    for i in range(2):
        down_out[i] = down_group(i).take(i, every, down_out[i]).astype(bf16)
    for i in (2, 3):
        down_out[i] = down_group(i).take(i, every, down_out[i]).astype(bf16)
        down_group(i).passed(i, every)
    down_group(3).given(3, every)
    for line in range(lines):
        result_copy(line).wait()
    for line_sum in line_sums:
        line_sum.finish()


def middle_bytes(lines, rows, width, padded):
    length = 2 * lines * rows
    return (
        14 * rows * width
        + 9 * length * width
        + 9 * padded * width
        + 10 * length * padded
    )


def middle_part(lines, operands, padded):
    own = operands[3]
    rows, width = own.shape
    places = 2 * lines
    shard = width // 4
    quarter = padded // 4
    pieces = 4
    in_vmem = pl.BlockSpec(memory_space=VMEM)
    anywhere = pl.BlockSpec(memory_space=pl.ANY)
    shape = jax.ShapeDtypeStruct
    return pl.pallas_call(
        functools.partial(middle_kernel, lines),
        out_shape=(
            shape((rows, width), f32),
            shape((1, width), f32),
            shape((lines, 2 * rows, 2 * padded), bf16),
            shape((4, quarter, shard), bf16),
            shape((places, rows, width), bf16),
            shape((places, rows, width), bf16),
        ),
        in_specs=[in_vmem] + [anywhere] * 5,
        out_specs=[in_vmem] * 2 + [anywhere, in_vmem] + [anywhere] * 2,
        scratch_shapes=[
            VMEM((places, rows, width), bf16),
            VMEM((4, shard, 2 * padded), bf16),
            VMEM((lines, 2 * rows, padded), f32),
            VMEM((lines, 2 * rows, padded), bf16),
            VMEM((2, places, rows, width // 2), bf16),
            VMEM((2, lines, rows, width // 2), bf16),
            VMEM((2, 2, lines - 1, rows, width // 2), bf16),
            VMEM((4, 2, quarter, shard), bf16),
            VMEM((2, quarter, shard), bf16),
            VMEM((4, quarter, shard), bf16),
            *held(operands[1:3]),
            VMEM((lines, 2 * rows, 2 * padded), bf16),
            DMA((lines,)),
            DMA((2,)),
            DMA((LineGather.sems, lines)),
            DMA((GroupGather.sems, pieces)),
            DMA((2, LineSum.sems, lines)),
            DMA((GroupSum.sems, 4)),
            DMA((4 + lines,)),
        ],
        compiler_params=pltpu.CompilerParams(
            collective_id=1, has_side_effects=True, vmem_limit_bytes=vmem_bytes
        ),
        name="middle",
    )(*operands)


def back_kernel(
    lines,
    with_result,
    grad_middle,
    tokens,
    gains,
    cosine,
    sine,
    w_out_in,
    probs_in,
    keyval_in,
    queries_in,
    mixed_in,
    w_query_in,
    w_keyval_in,
    down_in,
    *rest,
):
    if with_result:
        middle, result_in, result_out, *rest = rest
    (
        input_grad_out,
        gain_out,
        linear_out,
        out_slots,
        down_out,
        branch_all,
        linear_all,
        branch,
        linear,
        trade_parts,
        trade_slots,
        grad_mixed,
        kv_total,
        kv_parts,
        kv_side,
        kv_chain,
        query_parts,
        out_stage,
        w_out,
        probs,
        keyval,
        queries,
        mixed,
        w_query,
        w_keyval,
        fetch_sems,
        branch_sems,
        linear_sems,
        trade_sems,
        kv_sems,
        out_sems,
        piece_sems,
        own_sems,
        *rest,
    ) = rest
    p = Place(lines)
    rows, width = grad_middle.shape
    heads = queries.shape[0]
    length = probs_in.shape[2]
    long = is_long(length)
    operands = [
        (w_out_in, w_out),
        (keyval_in, keyval),
        (queries_in, queries),
        (mixed_in, mixed),
        (w_query_in, w_query),
        (w_keyval_in, w_keyval),
    ]
    fetch = Fetch(operands if long else operands + [(probs_in, probs)], fetch_sems)
    shard = w_out.shape[0]
    kv_width = 2 * HD
    per_owner = 2 * lines // 4
    others = [(jnp.full((), True), {"ctx": (p.c + d) % (2 * lines)}) for d in range(1, 2 * lines)]
    p.barrier(ctx=False, also=others)
    if with_result:
        result_parts, result_side, result_chain, result_sems = rest
        result_sum = Turns(
            LineSum(p, result_parts, result_side, result_chain, result_sems), lines
        )
        half = width // 2
        result_copies = [
            pltpu.make_async_copy(
                result_in.at[:, :, pl.ds(i * half, half)], result_parts.at[i], own_sems.at[2 + i]
            )
            for i in range(2)
        ]
        for copy in result_copies:
            copy.start()
        result_sums = [
            Turns(
                LineSum(
                    p, result_parts.at[i], result_side.at[i], result_chain.at[i], result_sems.at[i]
                ),
                lines,
            )
            for i in range(2)
        ]
    out_scatter = GroupScatter(p, per_owner, out_stage, out_slots, out_sems)

    branch[...] = grad_middle[...].astype(bf16)
    group = GroupGather(p, branch, branch_all, branch_sems, own_sems.at[0], 1)
    group.give(0)
    group.local().start()
    down_move = PieceMove(p, per_owner, down_in, down_out, piece_sems)
    down_move.start()
    if with_result:
        result_copies[0].wait()
        result_sums[0].start()
    back_trade = GroupReturn(p, trade_parts.at[0], trade_slots.at[0], trade_sems.at[0])

    def mixed_back(g):
        trade_parts[0, g] = contract_rows(branch_all[g], w_out[...]).astype(bf16)

    group.local().wait()
    fetch.wait(0)
    mixed_back(p.f)
    back_trade.own().start()
    group.near(0)
    mixed_back(p.twin_f)
    group.pass_on(0)
    mixed_back(p.cross_f)
    back_trade.send(2)
    group.last(0)
    mixed_back(p.diag_f)
    back_trade.send(1)
    back_trade.send(3)

    def out_block(i, g):
        left = mixed[...].reshape(4 * rows, shard)
        right = branch_all[:, :, pl.ds(pl.multiple_of(g * shard, 128), shard)]
        product = contract_tokens(left, right.reshape(4 * rows, shard)).astype(bf16)
        out_stage[i] = product.reshape(out_stage.shape[1:])

    fetch.wait(3)
    out_block(1, p.cross_f)
    out_scatter.copy(1, 0).start()
    out_block(0, p.twin_f)
    out_scatter.send(0)
    out_block(2, p.diag_f)
    out_block(3, p.f)
    out_own = pltpu.make_async_copy(out_stage.at[3], out_scatter.own(), own_sems.at[7])
    out_own.start()
    if with_result:
        result_sums[0].near(2)
        result_copies[1].wait()
        result_sums[1].sum.start(1)
    back_trade.wait()
    for g in range(4):
        grad_mixed[:, g * shard : (g + 1) * shard] = trade_slots[0, g]

    kv_total[...] = jnp.zeros_like(kv_total)
    kv_at, q_at = pl.ds(0, kv_width), pl.ds(kv_width, heads * HD)

    batch = 1 if long else 2
    fetch.wait(1, 2)
    if not long:
        fetch.wait(6)

    def some_heads(i, carry):
        keys = keyval[0].reshape(length, HD)
        values = keyval[1].reshape(length, HD)
        at = [pl.multiple_of((i * batch + h) * HD, 128) for h in range(batch)]
        outer = jnp.concatenate([grad_mixed[:, pl.ds(a, HD)] for a in at], axis=0)
        if batch == 1:
            one = pltpu.make_async_copy(probs_in.at[i], probs, own_sems.at[5])
            one.start()
            one.wait()
            weights = probs[...]
        else:
            weights = probs[pl.ds(batch * i, batch)].reshape(batch * rows, length)
        wide = weights.astype(f32)
        grad_weights = contract_rows(outer, values)
        delta = jnp.sum(wide * grad_weights, axis=-1, keepdims=True)
        grad_scores = (wide * (grad_weights - delta)).astype(bf16)
        product = jnp.dot(grad_scores, keys, preferred_element_type=f32) * HD**-0.5
        for h in range(batch):
            turned = rotated(product[h * rows : (h + 1) * rows], cosine[...], -sine[...])
            linear[:, pl.ds(kv_width + at[h], HD)] = turned.astype(bf16)
        two = queries[pl.ds(batch * i, batch)].reshape(batch * rows, HD)
        kv_total[:, :HD] += contract_tokens(grad_scores, two)
        kv_total[:, HD:] += contract_tokens(weights, outer)
        return carry

    lax.fori_loop(0, heads // batch, some_heads, 0, unroll=not long)
    linear_group = GroupGather(
        p, linear, linear_all, linear_sems, own_sems.at[1], 2, (q_at, kv_at)
    )
    linear_group.give(0)
    out_scatter.copy(1, 1).start()
    kv_parts[...] = kv_total[...].astype(bf16).reshape(kv_parts.shape)
    kv_sum = LineSum(p, kv_parts, kv_side, kv_chain, kv_sems)
    kv_sum.start(lines)
    if with_result:
        for turn in range(1, lines):
            result_sums[1].sum.across(turn).start()
        result_sums[0].near(lines)
        result_sums[0].far(1)
    fetch.wait(4, 5)

    def query_back(g, block):
        query_parts[g] = contract_rows(block, w_query[...])

    query_back(p.f, linear[:, q_at])
    linear_group.near(0)
    query_back(p.twin_f, linear_all[p.twin_f, :, q_at])
    kv_sum.turns(0)
    linear_group.pass_on(0)
    query_back(p.cross_f, linear_all[p.cross_f, :, q_at])
    linear_group.last(0)
    query_back(p.diag_f, linear_all[p.diag_f, :, q_at])
    own = kv_sum.total()
    linear[:, :HD] = rotated(own[:, :HD], cosine[...], -sine[...]).astype(bf16)
    linear[:, pl.ds(HD, HD)] = own[:, HD:].astype(bf16)
    linear_group.give(1)
    out_scatter.copy(2, 0).start()
    linear_group.local().start()
    if with_result:
        result_sums[0].far(2)
        result_sums[1].near(2)
    linear_group.pass_on(1)
    linear_group.local().wait()
    linear_group.near(1)
    linear_group.last(1)
    linear_copy = pltpu.make_async_copy(linear_all, linear_out, own_sems.at[4])
    linear_copy.start()

    last_trade = GroupReturn(p, trade_parts.at[1], trade_slots.at[1], trade_sems.at[1])

    def normed_back(g):
        product = contract_rows(linear_all[g, :, kv_at], w_keyval[...])
        trade_parts[1, g] = (product + query_parts[g]).astype(bf16)

    normed_back(p.cross_f)
    last_trade.send(2)
    normed_back(p.diag_f)
    normed_back(p.twin_f)
    last_trade.send(1)
    last_trade.send(3)
    out_scatter.copy(2, 1).start()
    normed_back(p.f)
    last_trade.own().start()
    if with_result:
        result_sums[0].far(3)
        result_sums[1].far(2)
    last_trade.wait()
    for g in range(4):
        grad_mixed[:, g * shard : (g + 1) * shard] = trade_slots[1, g]
    source = tokens[...].astype(f32)
    grad_values, gain = norm_back(source, gains[0:1], grad_mixed[...].astype(f32))
    input_grad_out[...] = (grad_middle[...] + grad_values).astype(bf16)
    gain_out[...] = gain
    if with_result:
        for i in range(2):
            cols = pl.ds(i * half, half)
            result_out[:, cols] = (middle[:, cols] + result_sums[i].total()).astype(bf16)
            result_sums[i].sum.finish()
    back_trade.finish()
    last_trade.finish()
    group.sent(0)
    linear_group.sent(0)
    linear_group.sent(1)
    kv_sum.finish()
    out_own.wait()
    for kind in range(3):
        out_scatter.arrived(kind)
    out_scatter.sent()
    linear_copy.wait()
    down_move.finish()


def back(lines, operands, result_operands):
    rows, width = operands[0].shape
    heads = operands[8].shape[0]
    places = 2 * lines
    length = places * rows
    shard = width // 4
    linear_width = width + 2 * HD
    tall = width // places
    pieces = operands[12].shape
    in_vmem = pl.BlockSpec(memory_space=VMEM)
    anywhere = pl.BlockSpec(memory_space=pl.ANY)
    shape = jax.ShapeDtypeStruct
    with_result = bool(result_operands)
    long = is_long(length)
    scratch = held(operands[5:12])
    if long:
        scratch[1] = VMEM((rows, length), bf16)
    result_scratch = [
        VMEM((2, places, rows, width // 2), bf16),
        VMEM((2, lines, rows, width // 2), bf16),
        VMEM((2, 2, lines - 1, rows, width // 2), bf16),
        DMA((2, LineSum.sems, lines)),
    ]
    return pl.pallas_call(
        functools.partial(back_kernel, lines, with_result),
        out_shape=((shape((rows, width), bf16),) if with_result else ())
        + (
            shape((rows, width), bf16),
            shape((1, width), f32),
            shape((4, rows, linear_width), bf16),
            shape((places, tall, shard), bf16),
            shape(pieces, bf16),
        ),
        in_specs=[in_vmem] * 5 + [anywhere] * 8 + ([in_vmem, anywhere] if with_result else []),
        out_specs=[in_vmem] * (3 if with_result else 2) + [anywhere] * 3,
        scratch_shapes=[
            VMEM((4, rows, width), bf16),
            VMEM((4, rows, linear_width), bf16),
            VMEM((rows, width), bf16),
            VMEM((rows, linear_width), bf16),
            VMEM((2, 4, rows, shard), bf16),
            VMEM((2, 4, rows, shard), bf16),
            VMEM((rows, width), bf16),
            VMEM((length, 2 * HD), f32),
            VMEM((places, rows, 2 * HD), bf16),
            VMEM((lines, rows, 2 * HD), bf16),
            VMEM((2, lines - 1, rows, 2 * HD), bf16),
            VMEM((4, rows, shard), f32),
            VMEM((4, places // 4, tall, shard), bf16),
            *scratch,
            DMA((7,)),
            DMA((GroupGather.sems, 1)),
            DMA((GroupGather.sems, 2)),
            DMA((2, GroupTrade.sems, 4)),
            DMA((LineSum.sems, lines)),
            DMA((GroupScatter.sems, 3)),
            DMA((3, 4)),
            DMA((8,)),
        ]
        + (result_scratch if with_result else []),
        compiler_params=pltpu.CompilerParams(
            collective_id=2, has_side_effects=True, vmem_limit_bytes=vmem_bytes
        ),
        name="back",
    )(*operands, *result_operands)


def grads_kernel(lines, with_columns, gain_one, gain_two, out_in, normed_in, linear_in, *rest):
    if with_columns:
        normed_two_in, hidden_grads_in, *rest = rest
    projection_out, gains_out, out_out, *rest = rest
    if with_columns:
        columns_out, *rest = rest
    (
        parts,
        side,
        chain,
        stage,
        out_parts,
        out_side,
        out_chain,
        gain_parts,
        gain_side,
        gain_chain,
        gain_slots,
        normed,
        linear_all,
        fetch_sems,
        projection_sems,
        out_sems,
        gain_sems,
        slot_sems,
        scatter_sems,
        *rest,
    ) = rest
    p = Place(lines)
    operands = [(out_in, out_parts)]
    if with_columns:
        (
            chunk_parts,
            near,
            passing,
            far,
            chunks,
            group_sems,
            trade_sems,
            normed_two,
            hidden_grads,
        ) = rest
    if with_columns:
        operands += [(normed_two_in, normed_two), (hidden_grads_in, hidden_grads)]
    operands += [(normed_in, normed), (linear_in, linear_all)]
    fetch = Fetch(operands, fetch_sems)
    places = 2 * lines
    shard = normed.shape[2]
    tokens = 4 * normed.shape[1]
    per_owner = places // 4
    tall = shard // per_owner
    kv_share = 2 * HD // 4
    others = [(jnp.full((), True), {"ctx": (p.c + d) % places}) for d in range(1, places)]
    p.barrier(ctx=False, also=others)

    for c in range(places):
        cols = slice(c * tall, (c + 1) * tall)
        gain_parts[c, 0:1, :tall] = gain_one[:, cols]
        gain_parts[c, 1:2, :tall] = gain_two[:, cols]
    gain_sum = LineSum(p, gain_parts, gain_side, gain_chain, gain_sems)
    gain_sum.start(lines)

    projection_sums = [
        Turns(
            LineSum(p, parts.at[i], side.at[i], chain.at[i], projection_sems.at[i]), lines
        )
        for i in range(2)
    ]
    out_sum = Turns(LineSum(p, out_parts, out_side, out_chain, out_sems))
    fetch.wait(0)
    out_sum.start()

    if with_columns:
        fetch.wait(1, 2)
        block = columns_out.shape[2]
        chunk = chunk_parts.shape[1]
        every = slice(None)

        def chunk_of(k):
            order = sorted(range(lines), key=lambda d: (d == 0, abs(d - lines // 2), d))
            return (p.line + order[k]) % lines

        def group(k):
            return GroupSum(p, chunk_parts, near.at[k], passing.at[k % 2], far.at[k], group_sems)

        def compute(k):
            cols = pl.ds(pl.multiple_of(chunk_of(k) * chunk, 128), chunk)

            def one(g, carry):
                left = normed_two[:, :, cols].reshape(-1, chunk)
                right = hidden_grads[:, :, pl.ds(pl.multiple_of(g * block, 128), block)]
                chunk_parts[g] = contract_tokens(left, right.reshape(-1, block)).astype(bf16)
                return carry

            lax.fori_loop(0, 4, one, 0, unroll=True)
            chunks[k] = chunk_parts[p.f]
            group(k).give(k, every)

        def halves(k):
            half = chunk // 2
            for lane in range(2):
                yield lane, 2 * chunk_of(k) + lane, chunks.at[k, pl.ds(lane * half, half)]

        def place_copy(k, lane, dest, src):
            return remote(
                src,
                columns_out.at[p.c],
                trade_sems.at[0, 2 * k + lane],
                trade_sems.at[1, p.c],
                {"ctx": dest},
            )

        def place_own(src):
            return pltpu.make_async_copy(src, columns_out.at[p.c], trade_sems.at[2, 0])

        def arrival(i):
            slot = columns_out.at[i]
            return remote(slot, slot, trade_sems.at[0, 0], trade_sems.at[1, i], p.beside)

        def complete(k):
            chunks[k] = group(k).take(k, every, chunks[k]).astype(bf16)
            for lane, dest, src in halves(k):
                pl.when(dest != p.c)(
                    lambda k=k, lane=lane, dest=dest, src=src: place_copy(k, lane, dest, src).start()
                )
                pl.when(dest == p.c)(lambda src=src: place_own(src).start())

        def chunk_step(k):
            if k >= 1:
                group(k - 1).given(k - 1, every)
            compute(k)
            if k >= 2:
                group(k - 2).passed(k - 2, every)
            group(k).pass_on(k, every)

        chunk_step(0)

    scatters = [
        GroupScatter(p, per_owner, stage.at[i], parts.at[i], scatter_sems.at[i]) for i in range(2)
    ]

    def projection_block(first, second, g):
        left = normed[...].reshape(tokens, shard)
        right = linear_all[:, :, pl.ds(pl.multiple_of(2 * HD + g * shard, 128), shard)]
        product = contract_tokens(left, right.reshape(tokens, shard)).astype(bf16)
        right = linear_all[:, :, pl.ds(pl.multiple_of(g * kv_share, 128), kv_share)]
        kv_product = contract_tokens(left, right.reshape(tokens, kv_share)).astype(bf16)
        first[...] = product[:, :half].reshape(per_owner, tall, half)
        if half < shard:
            kv_product = jnp.concatenate([product[:, half:], kv_product], axis=1)
        second[...] = kv_product.reshape(per_owner, tall, half)

    half = (shard + kv_share) // 2
    fetch.wait(*((3, 4) if with_columns else (1, 2)))
    for kind in (1, 2, 0):
        projection_block(stage.at[0, kind], stage.at[1, kind], scatters[0].places[kind])
        scatters[0].send(kind)
    for kind in (1, 2, 0):
        scatters[1].send(kind)
    projection_block(scatters[0].own(), scatters[1].own(), p.f)

    first, second = projection_sums
    if with_columns:
        chunk_step(1)
    out_sum.near(2)
    out_sum.far(1)
    if with_columns:
        complete(0)
        if lines > 2:
            chunk_step(2)
    out_sum.near(lines)
    for k in range(lines):
        gain_sum.near(k, 0)
    for kind in range(3):
        scatters[0].arrived(kind)
    first.start()
    out_sum.far(2)
    first.near(2)
    out_sum.far(3)
    first.near(lines)
    for kind in range(3):
        scatters[1].arrived(kind)
    second.start()
    first.far(1)
    for k in range(lines):
        gain_sum.far(k)
    out_out[...] = out_sum.total().astype(bf16)
    first.far(2)
    if with_columns:
        second.near(1)
        for k in range(1, lines):
            complete(k)
            if k + 2 < lines:
                chunk_step(k + 2)
            if k == 1:
                first.far(lines)
                second.near(lines)
            second.far(k)
        for k in (lines - 2, lines - 1):
            group(k).passed(k, every)
        group(lines - 1).given(lines - 1, every)

    own = gain_sum.total()
    gain_parts[p.c] = own

    def gain_copy(d):
        return remote(
            gain_parts.at[p.c],
            gain_slots.at[d],
            slot_sems.at[0, d],
            slot_sems.at[1, d],
            {"fsdp": (p.f + d) % 4},
        )

    for d in (1, 2, 3):
        gain_copy(d).start()
    for i in range(2):
        projection_out[:, i * half : (i + 1) * half] = projection_sums[i].total().astype(bf16)
    for d in (1, 2, 3):
        gain_copy(d).wait_recv()
        own = own + gain_slots[d]
    gains_out[...] = own

    for d in (1, 2, 3):
        gain_copy(d).wait_send()
    if with_columns:
        for k in range(lines):
            for lane, dest, src in halves(k):
                pl.when(dest != p.c)(
                    lambda k=k, lane=lane, dest=dest, src=src: place_copy(k, lane, dest, src).wait_send()
                )
                pl.when(dest == p.c)(lambda src=src: place_own(src).wait())
        for i in range(places):
            pl.when(p.c != i)(lambda i=i: arrival(i).wait_recv())
    gain_sum.finish()
    for projection_sum in projection_sums:
        projection_sum.sum.finish()
    out_sum.sum.finish()
    for scatter in scatters:
        scatter.sent()


def weight_grads(lines, operands, column_operands):
    rows, shard = operands[3].shape[1:]
    width = 4 * shard
    places = 2 * lines
    tall = width // places
    wide = shard + 2 * HD // 4
    gain_wide = -(-tall // 128) * 128
    in_vmem = pl.BlockSpec(memory_space=VMEM)
    anywhere = pl.BlockSpec(memory_space=pl.ANY)
    shape = jax.ShapeDtypeStruct
    with_columns = bool(column_operands)
    column_shapes, column_scratch = (), []
    if with_columns:
        block = column_operands[1].shape[2] // 4
        chunk = width // lines
        column_shapes = (shape((places, chunk // 2, block), bf16),)
        column_scratch = [
            VMEM((4, chunk, block), bf16),
            VMEM((lines, 2, chunk, block), bf16),
            VMEM((2, chunk, block), bf16),
            VMEM((lines, chunk, block), bf16),
            VMEM((lines, chunk, block), bf16),
            DMA((GroupSum.sems, lines)),
            DMA((3, places)),
            *held(column_operands),
        ]
    return pl.pallas_call(
        functools.partial(grads_kernel, lines, with_columns),
        out_shape=(shape((tall, wide), bf16), shape((8, gain_wide), f32), shape((tall, shard), bf16)) + column_shapes,
        in_specs=[in_vmem] * 2 + [anywhere] * (3 + len(column_operands)),
        out_specs=[in_vmem] * 3 + [anywhere] * len(column_shapes),
        scratch_shapes=[
            VMEM((2, places, tall, wide // 2), bf16),
            VMEM((2, lines, tall, wide // 2), bf16),
            VMEM((2, 2, lines - 1, tall, wide // 2), bf16),
            VMEM((2, 3, places // 4, tall, wide // 2), bf16),
            VMEM((places, tall, shard), bf16),
            VMEM((lines, tall, shard), bf16),
            VMEM((2, lines - 1, tall, shard), bf16),
            VMEM((places, 8, gain_wide), f32),
            VMEM((lines, 8, gain_wide), f32),
            VMEM((2, lines - 1, 8, gain_wide), f32),
            VMEM((4, 8, gain_wide), f32),
            *held(operands[3:5]),
            DMA((5,)),
            DMA((2, LineSum.sems, lines)),
            DMA((LineSum.sems, lines)),
            DMA((LineSum.sems, lines)),
            DMA((2, 4)),
            DMA((2, GroupScatter.sems, 3)),
        ]
        + column_scratch,
        compiler_params=pltpu.CompilerParams(
            collective_id=3, has_side_effects=True, vmem_limit_bytes=vmem_bytes
        ),
        name="grads",
    )(*operands, *column_operands)


def assemble_kernel(lines, piece, projection, out, down, columns, *outs):
    query_out, keyval_out, out_out, down_out, columns_out = outs
    shard = out.shape[1]
    padded_piece = columns.shape[2] // 2
    query_out[...] = projection[:, :shard].astype(f32)
    keyval_out[...] = projection[:, shard:].astype(f32)
    out_out[...] = out[...].astype(f32)
    for i in range(down.shape[0]):
        down_out[i * piece : (i + 1) * piece] = down[i, :piece].astype(f32)
    pieces = [
        columns[place_of_piece(n, lines), :, q * padded_piece : q * padded_piece + piece]
        for q in range(2)
        for n in range(2 * lines)
    ]
    columns_out[...] = jnp.concatenate(pieces, axis=1).astype(f32)


def assemble(lines, piece, projection, out, down, columns):
    tall, wide = projection.shape
    shard = out.shape[1]
    places = 2 * lines
    block = columns.shape[2]
    steps = 4 if tall % 64 == 0 else 1
    run = tall // steps
    full = 2 * places * piece

    def flat(rows, cols):
        return pl.BlockSpec((rows, cols), lambda i: (i, 0))

    shape = jax.ShapeDtypeStruct
    return pl.pallas_call(
        functools.partial(assemble_kernel, lines, piece),
        grid=(steps,),
        out_shape=(
            shape((tall, shard), f32),
            shape((tall, wide - shard), f32),
            shape((tall, shard), f32),
            shape((4 * piece, shard), f32),
            shape((tall, full), f32),
        ),
        in_specs=[
            flat(run, wide),
            flat(run, shard),
            pl.BlockSpec((4 // steps, down.shape[1], shard), lambda i: (i, 0, 0)),
            pl.BlockSpec((places, run, block), lambda i: (0, i, 0)),
        ],
        out_specs=[
            flat(run, shard),
            flat(run, wide - shard),
            flat(run, shard),
            flat(4 // steps * piece, shard),
            flat(run, full),
        ],
        compiler_params=pltpu.CompilerParams(vmem_limit_bytes=vmem_bytes),
        name="assemble",
    )(projection, out, down, columns)


def per_device(
    tokens,
    doc_bounds,
    cotangent,
    norm_one,
    query_weight,
    keyval_weight,
    out_weight,
    norm_two,
    gate_up_weight,
    down_weight,
):
    ctx_size = lax.axis_size("ctx")
    fsdp_size = lax.axis_size("fsdp")
    lines = ctx_size // 2
    rows = tokens.shape[1]
    width = tokens.shape[2]
    length = rows * ctx_size
    inner_width = query_weight.shape[1]
    head_count = inner_width // HD
    hidden_width = gate_up_weight.shape[1] // 2
    piece = hidden_width // (ctx_size * fsdp_size)
    padded_piece = -(-piece // 32) * 32
    padded = padded_piece * fsdp_size
    gains = jnp.stack([norm_one, norm_two])
    cot_rows = cotangent[0]
    down_rows = down_weight
    if piece % 16:
        first = hidden_piece(lax.axis_index("ctx"), lines) * piece
        down_rows = lax.dynamic_slice_in_dim(down_weight, first, piece, 0)
        down_rows = jnp.pad(down_rows, ((0, padded_piece - piece), (0, 0)))
    (
        normed,
        queries,
        window,
        weights,
        mixed,
        middle,
        normed_two,
        cosine,
        sine,
        w_columns,
        cot_all,
        w_down,
    ) = front(
        lines,
        (
            doc_bounds,
            tokens[0],
            gains,
            keyval_weight,
            query_weight,
            out_weight,
            cot_rows,
            down_rows,
            gate_up_weight,
        ),
        head_count,
        padded_piece,
    )
    w_down = w_down.reshape(padded, width)
    fits = middle_bytes(lines, rows, width, padded) <= vmem_bytes
    if fits:
        grad_middle, gain_two_term, grad_gate_up, down_part, normed_two, result_parts = middle_part(
            lines, (gains, cot_all, w_down, normed_two, middle, w_columns), padded
        )
    else:
        cot_all = cot_all.reshape(length, width)
        normed_two = lax.all_gather(normed_two, "ctx", axis=0, tiled=True)
        w_gate_up = lax.all_gather(w_columns, "fsdp", axis=0, tiled=True)
        projected = jnp.dot(normed_two, w_gate_up, preferred_element_type=f32)
        gelu, slope = gelu_parts(projected[:, :padded])
        up_part = projected[:, padded:]
        hidden = (gelu * up_part).astype(bf16)
        grad_hidden = contract_rows(cot_all, w_down)
        grad_gate_up = jnp.concatenate(
            [grad_hidden * up_part * slope, grad_hidden * gelu], axis=1
        ).astype(bf16)
        grad_normed_two = lax.psum_scatter(
            contract_rows(grad_gate_up, w_gate_up).astype(bf16),
            "ctx",
            scatter_dimension=0,
            tiled=True,
        ).astype(f32)
        grad_middle_norm, gain_two_term = norm_back(middle, norm_two[None], grad_normed_two)
        grad_middle = cot_rows.astype(f32) + grad_middle_norm
        result_parts = jnp.dot(hidden, w_down, preferred_element_type=f32).astype(bf16)
        down_part = lax.psum_scatter(
            contract_tokens(hidden, cot_all).astype(bf16),
            "fsdp",
            scatter_dimension=1,
            tiled=True,
        ).reshape(fsdp_size, padded_piece, -1)
    operands = (
        grad_middle,
        tokens[0],
        gains,
        cosine,
        sine,
        out_weight,
        weights,
        window,
        queries,
        mixed,
        query_weight,
        keyval_weight,
        down_part,
    )
    if fits:
        result, input_grad, gain_one_term, grad_linear, out_parts, down_grad = back(
            lines, operands, (middle, result_parts)
        )
    else:
        input_grad, gain_one_term, grad_linear, out_parts, down_grad = back(lines, operands, ())
        branch_two = lax.psum_scatter(result_parts, "ctx", scatter_dimension=0, tiled=True)
        result = (middle + branch_two.astype(f32)).astype(bf16)

    operands = (gain_one_term, gain_two_term, out_parts, normed, grad_linear)
    if fits:
        projection_grad, gain_grads, out_grad, gate_up_part = weight_grads(
            lines, operands, (normed_two, grad_gate_up)
        )
    else:
        projection_grad, gain_grads, out_grad = weight_grads(lines, operands, ())
        gate_up_part = lax.psum_scatter(
            contract_tokens(normed_two, grad_gate_up).astype(bf16),
            "fsdp",
            scatter_dimension=1,
            tiled=True,
        )
        gate_up_part = lax.all_to_all(
            gate_up_part.reshape(ctx_size, width // ctx_size, -1), "ctx", 0, 0, tiled=True
        )
    query_grad, keyval_grad, out_grad, down_grad, gate_up_grad = assemble(
        lines, piece, projection_grad, out_grad, down_grad, gate_up_part
    )
    share = width // (ctx_size * fsdp_size)
    gains = lax.dynamic_slice_in_dim(gain_grads, lax.axis_index("fsdp") * share, share, 1)
    return (
        result[None],
        input_grad[None],
        gains[0],
        query_grad,
        keyval_grad,
        out_grad,
        gains[1],
        gate_up_grad,
        down_grad,
    )


def solution(mesh):
    placed = (
        P("fsdp", "ctx", None),
        P("fsdp", None),
        P("fsdp", "ctx", None),
        P(),
        P("fsdp", None),
        P("fsdp", None),
        P("fsdp", None),
        P(),
        P("fsdp", None),
        P("fsdp", None),
    )
    return jax.shard_map(
        per_device,
        mesh=mesh,
        in_specs=placed,
        out_specs=(
            P("fsdp", "ctx", None),
            P("fsdp", "ctx", None),
            P(("ctx", "fsdp")),
            P("ctx", "fsdp"),
            P("ctx", "fsdp"),
            P("ctx", "fsdp"),
            P(("ctx", "fsdp")),
            P("ctx", "fsdp"),
            P("ctx", "fsdp"),
        ),
        check_vma=False,
    )
```

```python
import functools
import math

import jax
import jax.numpy as jnp
from jax import lax
from jax.experimental import pallas as pl
from jax.experimental.pallas import tpu as pltpu
from jax.sharding import PartitionSpec as P

HD = 256
WINDOW = 2048


epsilon = 1e-06
f32 = jnp.float32
bf16 = jnp.bfloat16
VMEM = pltpu.VMEM
DMA = pltpu.SemaphoreType.DMA
vmem_bytes = 62 * 1024 * 1024


def rms_norm(values, gain):
    return values * lax.rsqrt(jnp.mean(values * values, axis=-1, keepdims=True) + epsilon) * gain


def documents(index, bounds):
    return (index >= bounds[0]).astype(jnp.int32) + (index >= bounds[1]).astype(jnp.int32)


def contract_rows(left, right):
    return lax.dot_general(
        left, right, (((1,), (1,)), ((), ())), preferred_element_type=jnp.float32
    )


def contract_tokens(left, right):
    return lax.dot_general(
        left, right, (((0,), (0,)), ((), ())), preferred_element_type=jnp.float32
    )


def remote(src, dst, send_sem, recv_sem, device):
    return pltpu.make_async_remote_copy(
        src_ref=src,
        dst_ref=dst,
        send_sem=send_sem,
        recv_sem=recv_sem,
        device_id=device,
        device_id_type=pl.DeviceIdType.MESH,
    )


class Place:
    def __init__(self, lines):
        self.lines = lines
        self.c = lax.axis_index("ctx")
        self.f = lax.axis_index("fsdp")
        self.line = self.c // 2
        self.lane = self.c % 2
        self.chip = self.f // 2
        self.core = self.f % 2
        self.twin_f = self.f + 1 - 2 * self.core
        self.cross_f = (self.f + 2) % 4
        self.diag_f = (self.twin_f + 2) % 4
        self.twin = {"fsdp": self.twin_f}
        self.cross = {"fsdp": self.cross_f}
        self.diag = {"fsdp": self.diag_f}
        self.beside = {"ctx": self.c + 1 - 2 * self.lane}
        self.right = {"ctx": self.c + 2}
        self.left = {"ctx": self.c - 2}
        self.has_right = self.line < lines - 1
        self.has_left = self.line > 0

    def barrier(self, ctx=True, fsdp=True, also=()):
        sem = pltpu.get_barrier_semaphore()

        def greet(device):
            pl.semaphore_signal(sem, 1, device_id=device, device_id_type=pl.DeviceIdType.MESH)

        count = 0
        if fsdp:
            for device in (self.twin, self.cross, self.diag):
                greet(device)
            count = 3
        if ctx:
            greet(self.beside)
            pl.when(self.has_right)(lambda: greet(self.right))
            pl.when(self.has_left)(lambda: greet(self.left))
            count = (
                count + 1 + self.has_right.astype(jnp.int32) + self.has_left.astype(jnp.int32)
            )
        for needed, device in also:
            pl.when(needed)(lambda device=device: greet(device))
            count = count + needed.astype(jnp.int32)
        pl.semaphore_wait(sem, count)


class Fetch:
    def __init__(self, pairs, sems):
        self.copies = [
            pltpu.make_async_copy(src, dst, sems.at[i]) for i, (src, dst) in enumerate(pairs)
        ]
        for copy in self.copies:
            copy.start()

    def wait(self, *which):
        for i in which:
            self.copies[i].wait()


def held(operands):
    return [VMEM(operand.shape, operand.dtype) for operand in operands]


class LineGather:
    sems = 6

    def __init__(self, place, own, slots, sems):
        self.p, self.own, self.slots, self.s = place, own, slots, sems

    def rightward(self, step):
        at = 2 * (self.p.line - step) + self.p.lane
        src = self.own if step == 0 else self.slots.at[at]
        return remote(src, self.slots.at[at], self.s.at[0, step], self.s.at[1, step], self.p.right)

    def leftward(self, step):
        at = 2 * (self.p.line + step) + self.p.lane
        src = self.own if step == 0 else self.slots.at[at]
        return remote(src, self.slots.at[at], self.s.at[2, step], self.s.at[3, step], self.p.left)

    def across(self, line, own=False):
        at = 2 * line + self.p.lane
        src = self.own if own else self.slots.at[at]
        return remote(
            src, self.slots.at[at], self.s.at[4, line], self.s.at[5, line], self.p.beside
        )

    def from_left(self, step):
        at = 2 * (self.p.line - 1 - step) + self.p.lane
        slot = self.slots.at[at]
        return remote(slot, slot, self.s.at[0, step], self.s.at[1, step], self.p.right)

    def from_right(self, step):
        at = 2 * (self.p.line + 1 + step) + self.p.lane
        slot = self.slots.at[at]
        return remote(slot, slot, self.s.at[2, step], self.s.at[3, step], self.p.left)

    def start(self):
        pl.when(self.p.has_right)(lambda: self.rightward(0).start())
        pl.when(self.p.has_left)(lambda: self.leftward(0).start())
        self.across(self.p.line, True).start()

    def step(self, step):
        p = self.p

        @pl.when(p.line - 1 - step >= 0)
        def _():
            self.from_left(step).wait_recv()
            if step + 1 < p.lines - 1:
                pl.when(p.has_right)(lambda: self.rightward(step + 1).start())
            self.across(p.line - 1 - step).start()

        @pl.when(p.line + 1 + step <= p.lines - 1)
        def _():
            self.from_right(step).wait_recv()
            if step + 1 < p.lines - 1:
                pl.when(p.has_left)(lambda: self.leftward(step + 1).start())
            self.across(p.line + 1 + step).start()

    def steps(self):
        for step in range(self.p.lines - 1):
            self.step(step)

    def arrived_across(self, line):
        at = 2 * line + 1 - self.p.lane
        slot = self.slots.at[at]
        remote(slot, slot, self.s.at[4, line], self.s.at[5, line], self.p.beside).wait_recv()

    def finish(self, arrivals=True):
        p = self.p
        if arrivals:
            for line in range(p.lines):
                self.arrived_across(line)
        for step in range(p.lines - 1):
            pl.when(p.has_right & (p.line - step >= 0))(
                lambda step=step: self.rightward(step).wait_send()
            )
            pl.when(p.has_left & (p.line + step <= p.lines - 1))(
                lambda step=step: self.leftward(step).wait_send()
            )
        for line in range(p.lines):
            self.across(line).wait_send()


class LineSum:
    sems = 6

    def __init__(self, place, parts, side, chain, sems):
        self.p, self.parts, self.side, self.chain, self.s = place, parts, side, chain, sems

    def order(self, turn):
        lines, line = self.p.lines, self.p.line
        value = 0
        for a in range(lines):
            far = sorted(range(lines), key=lambda t: (-abs(t - a), t))
            value = value + jnp.where(line == a, far[turn], 0)
        return value

    def across(self, turn):
        t = self.order(turn)
        at = 2 * t + 1 - self.p.lane
        return remote(
            self.parts.at[at],
            self.side.at[t],
            self.s.at[0, t],
            self.s.at[1, t],
            self.p.beside,
        )

    def rightward(self, t):
        step = self.p.lines - 1 - t
        return remote(
            self.parts.at[2 * t + self.p.lane],
            self.chain.at[0, step],
            self.s.at[2, step],
            self.s.at[3, step],
            self.p.right,
        )

    def leftward(self, t):
        return remote(
            self.parts.at[2 * t + self.p.lane],
            self.chain.at[1, t],
            self.s.at[4, t],
            self.s.at[5, t],
            self.p.left,
        )

    def add(self, at, other):
        self.parts[at] = (self.parts[at].astype(f32) + other.astype(f32)).astype(self.parts.dtype)

    def start(self, ahead=2):
        for turn in range(min(ahead, self.p.lines)):
            self.across(turn).start()

    def near(self, turn, ahead=2):
        p = self.p
        t = self.order(turn)
        at = 2 * t + p.lane
        self.across(turn).wait_recv()
        if ahead and turn + ahead < p.lines:
            self.across(turn + ahead).start()
        self.add(at, self.side[t])
        pl.when((t > p.line) & (p.line == 0))(lambda: self.rightward(t).start())
        pl.when((t < p.line) & (p.line == p.lines - 1))(lambda: self.leftward(t).start())

    def far(self, turn):
        p = self.p
        t = self.order(turn)
        at = 2 * t + p.lane

        @pl.when((t > p.line) & p.has_left)
        def _():
            self.rightward(t).wait_recv()
            self.add(at, self.chain[0, p.lines - 1 - t])
            self.rightward(t).start()

        @pl.when((t < p.line) & p.has_right)
        def _():
            self.leftward(t).wait_recv()
            self.add(at, self.chain[1, t])
            self.leftward(t).start()

    def turns(self, ahead=2):
        for turn in range(self.p.lines):
            self.near(turn, ahead)
            if turn > 0:
                self.far(turn - 1)
        self.far(self.p.lines - 1)

    def total(self):
        p = self.p
        at = 2 * p.line + p.lane

        @pl.when(p.has_left)
        def _():
            self.rightward(p.line).wait_recv()
            self.add(at, self.chain[0, p.lines - 1 - p.line])

        @pl.when(p.has_right)
        def _():
            self.leftward(p.line).wait_recv()
            self.add(at, self.chain[1, p.line])

        return self.parts[at].astype(f32)

    def finish(self):
        p = self.p
        for turn in range(p.lines):
            self.across(turn).wait_send()
        for t in range(p.lines):
            pl.when(t > p.line)(lambda t=t: self.rightward(t).wait_send())
            pl.when(t < p.line)(lambda t=t: self.leftward(t).wait_send())


class Turns:
    def __init__(self, line_sum, ahead=2):
        self.sum, self.ahead, self.nears, self.fars = line_sum, ahead, 0, 0

    def start(self):
        self.sum.start(self.ahead)

    def near(self, upto):
        while self.nears < min(upto, self.sum.p.lines):
            self.sum.near(self.nears, self.ahead)
            self.nears += 1

    def far(self, upto):
        while self.fars < min(upto, self.sum.p.lines):
            self.near(self.fars + 1)
            self.sum.far(self.fars)
            self.fars += 1

    def total(self):
        self.far(self.sum.p.lines)
        return self.sum.total()


class GroupSum:
    sems = 6

    def __init__(self, place, parts, near, out, far, sems):
        self.p, self.parts, self.near, self.out, self.far, self.s = place, parts, near, out, far, sems

    def to_twin(self, i, which, cols):
        p = self.p
        block = p.diag_f if which == 0 else p.twin_f
        return remote(
            self.parts.at[block, :, cols],
            self.near.at[which, :, cols],
            self.s.at[which, i],
            self.s.at[2 + which, i],
            p.twin,
        )

    def to_cross(self, i, cols):
        return remote(
            self.out.at[:, cols], self.far.at[:, cols], self.s.at[4, i], self.s.at[5, i], self.p.cross
        )

    def give(self, i, cols):
        self.to_twin(i, 0, cols).start()
        self.to_twin(i, 1, cols).start()

    def pass_on(self, i, cols):
        self.to_twin(i, 0, cols).wait_recv()
        mine = self.parts[self.p.cross_f, :, cols].astype(f32)
        self.out[:, cols] = (mine + self.near[0, :, cols].astype(f32)).astype(bf16)
        self.to_cross(i, cols).start()

    def take(self, i, cols, own=None):
        self.to_twin(i, 1, cols).wait_recv()
        own = self.parts[self.p.f, :, cols] if own is None else own
        near = own.astype(f32) + self.near[1, :, cols].astype(f32)
        self.to_cross(i, cols).wait_recv()
        return near + self.far[:, cols].astype(f32)

    def given(self, i, cols):
        self.to_twin(i, 0, cols).wait_send()
        self.to_twin(i, 1, cols).wait_send()

    def passed(self, i, cols):
        self.to_cross(i, cols).wait_send()

    def finish(self, i, cols):
        self.given(i, cols)
        self.passed(i, cols)


class GroupTrade:
    sems = 2

    def __init__(self, place, whole, slots, sems, columns):
        self.p, self.whole, self.slots, self.s, self.n = place, whole, slots, sems, columns

    def block(self, g):
        return self.whole.at[:, pl.ds(pl.multiple_of(g * self.n, 128), self.n)]

    def send(self, d):
        self.copy(d).start()

    def copy(self, d):
        g = (self.p.f + d) % 4
        return remote(
            self.block(g), self.slots.at[self.p.f], self.s.at[0, d], self.s.at[1, d], {"fsdp": g}
        )

    def arrival(self, d):
        slot = self.slots.at[(self.p.f + 4 - d) % 4]
        return remote(slot, slot, self.s.at[0, d], self.s.at[1, d], {"fsdp": (self.p.f + d) % 4})

    def own(self):
        return pltpu.make_async_copy(
            self.block(self.p.f), self.slots.at[self.p.f], self.s.at[1, 0]
        )

    def start(self):
        for d in (2, 3, 1):
            self.copy(d).start()
        self.own().start()

    def wait(self):
        self.own().wait()
        for d in (1, 2, 3):
            self.arrival(d).wait_recv()

    def finish(self):
        for d in (1, 2, 3):
            self.copy(d).wait_send()


class GroupScatter:
    sems = 4

    def __init__(self, place, per_owner, stage, slots, sems):
        self.p, self.half, self.stage, self.slots, self.s = place, per_owner // 2, stage, slots, sems
        self.places = (place.twin_f, place.cross_f, place.diag_f)
        self.devices = (place.twin, place.cross, place.diag)

    def slot(self, f, half):
        return self.slots.at[pl.ds((2 * f + half) * self.half, self.half)]

    def own(self):
        return self.slots.at[pl.ds(2 * self.p.f * self.half, 2 * self.half)]

    def copy(self, kind, half):
        return remote(
            self.stage.at[kind, pl.ds(half * self.half, self.half)],
            self.slot(self.p.f, half),
            self.s.at[half, kind],
            self.s.at[2 + half, kind],
            self.devices[kind],
        )

    def arrived(self, kind):
        for half in range(2):
            slot = self.slot(self.places[kind], half)
            remote(
                slot, slot, self.s.at[half, kind], self.s.at[2 + half, kind], self.devices[kind]
            ).wait_recv()

    def send(self, kind):
        for half in range(2):
            self.copy(kind, half).start()

    def sent(self):
        for kind in range(3):
            for half in range(2):
                self.copy(kind, half).wait_send()


class PieceMove:
    def __init__(self, place, per_owner, pieces, slots, sems):
        p = place
        self.p, self.n, self.pieces, self.slots, self.s = p, per_owner, pieces, slots, sems
        self.at = hidden_piece(p.c, p.lines)

    def dest(self, q):
        return self.n * q + self.at // 4

    def copy(self, q):
        return remote(
            self.pieces.at[q],
            self.slots.at[self.at % 4],
            self.s.at[0, q],
            self.s.at[1, self.at % 4],
            {"ctx": self.dest(q)},
        )

    def stay(self, q):
        return pltpu.make_async_copy(self.pieces.at[q], self.slots.at[self.at % 4], self.s.at[2, 0])

    def start(self):
        for q in range(4):
            here = self.dest(q) == self.p.c
            pl.when(~here)(lambda q=q: self.copy(q).start())
            pl.when(here)(lambda q=q: self.stay(q).start())

    def finish(self):
        p = self.p
        for q in range(4):
            here = self.dest(q) == p.c
            pl.when(~here)(lambda q=q: self.copy(q).wait_send())
            pl.when(here)(lambda q=q: self.stay(q).wait())
        for i in range(4):
            source = place_of_piece(4 * (p.c % self.n) + i, p.lines)
            slot = self.slots.at[i]
            arrival = remote(slot, slot, self.s.at[0, 0], self.s.at[1, i], p.beside)
            pl.when(source != p.c)(lambda arrival=arrival: arrival.wait_recv())


def hidden_piece(c, lines):
    return (c % 2) * lines + c // 2


def place_of_piece(piece, lines):
    return (piece % lines) * 2 + piece // lines


class GroupReturn(GroupTrade):
    def __init__(self, place, whole, slots, sems):
        super().__init__(place, whole, slots, sems, 0)

    def block(self, g):
        return self.whole.at[g]


def rotary_tables(first, rows, bounds):
    index = first + lax.broadcasted_iota(jnp.int32, (rows, 128), 0)
    lane = lax.broadcasted_iota(jnp.int32, (rows, 128), 1)
    quarter = HD // 4
    member = documents(index, bounds)
    opening = jnp.where(member == 0, 0, jnp.where(member == 1, bounds[0], bounds[1]))
    frequency = jnp.exp((lane % quarter).astype(f32) * (-math.log(10000.0) / quarter))
    angles = (index - opening).astype(f32) * frequency
    sine = jnp.sin(angles)
    return jnp.cos(angles), jnp.where(lane < quarter, -sine, sine)


def rotated(v, cosine, sine):
    first = v[:, :128]
    return jnp.concatenate(
        [first * cosine + pltpu.roll(first, 64, 1) * sine, v[:, 128:]], axis=1
    )


class GroupGather:
    sems = 6

    def __init__(self, place, own, whole, sems, own_sem, pieces, cuts=None):
        self.p, self.own, self.whole, self.s, self.own_sem = place, own, whole, sems, own_sem
        self.pieces, self.n, self.cuts = pieces, own.shape[0] // pieces, cuts

    def span(self, i):
        return (slice(None), self.cuts[i]) if self.cuts else (pl.ds(i * self.n, self.n),)

    def part(self, i):
        return self.own.at[self.span(i)]

    def slot(self, g, i):
        return self.whole.at[(g,) + self.span(i)]

    def local(self):
        return pltpu.make_async_copy(self.own, self.whole.at[self.p.f], self.own_sem)

    def to_twin(self, i):
        return remote(
            self.part(i), self.slot(self.p.f, i), self.s.at[0, i], self.s.at[3, i], self.p.twin
        )

    def to_cross(self, i):
        return remote(
            self.part(i), self.slot(self.p.f, i), self.s.at[1, i], self.s.at[4, i], self.p.cross
        )

    def forward(self, i):
        slot = self.slot(self.p.cross_f, i)
        return remote(slot, slot, self.s.at[2, i], self.s.at[5, i], self.p.twin)

    def give(self, i):
        self.to_cross(i).start()
        self.to_twin(i).start()

    def near(self, i):
        twin = self.slot(self.p.twin_f, i)
        remote(twin, twin, self.s.at[0, i], self.s.at[3, i], self.p.twin).wait_recv()

    def pass_on(self, i):
        slot = self.slot(self.p.cross_f, i)
        remote(slot, slot, self.s.at[1, i], self.s.at[4, i], self.p.cross).wait_recv()
        self.forward(i).start()

    def last(self, i):
        diag = self.slot(self.p.diag_f, i)
        remote(diag, diag, self.s.at[2, i], self.s.at[5, i], self.p.twin).wait_recv()

    def sent(self, i):
        self.to_twin(i).wait_send()
        self.to_cross(i).wait_send()
        self.forward(i).wait_send()

    def finish(self, i):
        self.near(i)
        self.last(i)
        self.sent(i)


def is_long(length):
    return length > 2048


def tiles_of(first, count, tile):
    tile = tile if count % tile == 0 else 128

    def loop(body):
        def one(i, carry):
            body(pl.ds(pl.multiple_of(first + i * tile, 128), tile))
            return carry

        lax.fori_loop(0, count // tile, one, 0, unroll=True)

    return loop


def front_kernel(
    lines,
    bounds_ref,
    x_ref,
    gains,
    w_keyval_in,
    w_query_in,
    w_out_in,
    cot,
    w_down,
    w_gate_up,
    normed_dst,
    query_dst,
    keyval_dst,
    probs_dst,
    mixed_dst,
    middle_out,
    normed_two_out,
    cosine,
    sine,
    columns_dst,
    cot_all,
    rows_all,
    whole,
    slots,
    parts,
    near,
    out,
    far,
    keyval,
    mixed,
    bias,
    w_rows,
    windows,
    normed_out,
    query_out,
    keyval_out,
    probs_out,
    mixed_out,
    columns_out,
    put_sems,
    w_keyval,
    w_query,
    w_out,
    fetch_sems,
    trade_sems,
    sum_sems,
    keyval_sems,
    cot_sems,
    row_sems,
    own_sems,
):
    p = Place(lines)
    rows, width = x_ref.shape
    length = bias.shape[1]
    heads = query_out.shape[0]
    inner = heads * HD
    kv_width = 2 * HD
    fetch = Fetch(
        ((w_keyval_in, w_keyval), (w_query_in, w_query), (w_out_in, w_out)), fetch_sems
    )
    p.barrier()
    puts = []

    def put(src, dst):
        puts.append(pltpu.make_async_copy(src, dst, put_sems.at[len(puts)]))
        puts[-1].start()


    units = w_gate_up.shape[1] // 2
    piece = units // (4 * 2 * lines)
    padded_piece = w_rows.shape[0]
    own_piece = hidden_piece(p.c, lines)
    if w_down.shape[0] == padded_piece:
        rows_copy = pltpu.make_async_copy(w_down, w_rows, own_sems.at[2])
    else:
        rows_copy = pltpu.make_async_copy(
            w_down.at[pl.ds(pl.multiple_of(own_piece * piece, 16), piece)],
            w_rows.at[pl.ds(0, piece)],
            own_sems.at[2],
        )
    rows_copy.start()
    span = windows.shape[2]
    shard = w_gate_up.shape[0]

    def window_first(q):
        first = q * (units // 4) + own_piece * piece
        return jnp.minimum(first // 128 * 128, 2 * units - span), first

    def window(q):
        return pltpu.make_async_copy(
            w_gate_up.at[:, pl.ds(pl.multiple_of(window_first(q)[0], 128), span)],
            windows.at[q % 2],
            own_sems.at[3 + q % 2],
        )

    def pack_columns(q):
        window(q).wait()
        start, first = window_first(q)
        by = first - start
        lane = lax.broadcasted_iota(jnp.int32, (shard, 128), 1)
        tiles = [
            pltpu.roll(windows[q % 2, :, t * 128 : (t + 1) * 128].astype(f32), (128 - by % 128) % 128, 1)
            for t in range(span // 128)
        ]
        late = by >= 128
        turned = []
        for t in range(span // 128 - 1):
            turned.append(jnp.where(lane < 128 - by % 128, tiles[t], tiles[t + 1]))
        turned.append(jnp.where(lane < 128 - by % 128, tiles[-1], 0.0))
        turned = [
            jnp.where(late, turned[t + 1], turned[t]) for t in range(span // 128 - 1)
        ]
        turned = jnp.concatenate(turned, axis=1)[:, :padded_piece]
        lane = lax.broadcasted_iota(jnp.int32, (shard, padded_piece), 1)
        columns_out[:, q * padded_piece : (q + 1) * padded_piece] = jnp.where(
            lane < piece, turned, 0.0
        ).astype(bf16)
        if q + 2 < 8:
            window(q + 2).start()

    window(0).start()
    window(1).start()
    down = GroupGather(p, w_rows, rows_all, row_sems, own_sems.at[0], row_sems.shape[1])
    cot_gather = LineGather(p, cot, cot_all, cot_sems)
    cot_local = pltpu.make_async_copy(cot, cot_all.at[p.c], own_sems.at[1])

    def give(first, last):
        for i in range(first, min(last, down.pieces)):
            down.give(i)

    def pass_on(first, last):
        for i in range(first, min(last, down.pieces)):
            down.pass_on(i)

    source = x_ref[...].astype(f32)
    whole[...] = rms_norm(source, gains[0:1]).astype(bf16)
    trade = GroupTrade(p, whole, slots.at[0], trade_sems.at[0], slots.shape[3])
    trade.start()
    cot_local.start()
    cot_gather.start()
    bounds = (bounds_ref[0, 0], bounds_ref[0, 1])
    cosine[...], sine[...] = rotary_tables(p.c * rows, rows, bounds)
    query_at = p.c * rows + lax.broadcasted_iota(jnp.int32, (rows, length), 0)
    key_at = lax.broadcasted_iota(jnp.int32, (rows, length), 1)
    allowed = (
        (query_at >= key_at)
        & (query_at - key_at < WINDOW)
        & (documents(query_at, bounds) == documents(key_at, bounds))
    )
    bias[...] = jnp.where(allowed, 0.0, -1e30)
    rows_copy.wait()
    if w_down.shape[0] != padded_piece and piece < padded_piece:
        w_rows[pl.ds(piece, padded_piece - piece)] = jnp.zeros(
            (padded_piece - piece, width), bf16
        )
    down.local().start()
    give(0, 1)
    trade.wait()
    normed_out[...] = slots[0]
    put(normed_out, normed_dst)

    half = (heads // 2) * HD
    chunks = [(0, kv_width), (kv_width, half), (kv_width + half, inner - half)]
    group = GroupSum(p, parts, near, out, far, sum_sems.at[0])

    def project(lhs, weight, first, count, to):
        @tiles_of(first, count, 256)
        def _(cols):
            left = lhs[...].reshape(4 * rows, lhs.shape[-1])
            product = jnp.dot(left, weight[:, cols], preferred_element_type=f32)
            if to:
                cols = pl.ds(pl.multiple_of(cols.start + to, 128), cols.size)
            parts[:, :, cols] = product.astype(bf16).reshape(4, rows, cols.size)

    spans = [pl.ds(first, count) for first, count in chunks]
    fetch.wait(0, 1)
    project(slots.at[0], w_keyval, 0, kv_width, 0)
    group.give(0, spans[0])
    project(slots.at[0], w_query, 0, half, kv_width)
    group.give(1, spans[1])
    group.pass_on(0, spans[0])
    project(slots.at[0], w_query, half, inner - half, kv_width)
    group.give(2, spans[2])
    group.pass_on(1, spans[1])
    group.pass_on(2, spans[2])

    linear = group.take(0, spans[0])
    keyval[0, p.c] = rotated(linear[:, :HD], cosine[...], sine[...]).astype(bf16)
    keyval[1, p.c] = linear[:, HD:].astype(bf16)
    kv_gathers = [
        LineGather(p, keyval.at[i, p.c], keyval.at[i], keyval_sems.at[i]) for i in range(2)
    ]
    for gather in kv_gathers:
        gather.start()
    for gather in kv_gathers:
        gather.step(0)

    def take_queries(i):
        linear = group.take(i, spans[i])
        for h in range(linear.shape[1] // HD):
            turned = rotated(linear[:, h * HD : (h + 1) * HD], cosine[...], sine[...])
            at = h if i == 1 else h + heads // 2
            query_out[at] = (turned * HD**-0.5).astype(bf16)

    give(1, 4)
    take_queries(1)
    for step in range(1, lines - 1):
        for gather in kv_gathers:
            gather.step(step)
    cot_gather.step(0)
    take_queries(2)
    for gather in kv_gathers:
        gather.finish()
    keyval_out[...] = keyval[...]
    put(keyval_out, keyval_dst)
    put(query_out, query_dst)


    def two_heads(i, carry):
        keys = keyval[0].reshape(length, HD)
        values = keyval[1].reshape(length, HD)
        two = query_out[pl.ds(2 * i, 2)].reshape(2 * rows, HD)
        scores = contract_rows(two, keys).reshape(2, rows, length) + bias[...][None]
        scores = scores.reshape(2 * rows, length)
        weights = jnp.exp(scores - jnp.max(scores, axis=-1, keepdims=True))
        total = jnp.sum(weights, axis=-1, keepdims=True)
        weights = (weights / total).astype(bf16)
        probs_out[pl.ds(2 * i, 2)] = weights.reshape(2, rows, length)
        product = jnp.dot(weights, values, preferred_element_type=f32).astype(bf16)
        at = pl.multiple_of(i * 2 * HD, 128)
        mixed[:, pl.ds(at, HD)] = product[:rows]
        mixed[:, pl.ds(at + HD, HD)] = product[rows:]
        return carry

    lax.fori_loop(0, heads // 2, two_heads, 0, unroll=not is_long(length))
    trade_two = GroupTrade(p, mixed, slots.at[1], trade_sems.at[1], slots.shape[3])
    trade_two.start()
    give(4, 6)
    put(probs_out, probs_dst)
    for q in range(4):
        pack_columns(q)
    if lines > 2:
        cot_gather.step(1)
    for i in range(len(chunks)):
        group.finish(i, spans[i])
    trade_two.wait()
    mixed_out[...] = slots[1]
    put(mixed_out, mixed_dst)
    fetch.wait(2)

    half = width // 2
    spans_two = [pl.ds(0, half), pl.ds(half, half)]
    group_two = GroupSum(p, parts, near, out, far, sum_sems.at[1])
    for i in range(2):
        project(slots.at[1], w_out, i * half, half, 0)
        group_two.give(i, spans_two[i])
    for i in range(2):
        group_two.pass_on(i, spans_two[i])
    give(6, 8)
    for q in range(4, 8):
        pack_columns(q)
    put(columns_out, columns_dst)
    pass_on(0, 6)
    for step in range(2, lines - 1):
        cot_gather.step(step)
    for i in range(2):
        middle_out[:, spans_two[i]] = x_ref[:, spans_two[i]].astype(f32) + group_two.take(
            i, spans_two[i]
        )
    normed_two_out[...] = rms_norm(middle_out[...], gains[1:2]).astype(bf16)

    pass_on(6, 8)
    for i in range(2):
        group_two.finish(i, spans_two[i])
    trade.finish()
    trade_two.finish()
    for copy in puts:
        copy.wait()
    down.local().wait()
    cot_local.wait()
    for i in range(down.pieces):
        down.finish(i)
    cot_gather.finish()


def front(lines, operands, heads, padded_piece):
    x = operands[1]
    rows, width = x.shape
    places = 2 * lines
    length = places * rows
    inner = heads * HD
    shard = width // 4
    parts_width = inner + 2 * HD
    in_vmem = pl.BlockSpec(memory_space=VMEM)
    anywhere = pl.BlockSpec(memory_space=pl.ANY)
    shape = jax.ShapeDtypeStruct
    pieces = 8 if padded_piece % 128 == 0 else 1
    assert inner == width
    copied = [
        shape((4, rows, shard), bf16),
        shape((heads, rows, HD), bf16),
        shape((2, places, rows, HD), bf16),
        shape((heads, rows, length), bf16),
        shape((4, rows, shard), bf16),
        shape((shard, 8 * padded_piece), bf16),
    ]
    outs = (
        *copied[:5],
        shape((rows, width), f32),
        shape((rows, width), bf16),
        shape((rows, 128), f32),
        shape((rows, 128), f32),
        copied[5],
        shape((places, rows, width), bf16),
        shape((4, padded_piece, width), bf16),
    )
    return pl.pallas_call(
        functools.partial(front_kernel, lines),
        out_shape=outs,
        in_specs=[pl.BlockSpec(memory_space=pltpu.SMEM)] + [in_vmem] * 2 + [anywhere] * 6,
        out_specs=[anywhere] * 5 + [in_vmem] * 4 + [anywhere] * 3,
        scratch_shapes=[
            VMEM((rows, width), bf16),
            VMEM((2, 4, rows, shard), bf16),
            VMEM((4, rows, parts_width), bf16),
            VMEM((2, rows, parts_width), bf16),
            VMEM((rows, parts_width), bf16),
            VMEM((rows, parts_width), bf16),
            VMEM((2, places, rows, HD), bf16),
            VMEM((rows, inner), bf16),
            VMEM((rows, length), f32),
            VMEM((padded_piece, width), bf16),
            VMEM((2, shard, (padded_piece + 127) // 128 * 128 + 128), bf16),
            *held(copied),
            DMA((6,)),
            *held(operands[3:6]),
            DMA((3,)),
            DMA((2, GroupTrade.sems, 4)),
            DMA((2, GroupSum.sems, 3)),
            DMA((2, LineGather.sems, lines)),
            DMA((LineGather.sems, lines)),
            DMA((GroupGather.sems, pieces)),
            DMA((5,)),
        ],
        compiler_params=pltpu.CompilerParams(
            collective_id=0, has_side_effects=True, vmem_limit_bytes=vmem_bytes
        ),
        name="front",
    )(*operands)


def gelu_parts(v):
    k = 0.7978845608028654
    square = v * v
    inner = jnp.tanh(k * v * (1.0 + 0.044715 * square))
    half = 0.5 * (1.0 + inner)
    slope = half + 0.5 * v * (1.0 - inner * inner) * (k * (1.0 + 3 * 0.044715 * square))
    return v * half, slope


def norm_back(values, gain, grad):
    r = lax.rsqrt(jnp.mean(values * values, axis=-1, keepdims=True) + epsilon)
    scaled = values * r
    inner = grad * gain
    grad_values = r * (inner - scaled * jnp.mean(inner * scaled, axis=-1, keepdims=True))
    return grad_values, jnp.sum(grad * scaled, axis=0, keepdims=True)


def middle_kernel(
    lines,
    gains,
    cot_in,
    w_rows_in,
    own,
    middle,
    w_columns,
    grad_middle_out,
    gain_out,
    grads_dst,
    down_out,
    normed_all_out,
    result_parts,
    normed_all,
    weights,
    grad_hidden,
    hidden,
    parts,
    side,
    chain,
    down_near,
    down_stage,
    down_far,
    cot_all,
    w_rows,
    grads_out,
    put_sems,
    fetch_sems,
    gather_sems,
    column_sems,
    sum_sems,
    down_sems,
    own_sems,
):
    p = Place(lines)
    rows, width = own.shape
    two = 2 * rows
    padded = hidden.shape[2]
    shard = width // 4
    tile = 256 if padded % 256 == 0 else 128
    fetch = Fetch(((cot_in, cot_all), (w_rows_in, w_rows)), fetch_sems)
    p.barrier()

    columns = GroupGather(p, w_columns, weights, column_sems, own_sems.at[0], column_sems.shape[1])
    gather = LineGather(p, own, normed_all, gather_sems)
    gather.start()
    for i in range(columns.pieces):
        columns.give(i)
    columns.local().start()
    own_local = pltpu.make_async_copy(own, normed_all.at[p.c], own_sems.at[2 + lines])
    own_local.start()
    middle_local = pltpu.make_async_copy(middle, grad_middle_out, own_sems.at[3 + lines])
    middle_local.start()

    def hidden_grad(line):
        def one(i, carry):
            cols = pl.ds(pl.multiple_of(i * tile, 128), tile)
            left = cot_all[pl.ds(2 * line, 2)].reshape(two, width)
            right = w_rows[pl.ds(pl.multiple_of(i * tile, 16), tile)]
            grad_hidden[line, :, cols] = contract_rows(left, right)
            return carry

        lax.fori_loop(0, padded // tile, one, 0)

    fetch.wait(0, 1)
    done = 0
    for step in range(lines - 1):
        hidden_grad(done)
        done += 1
        gather.step(step)
        if step < columns.pieces:
            columns.pass_on(step)
    for i in range(lines - 1, columns.pieces):
        columns.pass_on(i)
    while done < lines:
        hidden_grad(done)
        done += 1
    gather.finish()
    own_local.wait()
    columns.local().wait()
    for i in range(columns.pieces):
        columns.finish(i)
    normed_local = pltpu.make_async_copy(normed_all, normed_all_out, own_sems.at[1])
    normed_local.start()

    line_sums = [
        LineSum(p, parts.at[i], side.at[i], chain.at[i], sum_sems.at[i]) for i in range(2)
    ]

    def near(turn):
        for line_sum in line_sums:
            line_sum.near(turn, 0)

    def far(turn):
        for line_sum in line_sums:
            line_sum.far(turn)

    def feed_forward(turn):
        line = line_sums[0].order(turn)

        def one(i, carry):
            cols = pl.ds(pl.multiple_of(i * tile, 128), tile)
            up_cols = pl.ds(pl.multiple_of(i * tile + padded, 128), tile)
            left = normed_all[pl.ds(2 * line, 2)].reshape(two, width)
            gate = jnp.dot(
                left, weights[:, :, cols].reshape(width, tile), preferred_element_type=f32
            )
            up = jnp.dot(
                left, weights[:, :, up_cols].reshape(width, tile), preferred_element_type=f32
            )
            gelu, slope = gelu_parts(gate)
            grad = grad_hidden[line, :, cols]
            hidden[line, :, cols] = (gelu * up).astype(bf16)
            grads_out[line, :, cols] = (grad * up * slope).astype(bf16)
            grads_out[line, :, up_cols] = (grad * gelu).astype(bf16)
            return carry

        lax.fori_loop(0, padded // tile, one, 0, unroll=True)

        def back(g, carry):
            product = contract_rows(grads_out[line], weights[g]).astype(bf16)
            cols = pl.ds(pl.multiple_of(g % 2 * shard, 128), shard)
            parts[g // 2, pl.ds(2 * line, 2), :, cols] = product.reshape(2, rows, shard)
            return carry

        pltpu.make_async_copy(grads_out.at[line], grads_dst.at[line], put_sems.at[turn]).start()
        for half in range(2):
            lax.fori_loop(2 * half, 2 * half + 2, back, 0, unroll=True)
            line_sums[half].across(turn).start()

    result_stage = normed_all

    def result_copy(line):
        blocks = pl.ds(2 * line, 2)
        return pltpu.make_async_copy(
            result_stage.at[blocks], result_parts.at[blocks], own_sems.at[2 + line]
        )

    def result_part(line):
        def one(i, carry):
            cols = pl.ds(pl.multiple_of(i * shard, 128), shard)
            product = jnp.dot(
                hidden[line], w_rows[:, cols], preferred_element_type=f32
            ).astype(bf16)
            result_stage[pl.ds(2 * line, 2), :, cols] = product.reshape(2, rows, shard)
            return carry

        lax.fori_loop(0, 4, one, 0, unroll=True)
        result_copy(line).start()

    quarter = padded // 4
    every = slice(None)
    down_parts = weights.at[:, pl.ds(0, quarter), pl.ds(0, shard)]

    def down_group(i):
        return GroupSum(p, down_parts, down_near.at[i], down_stage.at[i % 2], down_far.at[i], down_sems)

    def down_chunk(i):
        def one(g, carry):
            cols = pl.ds(pl.multiple_of(g * shard, 128), shard)
            left = hidden[:, :, i * quarter : (i + 1) * quarter].reshape(lines * two, quarter)
            right = cot_all[:, :, cols].reshape(lines * two, shard)
            down_parts[g] = contract_tokens(left, right).astype(bf16)
            return carry

        lax.fori_loop(0, 4, one, 0, unroll=True)
        down_out[i] = down_parts[p.f]
        down_group(i).give(i, every)

    for turn in range(lines):
        feed_forward(turn)
        if turn == lines - 2:
            near(0)
    normed_local.wait()
    for turn in range(lines):
        line = line_sums[0].order(turn)
        pltpu.make_async_copy(grads_out.at[line], grads_dst.at[line], put_sems.at[turn]).wait()

    for i in range(4):
        if i >= 1:
            down_group(i - 1).given(i - 1, every)
        if i >= 2:
            down_group(i - 2).passed(i - 2, every)
        down_chunk(i)
        down_group(i).pass_on(i, every)
        if i == 1:
            if lines > 2:
                near(1)
            far(0)
        if i == 2 and lines > 3:
            near(2)
            far(1)
            far(2)
    for line in range(lines):
        result_part(line)
    for turn in range(3, lines - 1):
        near(turn)
        far(turn)
    near(lines - 1)
    far(lines - 1)
    grad = jnp.concatenate([line_sum.total() for line_sum in line_sums], axis=1)
    middle_local.wait()
    grad_values, gain = norm_back(grad_middle_out[...], gains[1:2], grad)
    grad_middle_out[...] = cot_all[p.c].astype(f32) + grad_values
    gain_out[...] = gain
    for i in range(2):
        down_out[i] = down_group(i).take(i, every, down_out[i]).astype(bf16)
    for i in (2, 3):
        down_out[i] = down_group(i).take(i, every, down_out[i]).astype(bf16)
        down_group(i).passed(i, every)
    down_group(3).given(3, every)
    for line in range(lines):
        result_copy(line).wait()
    for line_sum in line_sums:
        line_sum.finish()


def middle_bytes(lines, rows, width, padded):
    length = 2 * lines * rows
    return (
        14 * rows * width
        + 9 * length * width
        + 9 * padded * width
        + 10 * length * padded
    )


def middle_part(lines, operands, padded):
    own = operands[3]
    rows, width = own.shape
    places = 2 * lines
    shard = width // 4
    quarter = padded // 4
    pieces = 4
    in_vmem = pl.BlockSpec(memory_space=VMEM)
    anywhere = pl.BlockSpec(memory_space=pl.ANY)
    shape = jax.ShapeDtypeStruct
    return pl.pallas_call(
        functools.partial(middle_kernel, lines),
        out_shape=(
            shape((rows, width), f32),
            shape((1, width), f32),
            shape((lines, 2 * rows, 2 * padded), bf16),
            shape((4, quarter, shard), bf16),
            shape((places, rows, width), bf16),
            shape((places, rows, width), bf16),
        ),
        in_specs=[in_vmem] + [anywhere] * 5,
        out_specs=[in_vmem] * 2 + [anywhere, in_vmem] + [anywhere] * 2,
        scratch_shapes=[
            VMEM((places, rows, width), bf16),
            VMEM((4, shard, 2 * padded), bf16),
            VMEM((lines, 2 * rows, padded), f32),
            VMEM((lines, 2 * rows, padded), bf16),
            VMEM((2, places, rows, width // 2), bf16),
            VMEM((2, lines, rows, width // 2), bf16),
            VMEM((2, 2, lines - 1, rows, width // 2), bf16),
            VMEM((4, 2, quarter, shard), bf16),
            VMEM((2, quarter, shard), bf16),
            VMEM((4, quarter, shard), bf16),
            *held(operands[1:3]),
            VMEM((lines, 2 * rows, 2 * padded), bf16),
            DMA((lines,)),
            DMA((2,)),
            DMA((LineGather.sems, lines)),
            DMA((GroupGather.sems, pieces)),
            DMA((2, LineSum.sems, lines)),
            DMA((GroupSum.sems, 4)),
            DMA((4 + lines,)),
        ],
        compiler_params=pltpu.CompilerParams(
            collective_id=1, has_side_effects=True, vmem_limit_bytes=vmem_bytes
        ),
        name="middle",
    )(*operands)


def back_kernel(
    lines,
    with_result,
    grad_middle,
    tokens,
    gains,
    cosine,
    sine,
    w_out_in,
    probs_in,
    keyval_in,
    queries_in,
    mixed_in,
    w_query_in,
    w_keyval_in,
    down_in,
    *rest,
):
    if with_result:
        middle, result_in, result_out, *rest = rest
    (
        input_grad_out,
        gain_out,
        linear_out,
        out_slots,
        down_out,
        branch_all,
        linear_all,
        branch,
        linear,
        trade_parts,
        trade_slots,
        grad_mixed,
        kv_total,
        kv_parts,
        kv_side,
        kv_chain,
        query_parts,
        out_stage,
        w_out,
        probs,
        keyval,
        queries,
        mixed,
        w_query,
        w_keyval,
        fetch_sems,
        branch_sems,
        linear_sems,
        trade_sems,
        kv_sems,
        out_sems,
        piece_sems,
        own_sems,
        *rest,
    ) = rest
    p = Place(lines)
    rows, width = grad_middle.shape
    heads = queries.shape[0]
    length = probs_in.shape[2]
    long = is_long(length)
    operands = [
        (w_out_in, w_out),
        (keyval_in, keyval),
        (queries_in, queries),
        (mixed_in, mixed),
        (w_query_in, w_query),
        (w_keyval_in, w_keyval),
    ]
    fetch = Fetch(operands if long else operands + [(probs_in, probs)], fetch_sems)
    shard = w_out.shape[0]
    kv_width = 2 * HD
    per_owner = 2 * lines // 4
    others = [(jnp.full((), True), {"ctx": (p.c + d) % (2 * lines)}) for d in range(1, 2 * lines)]
    p.barrier(ctx=False, also=others)
    if with_result:
        result_parts, result_side, result_chain, result_sems = rest
        result_sum = Turns(
            LineSum(p, result_parts, result_side, result_chain, result_sems), lines
        )
        half = width // 2
        result_copies = [
            pltpu.make_async_copy(
                result_in.at[:, :, pl.ds(i * half, half)], result_parts.at[i], own_sems.at[2 + i]
            )
            for i in range(2)
        ]
        for copy in result_copies:
            copy.start()
        result_sums = [
            Turns(
                LineSum(
                    p, result_parts.at[i], result_side.at[i], result_chain.at[i], result_sems.at[i]
                ),
                lines,
            )
            for i in range(2)
        ]
    out_scatter = GroupScatter(p, per_owner, out_stage, out_slots, out_sems)

    branch[...] = grad_middle[...].astype(bf16)
    group = GroupGather(p, branch, branch_all, branch_sems, own_sems.at[0], 1)
    group.give(0)
    group.local().start()
    down_move = PieceMove(p, per_owner, down_in, down_out, piece_sems)
    down_move.start()
    if with_result:
        result_copies[0].wait()
        result_sums[0].start()
    back_trade = GroupReturn(p, trade_parts.at[0], trade_slots.at[0], trade_sems.at[0])

    def mixed_back(g):
        trade_parts[0, g] = contract_rows(branch_all[g], w_out[...]).astype(bf16)

    group.local().wait()
    fetch.wait(0)
    mixed_back(p.f)
    back_trade.own().start()
    group.near(0)
    mixed_back(p.twin_f)
    group.pass_on(0)
    mixed_back(p.cross_f)
    back_trade.send(2)
    group.last(0)
    mixed_back(p.diag_f)
    back_trade.send(1)
    back_trade.send(3)

    def out_block(i, g):
        left = mixed[...].reshape(4 * rows, shard)
        right = branch_all[:, :, pl.ds(pl.multiple_of(g * shard, 128), shard)]
        product = contract_tokens(left, right.reshape(4 * rows, shard)).astype(bf16)
        out_stage[i] = product.reshape(out_stage.shape[1:])

    fetch.wait(3)
    out_block(1, p.cross_f)
    out_scatter.copy(1, 0).start()
    out_block(0, p.twin_f)
    out_scatter.send(0)
    out_block(2, p.diag_f)
    out_block(3, p.f)
    out_own = pltpu.make_async_copy(out_stage.at[3], out_scatter.own(), own_sems.at[7])
    out_own.start()
    if with_result:
        result_sums[0].near(2)
        result_copies[1].wait()
        result_sums[1].sum.start(1)
    back_trade.wait()
    for g in range(4):
        grad_mixed[:, g * shard : (g + 1) * shard] = trade_slots[0, g]

    kv_total[...] = jnp.zeros_like(kv_total)
    kv_at, q_at = pl.ds(0, kv_width), pl.ds(kv_width, heads * HD)

    batch = 1 if long else 2
    fetch.wait(1, 2)
    if not long:
        fetch.wait(6)

    def some_heads(i, carry):
        keys = keyval[0].reshape(length, HD)
        values = keyval[1].reshape(length, HD)
        at = [pl.multiple_of((i * batch + h) * HD, 128) for h in range(batch)]
        outer = jnp.concatenate([grad_mixed[:, pl.ds(a, HD)] for a in at], axis=0)
        if batch == 1:
            one = pltpu.make_async_copy(probs_in.at[i], probs, own_sems.at[5])
            one.start()
            one.wait()
            weights = probs[...]
        else:
            weights = probs[pl.ds(batch * i, batch)].reshape(batch * rows, length)
        wide = weights.astype(f32)
        grad_weights = contract_rows(outer, values)
        delta = jnp.sum(wide * grad_weights, axis=-1, keepdims=True)
        grad_scores = (wide * (grad_weights - delta)).astype(bf16)
        product = jnp.dot(grad_scores, keys, preferred_element_type=f32) * HD**-0.5
        for h in range(batch):
            turned = rotated(product[h * rows : (h + 1) * rows], cosine[...], -sine[...])
            linear[:, pl.ds(kv_width + at[h], HD)] = turned.astype(bf16)
        two = queries[pl.ds(batch * i, batch)].reshape(batch * rows, HD)
        kv_total[:, :HD] += contract_tokens(grad_scores, two)
        kv_total[:, HD:] += contract_tokens(weights, outer)
        return carry

    lax.fori_loop(0, heads // batch, some_heads, 0, unroll=not long)
    linear_group = GroupGather(
        p, linear, linear_all, linear_sems, own_sems.at[1], 2, (q_at, kv_at)
    )
    linear_group.give(0)
    out_scatter.copy(1, 1).start()
    kv_parts[...] = kv_total[...].astype(bf16).reshape(kv_parts.shape)
    kv_sum = LineSum(p, kv_parts, kv_side, kv_chain, kv_sems)
    kv_sum.start(lines)
    if with_result:
        for turn in range(1, lines):
            result_sums[1].sum.across(turn).start()
        result_sums[0].near(lines)
        result_sums[0].far(1)
    fetch.wait(4, 5)

    def query_back(g, block):
        query_parts[g] = contract_rows(block, w_query[...])

    query_back(p.f, linear[:, q_at])
    linear_group.near(0)
    query_back(p.twin_f, linear_all[p.twin_f, :, q_at])
    kv_sum.turns(0)
    linear_group.pass_on(0)
    query_back(p.cross_f, linear_all[p.cross_f, :, q_at])
    linear_group.last(0)
    query_back(p.diag_f, linear_all[p.diag_f, :, q_at])
    own = kv_sum.total()
    linear[:, :HD] = rotated(own[:, :HD], cosine[...], -sine[...]).astype(bf16)
    linear[:, pl.ds(HD, HD)] = own[:, HD:].astype(bf16)
    linear_group.give(1)
    out_scatter.copy(2, 0).start()
    linear_group.local().start()
    if with_result:
        result_sums[0].far(2)
        result_sums[1].near(2)
    linear_group.pass_on(1)
    linear_group.local().wait()
    linear_group.near(1)
    linear_group.last(1)
    linear_copy = pltpu.make_async_copy(linear_all, linear_out, own_sems.at[4])
    linear_copy.start()

    last_trade = GroupReturn(p, trade_parts.at[1], trade_slots.at[1], trade_sems.at[1])

    def normed_back(g):
        product = contract_rows(linear_all[g, :, kv_at], w_keyval[...])
        trade_parts[1, g] = (product + query_parts[g]).astype(bf16)

    normed_back(p.cross_f)
    last_trade.send(2)
    normed_back(p.diag_f)
    normed_back(p.twin_f)
    last_trade.send(1)
    last_trade.send(3)
    out_scatter.copy(2, 1).start()
    normed_back(p.f)
    last_trade.own().start()
    if with_result:
        result_sums[0].far(3)
        result_sums[1].far(3)
    last_trade.wait()
    for g in range(4):
        grad_mixed[:, g * shard : (g + 1) * shard] = trade_slots[1, g]
    source = tokens[...].astype(f32)
    grad_values, gain = norm_back(source, gains[0:1], grad_mixed[...].astype(f32))
    input_grad_out[...] = (grad_middle[...] + grad_values).astype(bf16)
    gain_out[...] = gain
    if with_result:
        for i in range(2):
            cols = pl.ds(i * half, half)
            result_out[:, cols] = (middle[:, cols] + result_sums[i].total()).astype(bf16)
            result_sums[i].sum.finish()
    back_trade.finish()
    last_trade.finish()
    group.sent(0)
    linear_group.sent(0)
    linear_group.sent(1)
    kv_sum.finish()
    out_own.wait()
    for kind in range(3):
        out_scatter.arrived(kind)
    out_scatter.sent()
    linear_copy.wait()
    down_move.finish()


def back(lines, operands, result_operands):
    rows, width = operands[0].shape
    heads = operands[8].shape[0]
    places = 2 * lines
    length = places * rows
    shard = width // 4
    linear_width = width + 2 * HD
    tall = width // places
    pieces = operands[12].shape
    in_vmem = pl.BlockSpec(memory_space=VMEM)
    anywhere = pl.BlockSpec(memory_space=pl.ANY)
    shape = jax.ShapeDtypeStruct
    with_result = bool(result_operands)
    long = is_long(length)
    scratch = held(operands[5:12])
    if long:
        scratch[1] = VMEM((rows, length), bf16)
    result_scratch = [
        VMEM((2, places, rows, width // 2), bf16),
        VMEM((2, lines, rows, width // 2), bf16),
        VMEM((2, 2, lines - 1, rows, width // 2), bf16),
        DMA((2, LineSum.sems, lines)),
    ]
    return pl.pallas_call(
        functools.partial(back_kernel, lines, with_result),
        out_shape=((shape((rows, width), bf16),) if with_result else ())
        + (
            shape((rows, width), bf16),
            shape((1, width), f32),
            shape((4, rows, linear_width), bf16),
            shape((places, tall, shard), bf16),
            shape(pieces, bf16),
        ),
        in_specs=[in_vmem] * 5 + [anywhere] * 8 + ([in_vmem, anywhere] if with_result else []),
        out_specs=[in_vmem] * (3 if with_result else 2) + [anywhere] * 3,
        scratch_shapes=[
            VMEM((4, rows, width), bf16),
            VMEM((4, rows, linear_width), bf16),
            VMEM((rows, width), bf16),
            VMEM((rows, linear_width), bf16),
            VMEM((2, 4, rows, shard), bf16),
            VMEM((2, 4, rows, shard), bf16),
            VMEM((rows, width), bf16),
            VMEM((length, 2 * HD), f32),
            VMEM((places, rows, 2 * HD), bf16),
            VMEM((lines, rows, 2 * HD), bf16),
            VMEM((2, lines - 1, rows, 2 * HD), bf16),
            VMEM((4, rows, shard), f32),
            VMEM((4, places // 4, tall, shard), bf16),
            *scratch,
            DMA((7,)),
            DMA((GroupGather.sems, 1)),
            DMA((GroupGather.sems, 2)),
            DMA((2, GroupTrade.sems, 4)),
            DMA((LineSum.sems, lines)),
            DMA((GroupScatter.sems, 3)),
            DMA((3, 4)),
            DMA((8,)),
        ]
        + (result_scratch if with_result else []),
        compiler_params=pltpu.CompilerParams(
            collective_id=2, has_side_effects=True, vmem_limit_bytes=vmem_bytes
        ),
        name="back",
    )(*operands, *result_operands)


def grads_kernel(lines, with_columns, gain_one, gain_two, out_in, normed_in, linear_in, *rest):
    if with_columns:
        normed_two_in, hidden_grads_in, *rest = rest
    projection_out, gains_out, out_out, *rest = rest
    if with_columns:
        columns_out, *rest = rest
    (
        parts,
        side,
        chain,
        stage,
        out_parts,
        out_side,
        out_chain,
        gain_parts,
        gain_side,
        gain_chain,
        gain_slots,
        normed,
        linear_all,
        fetch_sems,
        projection_sems,
        out_sems,
        gain_sems,
        slot_sems,
        scatter_sems,
        *rest,
    ) = rest
    p = Place(lines)
    operands = [(out_in, out_parts)]
    if with_columns:
        (
            chunk_parts,
            near,
            passing,
            far,
            chunks,
            group_sems,
            trade_sems,
            normed_two,
            hidden_grads,
        ) = rest
    if with_columns:
        operands += [(normed_two_in, normed_two), (hidden_grads_in, hidden_grads)]
    operands += [(normed_in, normed), (linear_in, linear_all)]
    fetch = Fetch(operands, fetch_sems)
    places = 2 * lines
    shard = normed.shape[2]
    tokens = 4 * normed.shape[1]
    per_owner = places // 4
    tall = shard // per_owner
    kv_share = 2 * HD // 4
    others = [(jnp.full((), True), {"ctx": (p.c + d) % places}) for d in range(1, places)]
    p.barrier(ctx=False, also=others)

    for c in range(places):
        cols = slice(c * tall, (c + 1) * tall)
        gain_parts[c, 0:1, :tall] = gain_one[:, cols]
        gain_parts[c, 1:2, :tall] = gain_two[:, cols]
    gain_sum = LineSum(p, gain_parts, gain_side, gain_chain, gain_sems)
    gain_sum.start(lines)

    projection_sums = [
        Turns(
            LineSum(p, parts.at[i], side.at[i], chain.at[i], projection_sems.at[i]), lines
        )
        for i in range(2)
    ]
    out_sum = Turns(LineSum(p, out_parts, out_side, out_chain, out_sems))
    fetch.wait(0)
    out_sum.start()

    if with_columns:
        fetch.wait(1, 2)
        block = columns_out.shape[2]
        chunk = chunk_parts.shape[1]
        every = slice(None)

        def chunk_of(k):
            order = sorted(range(lines), key=lambda d: (d == 0, abs(d - lines // 2), d))
            return (p.line + order[k]) % lines

        def group(k):
            return GroupSum(p, chunk_parts, near.at[k], passing.at[k % 2], far.at[k], group_sems)

        def compute(k):
            cols = pl.ds(pl.multiple_of(chunk_of(k) * chunk, 128), chunk)

            def one(g, carry):
                left = normed_two[:, :, cols].reshape(-1, chunk)
                right = hidden_grads[:, :, pl.ds(pl.multiple_of(g * block, 128), block)]
                chunk_parts[g] = contract_tokens(left, right.reshape(-1, block)).astype(bf16)
                return carry

            lax.fori_loop(0, 4, one, 0, unroll=True)
            chunks[k] = chunk_parts[p.f]
            group(k).give(k, every)

        def halves(k):
            half = chunk // 2
            for lane in range(2):
                yield lane, 2 * chunk_of(k) + lane, chunks.at[k, pl.ds(lane * half, half)]

        def place_copy(k, lane, dest, src):
            return remote(
                src,
                columns_out.at[p.c],
                trade_sems.at[0, 2 * k + lane],
                trade_sems.at[1, p.c],
                {"ctx": dest},
            )

        def place_own(src):
            return pltpu.make_async_copy(src, columns_out.at[p.c], trade_sems.at[2, 0])

        def arrival(i):
            slot = columns_out.at[i]
            return remote(slot, slot, trade_sems.at[0, 0], trade_sems.at[1, i], p.beside)

        def complete(k):
            chunks[k] = group(k).take(k, every, chunks[k]).astype(bf16)
            for lane, dest, src in halves(k):
                pl.when(dest != p.c)(
                    lambda k=k, lane=lane, dest=dest, src=src: place_copy(k, lane, dest, src).start()
                )
                pl.when(dest == p.c)(lambda src=src: place_own(src).start())

        def chunk_step(k):
            if k >= 1:
                group(k - 1).given(k - 1, every)
            compute(k)
            if k >= 2:
                group(k - 2).passed(k - 2, every)
            group(k).pass_on(k, every)

        chunk_step(0)

    scatters = [
        GroupScatter(p, per_owner, stage.at[i], parts.at[i], scatter_sems.at[i]) for i in range(2)
    ]

    def projection_block(first, second, g):
        left = normed[...].reshape(tokens, shard)
        right = linear_all[:, :, pl.ds(pl.multiple_of(2 * HD + g * shard, 128), shard)]
        product = contract_tokens(left, right.reshape(tokens, shard)).astype(bf16)
        right = linear_all[:, :, pl.ds(pl.multiple_of(g * kv_share, 128), kv_share)]
        kv_product = contract_tokens(left, right.reshape(tokens, kv_share)).astype(bf16)
        first[...] = product[:, :half].reshape(per_owner, tall, half)
        if half < shard:
            kv_product = jnp.concatenate([product[:, half:], kv_product], axis=1)
        second[...] = kv_product.reshape(per_owner, tall, half)

    half = (shard + kv_share) // 2
    fetch.wait(*((3, 4) if with_columns else (1, 2)))
    for kind in (1, 2, 0):
        projection_block(stage.at[0, kind], stage.at[1, kind], scatters[0].places[kind])
        scatters[0].send(kind)
    for kind in (1, 2, 0):
        scatters[1].send(kind)
    projection_block(scatters[0].own(), scatters[1].own(), p.f)

    first, second = projection_sums
    if with_columns:
        chunk_step(1)
    out_sum.near(2)
    out_sum.far(1)
    if with_columns:
        complete(0)
        if lines > 2:
            chunk_step(2)
    out_sum.near(lines)
    for k in range(lines):
        gain_sum.near(k, 0)
    for kind in range(3):
        scatters[0].arrived(kind)
    first.start()
    out_sum.far(2)
    first.near(2)
    out_sum.far(3)
    first.near(lines)
    for kind in range(3):
        scatters[1].arrived(kind)
    second.start()
    first.far(1)
    for k in range(lines):
        gain_sum.far(k)
    out_out[...] = out_sum.total().astype(bf16)
    first.far(2)
    if with_columns:
        second.near(1)
        for k in range(1, lines):
            complete(k)
            if k + 2 < lines:
                chunk_step(k + 2)
            if k == 1:
                first.far(lines)
                second.near(lines)
            second.far(k)
        for k in (lines - 2, lines - 1):
            group(k).passed(k, every)
        group(lines - 1).given(lines - 1, every)

    own = gain_sum.total()
    gain_parts[p.c] = own

    def gain_copy(d):
        return remote(
            gain_parts.at[p.c],
            gain_slots.at[d],
            slot_sems.at[0, d],
            slot_sems.at[1, d],
            {"fsdp": (p.f + d) % 4},
        )

    for d in (1, 2, 3):
        gain_copy(d).start()
    for i in range(2):
        projection_out[:, i * half : (i + 1) * half] = projection_sums[i].total().astype(bf16)
    for d in (1, 2, 3):
        gain_copy(d).wait_recv()
        own = own + gain_slots[d]
    gains_out[...] = own

    for d in (1, 2, 3):
        gain_copy(d).wait_send()
    if with_columns:
        for k in range(lines):
            for lane, dest, src in halves(k):
                pl.when(dest != p.c)(
                    lambda k=k, lane=lane, dest=dest, src=src: place_copy(k, lane, dest, src).wait_send()
                )
                pl.when(dest == p.c)(lambda src=src: place_own(src).wait())
        for i in range(places):
            pl.when(p.c != i)(lambda i=i: arrival(i).wait_recv())
    gain_sum.finish()
    for projection_sum in projection_sums:
        projection_sum.sum.finish()
    out_sum.sum.finish()
    for scatter in scatters:
        scatter.sent()


def weight_grads(lines, operands, column_operands):
    rows, shard = operands[3].shape[1:]
    width = 4 * shard
    places = 2 * lines
    tall = width // places
    wide = shard + 2 * HD // 4
    gain_wide = -(-tall // 128) * 128
    in_vmem = pl.BlockSpec(memory_space=VMEM)
    anywhere = pl.BlockSpec(memory_space=pl.ANY)
    shape = jax.ShapeDtypeStruct
    with_columns = bool(column_operands)
    column_shapes, column_scratch = (), []
    if with_columns:
        block = column_operands[1].shape[2] // 4
        chunk = width // lines
        column_shapes = (shape((places, chunk // 2, block), bf16),)
        column_scratch = [
            VMEM((4, chunk, block), bf16),
            VMEM((lines, 2, chunk, block), bf16),
            VMEM((2, chunk, block), bf16),
            VMEM((lines, chunk, block), bf16),
            VMEM((lines, chunk, block), bf16),
            DMA((GroupSum.sems, lines)),
            DMA((3, places)),
            *held(column_operands),
        ]
    return pl.pallas_call(
        functools.partial(grads_kernel, lines, with_columns),
        out_shape=(shape((tall, wide), bf16), shape((8, gain_wide), f32), shape((tall, shard), bf16)) + column_shapes,
        in_specs=[in_vmem] * 2 + [anywhere] * (3 + len(column_operands)),
        out_specs=[in_vmem] * 3 + [anywhere] * len(column_shapes),
        scratch_shapes=[
            VMEM((2, places, tall, wide // 2), bf16),
            VMEM((2, lines, tall, wide // 2), bf16),
            VMEM((2, 2, lines - 1, tall, wide // 2), bf16),
            VMEM((2, 3, places // 4, tall, wide // 2), bf16),
            VMEM((places, tall, shard), bf16),
            VMEM((lines, tall, shard), bf16),
            VMEM((2, lines - 1, tall, shard), bf16),
            VMEM((places, 8, gain_wide), f32),
            VMEM((lines, 8, gain_wide), f32),
            VMEM((2, lines - 1, 8, gain_wide), f32),
            VMEM((4, 8, gain_wide), f32),
            *held(operands[3:5]),
            DMA((5,)),
            DMA((2, LineSum.sems, lines)),
            DMA((LineSum.sems, lines)),
            DMA((LineSum.sems, lines)),
            DMA((2, 4)),
            DMA((2, GroupScatter.sems, 3)),
        ]
        + column_scratch,
        compiler_params=pltpu.CompilerParams(
            collective_id=3, has_side_effects=True, vmem_limit_bytes=vmem_bytes
        ),
        name="grads",
    )(*operands, *column_operands)


def assemble_kernel(lines, piece, projection, out, down, columns, *outs):
    query_out, keyval_out, out_out, down_out, columns_out = outs
    shard = out.shape[1]
    padded_piece = columns.shape[2] // 2
    query_out[...] = projection[:, :shard].astype(f32)
    keyval_out[...] = projection[:, shard:].astype(f32)
    out_out[...] = out[...].astype(f32)
    for i in range(down.shape[0]):
        down_out[i * piece : (i + 1) * piece] = down[i, :piece].astype(f32)
    pieces = [
        columns[place_of_piece(n, lines), :, q * padded_piece : q * padded_piece + piece]
        for q in range(2)
        for n in range(2 * lines)
    ]
    columns_out[...] = jnp.concatenate(pieces, axis=1).astype(f32)


def assemble(lines, piece, projection, out, down, columns):
    tall, wide = projection.shape
    shard = out.shape[1]
    places = 2 * lines
    block = columns.shape[2]
    steps = 4 if tall % 64 == 0 else 1
    run = tall // steps
    full = 2 * places * piece

    def flat(rows, cols):
        return pl.BlockSpec((rows, cols), lambda i: (i, 0))

    shape = jax.ShapeDtypeStruct
    return pl.pallas_call(
        functools.partial(assemble_kernel, lines, piece),
        grid=(steps,),
        out_shape=(
            shape((tall, shard), f32),
            shape((tall, wide - shard), f32),
            shape((tall, shard), f32),
            shape((4 * piece, shard), f32),
            shape((tall, full), f32),
        ),
        in_specs=[
            flat(run, wide),
            flat(run, shard),
            pl.BlockSpec((4 // steps, down.shape[1], shard), lambda i: (i, 0, 0)),
            pl.BlockSpec((places, run, block), lambda i: (0, i, 0)),
        ],
        out_specs=[
            flat(run, shard),
            flat(run, wide - shard),
            flat(run, shard),
            flat(4 // steps * piece, shard),
            flat(run, full),
        ],
        compiler_params=pltpu.CompilerParams(vmem_limit_bytes=vmem_bytes),
        name="assemble",
    )(projection, out, down, columns)


def per_device(
    tokens,
    doc_bounds,
    cotangent,
    norm_one,
    query_weight,
    keyval_weight,
    out_weight,
    norm_two,
    gate_up_weight,
    down_weight,
):
    ctx_size = lax.axis_size("ctx")
    fsdp_size = lax.axis_size("fsdp")
    lines = ctx_size // 2
    rows = tokens.shape[1]
    width = tokens.shape[2]
    length = rows * ctx_size
    inner_width = query_weight.shape[1]
    head_count = inner_width // HD
    hidden_width = gate_up_weight.shape[1] // 2
    piece = hidden_width // (ctx_size * fsdp_size)
    padded_piece = -(-piece // 32) * 32
    padded = padded_piece * fsdp_size
    gains = jnp.stack([norm_one, norm_two])
    cot_rows = cotangent[0]
    down_rows = down_weight
    if piece % 16:
        first = hidden_piece(lax.axis_index("ctx"), lines) * piece
        down_rows = lax.dynamic_slice_in_dim(down_weight, first, piece, 0)
        down_rows = jnp.pad(down_rows, ((0, padded_piece - piece), (0, 0)))
    (
        normed,
        queries,
        window,
        weights,
        mixed,
        middle,
        normed_two,
        cosine,
        sine,
        w_columns,
        cot_all,
        w_down,
    ) = front(
        lines,
        (
            doc_bounds,
            tokens[0],
            gains,
            keyval_weight,
            query_weight,
            out_weight,
            cot_rows,
            down_rows,
            gate_up_weight,
        ),
        head_count,
        padded_piece,
    )
    w_down = w_down.reshape(padded, width)
    fits = middle_bytes(lines, rows, width, padded) <= vmem_bytes
    if fits:
        grad_middle, gain_two_term, grad_gate_up, down_part, normed_two, result_parts = middle_part(
            lines, (gains, cot_all, w_down, normed_two, middle, w_columns), padded
        )
    else:
        cot_all = cot_all.reshape(length, width)
        normed_two = lax.all_gather(normed_two, "ctx", axis=0, tiled=True)
        w_gate_up = lax.all_gather(w_columns, "fsdp", axis=0, tiled=True)
        projected = jnp.dot(normed_two, w_gate_up, preferred_element_type=f32)
        gelu, slope = gelu_parts(projected[:, :padded])
        up_part = projected[:, padded:]
        hidden = (gelu * up_part).astype(bf16)
        grad_hidden = contract_rows(cot_all, w_down)
        grad_gate_up = jnp.concatenate(
            [grad_hidden * up_part * slope, grad_hidden * gelu], axis=1
        ).astype(bf16)
        grad_normed_two = lax.psum_scatter(
            contract_rows(grad_gate_up, w_gate_up).astype(bf16),
            "ctx",
            scatter_dimension=0,
            tiled=True,
        ).astype(f32)
        grad_middle_norm, gain_two_term = norm_back(middle, norm_two[None], grad_normed_two)
        grad_middle = cot_rows.astype(f32) + grad_middle_norm
        result_parts = jnp.dot(hidden, w_down, preferred_element_type=f32).astype(bf16)
        down_part = lax.psum_scatter(
            contract_tokens(hidden, cot_all).astype(bf16),
            "fsdp",
            scatter_dimension=1,
            tiled=True,
        ).reshape(fsdp_size, padded_piece, -1)
    operands = (
        grad_middle,
        tokens[0],
        gains,
        cosine,
        sine,
        out_weight,
        weights,
        window,
        queries,
        mixed,
        query_weight,
        keyval_weight,
        down_part,
    )
    if fits:
        result, input_grad, gain_one_term, grad_linear, out_parts, down_grad = back(
            lines, operands, (middle, result_parts)
        )
    else:
        input_grad, gain_one_term, grad_linear, out_parts, down_grad = back(lines, operands, ())
        branch_two = lax.psum_scatter(result_parts, "ctx", scatter_dimension=0, tiled=True)
        result = (middle + branch_two.astype(f32)).astype(bf16)

    operands = (gain_one_term, gain_two_term, out_parts, normed, grad_linear)
    if fits:
        projection_grad, gain_grads, out_grad, gate_up_part = weight_grads(
            lines, operands, (normed_two, grad_gate_up)
        )
    else:
        projection_grad, gain_grads, out_grad = weight_grads(lines, operands, ())
        gate_up_part = lax.psum_scatter(
            contract_tokens(normed_two, grad_gate_up).astype(bf16),
            "fsdp",
            scatter_dimension=1,
            tiled=True,
        )
        gate_up_part = lax.all_to_all(
            gate_up_part.reshape(ctx_size, width // ctx_size, -1), "ctx", 0, 0, tiled=True
        )
    query_grad, keyval_grad, out_grad, down_grad, gate_up_grad = assemble(
        lines, piece, projection_grad, out_grad, down_grad, gate_up_part
    )
    share = width // (ctx_size * fsdp_size)
    gains = lax.dynamic_slice_in_dim(gain_grads, lax.axis_index("fsdp") * share, share, 1)
    return (
        result[None],
        input_grad[None],
        gains[0],
        query_grad,
        keyval_grad,
        out_grad,
        gains[1],
        gate_up_grad,
        down_grad,
    )


def solution(mesh):
    placed = (
        P("fsdp", "ctx", None),
        P("fsdp", None),
        P("fsdp", "ctx", None),
        P(),
        P("fsdp", None),
        P("fsdp", None),
        P("fsdp", None),
        P(),
        P("fsdp", None),
        P("fsdp", None),
    )
    return jax.shard_map(
        per_device,
        mesh=mesh,
        in_specs=placed,
        out_specs=(
            P("fsdp", "ctx", None),
            P("fsdp", "ctx", None),
            P(("ctx", "fsdp")),
            P("ctx", "fsdp"),
            P("ctx", "fsdp"),
            P("ctx", "fsdp"),
            P(("ctx", "fsdp")),
            P("ctx", "fsdp"),
            P("ctx", "fsdp"),
        ),
        check_vma=False,
    )
```
